32 devices in a mesh: dp: 8 (over z, x), head: 4 (over y, core).
Axes of the slice: x: 2, y: 2, z: 4, core: 2. Of those that a mesh axis runs over, the one named last changes fastest.
Arguments:
- tokens: bfloat16 [16384, 1536], P('dp', 'head'), may hold values from -6 to 6
- cotangent: bfloat16 [16384, 1536], P('dp', 'head'), may hold values from -6 to 6
- order: int32 [8, 2048], P('dp'), may hold values from 0 to 2047, each once within a row
- lengths: int32 [16], P('dp'), may hold values from 128 to 1024, as said below
- norm_gain: bfloat16 [1536], P('dp'), may hold values from 0.5 to 1.5
- w_zx: bfloat16 [1536, 2, 3072], P('dp', None, 'head'), may hold values from -0.15625 to 0.15625
- w_bc: bfloat16 [1536, 256], P('dp'), may hold values from -0.15625 to 0.15625
- w_dt: bfloat16 [1536, 48], P('dp', 'head'), may hold values from -0.15625 to 0.15625
- w_out: bfloat16 [1536, 3072], P('dp', 'head'), may hold values from -0.109375 to 0.109375
- conv_x: float32 [5, 3072], P(None, 'head'), may hold values from -0.5 to 0.5
- conv_bc: float32 [5, 256], replicated, may hold values from -0.5 to 0.5
- head_params: float32 [3, 48], P(None, 'head'), may hold values from -8 to 3
- gate_gain: float32 [3072], P('head'), may hold values from 0.5 to 1.5
Outputs:
- block_output: bfloat16 [16384, 1536], P('dp', 'head')
- input_grad: bfloat16 [16384, 1536], P('dp', 'head')
- norm_gain_grad: float32 [1536], P('dp')
- w_zx_grad: float32 [1536, 2, 3072], P('dp', None, 'head')
- w_bc_grad: float32 [1536, 256], P('dp')
- w_dt_grad: float32 [1536, 48], P('dp', 'head')
- w_out_grad: float32 [1536, 3072], P('dp', 'head')
- conv_x_grad: float32 [5, 3072], P(None, 'head')
- conv_bc_grad: float32 [5, 256], replicated
- head_params_grad: float32 [3, 48], P(None, 'head')
- gate_gain_grad: float32 [3072], P('head')
The draws below stay inside these ranges and needn't reach their ends.
Inputs may be any that keep to these rules, and one draw needn't show every extreme that they name: Each row of order is a permutation of 0 to 2047. `lengths`: rows of a slot at or past its length are padding.
All inputs are finite; a program needn't handle non-finite values.
Results may differ from the reference program's by a relative error of at most 0.0076.
Values may be sent and summed in bfloat16 or wider, within the bound.
A program may use at most 320 MiB of HBM per device.

```python
import math
import jax
import jax.numpy as jnp
from jax import lax

D = 1536
E = 3072
H = 48
N = 128
K = 4
Q = 256
LEN = 1024
ROWS_DEV = 2048
SEQS = 16
TOKENS = 16384
N_DP = 8


def draw_lengths(key, part):
    key = jax.random.fold_in(key, 11)
    first_key, second_key = jax.random.split(key)
    values = jax.random.randint(first_key, (SEQS,), LEN // 8, LEN + 1)
    chosen = jax.random.randint(second_key, (), 0, SEQS)
    return jnp.where(jnp.arange(SEQS) == chosen, LEN, values).astype(jnp.int32)


def draw_head_params(key, part):
    key = jax.random.fold_in(key, 23)
    step_key, rate_key, skip_key = jax.random.split(key, 3)
    lowest, upper = (math.log(0.001), math.log(0.1))
    steps = jnp.exp(jax.random.uniform(step_key, (H,), jnp.float32, lowest, upper))
    bias = jnp.log(jnp.expm1(steps))
    rate_logs = jax.random.uniform(rate_key, (H,), jnp.float32, 0.0, math.log(16.0))
    skips = jax.random.uniform(skip_key, (H,), jnp.float32, 0.5, 1.5)
    return jnp.stack([bias, rate_logs, skips]).astype(jnp.float32)


def levels(key, shape, cuts, smallest, largest):
    loudness, own = 1.0, jax.random.fold_in(key, 6)
    for position, blocks in cuts:
        draws = jnp.exp(jax.random.uniform(jax.random.fold_in(own, position), (blocks,), jnp.float32, smallest / len(cuts), largest / len(cuts)))
        loudness = loudness * jnp.repeat(draws, shape[position] // blocks).reshape([-1 if axis == position else 1 for axis in range(len(shape))])
    return loudness


def centred(stream_key, extent, deviation, most, pieces=(), kind=jnp.bfloat16):
    array = deviation * jax.random.normal(stream_key, extent, jnp.float32)
    if pieces:
        array = array * levels(stream_key, extent, pieces, -0.22, 0.18)
    return jnp.clip(array, -most, most).astype(kind)


def setup_inputs(seed: int = 0) -> dict:
    keys = jax.random.split(jax.random.key(seed), 14)
    return {
        "tokens": centred(keys[0], (TOKENS, D), 1.0, 6.0, ((0, 8), (1, 4))),
        "cotangent": centred(keys[1], (TOKENS, D), 1.0, 6.0, ((0, 8), (1, 4))),
        "order": jax.vmap(lambda own: jax.random.permutation(own, ROWS_DEV))(jax.random.split(keys[2], N_DP)).reshape((N_DP, ROWS_DEV)).astype(jnp.int32),
        "lengths": draw_lengths(jax.random.fold_in(keys[13], 71), 0),
        "norm_gain": jnp.clip(1.0 + 0.1 * jax.random.normal(keys[4], (D,), jnp.float32), 0.5, 1.5).astype(jnp.bfloat16),
        "w_zx": centred(keys[5], (D, 2, E), D ** -0.5, 0.15625, ((0, 8), (2, 4))),
        "w_bc": centred(keys[6], (D, 2 * N), D ** -0.5, 0.15625, ((0, 8),)),
        "w_dt": centred(keys[7], (D, H), D ** -0.5, 0.15625, ((0, 8), (1, 4))),
        "w_out": centred(keys[8], (D, E), E ** -0.5, 0.109375, ((0, 8), (1, 4))),
        "conv_x": jnp.clip(jax.random.uniform(keys[9], (K + 1, E), jnp.float32, -0.5, 0.5) * levels(keys[9], (K + 1, E), ((1, 4),), -0.4, 0.0), -0.5, 0.5),
        "conv_bc": jnp.clip(jax.random.uniform(keys[10], (K + 1, 2 * N), jnp.float32, -0.5, 0.5), -0.5, 0.5),
        "head_params": draw_head_params(jax.random.fold_in(keys[13], 71), 0),
        "gate_gain": jnp.clip(1.0 + 0.1 * jax.random.normal(keys[12], (E,), jnp.float32), 0.5, 1.5),
    }


epsilon = 1e-05
highest = lax.Precision.HIGHEST

@jax.custom_vjp
def low(v):
    return lax.optimization_barrier(v.astype(jnp.bfloat16)).astype(jnp.float32)

@jax.custom_vjp
def low_back(v):
    return v

def low_keep(v):
    return (low(v), None)

def low_pass(kept, grad):
    return (grad,)

def back_keep(v):
    return (v, None)

def back_low(kept, grad):
    return (low(grad),)
low.defvjp(low_keep, low_pass)
low_back.defvjp(back_keep, back_low)

def causal_conv(values, taps):
    width = taps.shape[0] - 1
    length = values.shape[0]
    padded = jnp.pad(values, ((width - 1, 0), (0, 0)))
    total = taps[width] + jnp.zeros_like(values)
    for offset in range(width):
        total = total + taps[offset] * padded[offset:offset + length]
    return total

def group_scan(inputs, b_rows, c_rows, steps, rates):
    length, heads, head_dim = inputs.shape
    blocks = length // Q
    x_blocks = inputs.reshape(blocks, Q, heads, head_dim)
    b_blocks = b_rows.reshape(blocks, Q, -1)
    c_blocks = c_rows.reshape(blocks, Q, -1)
    step_blocks = steps.reshape(blocks, Q, heads)
    logs = jnp.cumsum(step_blocks * rates, axis=1)
    causal = (lax.broadcasted_iota(jnp.int32, (Q, Q), 0) >= lax.broadcasted_iota(jnp.int32, (Q, Q), 1))[None, :, :, None]
    gaps = logs[:, :, None, :] - logs[:, None, :, :]
    decays = jnp.where(causal, jnp.exp(jnp.where(causal, gaps, 0.0)), 0.0)
    scores = jnp.einsum('bin,bjn->bij', c_blocks, b_blocks, precision=highest)
    kernel = scores[:, :, :, None] * decays * step_blocks[:, None, :, :]
    inner = jnp.einsum('bijh,bjhp->bihp', kernel, x_blocks, precision=highest)
    tails = jnp.exp(logs[:, -1:, :] - logs) * step_blocks
    states = jnp.einsum('bjn,bjh,bjhp->bhpn', b_blocks, tails, x_blocks, precision=highest)

    def advance(state, pair):
        factor, fresh = pair
        return (state * factor[:, None, None] + fresh, state)
    start = jnp.zeros(states.shape[1:], states.dtype)
    closing, entering = lax.scan(advance, start, (jnp.exp(logs[:, -1, :]), states))
    outer = jnp.einsum('bin,bih,bhpn->bihp', c_blocks, jnp.exp(logs), entering, precision=highest)
    return (inner + outer).reshape(length, heads, head_dim)

def mamba_core(u_x, u_bc, u_dt, gate_z, conv_x, conv_bc, head_params):
    length, heads = u_dt.shape
    x_conv = jax.nn.silu(causal_conv(u_x, conv_x))
    bc_conv = jax.nn.silu(causal_conv(u_bc, conv_bc))
    state_dim = bc_conv.shape[1] // 2
    steps = jax.nn.softplus(u_dt + head_params[0])
    rates = -jnp.exp(head_params[1])
    x_heads = x_conv.reshape(length, heads, -1)
    scanned = group_scan(x_heads, bc_conv[:, :state_dim], bc_conv[:, state_dim:], steps, rates)
    scanned = scanned + head_params[2][None, :, None] * x_heads
    return scanned.reshape(length, -1) * jax.nn.silu(gate_z)

def reference(tokens, cotangent, order, lengths, norm_gain, w_zx, w_bc, w_dt, w_out, conv_x, conv_bc, head_params, gate_gain):
    piece = ROWS_DEV // N_DP
    target = jnp.arange(N_DP, dtype=jnp.int32)[:, None]
    source = (order // piece * ROWS_DEV + target * piece + order % piece).reshape(-1).astype(jnp.int32)
    x_rows = tokens.astype(jnp.float32)[source]
    grad_rows = cotangent.astype(jnp.float32)[source]
    padding = (jnp.arange(LEN, dtype=jnp.int32)[None, :] < lengths[:, None]).astype(jnp.float32)
    params = (norm_gain.astype(jnp.float32), w_zx.astype(jnp.float32), w_bc.astype(jnp.float32), w_dt.astype(jnp.float32), w_out.astype(jnp.float32), conv_x.astype(jnp.float32), conv_bc.astype(jnp.float32), head_params.astype(jnp.float32), gate_gain.astype(jnp.float32))

    def forward(inputs, weights):
        gain_one, proj_zx, proj_bc, proj_dt, proj_out, taps_x, taps_bc, per_head, gain_two = weights
        inv_one = lax.rsqrt(lax.optimization_barrier(jnp.mean(inputs * inputs, axis=1, keepdims=True)) + epsilon)
        normed = low(inputs * inv_one * gain_one)
        u_zx = low_back(jnp.einsum('rd,dke->rke', normed, proj_zx, precision=highest))
        u_bc = low_back(jnp.dot(normed, proj_bc, precision=highest))
        u_dt = low_back(jnp.dot(normed, proj_dt, precision=highest))

        def one_slot(items):
            zx_slot, bc_slot, dt_slot, mask_slot = items
            mixed = mamba_core(zx_slot[:, 1], bc_slot, dt_slot, zx_slot[:, 0], taps_x, taps_bc, per_head)
            inv_two = lax.rsqrt(lax.optimization_barrier(jnp.mean(mixed * mixed, axis=1, keepdims=True)) + epsilon)
            return mixed * inv_two * gain_two * mask_slot[:, None]
        gated = lax.map(jax.checkpoint(one_slot), (u_zx.reshape(SEQS, LEN, 2, E), u_bc.reshape(SEQS, LEN, 2 * N), u_dt.reshape(SEQS, LEN, H), padding))
        gated = low(gated.reshape(-1, E))
        return inputs + jnp.dot(gated, proj_out.T, precision=highest)
    result, pullback = jax.vjp(forward, x_rows, params)
    grad_inputs, grad_params = pullback(grad_rows)
    block_output = jnp.zeros_like(tokens).at[source].set(result.astype(jnp.bfloat16))
    input_grad = jnp.zeros_like(tokens).at[source].set(grad_inputs.astype(jnp.bfloat16))
    return (block_output, input_grad, grad_params[0], grad_params[1], grad_params[2], grad_params[3], grad_params[4], grad_params[5], grad_params[6], grad_params[7], grad_params[8])
```

```python
import functools

import jax
import jax.numpy as jnp
from jax import lax
from jax.experimental import pallas as pl
from jax.experimental.pallas import tpu as pltpu
from jax.sharding import PartitionSpec as P

LEN = 1024
T = 128
N = 128
HEAD = 64
EPS = 1e-05
NEG = -1e30
F32 = jnp.float32
BF16 = jnp.bfloat16


def dot(a, b):
    return lax.dot_general(a, b, (((1,), (0,)), ((), ())), preferred_element_type=F32)


def dot_nt(a, b):
    return lax.dot_general(a, b, (((1,), (1,)), ((), ())), preferred_element_type=F32)


def dot_exact(a, b):
    return lax.dot_general(
        a, b, (((1,), (0,)), ((), ())), preferred_element_type=F32, precision=lax.Precision.HIGHEST
    )


def iotas(rows, cols):
    return (
        lax.broadcasted_iota(jnp.int32, (rows, cols), 0),
        lax.broadcasted_iota(jnp.int32, (rows, cols), 1),
    )


def sigmoid(v):
    return 1.0 / (1.0 + jnp.exp(-v))


def softplus(v):
    return jnp.maximum(v, 0.0) + jnp.log1p(jnp.exp(-jnp.abs(v)))


def to_col(row):
    return jnp.broadcast_to(row, (T, T)).T


def to_row(col):
    return jnp.broadcast_to(col, (T, T)).T[0:1]


def lanes(value, pick):
    return jnp.broadcast_to(value[:, pick : pick + 1], (value.shape[0], 128))


def step_terms(ubd, head_ref, heads):
    row, col = iotas(T, T)
    raw = jnp.where(col < heads, ubd[:, 2 * N :] + head_ref[0:1], 0.0)
    steps = jnp.where(col < heads, softplus(raw), 0.0)
    rates = -jnp.exp(head_ref[1:2])
    tril = (row >= col).astype(F32)
    logs = dot_exact(tril, steps * rates)
    return raw, steps, rates, logs


def forward_kernel(heads, x_ref, z_ref, ubd_ref, par_ref, pbc_ref, head_ref, y_ref, ss_ref, c_ref, cb_ref, st_ref, ext_x, ext_b, state):
    @pl.when(pl.program_id(1) == 0)
    def _():
        ext_x[0:8] = jnp.zeros_like(ext_x[0:8])
        ext_b[0:8] = jnp.zeros_like(ext_b[0:8])
        state[...] = jnp.zeros_like(state)

    def conv(ext, values, taps):
        ext[8 : 8 + T] = values
        total = taps[4:5] + taps[3:4] * values
        for k in range(3):
            total = total + taps[k : k + 1] * ext[5 + k : 5 + k + T]
        ext[0:8] = ext[T : T + 8]
        return total

    row, col = iotas(T, T)
    low = col < HEAD
    low_row = lax.broadcasted_iota(jnp.int32, (1, 128), 1) < HEAD
    causal = row >= col
    ubd = ubd_ref[...]
    c = conv(ext_x, x_ref[...].astype(F32), par_ref)
    c_ref[...] = c.astype(BF16)
    cb = conv(ext_b, ubd[:, : 2 * N], pbc_ref)
    cb_ref[...] = cb
    bc = cb * sigmoid(cb)
    b_rows = bc[:, :N]
    b_t = b_rows.T.astype(BF16)
    b_low, c_low = b_rows.astype(BF16), bc[:, N:].astype(BF16)
    _, steps, _, logs = step_terms(ubd, head_ref, heads)
    logs_t = logs.T
    scores = dot_nt(c_low, b_low)
    entering = state[...].astype(BF16)
    st_ref[0] = entering
    outer = dot(c_low, entering)
    squares = jnp.zeros((T, 128), F32)
    for pair in range(heads // 2):
        span = slice(128 * pair, 128 * pair + 128)
        h0, h1 = 2 * pair, 2 * pair + 1
        log0, log1 = lanes(logs, h0), lanes(logs, h1)
        log_pair = jnp.where(low, log0, log1)
        step_pair = jnp.where(low, lanes(steps, h0), lanes(steps, h1))
        last_pair = log_pair[T - 1 : T]
        cp = c[:, span]
        xp = cp * sigmoid(cp)
        xd = xp * step_pair
        m0 = (scores * jnp.exp(jnp.where(causal, log0 - logs_t[h0 : h0 + 1], NEG))).astype(BF16)
        m1 = (scores * jnp.exp(jnp.where(causal, log1 - logs_t[h1 : h1 + 1], NEG))).astype(BF16)
        stacked = jnp.concatenate([jnp.where(low, xd, 0.0).astype(BF16), jnp.where(low, 0.0, xd).astype(BF16)], axis=0)
        y = dot(jnp.concatenate([m0, m1], axis=1), stacked)
        y = y + jnp.exp(log_pair) * outer[:, span] + par_ref[5:6, span] * xp
        tail = (jnp.exp(last_pair - log_pair) * xd).astype(BF16)
        state[:, span] = jnp.exp(last_pair) * state[:, span] + dot(b_t, tail)
        y_ref[:, span] = y.astype(BF16)
        zp = z_ref[:, span].astype(F32)
        w = y * zp * sigmoid(zp)
        squares = squares + w * w
    ss_ref[0] = to_row(jnp.sum(squares, axis=1, keepdims=True))


def gate_kernel(g_ref, wo_ref, y_ref, z_ref, par_ref, mask_ref, dyn_ref, co_ref):
    dyn = dot(g_ref[...], wo_ref[...])
    for part in range(dyn.shape[0] // T):
        rows = slice(part * T, part * T + T)
        mask = to_col(mask_ref[part])[:, 0:1]
        own = dyn[rows] * mask
        dyn_ref[rows] = own.astype(BF16)
        z = z_ref[rows].astype(F32)
        w = y_ref[rows].astype(F32) * z * sigmoid(z)
        co_ref[part] = to_row(jnp.sum(own * w * par_ref[6:7], axis=1, keepdims=True))


def mid_kernel(width, y_ref, z_ref, dyn_ref, par_ref, mask_ref, ss_ref, co_ref, yg_ref, dz_ref, dy_ref, gg_ref, rd_ref):
    @pl.when(pl.program_id(0) == 0)
    def _():
        gg_ref[...] = jnp.zeros_like(gg_ref)

    gain = par_ref[6:7]
    for part in range(y_ref.shape[0] // T):
        rows = slice(part * T, part * T + T)
        mask = to_col(mask_ref[part])[:, 0:1]
        inv_row = lax.rsqrt(ss_ref[part] / width + EPS)
        inv = to_col(inv_row)[:, 0:1]
        cube = to_col(inv_row * inv_row * inv_row * (co_ref[part] / width))[:, 0:1]
        y = y_ref[rows].astype(F32)
        z = z_ref[rows].astype(F32)
        dyn = dyn_ref[rows].astype(F32)
        s = sigmoid(z)
        act = z * s
        w = y * act
        wi = w * inv
        yg_ref[rows] = (wi * gain * mask).astype(BF16)
        gg_ref[0:1] += jnp.sum(dyn * wi, axis=0, keepdims=True)
        dw = inv * gain * dyn - w * cube
        dy_ref[rows] = (dw * act).astype(BF16)
        dz = dw * y * (s * (1.0 + z * (1.0 - s)))
        dz_ref[rows] = dz.astype(BF16)
        rd_ref[part] = to_row(jnp.sum(dz * z, axis=1, keepdims=True))


def backward_kernel(heads, dy_ref, x_ref, c_ref, cb_ref, ubd_ref, st_ref, par_ref, pbc_ref, head_ref, dx_ref, dbd_ref, gx_ref, gb_ref, gh_ref, rd_ref, d_state, ext_x, ext_b, rows_ref, prod, edy_ref, tail_ref):
    first = (pl.program_id(0) == 0) & (pl.program_id(1) == 0)

    @pl.when(first)
    def _():
        gx_ref[...] = jnp.zeros_like(gx_ref)
        gb_ref[...] = jnp.zeros_like(gb_ref)
        gh_ref[...] = jnp.zeros_like(gh_ref)
        rows_ref[...] = jnp.zeros_like(rows_ref)

    @pl.when(pl.program_id(1) == 0)
    def _():
        ext_x[T : T + 8] = jnp.zeros_like(ext_x[T : T + 8])
        ext_b[T : T + 8] = jnp.zeros_like(ext_b[T : T + 8])
        d_state[...] = jnp.zeros_like(d_state)

    row, col = iotas(T, T)
    low = col < HEAD
    upto = col >= row
    below = row < col
    reach = (row >= col).astype(BF16)
    ubd = ubd_ref[...]
    raw, steps, rates, logs = step_terms(ubd, head_ref, heads)
    logs_t = logs.T
    cb = cb_ref[...]
    sb = sigmoid(cb)
    bc = cb * sb
    b_low, c_low = bc[:, :N].astype(BF16), bc[:, N:].astype(BF16)
    c_t = bc[:, N:].T.astype(BF16)
    scores = dot_nt(b_low, c_low)
    entering = st_ref[0]
    outer = dot(c_low, entering)
    ds_low = d_state[...].astype(BF16)
    back = dot(b_low, ds_low)
    d_scores = jnp.zeros((T, T), F32)
    skip_parts, closing_parts = [], []
    for pair in range(heads // 2):
        span = slice(128 * pair, 128 * pair + 128)
        h0, h1 = 2 * pair, 2 * pair + 1
        log0, log1 = lanes(logs, h0), lanes(logs, h1)
        log_pair = jnp.where(low, log0, log1)
        step_pair = jnp.where(low, lanes(steps, h0), lanes(steps, h1))
        last_pair = log_pair[T - 1 : T]
        cp = c_ref[:, span].astype(F32)
        sp = sigmoid(cp)
        xp = cp * sp
        xd = xp * step_pair
        dy_low = dy_ref[:, span]
        dy = dy_low.astype(F32)
        decay0 = jnp.exp(jnp.where(upto, logs_t[h0 : h0 + 1] - log0, NEG))
        decay1 = jnp.exp(jnp.where(upto, logs_t[h1 : h1 + 1] - log1, NEG))
        m0, m1 = scores * decay0, scores * decay1
        zero = jnp.zeros_like(dy_low)
        x_stack = jnp.concatenate([jnp.where(low, xd, 0.0).astype(BF16), jnp.where(low, 0.0, xd).astype(BF16)], axis=0)
        dm = dot_nt(x_stack, dy_low)
        dm0, dm1 = dm[:T], dm[T:]
        d_scores = d_scores + dm0 * decay0 + dm1 * decay1
        dy_stack = jnp.concatenate([jnp.where(low, dy, 0.0).astype(BF16), jnp.where(low, 0.0, dy).astype(BF16)], axis=0)
        dxd = dot(jnp.concatenate([m0.astype(BF16), m1.astype(BF16)], axis=1), dy_stack)
        flow = jnp.concatenate([(dm0 * m0).astype(BF16), (dm1 * m1).astype(BF16)], axis=0)
        later = dot(flow, reach)
        rows_ref[h0 : h0 + 1] = jnp.sum(jnp.where(below, later[:T], 0.0), axis=0, keepdims=True)
        rows_ref[h1 : h1 + 1] = jnp.sum(jnp.where(below, later[T:], 0.0), axis=0, keepdims=True)
        grow = jnp.exp(log_pair)
        tail = jnp.exp(last_pair - log_pair)
        from_state = tail * back[:, span]
        dxd = dxd + from_state
        edy = grow * dy
        prod[0:T, span] = (edy * outer[:, span]).astype(BF16)
        prod[T : 2 * T, span] = (from_state * xd).astype(BF16)
        prod[2 * T : 3 * T, span] = (xp * dxd).astype(BF16)
        skip_parts.append(jnp.sum(xp * dy, axis=0, keepdims=True))
        edy_low = edy.astype(BF16)
        edy_ref[:, span] = edy_low
        tail_ref[:, span] = (tail * xd).astype(BF16)
        old = d_state[:, span]
        closing = jnp.exp(last_pair)
        closing_parts.append(closing * jnp.sum(old * entering[:, span].astype(F32), axis=0, keepdims=True))
        d_state[:, span] = closing * old + dot(c_t, edy_low)
        dx = dxd * step_pair + par_ref[5:6, span] * dy
        ext_x[0:T, span] = dx * (sp * (1.0 + cp * (1.0 - sp)))
    d_low = d_scores.astype(BF16)
    d_b = dot_nt(tail_ref[...], ds_low) + dot(d_low, c_low)
    d_c = dot_nt(edy_ref[...], entering) + dot(d_scores.T.astype(BF16), b_low)
    width = heads * HEAD
    lane_row, lane_col = iotas(width, 128)
    member = (lane_row // HEAD == lane_col).astype(BF16)
    sums = dot(prod[...], member)
    skip_all = jnp.concatenate(skip_parts, axis=1)
    closing_all = jnp.concatenate(closing_parts, axis=1)
    fill = jnp.zeros((6, width), F32)
    few = dot_exact(jnp.concatenate([skip_all, closing_all, fill], axis=0), member.astype(F32))
    d_logs = dot(upto.astype(BF16), sums[:T].astype(BF16)) + dot((col < row).astype(BF16), sums[T : 2 * T].astype(BF16))
    d_logs = d_logs + rows_ref[...].T + few[1:2]
    d_steps = sums[2 * T :] + rates * d_logs
    d_raw = jnp.where(col < heads, d_steps * sigmoid(raw), 0.0)
    gh_ref[0:1] += jnp.sum(d_raw, axis=0, keepdims=True)
    gh_ref[1:2] += rates * jnp.sum(steps * d_logs, axis=0, keepdims=True)
    gh_ref[2:3] += few[0:1]
    ext_b[0:T, 0:N] = d_b * (sb[:, :N] * (1.0 + cb[:, :N] * (1.0 - sb[:, :N])))
    ext_b[0:T, N:] = d_c * (sb[:, N:] * (1.0 + cb[:, N:] * (1.0 - sb[:, N:])))

    def conv_back(ext, values, taps, grads):
        now = ext[0:T]
        total = taps[3:4] * now
        grads[3:4] += jnp.sum(values * now, axis=0, keepdims=True)
        grads[4:5] += jnp.sum(now, axis=0, keepdims=True)
        for k in range(3):
            moved = ext[3 - k : 3 - k + T]
            total = total + taps[k : k + 1] * moved
            grads[k : k + 1] += jnp.sum(values * moved, axis=0, keepdims=True)
        ext[T : T + 8] = ext[0:8]
        return total

    ux = x_ref[...].astype(F32)
    dux = conv_back(ext_x, ux, par_ref, gx_ref)
    dx_ref[...] = dux.astype(BF16)
    ubc = ubd[:, : 2 * N]
    dubc = conv_back(ext_b, ubc, pbc_ref, gb_ref)
    dbd_ref[:, : 2 * N] = dubc.astype(BF16)
    dbd_ref[:, 2 * N :] = d_raw.astype(BF16)
    total = jnp.sum(dux * ux, axis=1, keepdims=True) + jnp.sum(dubc * ubc, axis=1, keepdims=True)
    total = total + jnp.sum(jnp.where(col < heads, d_raw * ubd[:, 2 * N :], 0.0), axis=1, keepdims=True)
    rd_ref[0] = to_row(total)


def params(*semantics):
    return pltpu.CompilerParams(dimension_semantics=semantics, vmem_limit_bytes=56 * 1024 * 1024)


def run_forward(heads, u_zx, u_bd, par, pbc, hp):
    rows, width = u_zx.shape[0], heads * HEAD
    slots, chunks = rows // LEN, LEN // T
    at = lambda s, i: (s * chunks + i, 0)
    fixed = lambda s, i: (0, 0)
    return pl.pallas_call(
        functools.partial(forward_kernel, heads),
        grid=(slots, chunks),
        in_specs=[
            pl.BlockSpec((T, width), lambda s, i: (s * chunks + i, 1)),
            pl.BlockSpec((T, width), at),
            pl.BlockSpec((T, 3 * N), at),
            pl.BlockSpec((8, width), fixed),
            pl.BlockSpec((8, 2 * N), fixed),
            pl.BlockSpec((8, 128), fixed),
        ],
        out_specs=[
            pl.BlockSpec((T, width), at),
            pl.BlockSpec((1, 1, T), lambda s, i: (s * chunks + i, 0, 0)),
            pl.BlockSpec((T, width), at),
            pl.BlockSpec((T, 2 * N), at),
            pl.BlockSpec((1, N, width), lambda s, i: (s * chunks + i, 0, 0)),
        ],
        out_shape=[
            jax.ShapeDtypeStruct((rows, width), BF16),
            jax.ShapeDtypeStruct((rows // T, 1, T), F32),
            jax.ShapeDtypeStruct((rows, width), BF16),
            jax.ShapeDtypeStruct((rows, 2 * N), F32),
            jax.ShapeDtypeStruct((rows // T, N, width), BF16),
        ],
        scratch_shapes=[pltpu.VMEM((T + 8, width), F32), pltpu.VMEM((T + 8, 2 * N), F32), pltpu.VMEM((N, width), F32)],
        compiler_params=params("arbitrary", "arbitrary"),
        cost_estimate=pl.CostEstimate(flops=rows * width * 2 * 1200, bytes_accessed=rows * width * 8, transcendentals=rows * width * 6),
        name="scan_forward",
    )(u_zx, u_zx, u_bd, par, pbc, hp)


def run_gate(full_grad, w_out, y, u_zx, par, mask):
    rows, width = y.shape
    deep = full_grad.shape[1]
    step = 256
    at = lambda i: (i, 0)
    fixed = lambda i: (0, 0)
    thin = pl.BlockSpec((step // T, 1, T), lambda i: (i, 0, 0))
    return pl.pallas_call(
        gate_kernel,
        grid=(rows // step,),
        in_specs=[
            pl.BlockSpec((step, deep), at),
            pl.BlockSpec((deep, width), fixed),
            pl.BlockSpec((step, width), at),
            pl.BlockSpec((step, width), at),
            pl.BlockSpec((8, width), fixed),
            thin,
        ],
        out_specs=[pl.BlockSpec((step, width), at), thin],
        out_shape=[jax.ShapeDtypeStruct((rows, width), BF16), jax.ShapeDtypeStruct((rows // T, 1, T), F32)],
        compiler_params=params("arbitrary"),
        cost_estimate=pl.CostEstimate(flops=rows * width * deep * 2, bytes_accessed=rows * (width * 6 + deep * 2), transcendentals=rows * width),
        name="gate_back",
    )(full_grad, w_out, y, u_zx, par, mask)


def run_mid(all_width, y, u_zx, dyn, par, mask, ss, co):
    rows, width = y.shape
    step = 256
    at = lambda i: (i, 0)
    fixed = lambda i: (0, 0)
    thin = pl.BlockSpec((step // T, 1, T), lambda i: (i, 0, 0))
    wide = pl.BlockSpec((step, width), at)
    return pl.pallas_call(
        functools.partial(mid_kernel, float(all_width)),
        grid=(rows // step,),
        in_specs=[wide, wide, wide, pl.BlockSpec((8, width), fixed), thin, thin, thin],
        out_specs=[wide, wide, wide, pl.BlockSpec((8, width), fixed), thin],
        out_shape=[jax.ShapeDtypeStruct((rows, width), BF16)] * 3
        + [jax.ShapeDtypeStruct((8, width), F32), jax.ShapeDtypeStruct((rows // T, 1, T), F32)],
        compiler_params=params("arbitrary"),
        cost_estimate=pl.CostEstimate(flops=rows * width * 30, bytes_accessed=rows * width * 12, transcendentals=rows * width),
        name="gate_mid",
    )(y, u_zx, dyn, par, mask, ss, co)


def run_backward(heads, dy, u_zx, c, cb, u_bd, st, par, pbc, hp):
    rows, width = dy.shape
    slots, chunks = rows // LEN, LEN // T
    place = lambda s, i: s * chunks + chunks - 1 - i
    at = lambda s, i: (place(s, i), 0)
    at3 = lambda s, i: (place(s, i), 0, 0)
    fixed = lambda s, i: (0, 0)
    return pl.pallas_call(
        functools.partial(backward_kernel, heads),
        grid=(slots, chunks),
        in_specs=[
            pl.BlockSpec((T, width), at),
            pl.BlockSpec((T, width), lambda s, i: (place(s, i), 1)),
            pl.BlockSpec((T, width), at),
            pl.BlockSpec((T, 2 * N), at),
            pl.BlockSpec((T, 3 * N), at),
            pl.BlockSpec((1, N, width), at3),
            pl.BlockSpec((8, width), fixed),
            pl.BlockSpec((8, 2 * N), fixed),
            pl.BlockSpec((8, 128), fixed),
        ],
        out_specs=[
            pl.BlockSpec((T, width), at),
            pl.BlockSpec((T, 3 * N), at),
            pl.BlockSpec((8, width), fixed),
            pl.BlockSpec((8, 2 * N), fixed),
            pl.BlockSpec((8, 128), fixed),
            pl.BlockSpec((1, 1, T), at3),
        ],
        out_shape=[
            jax.ShapeDtypeStruct((rows, width), BF16),
            jax.ShapeDtypeStruct((rows, 3 * N), BF16),
            jax.ShapeDtypeStruct((8, width), F32),
            jax.ShapeDtypeStruct((8, 2 * N), F32),
            jax.ShapeDtypeStruct((8, 128), F32),
            jax.ShapeDtypeStruct((rows // T, 1, T), F32),
        ],
        scratch_shapes=[
            pltpu.VMEM((N, width), F32),
            pltpu.VMEM((T + 8, width), F32),
            pltpu.VMEM((T + 8, 2 * N), F32),
            pltpu.VMEM((128, 128), F32),
            pltpu.VMEM((3 * T, width), BF16),
            pltpu.VMEM((T, width), BF16),
            pltpu.VMEM((T, width), BF16),
        ],
        compiler_params=params("arbitrary", "arbitrary"),
        cost_estimate=pl.CostEstimate(flops=rows * width * 2 * 3000, bytes_accessed=rows * width * 12, transcendentals=rows * width * 8),
        name="scan_backward",
    )(dy, u_zx, c, cb, u_bd, st, par, pbc, hp)


def mm(a, b, contract, kind):
    return lax.dot_general(a, b, (contract, ((), ())), preferred_element_type=F32).astype(kind)


def body(tokens, cotangent, order, lengths, norm_gain, w_zx, w_bc, w_dt, w_out, conv_x, conv_bc, head_params, gate_gain):
    rows, quarter = tokens.shape
    heads = head_params.shape[1]
    width = heads * HEAD
    place = lax.axis_index("head")
    groups = lax.axis_size("head")
    all_width = width * groups
    deep = quarter * groups
    arrange = order[0]

    arrived_x = lax.all_to_all(tokens, "dp", split_axis=0, concat_axis=0, tiled=True)
    own_x = arrived_x[arrange]
    own_w = w_zx.shape[0]
    packed = jnp.concatenate(
        [
            w_zx.reshape(own_w, 2 * width),
            w_bc,
            w_dt,
            norm_gain[:, None],
            jnp.zeros((own_w, 127 - heads), BF16),
        ],
        axis=1,
    )
    w_in = lax.all_gather(packed, "dp", axis=0, tiled=True)
    full_x = lax.all_gather(own_x, "head", axis=1, tiled=True)
    arrived_g = lax.all_to_all(cotangent, "dp", split_axis=0, concat_axis=0, tiled=True)
    own_g = arrived_g[arrange]
    full_g = lax.all_gather(own_g, "head", axis=1, tiled=True)
    w_o = lax.all_gather(w_out, "dp", axis=0, tiled=True)

    gain = w_in[:, 2 * width + 2 * N + heads].astype(F32)
    xf = full_x.astype(F32)
    inv_one = lax.rsqrt(jnp.mean(xf * xf, axis=1, keepdims=True) + EPS)
    normed = (xf * inv_one * gain).astype(BF16)
    u_zx = mm(normed, w_in[:, : 2 * width], ((1,), (0,)), BF16)
    u_bd = mm(normed, w_in[:, 2 * width :], ((1,), (0,)), F32)

    par = jnp.concatenate([conv_x, jnp.repeat(head_params[2:3], HEAD, axis=1), gate_gain[None], jnp.zeros((1, width), F32)], axis=0)
    pbc = jnp.concatenate([conv_bc, jnp.zeros((3, 2 * N), F32)], axis=0)
    hp = jnp.pad(head_params, ((0, 5), (0, 128 - heads)))
    positions = lax.broadcasted_iota(jnp.int32, (lengths.shape[0], LEN), 1)
    mask = (positions < lengths[:, None]).astype(F32).reshape(rows // T, 1, T)

    y, ss, c, cb, st = run_forward(heads, u_zx, u_bd, par, pbc, hp)
    dyn, co = run_gate(full_g, w_o, y, u_zx, par, mask)
    ss, co = lax.psum((ss, co), "head")
    yg, dz, dy, gg, rd_z = run_mid(all_width, y, u_zx, dyn, par, mask, ss, co)

    branch = mm(yg, w_o, ((1,), (1,)), BF16)
    shares = lax.psum_scatter(branch, "head", scatter_dimension=1, tiled=True)
    grad_out = mm(full_g, yg, ((0,), (0,)), BF16)
    grad_out = lax.psum_scatter(grad_out, "dp", scatter_dimension=0, tiled=True)
    grad_z = mm(normed, dz, ((0,), (0,)), BF16)
    grad_z = lax.psum_scatter(grad_z, "dp", scatter_dimension=0, tiled=True)

    out_rows = (own_x.astype(F32) + shares.astype(F32)).astype(BF16)
    sent_out = jnp.zeros_like(out_rows).at[arrange].set(out_rows)
    final_out = lax.all_to_all(sent_out, "dp", split_axis=0, concat_axis=0, tiled=True)

    dux, dbd, gx, gb, gh, rd_x = run_backward(heads, dy, u_zx, c, cb, u_bd, st, par, pbc, hp)

    terms = mm(dz, w_in[:, :width], ((1,), (1,)), F32)
    terms = terms + mm(dux, w_in[:, width : 2 * width], ((1,), (1,)), F32)
    terms = terms + mm(dbd, w_in[:, 2 * width :], ((1,), (1,)), F32)
    dxn = lax.psum_scatter(terms.astype(BF16), "head", scatter_dimension=1, tiled=True).astype(F32)
    row_dot = lax.psum(rd_z + rd_x, "head").reshape(rows, 1)

    grad_x = mm(normed, dux, ((0,), (0,)), BF16)
    grad_x = lax.psum_scatter(grad_x, "dp", scatter_dimension=0, tiled=True)
    grad_bd = mm(normed, dbd, ((0,), (0,)), BF16)
    grad_bd = lax.psum_scatter(grad_bd, "dp", scatter_dimension=0, tiled=True).astype(F32)
    grad_bc = lax.psum(grad_bd[:, : 2 * N], "head")
    grad_dt = grad_bd[:, 2 * N : 2 * N + heads]

    gain_own = lax.dynamic_slice_in_dim(gain, place * quarter, quarter, 0)
    inv_own = inv_one
    xs = own_x.astype(F32)
    grad_rows = own_g.astype(F32) + inv_own * gain_own * dxn - xs * inv_own**2 * (row_dot / deep)
    grad_rows = grad_rows.astype(BF16)
    gain_part = jnp.sum(dxn * xs * inv_own, axis=0)
    sent_back = jnp.zeros_like(grad_rows).at[arrange].set(grad_rows)
    final_back = lax.all_to_all(sent_back, "dp", split_axis=0, concat_axis=0, tiled=True)

    gain_part = lax.dynamic_update_slice_in_dim(jnp.zeros((deep,), F32), gain_part, place * quarter, 0)
    gx, gh, gg = lax.psum((gx[:5], gh[:3, :heads], gg[0]), "dp")
    gain_all, gb = lax.psum((gain_part, gb[:5]), ("dp", "head"))
    own_d = norm_gain.shape[0]
    grad_gain = lax.dynamic_slice_in_dim(gain_all, lax.axis_index("dp") * own_d, own_d, 0)
    grad_zx = jnp.stack([grad_z, grad_x], axis=1).astype(F32)
    return (final_out, final_back, grad_gain, grad_zx, grad_bc, grad_dt, grad_out.astype(F32), gx, gb, gh, gg)


def solution(mesh):
    return jax.shard_map(
        body,
        mesh=mesh,
        in_specs=(
            P("dp", "head"),
            P("dp", "head"),
            P("dp", None),
            P("dp"),
            P("dp"),
            P("dp", None, "head"),
            P("dp", None),
            P("dp", "head"),
            P("dp", "head"),
            P(None, "head"),
            P(),
            P(None, "head"),
            P("head"),
        ),
        out_specs=(
            P("dp", "head"),
            P("dp", "head"),
            P("dp"),
            P("dp", None, "head"),
            P("dp", None),
            P("dp", "head"),
            P("dp", "head"),
            P(None, "head"),
            P(),
            P(None, "head"),
            P("head"),
        ),
        check_vma=False,
    )
```

```python
import functools

import jax
import jax.numpy as jnp
from jax import lax
from jax.experimental import pallas as pl
from jax.experimental.pallas import tpu as pltpu
from jax.sharding import PartitionSpec as P

LEN = 1024
T = 128
N = 128
HEAD = 64
EPS = 1e-05
NEG = -1e30
F32 = jnp.float32
BF16 = jnp.bfloat16


def dot(a, b):
    return lax.dot_general(a, b, (((1,), (0,)), ((), ())), preferred_element_type=F32)


def dot_nt(a, b):
    return lax.dot_general(a, b, (((1,), (1,)), ((), ())), preferred_element_type=F32)


def dot_exact(a, b):
    return lax.dot_general(
        a, b, (((1,), (0,)), ((), ())), preferred_element_type=F32, precision=lax.Precision.HIGHEST
    )


def iotas(rows, cols):
    return (
        lax.broadcasted_iota(jnp.int32, (rows, cols), 0),
        lax.broadcasted_iota(jnp.int32, (rows, cols), 1),
    )


def sigmoid(v):
    return 1.0 / (1.0 + jnp.exp(-v))


def softplus(v):
    return jnp.maximum(v, 0.0) + jnp.log1p(jnp.exp(-jnp.abs(v)))


def to_col(row):
    return jnp.broadcast_to(row, (T, T)).T


def to_row(col):
    return jnp.broadcast_to(col, (T, T)).T[0:1]


def lanes(value, pick):
    return jnp.broadcast_to(value[:, pick : pick + 1], (value.shape[0], 128))


def step_terms(ubd, head_ref, heads):
    row, col = iotas(T, T)
    raw = jnp.where(col < heads, ubd[:, 2 * N :] + head_ref[0:1], 0.0)
    steps = jnp.where(col < heads, softplus(raw), 0.0)
    rates = -jnp.exp(head_ref[1:2])
    tril = (row >= col).astype(F32)
    logs = dot_exact(tril, steps * rates)
    return raw, steps, rates, logs


def forward_kernel(heads, x_ref, z_ref, ubd_ref, par_ref, pbc_ref, head_ref, y_ref, ss_ref, c_ref, cb_ref, st_ref, ext_x, ext_b, state):
    @pl.when(pl.program_id(1) == 0)
    def _():
        ext_x[0:8] = jnp.zeros_like(ext_x[0:8])
        ext_b[0:8] = jnp.zeros_like(ext_b[0:8])
        state[...] = jnp.zeros_like(state)

    def conv(ext, values, taps):
        ext[8 : 8 + T] = values
        total = taps[4:5] + taps[3:4] * values
        for k in range(3):
            total = total + taps[k : k + 1] * ext[5 + k : 5 + k + T]
        ext[0:8] = ext[T : T + 8]
        return total

    row, col = iotas(T, T)
    low = col < HEAD
    low_row = lax.broadcasted_iota(jnp.int32, (1, 128), 1) < HEAD
    causal = row >= col
    ubd = ubd_ref[...]
    c = conv(ext_x, x_ref[...].astype(F32), par_ref)
    c_ref[...] = c.astype(BF16)
    cb = conv(ext_b, ubd[:, : 2 * N], pbc_ref)
    cb_ref[...] = cb
    bc = cb * sigmoid(cb)
    b_rows = bc[:, :N]
    b_t = b_rows.T.astype(BF16)
    b_low, c_low = b_rows.astype(BF16), bc[:, N:].astype(BF16)
    _, steps, _, logs = step_terms(ubd, head_ref, heads)
    logs_t = logs.T
    scores = dot_nt(c_low, b_low)
    entering = state[...].astype(BF16)
    st_ref[0] = entering
    outer = dot(c_low, entering)
    squares = jnp.zeros((T, 128), F32)
    for pair in range(heads // 2):
        span = slice(128 * pair, 128 * pair + 128)
        h0, h1 = 2 * pair, 2 * pair + 1
        log0, log1 = lanes(logs, h0), lanes(logs, h1)
        log_pair = jnp.where(low, log0, log1)
        step_pair = jnp.where(low, lanes(steps, h0), lanes(steps, h1))
        last_pair = log_pair[T - 1 : T]
        cp = c[:, span]
        xp = cp * sigmoid(cp)
        xd = xp * step_pair
        m0 = (scores * jnp.exp(jnp.where(causal, log0 - logs_t[h0 : h0 + 1], NEG))).astype(BF16)
        m1 = (scores * jnp.exp(jnp.where(causal, log1 - logs_t[h1 : h1 + 1], NEG))).astype(BF16)
        stacked = jnp.concatenate([jnp.where(low, xd, 0.0).astype(BF16), jnp.where(low, 0.0, xd).astype(BF16)], axis=0)
        y = dot(jnp.concatenate([m0, m1], axis=1), stacked)
        y = y + jnp.exp(log_pair) * outer[:, span] + par_ref[5:6, span] * xp
        tail = (jnp.exp(last_pair - log_pair) * xd).astype(BF16)
        state[:, span] = jnp.exp(last_pair) * state[:, span] + dot(b_t, tail)
        y_ref[:, span] = y.astype(BF16)
        zp = z_ref[:, span].astype(F32)
        w = y * zp * sigmoid(zp)
        squares = squares + w * w
    ss_ref[0] = to_row(jnp.sum(squares, axis=1, keepdims=True))


def norm_kernel(x_ref, gain_ref, out_ref, inv_ref):
    x = x_ref[...].astype(F32)
    inv = lax.rsqrt(jnp.sum(x * x, axis=1, keepdims=True) / x.shape[1] + EPS)
    out_ref[...] = (x * inv * gain_ref[0:1]).astype(BF16)
    for part in range(x.shape[0] // T):
        inv_ref[part] = to_row(inv[part * T : part * T + T])


def gate_kernel(g_ref, wo_ref, y_ref, z_ref, par_ref, mask_ref, dyn_ref, co_ref):
    dyn = dot(g_ref[...], wo_ref[...])
    for part in range(dyn.shape[0] // T):
        rows = slice(part * T, part * T + T)
        mask = to_col(mask_ref[part])[:, 0:1]
        own = dyn[rows] * mask
        dyn_ref[rows] = own.astype(BF16)
        z = z_ref[rows].astype(F32)
        w = y_ref[rows].astype(F32) * z * sigmoid(z)
        co_ref[part] = to_row(jnp.sum(own * w * par_ref[6:7], axis=1, keepdims=True))


def mid_kernel(width, y_ref, z_ref, dyn_ref, par_ref, mask_ref, ss_ref, co_ref, yg_ref, dz_ref, dy_ref, gg_ref, rd_ref):
    @pl.when(pl.program_id(0) == 0)
    def _():
        gg_ref[...] = jnp.zeros_like(gg_ref)

    gain = par_ref[6:7]
    for part in range(y_ref.shape[0] // T):
        rows = slice(part * T, part * T + T)
        mask = to_col(mask_ref[part])[:, 0:1]
        inv_row = lax.rsqrt(ss_ref[part] / width + EPS)
        inv = to_col(inv_row)[:, 0:1]
        cube = to_col(inv_row * inv_row * inv_row * (co_ref[part] / width))[:, 0:1]
        y = y_ref[rows].astype(F32)
        z = z_ref[rows].astype(F32)
        dyn = dyn_ref[rows].astype(F32)
        s = sigmoid(z)
        act = z * s
        w = y * act
        wi = w * inv
        yg_ref[rows] = (wi * gain * mask).astype(BF16)
        gg_ref[0:1] += jnp.sum(dyn * wi, axis=0, keepdims=True)
        dw = inv * gain * dyn - w * cube
        dy_ref[rows] = (dw * act).astype(BF16)
        dz = dw * y * (s * (1.0 + z * (1.0 - s)))
        dz_ref[rows] = dz.astype(BF16)
        rd_ref[part] = to_row(jnp.sum(dz * z, axis=1, keepdims=True))


def background(moves, last, srcs, dsts, sems):
    place = {"dp": lax.axis_index("dp"), "head": lax.axis_index("head")}

    def peer(axis, flip):
        return tuple(place[name] ^ flip if name == axis else place[name] for name in ("dp", "head"))

    copies = [
        pltpu.make_async_remote_copy(
            src_ref=src, dst_ref=dst, send_sem=sems.at[0, i], recv_sem=sems.at[1, i], device_id=peer(*move), device_id_type=MESH
        )
        for i, (move, src, dst) in enumerate(zip(moves, srcs, dsts))
    ]
    first = (pl.program_id(0) == 0) & (pl.program_id(1) == 0)

    @pl.when(first)
    def _():
        greet([peer(*move) for move in dict.fromkeys(moves)])
        for copy in copies:
            copy.start()

    @pl.when(last)
    def _():
        for copy in copies:
            copy.wait()


def backward_kernel(heads, extra, moves, dy_ref, x_ref, c_ref, cb_ref, ubd_ref, st_ref, par_ref, pbc_ref, head_ref, *refs):
    count = len(moves)
    srcs, refs = refs[:count], refs[count + extra :]
    dx_ref, dbd_ref, gx_ref, gb_ref, gh_ref, rd_ref = refs[:6]
    dsts, refs = refs[6 : 6 + count], refs[6 + count :]
    d_state, ext_x, ext_b, rows_ref, prod, edy_ref, tail_ref = refs[:7]
    if moves:
        ended = (pl.program_id(0) == pl.num_programs(0) - 1) & (pl.program_id(1) == pl.num_programs(1) - 1)
        background(moves, ended, srcs, dsts, refs[7])
    first = (pl.program_id(0) == 0) & (pl.program_id(1) == 0)

    @pl.when(first)
    def _():
        gx_ref[...] = jnp.zeros_like(gx_ref)
        gb_ref[...] = jnp.zeros_like(gb_ref)
        gh_ref[...] = jnp.zeros_like(gh_ref)
        rows_ref[...] = jnp.zeros_like(rows_ref)

    @pl.when(pl.program_id(1) == 0)
    def _():
        ext_x[T : T + 8] = jnp.zeros_like(ext_x[T : T + 8])
        ext_b[T : T + 8] = jnp.zeros_like(ext_b[T : T + 8])
        d_state[...] = jnp.zeros_like(d_state)

    row, col = iotas(T, T)
    low = col < HEAD
    upto = col >= row
    below = row < col
    reach = (row >= col).astype(BF16)
    ubd = ubd_ref[...]
    raw, steps, rates, logs = step_terms(ubd, head_ref, heads)
    logs_t = logs.T
    cb = cb_ref[...]
    sb = sigmoid(cb)
    bc = cb * sb
    b_low, c_low = bc[:, :N].astype(BF16), bc[:, N:].astype(BF16)
    c_t = bc[:, N:].T.astype(BF16)
    scores = dot_nt(b_low, c_low)
    entering = st_ref[0]
    outer = dot(c_low, entering)
    ds_low = d_state[...].astype(BF16)
    back = dot(b_low, ds_low)
    d_scores = jnp.zeros((T, T), F32)
    skip_parts, closing_parts = [], []
    for pair in range(heads // 2):
        span = slice(128 * pair, 128 * pair + 128)
        h0, h1 = 2 * pair, 2 * pair + 1
        log0, log1 = lanes(logs, h0), lanes(logs, h1)
        log_pair = jnp.where(low, log0, log1)
        step_pair = jnp.where(low, lanes(steps, h0), lanes(steps, h1))
        last_pair = log_pair[T - 1 : T]
        cp = c_ref[:, span].astype(F32)
        sp = sigmoid(cp)
        xp = cp * sp
        xd = xp * step_pair
        dy_low = dy_ref[:, span]
        dy = dy_low.astype(F32)
        decay0 = jnp.exp(jnp.where(upto, logs_t[h0 : h0 + 1] - log0, NEG))
        decay1 = jnp.exp(jnp.where(upto, logs_t[h1 : h1 + 1] - log1, NEG))
        m0, m1 = scores * decay0, scores * decay1
        zero = jnp.zeros_like(dy_low)
        x_stack = jnp.concatenate([jnp.where(low, xd, 0.0).astype(BF16), jnp.where(low, 0.0, xd).astype(BF16)], axis=0)
        dm = dot_nt(x_stack, dy_low)
        dm0, dm1 = dm[:T], dm[T:]
        d_scores = d_scores + dm0 * decay0 + dm1 * decay1
        dy_stack = jnp.concatenate([jnp.where(low, dy, 0.0).astype(BF16), jnp.where(low, 0.0, dy).astype(BF16)], axis=0)
        dxd = dot(jnp.concatenate([m0.astype(BF16), m1.astype(BF16)], axis=1), dy_stack)
        flow = jnp.concatenate([(dm0 * m0).astype(BF16), (dm1 * m1).astype(BF16)], axis=0)
        later = dot(flow, reach)
        rows_ref[h0 : h0 + 1] = jnp.sum(jnp.where(below, later[:T], 0.0), axis=0, keepdims=True)
        rows_ref[h1 : h1 + 1] = jnp.sum(jnp.where(below, later[T:], 0.0), axis=0, keepdims=True)
        grow = jnp.exp(log_pair)
        tail = jnp.exp(last_pair - log_pair)
        from_state = tail * back[:, span]
        dxd = dxd + from_state
        edy = grow * dy
        prod[0:T, span] = (edy * outer[:, span]).astype(BF16)
        prod[T : 2 * T, span] = (from_state * xd).astype(BF16)
        prod[2 * T : 3 * T, span] = (xp * dxd).astype(BF16)
        skip_parts.append(jnp.sum(xp * dy, axis=0, keepdims=True))
        edy_low = edy.astype(BF16)
        edy_ref[:, span] = edy_low
        tail_ref[:, span] = (tail * xd).astype(BF16)
        old = d_state[:, span]
        closing = jnp.exp(last_pair)
        closing_parts.append(closing * jnp.sum(old * entering[:, span].astype(F32), axis=0, keepdims=True))
        d_state[:, span] = closing * old + dot(c_t, edy_low)
        dx = dxd * step_pair + par_ref[5:6, span] * dy
        ext_x[0:T, span] = dx * (sp * (1.0 + cp * (1.0 - sp)))
    d_low = d_scores.astype(BF16)
    d_b = dot_nt(tail_ref[...], ds_low) + dot(d_low, c_low)
    d_c = dot_nt(edy_ref[...], entering) + dot(d_scores.T.astype(BF16), b_low)
    width = heads * HEAD
    lane_row, lane_col = iotas(width, 128)
    member = (lane_row // HEAD == lane_col).astype(BF16)
    sums = dot(prod[...], member)
    skip_all = jnp.concatenate(skip_parts, axis=1)
    closing_all = jnp.concatenate(closing_parts, axis=1)
    fill = jnp.zeros((6, width), F32)
    few = dot_exact(jnp.concatenate([skip_all, closing_all, fill], axis=0), member.astype(F32))
    d_logs = dot(upto.astype(BF16), sums[:T].astype(BF16)) + dot((col < row).astype(BF16), sums[T : 2 * T].astype(BF16))
    d_logs = d_logs + rows_ref[...].T + few[1:2]
    d_steps = sums[2 * T :] + rates * d_logs
    d_raw = jnp.where(col < heads, d_steps * sigmoid(raw), 0.0)
    gh_ref[0:1] += jnp.sum(d_raw, axis=0, keepdims=True)
    gh_ref[1:2] += rates * jnp.sum(steps * d_logs, axis=0, keepdims=True)
    gh_ref[2:3] += few[0:1]
    ext_b[0:T, 0:N] = d_b * (sb[:, :N] * (1.0 + cb[:, :N] * (1.0 - sb[:, :N])))
    ext_b[0:T, N:] = d_c * (sb[:, N:] * (1.0 + cb[:, N:] * (1.0 - sb[:, N:])))

    def conv_back(ext, values, taps, grads):
        now = ext[0:T]
        total = taps[3:4] * now
        grads[3:4] += jnp.sum(values * now, axis=0, keepdims=True)
        grads[4:5] += jnp.sum(now, axis=0, keepdims=True)
        for k in range(3):
            moved = ext[3 - k : 3 - k + T]
            total = total + taps[k : k + 1] * moved
            grads[k : k + 1] += jnp.sum(values * moved, axis=0, keepdims=True)
        ext[T : T + 8] = ext[0:8]
        return total

    ux = x_ref[...].astype(F32)
    dux = conv_back(ext_x, ux, par_ref, gx_ref)
    dx_ref[...] = dux.astype(BF16)
    ubc = ubd[:, : 2 * N]
    dubc = conv_back(ext_b, ubc, pbc_ref, gb_ref)
    dbd_ref[:, : 2 * N] = dubc.astype(BF16)
    dbd_ref[:, 2 * N :] = d_raw.astype(BF16)
    total = jnp.sum(dux * ux, axis=1, keepdims=True) + jnp.sum(dubc * ubc, axis=1, keepdims=True)
    total = total + jnp.sum(jnp.where(col < heads, d_raw * ubd[:, 2 * N :], 0.0), axis=1, keepdims=True)
    rd_ref[0] = to_row(total)


def params(*semantics, number=0):
    if number:
        return pltpu.CompilerParams(
            dimension_semantics=semantics, vmem_limit_bytes=56 * 1024 * 1024, collective_id=number, has_side_effects=True
        )
    return pltpu.CompilerParams(dimension_semantics=semantics, vmem_limit_bytes=56 * 1024 * 1024)


def run_forward(heads, u_zx, u_bd, par, pbc, hp):
    rows, width = u_zx.shape[0], heads * HEAD
    slots, chunks = rows // LEN, LEN // T
    at = lambda s, i: (s * chunks + i, 0)
    fixed = lambda s, i: (0, 0)
    return pl.pallas_call(
        functools.partial(forward_kernel, heads),
        grid=(slots, chunks),
        in_specs=[
            pl.BlockSpec((T, width), lambda s, i: (s * chunks + i, 1)),
            pl.BlockSpec((T, width), at),
            pl.BlockSpec((T, 3 * N), at),
            pl.BlockSpec((8, width), fixed),
            pl.BlockSpec((8, 2 * N), fixed),
            pl.BlockSpec((8, 128), fixed),
        ],
        out_specs=[
            pl.BlockSpec((T, width), at),
            pl.BlockSpec((1, 1, T), lambda s, i: (s * chunks + i, 0, 0)),
            pl.BlockSpec((T, width), at),
            pl.BlockSpec((T, 2 * N), at),
            pl.BlockSpec((1, N, width), lambda s, i: (s * chunks + i, 0, 0)),
        ],
        out_shape=[
            jax.ShapeDtypeStruct((rows, width), BF16),
            jax.ShapeDtypeStruct((rows // T, 1, T), F32),
            jax.ShapeDtypeStruct((rows, width), BF16),
            jax.ShapeDtypeStruct((rows, 2 * N), F32),
            jax.ShapeDtypeStruct((rows // T, N, width), BF16),
        ],
        scratch_shapes=[pltpu.VMEM((T + 8, width), F32), pltpu.VMEM((T + 8, 2 * N), F32), pltpu.VMEM((N, width), F32)],
        compiler_params=params("arbitrary", "arbitrary"),
        cost_estimate=pl.CostEstimate(flops=rows * width * 2 * 1200, bytes_accessed=rows * width * 8, transcendentals=rows * width * 6),
        name="scan_forward",
    )(u_zx, u_zx, u_bd, par, pbc, hp)


def run_norm(x, gain):
    rows, deep = x.shape
    step = 256
    at = lambda i: (i, 0)
    return pl.pallas_call(
        norm_kernel,
        grid=(rows // step,),
        in_specs=[pl.BlockSpec((step, deep), at), pl.BlockSpec((8, deep), lambda i: (0, 0))],
        out_specs=[pl.BlockSpec((step, deep), at), pl.BlockSpec((step // T, 1, T), lambda i: (i, 0, 0))],
        out_shape=[jax.ShapeDtypeStruct((rows, deep), BF16), jax.ShapeDtypeStruct((rows // T, 1, T), F32)],
        compiler_params=params("arbitrary"),
        cost_estimate=pl.CostEstimate(flops=rows * deep * 6, bytes_accessed=rows * deep * 4, transcendentals=rows),
        name="norm_rows",
    )(x, gain)


def run_gate(full_grad, w_out, y, u_zx, par, mask):
    rows, width = y.shape
    deep = full_grad.shape[1]
    step = 256
    at = lambda i: (i, 0)
    fixed = lambda i: (0, 0)
    thin = pl.BlockSpec((step // T, 1, T), lambda i: (i, 0, 0))
    return pl.pallas_call(
        gate_kernel,
        grid=(rows // step,),
        in_specs=[
            pl.BlockSpec((step, deep), at),
            pl.BlockSpec((deep, width), fixed),
            pl.BlockSpec((step, width), at),
            pl.BlockSpec((step, width), at),
            pl.BlockSpec((8, width), fixed),
            thin,
        ],
        out_specs=[pl.BlockSpec((step, width), at), thin],
        out_shape=[jax.ShapeDtypeStruct((rows, width), BF16), jax.ShapeDtypeStruct((rows // T, 1, T), F32)],
        compiler_params=params("arbitrary"),
        cost_estimate=pl.CostEstimate(flops=rows * width * deep * 2, bytes_accessed=rows * (width * 6 + deep * 2), transcendentals=rows * width),
        name="gate_back",
    )(full_grad, w_out, y, u_zx, par, mask)


def run_mid(all_width, y, u_zx, dyn, par, mask, ss, co):
    rows, width = y.shape
    step = 256
    at = lambda i: (i, 0)
    fixed = lambda i: (0, 0)
    thin = pl.BlockSpec((step // T, 1, T), lambda i: (i, 0, 0))
    wide = pl.BlockSpec((step, width), at)
    return pl.pallas_call(
        functools.partial(mid_kernel, float(all_width)),
        grid=(rows // step,),
        in_specs=[wide, wide, wide, pl.BlockSpec((8, width), fixed), thin, thin, thin],
        out_specs=[wide, wide, wide, pl.BlockSpec((8, width), fixed), thin],
        out_shape=[jax.ShapeDtypeStruct((rows, width), BF16)] * 3
        + [jax.ShapeDtypeStruct((8, width), F32), jax.ShapeDtypeStruct((rows // T, 1, T), F32)],
        compiler_params=params("arbitrary"),
        cost_estimate=pl.CostEstimate(flops=rows * width * 30, bytes_accessed=rows * width * 12, transcendentals=rows * width),
        name="gate_mid",
    )(y, u_zx, dyn, par, mask, ss, co)


def run_backward(heads, slot, slots, dy, u_zx, c, cb, u_bd, st, par, pbc, hp, deps, swaps=(), number=0):
    width = dy.shape[1]
    chunks = LEN // T
    rows = slots * LEN
    here = lambda s, i: s * chunks + chunks - 1 - i
    place = lambda s, i: (slot + s) * chunks + chunks - 1 - i
    at = lambda s, i: (place(s, i), 0)
    at3 = lambda s, i: (place(s, i), 0, 0)
    fixed = lambda s, i: (0, 0)
    return pl.pallas_call(
        functools.partial(backward_kernel, heads, len(deps), tuple(move for move, _ in swaps)),
        grid=(slots, chunks),
        in_specs=[
            pl.BlockSpec((T, width), at),
            pl.BlockSpec((T, width), lambda s, i: (place(s, i), 1)),
            pl.BlockSpec((T, width), at),
            pl.BlockSpec((T, 2 * N), at),
            pl.BlockSpec((T, 3 * N), at),
            pl.BlockSpec((1, N, width), at3),
            pl.BlockSpec((8, width), fixed),
            pl.BlockSpec((8, 2 * N), fixed),
            pl.BlockSpec((8, 128), fixed),
        ]
        + [pl.BlockSpec(memory_space=pl.ANY)] * (len(swaps) + len(deps)),
        out_specs=[
            pl.BlockSpec((T, width), lambda s, i: (here(s, i), 0)),
            pl.BlockSpec((T, 3 * N), lambda s, i: (here(s, i), 0)),
            pl.BlockSpec((8, width), fixed),
            pl.BlockSpec((8, 2 * N), fixed),
            pl.BlockSpec((8, 128), fixed),
            pl.BlockSpec((1, 1, T), lambda s, i: (here(s, i), 0, 0)),
        ]
        + [pl.BlockSpec(memory_space=pl.ANY)] * len(swaps),
        out_shape=[
            jax.ShapeDtypeStruct((rows, width), BF16),
            jax.ShapeDtypeStruct((rows, 3 * N), BF16),
            jax.ShapeDtypeStruct((8, width), F32),
            jax.ShapeDtypeStruct((8, 2 * N), F32),
            jax.ShapeDtypeStruct((8, 128), F32),
            jax.ShapeDtypeStruct((rows // T, 1, T), F32),
        ]
        + [jax.ShapeDtypeStruct(value.shape, value.dtype) for _, value in swaps],
        scratch_shapes=[
            pltpu.VMEM((N, width), F32),
            pltpu.VMEM((T + 8, width), F32),
            pltpu.VMEM((T + 8, 2 * N), F32),
            pltpu.VMEM((128, 128), F32),
            pltpu.VMEM((3 * T, width), BF16),
            pltpu.VMEM((T, width), BF16),
            pltpu.VMEM((T, width), BF16),
        ]
        + ([pltpu.SemaphoreType.DMA((2, len(swaps)))] if swaps else []),
        compiler_params=params("arbitrary", "arbitrary", number=number),
        cost_estimate=pl.CostEstimate(flops=rows * width * 2 * 3000, bytes_accessed=rows * width * 12, transcendentals=rows * width * 8),
        name="scan_backward",
    )(dy, u_zx, c, cb, u_bd, st, par, pbc, hp, *[value for _, value in swaps], *deps)


def pieces_kernel(count, me_ref, *refs):
    values, weights, outs = refs[:count], refs[count : 2 * count], refs[2 * count :]
    quarter = outs[0].shape[1]
    for k, out in enumerate(outs):
        at = pl.ds(pl.multiple_of((me_ref[0] ^ k) * quarter, 128), quarter)
        total = None
        for value, weight in zip(values, weights):
            term = dot_nt(value[...], weight[at, :])
            total = term if total is None else total + term
        out[...] = total.astype(out.dtype)


def run_pieces(me, values, weights, quarter, first, rows, name):
    step = 256
    specs = [pl.BlockSpec((step, v.shape[1]), lambda i, m: (first // step + i, 0)) for v in values]
    specs += [pl.BlockSpec(w.shape, lambda i, m: (0, 0)) for w in weights]
    depth = sum(v.shape[1] for v in values)
    return pl.pallas_call(
        functools.partial(pieces_kernel, len(values)),
        grid_spec=pltpu.PrefetchScalarGridSpec(
            num_scalar_prefetch=1,
            grid=(rows // step,),
            in_specs=specs,
            out_specs=[pl.BlockSpec((step, quarter), lambda i, m: (i, 0))] * 4,
        ),
        out_shape=[jax.ShapeDtypeStruct((rows, quarter), BF16)] * 4,
        compiler_params=params("arbitrary"),
        cost_estimate=pl.CostEstimate(flops=rows * depth * quarter * 8, bytes_accessed=rows * (depth + 4 * quarter) * 2, transcendentals=0),
        name=name,
    )(me, *values, *weights)


MESH = pl.DeviceIdType.MESH


def greet(peers):
    barrier = pltpu.get_barrier_semaphore()
    for peer in peers:
        pl.semaphore_signal(barrier, inc=1, device_id=peer, device_id_type=MESH)
    pl.semaphore_wait(barrier, len(peers))


def entry_kernel(parts, *refs):
    x_ref, g_ref, wi_ref, wo_ref, fx_ref, fg_ref, fwi_ref, fwo_ref = refs[:8]
    row_sems, far_sems, near_sems, back_sems, across_sems, side_sems, local_sems = refs[8:]
    size = x_ref.shape[0]
    quarter = x_ref.shape[2]
    me, own = lax.axis_index("dp"), lax.axis_index("head")
    columns = lambda head: pl.ds(pl.multiple_of(head * quarter, 128), quarter)

    def remote(src, dst, sems, slot, peer):
        return pltpu.make_async_remote_copy(
            src_ref=src, dst_ref=dst, send_sem=sems.at[(0,) + slot], recv_sem=sems.at[(1,) + slot], device_id=peer, device_id_type=MESH
        )

    def rows_copy(which, k):
        src, dst = ((x_ref, fx_ref), (g_ref, fg_ref))[which]
        return remote(src.at[me ^ k], dst.at[me, :, columns(own)], row_sems, (which, k), (me ^ k, own))

    def far_copy(which, k):
        ref = (fx_ref, fg_ref)[which]
        block = ref.at[me ^ k, :, columns(own)]
        return remote(block, block, far_sems, (which, k), (me, own ^ 2))

    def near_copy(which, k):
        ref = (fx_ref, fg_ref)[which]
        block = ref.at[me ^ k, :, columns(own)]
        return remote(block, block, near_sems, (which, k), (me, own ^ 1))

    def back_copy(which, k):
        ref = (fx_ref, fg_ref)[which]
        block = ref.at[me ^ k, :, columns(own ^ 2)]
        return remote(block, block, back_sems, (which, k), (me, own ^ 1))

    line = size // 2

    def across_copy(which, part, j):
        src, dst = ((wi_ref, fwi_ref), (wo_ref, fwo_ref))[which]
        return remote(src.at[part], dst.at[me, part], across_sems, (which, part, j), (me ^ (2 * j), own))

    def side_copy(which, part, j):
        src, dst = ((wi_ref, fwi_ref), (wo_ref, fwo_ref))[which]
        here = dst.at[me ^ (2 * j), part]
        return remote(src.at[part] if j == 0 else here, here, side_sems, (which, part, j), (me ^ 1, own))

    greet([(me ^ k, own) for k in range(1, size)] + [(me, own ^ 1), (me, own ^ 2)])

    order = sorted(range(1, size), key=lambda k: (-(k & ~1), k & 1))
    locals_ = []
    for which, (src, dst) in enumerate(((x_ref, fx_ref), (g_ref, fg_ref))):
        locals_.append(pltpu.make_async_copy(src.at[me], dst.at[me, :, columns(own)], local_sems.at[which]))
    for which, (src, dst) in enumerate(((wi_ref, fwi_ref), (wo_ref, fwo_ref))):
        locals_.append(pltpu.make_async_copy(src, dst.at[me], local_sems.at[2 + which]))

    def send_rows(which):
        for k in order:
            rows_copy(which, k).start()

    def forward(which, done):
        locals_[which].wait()
        far_copy(which, 0).start()
        near_copy(which, 0).start()
        waiting = [0]
        for k in order:
            rows_copy(which, k).wait_recv()
            far_copy(which, k).start()
            near_copy(which, k).start()
            waiting.append(k)
        return waiting

    def spread(which):
        for part in range(parts):
            side_copy(which, part, 0).start()
        for part in range(min(2, parts)):
            for j in range(1, line):
                across_copy(which, part, j).start()
        for part in range(parts):
            for j in range(1, line):
                across_copy(which, part, j).wait_recv()
                side_copy(which, part, j).start()
            if part + 2 < parts:
                for j in range(1, line):
                    across_copy(which, part + 2, j).start()

    def finish_rows(which, waiting):
        for k in waiting:
            far_copy(which, k).wait_recv()
            back_copy(which, k).start()

    for copy in locals_:
        copy.start()
    send_rows(0)
    waiting = forward(0, None)
    finish_now = lambda: finish_rows(0, waiting)
    for part in range(parts):
        side_copy(0, part, 0).start()
    for part in range(min(2, parts)):
        for j in range(1, line):
            across_copy(0, part, j).start()
    finish_now()
    for part in range(parts):
        for j in range(1, line):
            across_copy(0, part, j).wait_recv()
            side_copy(0, part, j).start()
        if part + 2 < parts:
            for j in range(1, line):
                across_copy(0, part + 2, j).start()
    send_rows(1)
    waiting = forward(1, None)
    spread(1)
    finish_rows(1, waiting)
    for copy in locals_[2:]:
        copy.wait()
    for which in range(2):
        for k in range(size):
            near_copy(which, k).wait_recv()
            back_copy(which, k).wait_recv()
            near_copy(which, k).wait_send()
            back_copy(which, k).wait_send()
            far_copy(which, k).wait_send()
            if k:
                rows_copy(which, k).wait_send()
        for part in range(parts):
            for j in range(line):
                side_copy(which, part, j).wait()
                if j:
                    across_copy(which, part, j).wait_send()


def run_entry(tokens, cotangent, w_in, w_out):
    size = lax.axis_size("dp")
    parts = 4
    rows, quarter = tokens.shape
    deep = quarter * 4
    block = rows // size
    shard = w_in.shape[0]
    line = size // 2
    cut = lambda w: w.reshape(parts, shard // parts, w.shape[1])
    full = lambda w: jax.ShapeDtypeStruct((size, parts, shard // parts, w.shape[1]), BF16)
    sems = pltpu.SemaphoreType.DMA
    outs = pl.pallas_call(
        functools.partial(entry_kernel, parts),
        in_specs=[pl.BlockSpec(memory_space=pl.ANY)] * 4,
        out_specs=[pl.BlockSpec(memory_space=pl.ANY)] * 4,
        out_shape=[jax.ShapeDtypeStruct((size, block, deep), BF16)] * 2 + [full(w_in), full(w_out)],
        scratch_shapes=[sems((2, 2, size))] * 4 + [sems((2, 2, parts, line))] * 2 + [sems((4,))],
        compiler_params=pltpu.CompilerParams(collective_id=0, has_side_effects=True, vmem_limit_bytes=1024 * 1024),
        name="entry",
    )(tokens.reshape(size, block, quarter), cotangent.reshape(size, block, quarter), cut(w_in), cut(w_out))
    return (
        outs[0].reshape(rows, deep),
        outs[1].reshape(rows, deep),
        outs[2].reshape(size * shard, w_in.shape[1]),
        outs[3].reshape(size * shard, w_out.shape[1]),
    )


def mm(a, b, contract, kind):
    return lax.dot_general(a, b, (contract, ((), ())), preferred_element_type=F32).astype(kind)


def swap(value, axis, bit):
    size = lax.axis_size(axis)
    return lax.ppermute(value, axis, [(i, i ^ (1 << bit)) for i in range(size)])


def bits_of(axis):
    return lax.axis_size(axis).bit_length() - 1


def scatter_rows(value, axis):
    place = lax.axis_index(axis)
    count = bits_of(axis)
    size = lax.axis_size(axis)
    current = value.reshape(size, -1, value.shape[1])
    bit = 0
    while count - bit > 2:
        current = current.reshape(-1, 2, current.shape[1], current.shape[2])
        mine = (place >> bit) & 1
        keep = lax.dynamic_index_in_dim(current, mine, 1, keepdims=False)
        send = lax.dynamic_index_in_dim(current, 1 - mine, 1, keepdims=False)
        current = keep.astype(F32) + swap(send.astype(BF16), axis, bit).astype(F32)
        bit += 1
    high = place >> bit
    total = lax.dynamic_index_in_dim(current, high, 0, keepdims=False).astype(F32)
    low_current = current.astype(BF16)
    for k in (2, 3, 1)[: 2 ** (count - bit)]:
        send = lax.dynamic_index_in_dim(low_current, high ^ k, 0, keepdims=False)
        total = total + lax.ppermute(send, axis, [(i, i ^ (k << bit)) for i in range(size)]).astype(F32)
    return total


def sum_all(value, axis):
    for bit in range(bits_of(axis)):
        value = value + swap(value, axis, bit)
    return value


def head_sum(pieces):
    from_third, from_first = swap((pieces[3], pieces[1]), "head", 0)
    passed = (pieces[2].astype(F32) + from_third.astype(F32)).astype(BF16)
    arrived = swap(passed, "head", 1)
    return pieces[0].astype(F32) + from_first.astype(F32) + arrived.astype(F32)


def body(tokens, cotangent, order, lengths, norm_gain, w_zx, w_bc, w_dt, w_out, conv_x, conv_bc, head_params, gate_gain):
    rows, quarter = tokens.shape
    heads = head_params.shape[1]
    width = heads * HEAD
    place = lax.axis_index("head")
    me = place.astype(jnp.int32).reshape(1)
    groups = lax.axis_size("head")
    all_width = width * groups
    deep = quarter * groups
    arrange = order[0]
    own_w = w_zx.shape[0]
    packed = jnp.concatenate(
        [
            w_zx.reshape(own_w, 2 * width),
            w_bc,
            w_dt,
            norm_gain[:, None],
            jnp.zeros((own_w, 127 - heads), BF16),
        ],
        axis=1,
    )
    came_x, came_g, w_in, w_o = run_entry(tokens, cotangent, packed, w_out)
    full_x = came_x[arrange]
    full_g = came_g[arrange]
    w_zx_in, w_bd = w_in[:, : 2 * width], w_in[:, 2 * width :]

    gain = w_in[:, 2 * width + 2 * N + heads].astype(F32)
    normed, inv_one = run_norm(full_x, jnp.broadcast_to(gain[None], (8, deep)))
    inv_one = inv_one.reshape(rows, 1)
    own_x = lax.dynamic_slice_in_dim(full_x, place * quarter, quarter, 1)
    u_zx = mm(normed, w_zx_in, ((1,), (0,)), BF16)
    u_bd = mm(normed, w_bd, ((1,), (0,)), F32)

    par = jnp.concatenate([conv_x, jnp.repeat(head_params[2:3], HEAD, axis=1), gate_gain[None], jnp.zeros((1, width), F32)], axis=0)
    pbc = jnp.concatenate([conv_bc, jnp.zeros((3, 2 * N), F32)], axis=0)
    hp = jnp.pad(head_params, ((0, 5), (0, 128 - heads)))
    positions = lax.broadcasted_iota(jnp.int32, (lengths.shape[0], LEN), 1)
    mask = (positions < lengths[:, None]).astype(F32).reshape(rows // T, 1, T)

    y, ss, c, cb, st = run_forward(heads, u_zx, u_bd, par, pbc, hp)
    dyn, co = run_gate(full_g, w_o, y, u_zx, par, mask)
    ss, co = lax.psum((ss, co), "head")
    yg, dz, dy, gg, rd_z = run_mid(all_width, y, u_zx, dyn, par, mask, ss, co)

    grad_out = mm(full_g, yg, ((0,), (0,)), BF16)
    out_pieces = run_pieces(me, [yg], [w_o], quarter, 0, rows, "branch_pieces")
    grad_out = scatter_rows(grad_out, "dp")
    from_third, from_first = swap((out_pieces[3], out_pieces[1]), "head", 0)
    passed = (out_pieces[2].astype(F32) + from_third.astype(F32)).astype(BF16)
    grad_z = scatter_rows(mm(normed, dz, ((0,), (0,)), BF16), "dp")

    slots = rows // LEN
    deps = list(out_pieces)
    parts = []
    for slot in range(slots):
        if slot == 0:
            own = run_backward(heads, slot, 1, dy, u_zx, c, cb, u_bd, st, par, pbc, hp, deps, [(("head", 2), passed)], 1)
            shares = (out_pieces[0].astype(F32) + from_first.astype(F32) + own[6].astype(F32)).astype(BF16)
            sent_out = jnp.zeros_like(shares).at[arrange].set(shares)
            final_out = lax.all_to_all(sent_out, "dp", split_axis=0, concat_axis=0, tiled=True)
            final_out = (tokens.astype(F32) + final_out.astype(F32)).astype(BF16)
        else:
            own = run_backward(heads, slot, 1, dy, u_zx, c, cb, u_bd, st, par, pbc, hp, deps)
        start = slot * LEN
        d_pieces = run_pieces(
            me,
            [lax.slice_in_dim(dz, start, start + LEN, axis=0), own[0], own[1]],
            [w_in[:, :width], w_in[:, width : 2 * width], w_bd],
            quarter,
            0,
            LEN,
            "input_pieces",
        )
        parts.append((own, head_sum(d_pieces)))
        deps = list(d_pieces)
    dxn = jnp.concatenate([part[1] for part in parts], axis=0)
    rd_x = jnp.concatenate([part[0][5] for part in parts], axis=0)
    gx, gb, gh = (sum(part[0][i] for part in parts) for i in (2, 3, 4))
    row_dot = lax.psum(rd_z + rd_x, "head").reshape(rows, 1)

    def over_slots(pick):
        return sum(
            mm(lax.slice_in_dim(normed, slot * LEN, slot * LEN + LEN, axis=0), parts[slot][0][pick], ((0,), (0,)), F32) for slot in range(slots)
        ).astype(BF16)

    grad_x = scatter_rows(over_slots(0), "dp")
    grad_bd = scatter_rows(over_slots(1), "dp")
    grad_bc = sum_all(grad_bd[:, : 2 * N], "head")
    grad_dt = grad_bd[:, 2 * N : 2 * N + heads]

    gain_own = lax.dynamic_slice_in_dim(gain, place * quarter, quarter, 0)
    hat = own_x.astype(F32) * inv_one
    grad_rows = (inv_one * (gain_own * dxn - hat * (row_dot / deep))).astype(BF16)
    gain_part = jnp.sum(dxn * hat, axis=0)
    sent_back = jnp.zeros_like(grad_rows).at[arrange].set(grad_rows)
    final_back = lax.all_to_all(sent_back, "dp", split_axis=0, concat_axis=0, tiled=True)
    final_back = (cotangent.astype(F32) + final_back.astype(F32)).astype(BF16)

    small = jnp.concatenate([gx[:5].reshape(-1), gg[0], gh[:3].reshape(-1)])
    small = sum_all(small, "dp")
    gx, gg, gh = small[: 5 * width].reshape(5, width), small[5 * width : 6 * width], small[6 * width :].reshape(3, 128)[:, :heads]
    gain_part = lax.dynamic_update_slice_in_dim(jnp.zeros((deep,), F32), gain_part, place * quarter, 0)
    shared = sum_all(sum_all(jnp.concatenate([gb[:5].reshape(-1), gain_part]), "head"), "dp")
    gb, gain_all = shared[: 10 * N].reshape(5, 2 * N), shared[10 * N :]
    own_d = norm_gain.shape[0]
    grad_gain = lax.dynamic_slice_in_dim(gain_all, lax.axis_index("dp") * own_d, own_d, 0)
    grad_zx = jnp.stack([grad_z, grad_x], axis=1)
    return (final_out, final_back, grad_gain, grad_zx, grad_bc, grad_dt, grad_out, gx, gb, gh, gg)


def solution(mesh):
    return jax.shard_map(
        body,
        mesh=mesh,
        in_specs=(
            P("dp", "head"),
            P("dp", "head"),
            P("dp", None),
            P("dp"),
            P("dp"),
            P("dp", None, "head"),
            P("dp", None),
            P("dp", "head"),
            P("dp", "head"),
            P(None, "head"),
            P(),
            P(None, "head"),
            P("head"),
        ),
        out_specs=(
            P("dp", "head"),
            P("dp", "head"),
            P("dp"),
            P("dp", None, "head"),
            P("dp", None),
            P("dp", "head"),
            P("dp", "head"),
            P(None, "head"),
            P(),
            P(None, "head"),
            P("head"),
        ),
        check_vma=False,
    )
```

```python
import functools

import jax
import jax.numpy as jnp
from jax import lax
from jax.experimental import pallas as pl
from jax.experimental.pallas import tpu as pltpu
from jax.sharding import PartitionSpec as P

LEN = 1024
T = 128
N = 128
HEAD = 64
EPS = 1e-05
NEG = -1e30
LIMIT = 60 * 1024 * 1024
AXES = ("dp", "head")
F32 = jnp.float32
BF16 = jnp.bfloat16


def dot(a, b):
    return lax.dot_general(a, b, (((1,), (0,)), ((), ())), preferred_element_type=F32)


def dot_nt(a, b):
    return lax.dot_general(a, b, (((1,), (1,)), ((), ())), preferred_element_type=F32)


def dot_exact(a, b):
    return lax.dot_general(
        a, b, (((1,), (0,)), ((), ())), preferred_element_type=F32, precision=lax.Precision.HIGHEST
    )


def iotas(rows, cols):
    return (
        lax.broadcasted_iota(jnp.int32, (rows, cols), 0),
        lax.broadcasted_iota(jnp.int32, (rows, cols), 1),
    )


MESH = pl.DeviceIdType.MESH


def greet(peers):
    barrier = pltpu.get_barrier_semaphore()
    for peer in peers:
        pl.semaphore_signal(barrier, inc=1, device_id=peer, device_id_type=MESH)
    pl.semaphore_wait(barrier, len(peers))


def place_of():
    return {name: lax.axis_index(name) for name in AXES}


def move_copies(move, src, dst):
    kind, axis = move[0], move[1]
    place = place_of()
    me = place[axis]

    def peer(flip):
        return tuple(place[name] ^ flip if name == axis else place[name] for name in AXES)

    if kind == "whole":
        return [(peer(move[2]), src, dst)], []
    if kind == "rows":
        return [(peer(move[2]), src.at[pl.ds(move[3], move[4])], dst)], []
    if kind == "half":
        return [(peer(1 << move[2]), src.at[:, 1 - ((me >> move[2]) & 1)], dst)], []
    if kind == "direct":
        high = me >> move[2]
        return [(peer(j << move[2]), src.at[high ^ j], dst.at[j - 1]) for j in range(1, dst.shape[0] + 1)], []
    if kind == "all":
        groups = lax.axis_size("head")
        flips = [divmod(flat, groups) for flat in range(1, dst.shape[0] + 1)]
        return [((place["dp"] ^ f, place["head"] ^ e), src, dst.at[i]) for i, (f, e) in enumerate(flips)], []
    if kind == "spread":
        return [(peer(flip), src, dst.at[flip - 1]) for flip in range(1, dst.shape[0] + 1)], []
    remote = [(peer(k), src.at[me ^ k], dst.at[me]) for k in turn_order(src.shape[0])]
    return remote, [(src.at[me], dst.at[me])]


def turn_order(size):
    return sorted(range(1, size), key=lambda k: (-(k & ~1), k & 1))


def move_shape(move, shape):
    kind = move[0]
    if kind == "rows":
        return (move[4],) + shape[1:]
    if kind == "half":
        return (shape[0],) + shape[2:]
    if kind == "direct":
        return (shape[0] - 1,) + shape[1:]
    if kind == "spread":
        return (lax.axis_size(move[1]) - 1,) + shape
    if kind == "all":
        return (lax.axis_size("dp") * lax.axis_size("head") - 1,) + shape
    return shape


def move_counts(moves, values):
    remote = local = 0
    for move, value in zip(moves, values):
        size = lax.axis_size(move[1])
        world = lax.axis_size("dp") * lax.axis_size("head")
        count = {"direct": value.shape[0] - 1, "spread": size - 1, "turn": size - 1, "all": world - 1}.get(move[0], 1)
        remote, local = remote + count, local + (move[0] == "turn")
    return remote, local


def move_scratch(moves, values):
    remote, local = move_counts(moves, values)
    return [pltpu.SemaphoreType.DMA((2, remote)), pltpu.SemaphoreType.DMA((max(local, 1),))] if moves else []


def move_outs(moves, values):
    return [jax.ShapeDtypeStruct(move_shape(move, value.shape), value.dtype) for move, value in zip(moves, values)]


def make_moves(moves, srcs, dsts, sems, local_sems):
    remote, local = [], []
    for move, src, dst in zip(moves, srcs, dsts):
        here, there = move_copies(move, src, dst)
        remote += here
        local += there
    copies = [
        pltpu.make_async_remote_copy(src_ref=a, dst_ref=b, send_sem=sems.at[0, i], recv_sem=sems.at[1, i], device_id=peer, device_id_type=MESH)
        for i, (peer, a, b) in enumerate(remote)
    ]
    copies += [pltpu.make_async_copy(a, b, local_sems.at[i]) for i, (a, b) in enumerate(local)]
    return move_peers(moves, dsts), copies


def move_peers(moves, dsts):
    flips = {}
    for move, dst in zip(moves, dsts):
        kind, axis = move[0], move[1]
        if kind in ("whole", "rows"):
            own = [move[2]]
        elif kind == "half":
            own = [1 << move[2]]
        elif kind == "direct":
            own = [j << move[2] for j in range(1, dst.shape[0] + 1)]
        elif kind == "all":
            groups = lax.axis_size("head")
            for flat in range(1, dst.shape[0] + 1):
                flips[divmod(flat, groups)] = None
            continue
        elif kind == "spread":
            own = range(1, dst.shape[0] + 1)
        else:
            own = range(1, dst.shape[0])
        for flip in own:
            flips[(flip, 0) if axis == "dp" else (0, flip)] = None
    place = place_of()
    return [(place["dp"] ^ f, place["head"] ^ e) for f, e in flips]


def background(first, last, moves, srcs, dsts, sems, local_sems):
    peers, copies = make_moves(moves, srcs, dsts, sems, local_sems)

    @pl.when(first)
    def _():
        greet(peers)
        for copy in copies:
            copy.start()

    @pl.when(last)
    def _():
        for copy in copies:
            copy.wait()


def exchange_kernel(moves, *refs):
    count = len(moves)
    peers, copies = make_moves(moves, refs[:count], refs[count : 2 * count], refs[2 * count], refs[2 * count + 1])
    greet(peers)
    for copy in copies:
        copy.start()
    for copy in copies:
        copy.wait()


def run_exchange(moves, values, number):
    return pl.pallas_call(
        functools.partial(exchange_kernel, tuple(moves)),
        in_specs=[pl.BlockSpec(memory_space=pl.ANY)] * len(moves),
        out_specs=[pl.BlockSpec(memory_space=pl.ANY)] * len(moves),
        out_shape=move_outs(moves, values),
        scratch_shapes=move_scratch(moves, values),
        compiler_params=pltpu.CompilerParams(collective_id=number, has_side_effects=True, vmem_limit_bytes=LIMIT),
        name="exchange",
    )(*values)


def sigmoid(v):
    return 1.0 / (1.0 + jnp.exp(-v))


def softplus(v):
    return jnp.maximum(v, 0.0) + jnp.log1p(jnp.exp(-jnp.abs(v)))


def to_col(row):
    return jnp.broadcast_to(row, (T, T)).T


def to_row(col):
    return jnp.broadcast_to(col, (T, T)).T[0:1]


def lanes(value, pick):
    return jnp.broadcast_to(value[:, pick : pick + 1], (value.shape[0], 128))


def step_terms(ubd, head_ref, heads):
    row, col = iotas(T, T)
    raw = jnp.where(col < heads, ubd[:, 2 * N :] + head_ref[0:1], 0.0)
    steps = jnp.where(col < heads, softplus(raw), 0.0)
    rates = -jnp.exp(head_ref[1:2])
    tril = (row >= col).astype(F32)
    logs = dot_exact(tril, steps * rates)
    return raw, steps, rates, logs


def forward_moves(steps, rows_ref, w_ref, full_ref, fw_ref, pass_sems, across_sems, side_sems, local_sems):
    size, quarter = rows_ref.shape[0], rows_ref.shape[2]
    line = size // 2
    parts = w_ref.shape[0]
    me, own = lax.axis_index("dp"), lax.axis_index("head")
    step = pl.program_id(0) * pl.num_programs(1) + pl.program_id(1)
    far, near, back = row_forward(size, quarter, rows_ref, full_ref, pass_sems)
    across, side = shard_spread(w_ref, fw_ref, across_sems, side_sems)
    mine = pl.ds(pl.multiple_of(own * quarter, 128), quarter)
    held = [
        pltpu.make_async_copy(rows_ref, full_ref.at[:, :, mine], local_sems.at[0]),
        pltpu.make_async_copy(w_ref, fw_ref.at[me], local_sems.at[1]),
    ]

    @pl.when(step == 0)
    def _():
        greet([(me ^ 1, own)] + [(me ^ (2 * j), own) for j in range(1, line)] + [(me, own ^ 1), (me, own ^ 2)])
        for copy in held:
            copy.start()
        for k in range(size):
            near(k).start()
        for k in range(size // 2):
            far(k).start()
        for part in range(parts):
            side(part, 0).start()
        for part in range(min(2, parts)):
            for j in range(1, line):
                across(part, j).start()

    for part in range(parts):

        @pl.when(step == min(steps - 1, (part + 2) * steps // (parts + 1)))
        def _():
            for j in range(1, line):
                across(part, j).wait_recv()
                side(part, j).start()
            if part + 2 < parts:
                for j in range(1, line):
                    across(part + 2, j).start()

    groups = 4
    for group in range(groups):
        members = range(group * size // groups, (group + 1) * size // groups)

        @pl.when(step == min(steps - 1, ((group + 1) * 3 * steps) // (2 * groups)))
        def _():
            for k in members:
                far(k).wait_recv()
                back(k).start()
                if k < size // 2:
                    far(k + size // 2).start()

    @pl.when(step == steps - 1)
    def _():
        for copy in held:
            copy.wait()
        for k in range(size):
            near(k).wait()
            back(k).wait()
            far(k).wait_send()
        for part in range(parts):
            for j in range(line):
                side(part, j).wait()
                if j:
                    across(part, j).wait_send()


def forward_kernel(heads, steps, x_ref, z_ref, ubd_ref, par_ref, pbc_ref, head_ref, rows_ref, w_ref, y_ref, ss_ref, c_ref, cb_ref, st_ref, full_ref, fw_ref, ext_x, ext_b, state, *sems):
    forward_moves(steps, rows_ref, w_ref, full_ref, fw_ref, *sems)

    @pl.when(pl.program_id(1) == 0)
    def _():
        ext_x[0:8] = jnp.zeros_like(ext_x[0:8])
        ext_b[0:8] = jnp.zeros_like(ext_b[0:8])
        state[...] = jnp.zeros_like(state)

    def conv(ext, values, taps):
        ext[8 : 8 + T] = values
        total = taps[4:5] + taps[3:4] * values
        for k in range(3):
            total = total + taps[k : k + 1] * ext[5 + k : 5 + k + T]
        ext[0:8] = ext[T : T + 8]
        return total

    row, col = iotas(T, T)
    low = col < HEAD
    low_row = lax.broadcasted_iota(jnp.int32, (1, 128), 1) < HEAD
    causal = row >= col
    ubd = ubd_ref[...]
    c = conv(ext_x, x_ref[...].astype(F32), par_ref)
    c_ref[...] = c.astype(BF16)
    cb = conv(ext_b, ubd[:, : 2 * N], pbc_ref)
    cb_ref[...] = cb
    bc = cb * sigmoid(cb)
    b_rows = bc[:, :N]
    b_t = b_rows.T.astype(BF16)
    b_low, c_low = b_rows.astype(BF16), bc[:, N:].astype(BF16)
    _, steps, _, logs = step_terms(ubd, head_ref, heads)
    logs_t = logs.T
    scores = dot_nt(c_low, b_low)
    entering = state[...].astype(BF16)
    st_ref[0] = entering
    outer = dot(c_low, entering)
    squares = jnp.zeros((T, 128), F32)
    for pair in range(heads // 2):
        span = slice(128 * pair, 128 * pair + 128)
        h0, h1 = 2 * pair, 2 * pair + 1
        log0, log1 = lanes(logs, h0), lanes(logs, h1)
        log_pair = jnp.where(low, log0, log1)
        step_pair = jnp.where(low, lanes(steps, h0), lanes(steps, h1))
        last_pair = log_pair[T - 1 : T]
        cp = c[:, span]
        xp = cp * sigmoid(cp)
        xd = xp * step_pair
        m0 = (scores * jnp.exp(jnp.where(causal, log0 - logs_t[h0 : h0 + 1], NEG))).astype(BF16)
        m1 = (scores * jnp.exp(jnp.where(causal, log1 - logs_t[h1 : h1 + 1], NEG))).astype(BF16)
        stacked = jnp.concatenate([jnp.where(low, xd, 0.0).astype(BF16), jnp.where(low, 0.0, xd).astype(BF16)], axis=0)
        y = dot(jnp.concatenate([m0, m1], axis=1), stacked)
        y = y + jnp.exp(log_pair) * outer[:, span] + par_ref[5:6, span] * xp
        tail = (jnp.exp(last_pair - log_pair) * xd).astype(BF16)
        state[:, span] = jnp.exp(last_pair) * state[:, span] + dot(b_t, tail)
        y_ref[:, span] = y.astype(BF16)
        zp = z_ref[:, span].astype(F32)
        w = y * zp * sigmoid(zp)
        squares = squares + w * w
    ss_ref[0] = to_row(jnp.sum(squares, axis=1, keepdims=True))


def row_picks(order_ref, count):
    lane = lax.broadcasted_iota(jnp.int32, (T, T), 1).astype(F32)
    blocks = []
    for part in range(order_ref.shape[0]):
        wanted = to_col(order_ref[part])
        blocks.append(jnp.concatenate([(wanted == lane + float(T * j)).astype(F32).astype(BF16) for j in range(count)], axis=1))
    return jnp.concatenate(blocks, axis=0)


def project_kernel(heads, moves, order_ref, x_ref, w_ref, src_ref, out_ref, inv_ref, uzx_ref, ubd_ref, dst_ref, gain_ref, *sems):
    deep, width = x_ref.shape[1], 2 * heads * HEAD
    at_step = pl.program_id(0)
    background(at_step == 0, at_step == pl.num_programs(0) - 1, moves, (src_ref,), (dst_ref,), *sems)

    @pl.when(pl.program_id(0) == 0)
    def _():
        for j in range(deep // T):
            span = slice(j * T, j * T + T)
            gain_ref[0:1, span] = w_ref[span, width + 2 * N : width + 3 * N].astype(F32).T[heads : heads + 1]

    x = dot(row_picks(order_ref, x_ref.shape[0] // T), x_ref[...])
    inv = lax.rsqrt(jnp.sum(x * x, axis=1, keepdims=True) / deep + EPS)
    normed = (x * inv * gain_ref[0:1]).astype(BF16)
    out_ref[...] = normed
    for part in range(x.shape[0] // T):
        inv_ref[part] = to_row(inv[part * T : part * T + T])
    uzx_ref[...] = dot(normed, w_ref[:, :width]).astype(BF16)
    ubd_ref[...] = dot(normed, w_ref[:, width:])


def sort_kernel(order_ref, rows_ref, out_ref):
    out_ref[...] = dot(row_picks(order_ref, rows_ref.shape[0] // T), rows_ref[...]).astype(BF16)


def gate_kernel(g_ref, wo_ref, y_ref, z_ref, par_ref, mask_ref, dyn_ref, co_ref):
    dyn = dot(g_ref[...], wo_ref[...])
    for part in range(dyn.shape[0] // T):
        rows = slice(part * T, part * T + T)
        mask = to_col(mask_ref[part])[:, 0:1]
        own = dyn[rows] * mask
        dyn_ref[rows] = own.astype(BF16)
        z = z_ref[rows].astype(F32)
        w = y_ref[rows].astype(F32) * z * sigmoid(z)
        co_ref[part] = to_row(jnp.sum(own * w * par_ref[6:7], axis=1, keepdims=True))


def home_kernel(last, deep, order_ref, a_ref, b_ref, *refs):
    out_ref, held_ref = refs[-2:]
    step = pl.program_id(0)
    many = held_ref.shape[0] // a_ref.shape[0]
    size = a_ref.shape[0]

    @pl.when(step < many)
    def _():
        value = a_ref[...].astype(F32) + b_ref[...].astype(F32)
        if last:
            normed_ref, inv_ref, gain_ref, rdz_ref, rdx_ref, more_ref = refs[:6]
            gain = gain_ref[0:1]
            hat = normed_ref[...].astype(F32) / gain
            parts = []
            for part in range(size // T):
                inv_row = inv_ref[part]
                dots = rdz_ref[part] + rdx_ref[part] + more_ref[0, part] + more_ref[1, part] + more_ref[2, part]
                rows = slice(part * T, part * T + T)
                inv = to_col(inv_row)[:, 0:1]
                mean = to_col(dots / deep)[:, 0:1]
                parts.append(inv * (gain * value[rows] - hat[rows] * mean))
            value = jnp.concatenate(parts, axis=0)
        held_ref[pl.ds(pl.multiple_of(step * size, size), size), :] = value.astype(BF16)

    @pl.when(step >= many)
    def _():
        base = ((step - many) * size).astype(F32)
        row = lax.broadcasted_iota(jnp.int32, (size, T), 0).astype(F32) + base
        picks = jnp.concatenate([(row == order_ref[j]).astype(F32).astype(BF16) for j in range(order_ref.shape[0])], axis=1)
        out_ref[...] = dot(picks, held_ref[...]).astype(BF16)


def mid_kernel(width, moves, y_ref, z_ref, dyn_ref, par_ref, mask_ref, ss_ref, co_ref, yg_ref, dz_ref, dy_ref, gg_ref, rd_ref, got_ss, got_co, sems, local_sems):
    step = pl.program_id(0)

    @pl.when(step == 0)
    def _():
        gg_ref[...] = jnp.zeros_like(gg_ref)
        peers, copies = make_moves(moves, (ss_ref, co_ref), (got_ss, got_co), sems, local_sems)
        greet(peers)
        for copy in copies:
            copy.start()
        for copy in copies:
            copy.wait()

    gain = par_ref[6:7]
    parts = y_ref.shape[0] // T
    for part in range(parts):
        rows = slice(part * T, part * T + T)
        here = step * parts + part
        ss, co = ss_ref[here], co_ref[here]
        for other in range(got_ss.shape[0]):
            ss, co = ss + got_ss[other, here], co + got_co[other, here]
        mask = to_col(mask_ref[part])[:, 0:1]
        inv_row = lax.rsqrt(ss / width + EPS)
        inv = to_col(inv_row)[:, 0:1]
        cube = to_col(inv_row * inv_row * inv_row * (co / width))[:, 0:1]
        y = y_ref[rows].astype(F32)
        z = z_ref[rows].astype(F32)
        dyn = dyn_ref[rows].astype(F32)
        s = sigmoid(z)
        act = z * s
        w = y * act
        wi = w * inv
        yg_ref[rows] = (wi * gain * mask).astype(BF16)
        gg_ref[0:1] += jnp.sum(dyn * wi, axis=0, keepdims=True)
        dw = inv * gain * dyn - w * cube
        dy_ref[rows] = (dw * act).astype(BF16)
        dz = dw * y * (s * (1.0 + z * (1.0 - s)))
        dz_ref[rows] = dz.astype(BF16)
        rd_ref[part] = to_row(jnp.sum(dz * z, axis=1, keepdims=True))


def backward_kernel(heads, extra, moves, dy_ref, x_ref, c_ref, cb_ref, ubd_ref, st_ref, par_ref, pbc_ref, head_ref, *refs):
    count = len(moves)
    srcs, refs = refs[:count], refs[count + extra :]
    dx_ref, dbd_ref, rd_ref, gx_ref, gb_ref, gh_ref = refs[:6]
    dsts, refs = refs[6 : 6 + count], refs[6 + count :]
    d_state, ext_x, ext_b, rows_ref, prod, edy_ref, tail_ref = refs[:7]
    if moves:
        began = (pl.program_id(0) == 0) & (pl.program_id(1) == 0)
        ended = (pl.program_id(0) == pl.num_programs(0) - 1) & (pl.program_id(1) == pl.num_programs(1) - 1)
        background(began, ended, moves, srcs, dsts, *refs[7:])
    first = (pl.program_id(0) == 0) & (pl.program_id(1) == 0)

    @pl.when(first)
    def _():
        gx_ref[...] = jnp.zeros_like(gx_ref)
        gb_ref[...] = jnp.zeros_like(gb_ref)
        gh_ref[...] = jnp.zeros_like(gh_ref)
        rows_ref[...] = jnp.zeros_like(rows_ref)

    @pl.when(pl.program_id(1) == 0)
    def _():
        ext_x[T : T + 8] = jnp.zeros_like(ext_x[T : T + 8])
        ext_b[T : T + 8] = jnp.zeros_like(ext_b[T : T + 8])
        d_state[...] = jnp.zeros_like(d_state)

    row, col = iotas(T, T)
    low = col < HEAD
    upto = col >= row
    below = row < col
    reach = (row >= col).astype(BF16)
    ubd = ubd_ref[...]
    raw, steps, rates, logs = step_terms(ubd, head_ref, heads)
    logs_t = logs.T
    cb = cb_ref[...]
    sb = sigmoid(cb)
    bc = cb * sb
    b_low, c_low = bc[:, :N].astype(BF16), bc[:, N:].astype(BF16)
    c_t = bc[:, N:].T.astype(BF16)
    scores = dot_nt(b_low, c_low)
    entering = st_ref[0]
    outer = dot(c_low, entering)
    ds_low = d_state[...].astype(BF16)
    back = dot(b_low, ds_low)
    d_scores = jnp.zeros((T, T), F32)
    skip_parts, closing_parts = [], []
    for pair in range(heads // 2):
        span = slice(128 * pair, 128 * pair + 128)
        h0, h1 = 2 * pair, 2 * pair + 1
        log0, log1 = lanes(logs, h0), lanes(logs, h1)
        log_pair = jnp.where(low, log0, log1)
        step_pair = jnp.where(low, lanes(steps, h0), lanes(steps, h1))
        last_pair = log_pair[T - 1 : T]
        cp = c_ref[:, span].astype(F32)
        sp = sigmoid(cp)
        xp = cp * sp
        xd = xp * step_pair
        dy_low = dy_ref[:, span]
        dy = dy_low.astype(F32)
        decay0 = jnp.exp(jnp.where(upto, logs_t[h0 : h0 + 1] - log0, NEG))
        decay1 = jnp.exp(jnp.where(upto, logs_t[h1 : h1 + 1] - log1, NEG))
        m0, m1 = scores * decay0, scores * decay1
        zero = jnp.zeros_like(dy_low)
        x_stack = jnp.concatenate([jnp.where(low, xd, 0.0).astype(BF16), jnp.where(low, 0.0, xd).astype(BF16)], axis=0)
        dm = dot_nt(x_stack, dy_low)
        dm0, dm1 = dm[:T], dm[T:]
        d_scores = d_scores + dm0 * decay0 + dm1 * decay1
        dy_stack = jnp.concatenate([jnp.where(low, dy, 0.0).astype(BF16), jnp.where(low, 0.0, dy).astype(BF16)], axis=0)
        dxd = dot(jnp.concatenate([m0.astype(BF16), m1.astype(BF16)], axis=1), dy_stack)
        flow = jnp.concatenate([(dm0 * m0).astype(BF16), (dm1 * m1).astype(BF16)], axis=0)
        later = dot(flow, reach)
        rows_ref[h0 : h0 + 1] = jnp.sum(jnp.where(below, later[:T], 0.0), axis=0, keepdims=True)
        rows_ref[h1 : h1 + 1] = jnp.sum(jnp.where(below, later[T:], 0.0), axis=0, keepdims=True)
        grow = jnp.exp(log_pair)
        tail = jnp.exp(last_pair - log_pair)
        from_state = tail * back[:, span]
        dxd = dxd + from_state
        edy = grow * dy
        prod[0:T, span] = (edy * outer[:, span]).astype(BF16)
        prod[T : 2 * T, span] = (from_state * xd).astype(BF16)
        prod[2 * T : 3 * T, span] = (xp * dxd).astype(BF16)
        skip_parts.append(jnp.sum(xp * dy, axis=0, keepdims=True))
        edy_low = edy.astype(BF16)
        edy_ref[:, span] = edy_low
        tail_ref[:, span] = (tail * xd).astype(BF16)
        old = d_state[:, span]
        closing = jnp.exp(last_pair)
        closing_parts.append(closing * jnp.sum(old * entering[:, span].astype(F32), axis=0, keepdims=True))
        d_state[:, span] = closing * old + dot(c_t, edy_low)
        dx = dxd * step_pair + par_ref[5:6, span] * dy
        ext_x[0:T, span] = dx * (sp * (1.0 + cp * (1.0 - sp)))
    d_low = d_scores.astype(BF16)
    d_b = dot_nt(tail_ref[...], ds_low) + dot(d_low, c_low)
    d_c = dot_nt(edy_ref[...], entering) + dot(d_scores.T.astype(BF16), b_low)
    width = heads * HEAD
    lane_row, lane_col = iotas(width, 128)
    member = (lane_row // HEAD == lane_col).astype(BF16)
    sums = dot(prod[...], member)
    skip_all = jnp.concatenate(skip_parts, axis=1)
    closing_all = jnp.concatenate(closing_parts, axis=1)
    fill = jnp.zeros((6, width), F32)
    few = dot_exact(jnp.concatenate([skip_all, closing_all, fill], axis=0), member.astype(F32))
    d_logs = dot(upto.astype(BF16), sums[:T].astype(BF16)) + dot((col < row).astype(BF16), sums[T : 2 * T].astype(BF16))
    d_logs = d_logs + rows_ref[...].T + few[1:2]
    d_steps = sums[2 * T :] + rates * d_logs
    d_raw = jnp.where(col < heads, d_steps * sigmoid(raw), 0.0)
    gh_ref[0:1] += jnp.sum(d_raw, axis=0, keepdims=True)
    gh_ref[1:2] += rates * jnp.sum(steps * d_logs, axis=0, keepdims=True)
    gh_ref[2:3] += few[0:1]
    ext_b[0:T, 0:N] = d_b * (sb[:, :N] * (1.0 + cb[:, :N] * (1.0 - sb[:, :N])))
    ext_b[0:T, N:] = d_c * (sb[:, N:] * (1.0 + cb[:, N:] * (1.0 - sb[:, N:])))

    def conv_back(ext, values, taps, grads):
        now = ext[0:T]
        total = taps[3:4] * now
        grads[3:4] += jnp.sum(values * now, axis=0, keepdims=True)
        grads[4:5] += jnp.sum(now, axis=0, keepdims=True)
        for k in range(3):
            moved = ext[3 - k : 3 - k + T]
            total = total + taps[k : k + 1] * moved
            grads[k : k + 1] += jnp.sum(values * moved, axis=0, keepdims=True)
        ext[T : T + 8] = ext[0:8]
        return total

    ux = x_ref[...].astype(F32)
    dux = conv_back(ext_x, ux, par_ref, gx_ref)
    dx_ref[...] = dux.astype(BF16)
    ubc = ubd[:, : 2 * N]
    dubc = conv_back(ext_b, ubc, pbc_ref, gb_ref)
    dbd_ref[:, : 2 * N] = dubc.astype(BF16)
    dbd_ref[:, 2 * N :] = d_raw.astype(BF16)
    total = jnp.sum(dux * ux, axis=1, keepdims=True) + jnp.sum(dubc * ubc, axis=1, keepdims=True)
    total = total + jnp.sum(jnp.where(col < heads, d_raw * ubd[:, 2 * N :], 0.0), axis=1, keepdims=True)
    rd_ref[0] = to_row(total)


def params(*semantics, number=0):
    if number:
        return pltpu.CompilerParams(
            dimension_semantics=semantics, vmem_limit_bytes=LIMIT, collective_id=number, has_side_effects=True
        )
    return pltpu.CompilerParams(dimension_semantics=semantics, vmem_limit_bytes=LIMIT)


def run_forward(heads, u_zx, u_bd, par, pbc, hp, came, w_out, number):
    rows, width = u_zx.shape[0], heads * HEAD
    slots, chunks = rows // LEN, LEN // T
    at = lambda s, i: (s * chunks + i, 0)
    fixed = lambda s, i: (0, 0)
    size, block, quarter = came.shape
    line = size // 2
    anywhere = pl.BlockSpec(memory_space=pl.ANY)
    sems = pltpu.SemaphoreType.DMA
    return pl.pallas_call(
        functools.partial(forward_kernel, heads, slots * chunks),
        grid=(slots, chunks),
        in_specs=[
            pl.BlockSpec((T, width), lambda s, i: (s * chunks + i, 1)),
            pl.BlockSpec((T, width), at),
            pl.BlockSpec((T, 3 * N), at),
            pl.BlockSpec((8, width), fixed),
            pl.BlockSpec((8, 2 * N), fixed),
            pl.BlockSpec((8, 128), fixed),
            anywhere,
            anywhere,
        ],
        out_specs=[
            pl.BlockSpec((T, width), at),
            pl.BlockSpec((1, 1, T), lambda s, i: (s * chunks + i, 0, 0)),
            pl.BlockSpec((T, width), at),
            pl.BlockSpec((T, 2 * N), at),
            pl.BlockSpec((1, N, width), lambda s, i: (s * chunks + i, 0, 0)),
            anywhere,
            anywhere,
        ],
        out_shape=[
            jax.ShapeDtypeStruct((rows, width), BF16),
            jax.ShapeDtypeStruct((rows // T, 1, T), F32),
            jax.ShapeDtypeStruct((rows, width), BF16),
            jax.ShapeDtypeStruct((rows, 2 * N), F32),
            jax.ShapeDtypeStruct((rows // T, N, width), BF16),
            jax.ShapeDtypeStruct((size, block, quarter * 4), BF16),
            full_shape(size, w_out),
        ],
        scratch_shapes=[
            pltpu.VMEM((T + 8, width), F32),
            pltpu.VMEM((T + 8, 2 * N), F32),
            pltpu.VMEM((N, width), F32),
            sems((2, 3, size)),
            sems((2, PARTS, line)),
            sems((2, PARTS, line)),
            sems((2,)),
        ],
        compiler_params=params("arbitrary", "arbitrary", number=number),
        cost_estimate=pl.CostEstimate(flops=rows * width * 2 * 1200, bytes_accessed=rows * width * 8, transcendentals=rows * width * 6),
        name="scan_forward",
    )(u_zx, u_zx, u_bd, par, pbc, hp, came, cut_shard(w_out))


def run_project(heads, order, x, w_in, moved, number):
    rows, deep = x.shape
    wide = w_in.shape[1]
    width = 2 * heads * HEAD
    step = 256
    moves = (("turn", "dp"),)
    anywhere = pl.BlockSpec(memory_space=pl.ANY)
    at = lambda i: (i, 0)
    fixed = lambda i: (0, 0)
    thin = pl.BlockSpec((step // T, 1, T), lambda i: (i, 0, 0))
    return pl.pallas_call(
        functools.partial(project_kernel, heads, moves),
        grid=(rows // step,),
        in_specs=[thin, pl.BlockSpec((rows, deep), fixed), pl.BlockSpec((deep, wide), fixed), anywhere],
        out_specs=[pl.BlockSpec((step, deep), at), thin, pl.BlockSpec((step, width), at), pl.BlockSpec((step, wide - width), at), anywhere],
        out_shape=[
            jax.ShapeDtypeStruct((rows, deep), BF16),
            jax.ShapeDtypeStruct((rows // T, 1, T), F32),
            jax.ShapeDtypeStruct((rows, width), BF16),
            jax.ShapeDtypeStruct((rows, wide - width), F32),
        ]
        + move_outs(moves, (moved,)),
        scratch_shapes=[pltpu.VMEM((8, deep), F32)] + move_scratch(moves, (moved,)),
        compiler_params=params("arbitrary", number=number),
        cost_estimate=pl.CostEstimate(flops=rows * deep * (rows + wide) * 2, bytes_accessed=rows * deep * 8, transcendentals=rows),
        name="project",
    )(order, x, w_in, moved)


def run_sort(order, values):
    rows, wide = values.shape
    step = 512
    return pl.pallas_call(
        sort_kernel,
        grid=(rows // step,),
        in_specs=[pl.BlockSpec((step // T, 1, T), lambda i: (i, 0, 0)), pl.BlockSpec((rows, wide), lambda i: (0, 0))],
        out_specs=pl.BlockSpec((step, wide), lambda i: (i, 0)),
        out_shape=jax.ShapeDtypeStruct((rows, wide), BF16),
        compiler_params=params("arbitrary"),
        cost_estimate=pl.CostEstimate(flops=rows * rows * wide * 2, bytes_accessed=rows * wide * 4, transcendentals=0),
        name="sort_rows",
    )(order, values)


def run_gate(grads, w_out, y, u_zx, par, mask):
    rows, width = y.shape
    deep = grads.shape[1]
    step = 256
    at = lambda i: (i, 0)
    fixed = lambda i: (0, 0)
    thin = pl.BlockSpec((step // T, 1, T), lambda i: (i, 0, 0))
    return pl.pallas_call(
        gate_kernel,
        grid=(rows // step,),
        in_specs=[
            pl.BlockSpec((step, deep), at),
            pl.BlockSpec((deep, width), fixed),
            pl.BlockSpec((step, width), at),
            pl.BlockSpec((step, width), at),
            pl.BlockSpec((8, width), fixed),
            thin,
        ],
        out_specs=[pl.BlockSpec((step, width), at), thin],
        out_shape=[jax.ShapeDtypeStruct((rows, width), BF16), jax.ShapeDtypeStruct((rows // T, 1, T), F32)],
        compiler_params=params("arbitrary"),
        cost_estimate=pl.CostEstimate(flops=rows * deep * width * 2, bytes_accessed=rows * deep * 2 + rows * width * 6, transcendentals=rows * width),
        name="gate_back",
    )(grads, w_out, y, u_zx, par, mask)


def run_home(order, sums, extra, deep, name):
    rows, quarter = sums[0].shape
    step = 512
    many = rows // step
    into = lambda i: (jnp.minimum(i, many - 1), 0)
    into3 = lambda i: (jnp.minimum(i, many - 1), 0, 0)
    thin = pl.BlockSpec((step // T, 1, T), into3)
    specs = [pl.BlockSpec((rows // T, 1, T), lambda i: (0, 0, 0))] + [pl.BlockSpec((step, quarter), into)] * 2
    values = list(sums)
    if extra is not None:
        specs += [pl.BlockSpec((step, quarter), into), thin, pl.BlockSpec((8, quarter), lambda i: (0, 0)), thin, thin]
        specs += [pl.BlockSpec((3, step // T, 1, T), lambda i: (0, jnp.minimum(i, many - 1), 0, 0))]
        values += list(extra)
    return pl.pallas_call(
        functools.partial(home_kernel, extra is not None, float(deep)),
        grid=(2 * many,),
        in_specs=specs,
        out_specs=pl.BlockSpec((step, quarter), lambda i: (jnp.maximum(i - many, 0), 0)),
        out_shape=jax.ShapeDtypeStruct((rows, quarter), BF16),
        scratch_shapes=[pltpu.VMEM((rows, quarter), BF16)],
        compiler_params=params("arbitrary"),
        cost_estimate=pl.CostEstimate(flops=rows * rows * quarter * 2, bytes_accessed=rows * quarter * 10, transcendentals=0),
        name=name,
    )(order, *values)


def run_mid(all_width, y, u_zx, dyn, par, mask, ss, co, number):
    rows, width = y.shape
    step = 256
    at = lambda i: (i, 0)
    fixed = lambda i: (0, 0)
    thin = pl.BlockSpec((step // T, 1, T), lambda i: (i, 0, 0))
    whole = pl.BlockSpec((rows // T, 1, T), lambda i: (0, 0, 0))
    wide = pl.BlockSpec((step, width), at)
    moves = (("spread", "head"), ("spread", "head"))
    others = lax.axis_size("head") - 1
    return pl.pallas_call(
        functools.partial(mid_kernel, float(all_width), moves),
        grid=(rows // step,),
        in_specs=[wide, wide, wide, pl.BlockSpec((8, width), fixed), thin, whole, whole],
        out_specs=[wide, wide, wide, pl.BlockSpec((8, width), fixed), thin],
        out_shape=[jax.ShapeDtypeStruct((rows, width), BF16)] * 3
        + [jax.ShapeDtypeStruct((8, width), F32), jax.ShapeDtypeStruct((rows // T, 1, T), F32)],
        scratch_shapes=[pltpu.VMEM((others, rows // T, 1, T), F32)] * 2 + move_scratch(moves, (ss, co)),
        compiler_params=params("arbitrary", number=number),
        cost_estimate=pl.CostEstimate(flops=rows * width * 30, bytes_accessed=rows * width * 12, transcendentals=rows * width),
        name="gate_mid",
    )(y, u_zx, dyn, par, mask, ss, co)


def run_backward(heads, slot, dy, u_zx, c, cb, u_bd, st, par, pbc, hp, before, moves, values, number):
    rows, width = dy.shape
    chunks = LEN // T
    place = lambda s, i: slot * chunks + chunks - 1 - i
    at = lambda s, i: (place(s, i), 0)
    at3 = lambda s, i: (place(s, i), 0, 0)
    fixed = lambda s, i: (0, 0)
    anywhere = pl.BlockSpec(memory_space=pl.ANY)
    return pl.pallas_call(
        functools.partial(backward_kernel, heads, len(before), tuple(moves)),
        grid=(1, chunks),
        in_specs=[
            pl.BlockSpec((T, width), at),
            pl.BlockSpec((T, width), lambda s, i: (place(s, i), 1)),
            pl.BlockSpec((T, width), at),
            pl.BlockSpec((T, 2 * N), at),
            pl.BlockSpec((T, 3 * N), at),
            pl.BlockSpec((1, N, width), at3),
            pl.BlockSpec((8, width), fixed),
            pl.BlockSpec((8, 2 * N), fixed),
            pl.BlockSpec((8, 128), fixed),
        ]
        + [anywhere] * (len(moves) + len(before)),
        out_specs=[
            pl.BlockSpec((T, width), at),
            pl.BlockSpec((T, 3 * N), at),
            pl.BlockSpec((1, 1, T), at3),
            pl.BlockSpec((8, width), fixed),
            pl.BlockSpec((8, 2 * N), fixed),
            pl.BlockSpec((8, 128), fixed),
        ]
        + [anywhere] * len(moves),
        out_shape=[
            jax.ShapeDtypeStruct((rows, width), BF16),
            jax.ShapeDtypeStruct((rows, 3 * N), BF16),
            jax.ShapeDtypeStruct((rows // T, 1, T), F32),
            jax.ShapeDtypeStruct((8, width), F32),
            jax.ShapeDtypeStruct((8, 2 * N), F32),
            jax.ShapeDtypeStruct((8, 128), F32),
        ]
        + move_outs(moves, values),
        scratch_shapes=[
            pltpu.VMEM((N, width), F32),
            pltpu.VMEM((T + 8, width), F32),
            pltpu.VMEM((T + 8, 2 * N), F32),
            pltpu.VMEM((128, 128), F32),
            pltpu.VMEM((3 * T, width), BF16),
            pltpu.VMEM((T, width), BF16),
            pltpu.VMEM((T, width), BF16),
        ]
        + move_scratch(moves, values),
        input_output_aliases={9 + len(moves) + i: i for i in range(len(before))},
        compiler_params=params("arbitrary", "arbitrary", number=number),
        cost_estimate=pl.CostEstimate(flops=LEN * width * 2 * 3000, bytes_accessed=LEN * width * 12, transcendentals=LEN * width * 8),
        name="scan_backward",
    )(dy, u_zx, c, cb, u_bd, st, par, pbc, hp, *values, *before)


def pieces_kernel(count, many, moves, *refs):
    total = len(moves)
    values, weights, srcs = refs[:count], refs[count : 2 * count], refs[2 * count : 2 * count + total]
    refs = refs[2 * count + total :]
    far_ref, own_ref = refs[:2]
    dsts, refs = refs[2 : 2 + total], refs[2 + total :]
    sent_ref, came_ref, near_sems = refs[:3]
    step = pl.program_id(0)
    rows, quarter = far_ref.shape
    dp, own = lax.axis_index("dp"), lax.axis_index("head")
    near = (dp, own ^ 1)
    peers, copies = make_moves(moves, srcs, dsts, *refs[3:]) if moves else ([], [])

    @pl.when(step == 0)
    def _():
        greet(peers if near_in(moves) else [near] + peers)
        for copy in copies:
            copy.start()

    def product(k):
        at = pl.ds(pl.multiple_of((own ^ k) * quarter, 128), quarter)
        out = None
        for value, weight in zip(values, weights):
            term = dot_nt(value[...], weight[at, :])
            out = term if out is None else out + term
        return out

    def near_copy(block):
        return pltpu.make_async_remote_copy(
            src_ref=sent_ref.at[block],
            dst_ref=came_ref.at[block],
            send_sem=near_sems.at[0, block],
            recv_sem=near_sems.at[1, block],
            device_id=near,
            device_id_type=MESH,
        )

    @pl.when(step < many)
    def _():
        sent_ref[step, :, :quarter] = product(3).astype(BF16)
        sent_ref[step, :, quarter:] = product(1).astype(BF16)
        near_copy(step).start()

    @pl.when(step >= many)
    def _():
        block = step - many
        far, mine = product(2), product(0)
        near_copy(block).wait_recv()
        far_ref[...] = (far + came_ref[block, :, :quarter].astype(F32)).astype(BF16)
        own_ref[...] = (mine + came_ref[block, :, quarter:].astype(F32)).astype(BF16)

    @pl.when(step == 2 * many - 1)
    def _():
        for block in range(many):
            near_copy(block).wait_send()
        for copy in copies:
            copy.wait()


def near_in(moves):
    return any(move[0] == "spread" and move[1] == "head" for move in moves)


def run_pieces(values, weights, quarter, name, moves, moved, number):
    rows = values[0].shape[0]
    step = 256
    many = rows // step
    anywhere = pl.BlockSpec(memory_space=pl.ANY)
    specs = [pl.BlockSpec((step, v.shape[1]), lambda i: (lax.rem(i, many), 0)) for v in values]
    for weight, block, wide in weights:
        specs.append(pl.BlockSpec((weight.shape[0], wide), lambda i, block=block: (0, block)))
    depth = sum(v.shape[1] for v in values)
    return pl.pallas_call(
        functools.partial(pieces_kernel, len(values), many, tuple(moves)),
        grid=(2 * many,),
        in_specs=specs + [anywhere] * len(moves),
        out_specs=[pl.BlockSpec((step, quarter), lambda i: (jnp.maximum(i - many, 0), 0))] * 2 + [anywhere] * len(moves),
        out_shape=[jax.ShapeDtypeStruct((rows, quarter), BF16)] * 2 + move_outs(moves, moved),
        scratch_shapes=[pltpu.VMEM((many, step, 2 * quarter), BF16)] * 2 + [pltpu.SemaphoreType.DMA((2, many))] + move_scratch(moves, moved),
        compiler_params=params("arbitrary", number=number),
        cost_estimate=pl.CostEstimate(flops=rows * depth * quarter * 8, bytes_accessed=rows * (depth + 4 * quarter) * 2, transcendentals=0),
        name=name,
    )(*values, *[w for w, _, _ in weights], *moved)


def grads_kernel(count, parts, moves, *refs):
    total = len(moves)
    lefts, rights, srcs = refs[:count], refs[count : 2 * count], refs[2 * count : 2 * count + total]
    refs = refs[2 * count + total :]
    outs, dsts, sems = refs[:count], refs[count : count + total], refs[count + total :]
    step = pl.program_id(0)
    if moves:
        background(step == 0, step == count * parts - 1, moves, srcs, dsts, *sems)
    for which in range(count):

        @pl.when((step >= which * parts) & (step < (which + 1) * parts))
        def _():
            out = lax.dot_general(lefts[which][...], rights[which][...], (((0,), (0,)), ((), ())), preferred_element_type=F32)
            outs[which][...] = out.astype(BF16)


def run_grads(pairs, name, moves=(), moved=(), number=0):
    rows, deep = pairs[0][0].shape
    step = 512
    parts = deep // step
    count = len(pairs)
    anywhere = pl.BlockSpec(memory_space=pl.ANY)
    into = lambda which: lambda i: jnp.clip(i - which * parts, 0, parts - 1)
    specs = [pl.BlockSpec((rows, step), lambda i, at=into(w): (0, at(i))) for w in range(count)]
    specs += [pl.BlockSpec(right.shape, lambda i: (0, 0)) for _, right in pairs]
    return pl.pallas_call(
        functools.partial(grads_kernel, count, parts, tuple(moves)),
        grid=(count * parts,),
        in_specs=specs + [anywhere] * len(moves),
        out_specs=[pl.BlockSpec((step, right.shape[1]), lambda i, at=into(w): (at(i), 0)) for w, (_, right) in enumerate(pairs)]
        + [anywhere] * len(moves),
        out_shape=[jax.ShapeDtypeStruct((deep, right.shape[1]), BF16) for _, right in pairs] + move_outs(moves, moved),
        scratch_shapes=move_scratch(moves, moved),
        compiler_params=params("arbitrary", number=number),
        cost_estimate=pl.CostEstimate(
            flops=sum(rows * deep * right.shape[1] * 2 for _, right in pairs), bytes_accessed=rows * deep * 2 * count, transcendentals=0
        ),
        name=name,
    )(*[left for left, _ in pairs], *[right for _, right in pairs], *moved)


def last_kernel(moves, *refs):
    count = len(moves)
    srcs, pair_ref = refs[:count], refs[count]
    dsts, out_ref = refs[count + 1 : 2 * count + 1], refs[2 * count + 1]
    kept_ref, line_ref, came_ref, own_ref, pair_sems, sems, local_sems = refs[2 * count + 2 :]
    me, head = lax.axis_index("dp"), lax.axis_index("head")
    peers, copies = make_moves(moves, srcs, dsts, sems, local_sems)

    def remote(src, dst, slot, peer):
        return pltpu.make_async_remote_copy(
            src_ref=src, dst_ref=dst, send_sem=pair_sems.at[0, slot], recv_sem=pair_sems.at[1, slot], device_id=(peer, head), device_id_type=MESH
        )

    high = me >> 1
    half = remote(pair_ref.at[:, 1 - (me & 1)], came_ref, 0, me ^ 1)
    line = [remote(kept_ref.at[high ^ j], line_ref.at[j - 1], j, me ^ (2 * j)) for j in range(1, own_ref.shape[0])]
    own = pltpu.make_async_copy(pair_ref.at[:, me & 1], own_ref, pair_sems.at[2, 0])
    greet(peers)
    half.start()
    own.start()
    for copy in copies:
        copy.start()
    own.wait()
    half.wait()
    for j in range(own_ref.shape[0]):
        kept_ref[j] = (own_ref[j].astype(F32) + came_ref[j].astype(F32)).astype(BF16)
    for copy in line:
        copy.start()
    for copy in line:
        copy.wait()
    total = kept_ref[high].astype(F32)
    for j in range(1, own_ref.shape[0]):
        total = total + line_ref[j - 1].astype(F32)
    out_ref[...] = total
    for copy in copies:
        copy.wait()


def run_last(moves, values, paired, number):
    many, _, block, wide = paired.shape
    anywhere = pl.BlockSpec(memory_space=pl.ANY)
    own = pltpu.VMEM((many, block, wide), BF16)
    return pl.pallas_call(
        functools.partial(last_kernel, tuple(moves)),
        in_specs=[anywhere] * (len(moves) + 1),
        out_specs=[anywhere] * len(moves) + [pl.BlockSpec(memory_space=pltpu.VMEM)],
        out_shape=move_outs(moves, values) + [jax.ShapeDtypeStruct((block, wide), F32)],
        scratch_shapes=[own, pltpu.VMEM((many - 1, block, wide), BF16), own, own, pltpu.SemaphoreType.DMA((3, many))] + move_scratch(moves, values),
        compiler_params=pltpu.CompilerParams(collective_id=number, has_side_effects=True, vmem_limit_bytes=LIMIT),
        name="last_exchange",
    )(*values, paired)


def row_forward(size, quarter, own_ref, full_ref, sems):
    me, own = lax.axis_index("dp"), lax.axis_index("head")
    columns = lambda head: pl.ds(pl.multiple_of(head * quarter, 128), quarter)

    def copy(src, dst, stage, k, head):
        return pltpu.make_async_remote_copy(
            src_ref=src, dst_ref=dst, send_sem=sems.at[0, stage, k], recv_sem=sems.at[1, stage, k], device_id=(me, head), device_id_type=MESH
        )

    def source(k):
        return full_ref.at[me ^ k, :, columns(own)] if own_ref is None else own_ref.at[me ^ k]

    def far(k):
        return copy(source(k), full_ref.at[me ^ k, :, columns(own)], 0, k, own ^ 2)

    def near(k):
        return copy(source(k), full_ref.at[me ^ k, :, columns(own)], 1, k, own ^ 1)

    def back(k):
        block = full_ref.at[me ^ k, :, columns(own ^ 2)]
        return copy(block, block, 2, k, own ^ 1)

    return far, near, back


def shard_spread(src, dst, across_sems, side_sems):
    me, own = lax.axis_index("dp"), lax.axis_index("head")

    def copy(a, b, sems, part, j, peer):
        return pltpu.make_async_remote_copy(
            src_ref=a, dst_ref=b, send_sem=sems.at[0, part, j], recv_sem=sems.at[1, part, j], device_id=(peer, own), device_id_type=MESH
        )

    def across(part, j):
        return copy(src.at[part], dst.at[me, part], across_sems, part, j, me ^ (2 * j))

    def side(part, j):
        here = dst.at[me ^ (2 * j), part]
        return copy(src.at[part] if j == 0 else here, here, side_sems, part, j, me ^ 1)

    return across, side


def entry_kernel(parts, x_ref, w_ref, fx_ref, fw_ref, row_sems, pass_sems, across_sems, side_sems, local_sems):
    size, quarter = x_ref.shape[0], x_ref.shape[2]
    line = size // 2
    me, own = lax.axis_index("dp"), lax.axis_index("head")
    mine = pl.ds(pl.multiple_of(own * quarter, 128), quarter)
    far, near, back = row_forward(size, quarter, None, fx_ref, pass_sems)
    across, side = shard_spread(w_ref, fw_ref, across_sems, side_sems)

    def rows(k):
        return pltpu.make_async_remote_copy(
            src_ref=x_ref.at[me ^ k],
            dst_ref=fx_ref.at[me, :, mine],
            send_sem=row_sems.at[0, k],
            recv_sem=row_sems.at[1, k],
            device_id=(me ^ k, own),
            device_id_type=MESH,
        )

    greet([(me ^ k, own) for k in range(1, size)] + [(me, own ^ 1), (me, own ^ 2)])
    held = [
        pltpu.make_async_copy(x_ref.at[me], fx_ref.at[me, :, mine], local_sems.at[0]),
        pltpu.make_async_copy(w_ref, fw_ref.at[me], local_sems.at[1]),
    ]
    for copy in held:
        copy.start()
    order = turn_order(size)
    for k in order:
        rows(k).start()
    for part in range(parts):
        side(part, 0).start()
    held[0].wait()
    far(0).start()
    near(0).start()
    for k in order:
        rows(k).wait_recv()
        far(k).start()
        near(k).start()
    for part in range(min(2, parts)):
        for j in range(1, line):
            across(part, j).start()
    for k in [0] + order:
        far(k).wait_recv()
        back(k).start()
    for part in range(parts):
        for j in range(1, line):
            across(part, j).wait_recv()
            side(part, j).start()
        if part + 2 < parts:
            for j in range(1, line):
                across(part + 2, j).start()
    held[1].wait()
    for k in range(size):
        near(k).wait()
        back(k).wait()
        far(k).wait_send()
        if k:
            rows(k).wait_send()
    for part in range(parts):
        for j in range(line):
            side(part, j).wait()
            if j:
                across(part, j).wait_send()


PARTS = 4


def cut_shard(w):
    return w.reshape(PARTS, w.shape[0] // PARTS, w.shape[1])


def full_shape(size, w):
    return jax.ShapeDtypeStruct((size, PARTS, w.shape[0] // PARTS, w.shape[1]), BF16)


def run_entry(tokens, w_in, number):
    size = lax.axis_size("dp")
    rows, quarter = tokens.shape
    line = size // 2
    anywhere = pl.BlockSpec(memory_space=pl.ANY)
    sems = pltpu.SemaphoreType.DMA
    came, full = pl.pallas_call(
        functools.partial(entry_kernel, PARTS),
        in_specs=[anywhere] * 2,
        out_specs=[anywhere] * 2,
        out_shape=[jax.ShapeDtypeStruct((size, rows // size, quarter * 4), BF16), full_shape(size, w_in)],
        scratch_shapes=[sems((2, size)), sems((2, 3, size)), sems((2, PARTS, line)), sems((2, PARTS, line)), sems((2,))],
        compiler_params=pltpu.CompilerParams(collective_id=number, has_side_effects=True, vmem_limit_bytes=LIMIT),
        name="entry",
    )(tokens.reshape(size, rows // size, quarter), cut_shard(w_in))
    return came.reshape(rows, quarter * 4), full.reshape(size * w_in.shape[0], w_in.shape[1])


def mm(a, b, contract, kind):
    return lax.dot_general(a, b, (contract, ((), ())), preferred_element_type=F32).astype(kind)


def body(tokens, cotangent, order, lengths, norm_gain, w_zx, w_bc, w_dt, w_out, conv_x, conv_bc, head_params, gate_gain):
    rows, quarter = tokens.shape
    heads = head_params.shape[1]
    width = heads * HEAD
    place = lax.axis_index("head")
    size = lax.axis_size("dp")
    here = lax.axis_index("dp")
    all_width = width * lax.axis_size("head")
    deep = quarter * lax.axis_size("head")
    own_w = w_zx.shape[0]
    arrange = order.astype(F32).reshape(rows // T, 1, T)

    packed = jnp.concatenate(
        [w_zx.reshape(own_w, 2 * width), w_bc, w_dt, norm_gain[:, None], jnp.zeros((own_w, 127 - heads), BF16)], axis=1
    )
    blocks = lambda value: value.reshape(size, rows // size, quarter)
    came_x, w_in = run_entry(tokens, packed, 1)
    normed, inv_one, u_zx, u_bd, own_g = run_project(heads, arrange, came_x, w_in, blocks(cotangent), 2)

    par = jnp.concatenate([conv_x, jnp.repeat(head_params[2:3], HEAD, axis=1), gate_gain[None], jnp.zeros((1, width), F32)], axis=0)
    pbc = jnp.concatenate([conv_bc, jnp.zeros((3, 2 * N), F32)], axis=0)
    hp = jnp.pad(head_params, ((0, 5), (0, 128 - heads)))
    positions = lax.broadcasted_iota(jnp.int32, (lengths.shape[0], LEN), 1)
    mask = (positions < lengths[:, None]).astype(F32).reshape(rows // T, 1, T)

    sorted_g = run_sort(arrange, own_g.reshape(rows, quarter))
    y, ss, c, cb, st, full_g, w_o = run_forward(heads, u_zx, u_bd, par, pbc, hp, blocks(sorted_g), w_out, 3)
    w_o = w_o.reshape(deep, width)
    full_g = full_g.reshape(rows, deep)
    dyn, co = run_gate(full_g, w_o, y, u_zx, par, mask)
    yg, dz, dy, gg, rd_z = run_mid(all_width, y, u_zx, dyn, par, mask, ss, co, 4)

    def keep(paired, came, bit):
        own = lax.dynamic_index_in_dim(paired, (here >> bit) & 1, 1, keepdims=False)
        return (own.astype(F32) + came.astype(F32)).astype(BF16)

    def total(kept, came, shift):
        own = lax.dynamic_index_in_dim(kept, here >> shift, 0, keepdims=False)
        return own.astype(F32) + jnp.sum(came.astype(F32), axis=0)

    def pairs(grads):
        return grads.reshape(size // 2, 2, own_w, grads.shape[1])

    def fours(grads):
        return grads.reshape(size // 4, 2, -1, own_w, grads.shape[-1])

    scan = functools.partial(run_backward, heads)
    shared = (dy, u_zx, c, cb, u_bd, st, par, pbc, hp)
    half_rows = rows // 2
    out_far, out_own = run_pieces([yg], [(w_o, 0, width)], quarter, "branch_pieces", [], [], 5)
    grad_o, grad_z, far0 = run_grads([(full_g, yg), (normed, dz)], "gate_grads", [("rows", "head", 2, 0, half_rows)], [out_far], 6)
    grad_o, grad_z = pairs(grad_o), fours(grad_z)
    *back0, gx0, gb0, gh0, came_o, came_z, far1 = scan(
        0, *shared, (), [("half", "dp", 0), ("half", "dp", 1), ("rows", "head", 2, half_rows, half_rows)], [grad_o, grad_z, out_far], 7
    )
    sent_out = run_home(arrange, [out_own, jnp.concatenate([far0, far1], axis=0)], None, deep, "home_out")
    kept_o = keep(grad_o, came_o, 0).reshape(size // 4, 2, own_w, width)
    kept_z = keep(grad_z, came_z, 1)
    *back1, gx1, gb1, gh1, got_out, came_z, came_o = scan(
        1, *shared, back0, [("turn", "dp"), ("half", "dp", 0), ("half", "dp", 1)], [blocks(sent_out), kept_z, kept_o], 8
    )
    dux, dbd, rd_x = back1
    kept_z, kept_o = keep(kept_z, came_z, 0), keep(kept_o, came_o, 1)
    grad_x, grad_bd = run_grads([(normed, dux), (normed, dbd)], "scan_grads")
    grad_x, grad_bd = pairs(grad_x), pairs(grad_bd)
    gb = gb0 + gb1
    d_far, d_own, line_o, line_z, came_x2, got_rows, got_gb = run_pieces(
        [dz, dux, dbd],
        [(w_in, 0, width), (w_in, 1, width), (w_in, 2 * width // (3 * N), 3 * N)],
        quarter,
        "input_pieces",
        [("direct", "dp", 2), ("direct", "dp", 2), ("half", "dp", 0), ("spread", "head"), ("spread", "head")],
        [kept_o, kept_z, grad_x, rd_z + rd_x, gb],
        9,
    )
    kept_x = keep(grad_x, came_x2, 0)
    gb = gb[:5] + jnp.sum(got_gb, axis=0)[:5]
    gh = gh0 + gh1
    ends = jnp.concatenate([gb[3], gb[4]] + [gh[i, :32] for i in range(3)] + [jnp.zeros((width - 4 * N - 96,), F32)])
    small = jnp.concatenate([(gx0 + gx1)[:5], gg[:1], jnp.concatenate([gb[0], gb[1], gb[2]])[None], ends[None]], axis=0)
    d_arrived, line_x, got_small, grad_bd = run_last(
        [("whole", "head", 2), ("direct", "dp", 1), ("spread", "dp")], [d_far, kept_x, small], grad_bd, 10
    )

    gain_all = w_in[:, 2 * width + 2 * N + heads].astype(F32)
    gain_own = jnp.broadcast_to(lax.dynamic_slice_in_dim(gain_all, place * quarter, quarter, 0)[None], (8, quarter))
    normed_own = lax.dynamic_slice_in_dim(normed, place * quarter, quarter, 1)
    sent_back = run_home(arrange, [d_own, d_arrived], [normed_own, inv_one, gain_own, rd_z, rd_x, got_rows], deep, "home_back")
    got_back = lax.all_to_all(sent_back, "dp", split_axis=0, concat_axis=0, tiled=True)
    final_back = (cotangent.astype(F32) + got_back.astype(F32)).astype(BF16)

    final_out = (tokens.astype(F32) + got_out.reshape(rows, quarter).astype(F32)).astype(BF16)
    grad_out, grad_z = total(kept_o, line_o, 2), total(kept_z, line_z, 2)
    grad_x = total(kept_x, line_x, 1)
    small = small + jnp.sum(got_small, axis=0)
    grad_zx = jnp.stack([grad_z, grad_x], axis=1)
    of_gain = jnp.sum(grad_z * w_zx[:, 0].astype(F32), axis=1) + jnp.sum(grad_x * w_zx[:, 1].astype(F32), axis=1)
    of_gain = of_gain + jnp.sum(grad_bd[:, : 2 * N] * w_bc.astype(F32), axis=1)
    of_gain = of_gain + jnp.sum(grad_bd[:, 2 * N : 2 * N + heads] * w_dt.astype(F32), axis=1)
    last = jnp.concatenate([grad_bd[:, : 2 * N], jnp.broadcast_to(of_gain[:, None], (own_w, 128))], axis=1)
    others, = run_exchange([("spread", "head")], [last], 11)
    last = last + jnp.sum(others, axis=0)
    grad_gain = last[:, 2 * N] / norm_gain.astype(F32)
    gx, gg = small[0:5], small[5]
    gb = jnp.concatenate([small[6].reshape(3, 2 * N), small[7, : 4 * N].reshape(2, 2 * N)], axis=0)
    gh = small[7, 4 * N : 4 * N + 96].reshape(3, 32)[:, :heads]
    return (final_out, final_back, grad_gain, grad_zx, last[:, : 2 * N], grad_bd[:, 2 * N : 2 * N + heads], grad_out, gx, gb, gh, gg)


def solution(mesh):
    return jax.shard_map(
        body,
        mesh=mesh,
        in_specs=(
            P("dp", "head"),
            P("dp", "head"),
            P("dp", None),
            P("dp"),
            P("dp"),
            P("dp", None, "head"),
            P("dp", None),
            P("dp", "head"),
            P("dp", "head"),
            P(None, "head"),
            P(),
            P(None, "head"),
            P("head"),
        ),
        out_specs=(
            P("dp", "head"),
            P("dp", "head"),
            P("dp"),
            P("dp", None, "head"),
            P("dp", None),
            P("dp", "head"),
            P("dp", "head"),
            P(None, "head"),
            P(),
            P(None, "head"),
            P("head"),
        ),
        check_vma=False,
    )
```

```python
import functools

import jax
import jax.numpy as jnp
from jax import lax
from jax.experimental import pallas as pl
from jax.experimental.pallas import tpu as pltpu
from jax.sharding import PartitionSpec as P

LEN = 1024
T = 128
N = 128
HEAD = 64
EPS = 1e-05
NEG = -1e30
LIGHT = 1000
LIMIT = 60 * 1024 * 1024
AXES = ("dp", "head")
F32 = jnp.float32
BF16 = jnp.bfloat16


def dot(a, b):
    return lax.dot_general(a, b, (((1,), (0,)), ((), ())), preferred_element_type=F32)


def dot_nt(a, b):
    return lax.dot_general(a, b, (((1,), (1,)), ((), ())), preferred_element_type=F32)


def dot_exact(a, b):
    return lax.dot_general(
        a, b, (((1,), (0,)), ((), ())), preferred_element_type=F32, precision=lax.Precision.HIGHEST
    )


def iotas(rows, cols):
    return (
        lax.broadcasted_iota(jnp.int32, (rows, cols), 0),
        lax.broadcasted_iota(jnp.int32, (rows, cols), 1),
    )


MESH = pl.DeviceIdType.MESH


def greet(peers):
    barrier = pltpu.get_barrier_semaphore()
    for peer in peers:
        pl.semaphore_signal(barrier, inc=1, device_id=peer, device_id_type=MESH)
    pl.semaphore_wait(barrier, len(peers))


def place_of():
    return {name: lax.axis_index(name) for name in AXES}


def move_copies(move, src, dst):
    kind, axis = move[0], move[1]
    place = place_of()
    me = place[axis]

    def peer(flip):
        return tuple(place[name] ^ flip if name == axis else place[name] for name in AXES)

    if kind == "whole":
        return [(peer(move[2]), src, dst)], []
    if kind == "rows":
        return [(peer(move[2]), src.at[pl.ds(move[3], move[4])], dst)], []
    if kind == "half":
        return [(peer(1 << move[2]), src.at[:, 1 - ((me >> move[2]) & 1)], dst)], []
    if kind == "direct":
        high = me >> move[2]
        return [(peer(j << move[2]), src.at[high ^ j], dst.at[j - 1]) for j in range(1, dst.shape[0] + 1)], []
    if kind == "all":
        groups = lax.axis_size("head")
        flips = [divmod(flat, groups) for flat in range(1, dst.shape[0] + 1)]
        return [((place["dp"] ^ f, place["head"] ^ e), src, dst.at[i]) for i, (f, e) in enumerate(flips)], []
    if kind == "spread":
        return [(peer(flip), src, dst.at[flip - 1]) for flip in range(1, dst.shape[0] + 1)], []
    remote = [(peer(k), src.at[me ^ k], dst.at[me]) for k in turn_order(src.shape[0])]
    return remote, [(src.at[me], dst.at[me])]


def turn_order(size):
    return sorted(range(1, size), key=lambda k: (-(k & ~1), k & 1))


def move_shape(move, shape):
    kind = move[0]
    if kind == "rows":
        return (move[4],) + shape[1:]
    if kind == "half":
        return (shape[0],) + shape[2:]
    if kind == "direct":
        return (shape[0] - 1,) + shape[1:]
    if kind == "spread":
        return (lax.axis_size(move[1]) - 1,) + shape
    if kind == "all":
        return (lax.axis_size("dp") * lax.axis_size("head") - 1,) + shape
    return shape


def move_counts(moves, values):
    remote = local = 0
    for move, value in zip(moves, values):
        size = lax.axis_size(move[1])
        world = lax.axis_size("dp") * lax.axis_size("head")
        count = {"direct": value.shape[0] - 1, "spread": size - 1, "turn": size - 1, "all": world - 1}.get(move[0], 1)
        remote, local = remote + count, local + (move[0] == "turn")
    return remote, local


def move_scratch(moves, values):
    remote, local = move_counts(moves, values)
    return [pltpu.SemaphoreType.DMA((2, remote)), pltpu.SemaphoreType.DMA((max(local, 1),))] if moves else []


def move_outs(moves, values):
    return [jax.ShapeDtypeStruct(move_shape(move, value.shape), value.dtype) for move, value in zip(moves, values)]


def make_moves(moves, srcs, dsts, sems, local_sems):
    remote, local = [], []
    for move, src, dst in zip(moves, srcs, dsts):
        here, there = move_copies(move, src, dst)
        remote += here
        local += there
    copies = [
        pltpu.make_async_remote_copy(src_ref=a, dst_ref=b, send_sem=sems.at[0, i], recv_sem=sems.at[1, i], device_id=peer, device_id_type=MESH)
        for i, (peer, a, b) in enumerate(remote)
    ]
    copies += [pltpu.make_async_copy(a, b, local_sems.at[i]) for i, (a, b) in enumerate(local)]
    return move_peers(moves, dsts), copies


def move_peers(moves, dsts):
    flips = {}
    for move, dst in zip(moves, dsts):
        kind, axis = move[0], move[1]
        if kind in ("whole", "rows"):
            own = [move[2]]
        elif kind == "half":
            own = [1 << move[2]]
        elif kind == "direct":
            own = [j << move[2] for j in range(1, dst.shape[0] + 1)]
        elif kind == "all":
            groups = lax.axis_size("head")
            for flat in range(1, dst.shape[0] + 1):
                flips[divmod(flat, groups)] = None
            continue
        elif kind == "spread":
            own = range(1, dst.shape[0] + 1)
        else:
            own = range(1, dst.shape[0])
        for flip in own:
            flips[(flip, 0) if axis == "dp" else (0, flip)] = None
    place = place_of()
    return [(place["dp"] ^ f, place["head"] ^ e) for f, e in flips]


def background(first, last, moves, srcs, dsts, sems, local_sems):
    peers, copies = make_moves(moves, srcs, dsts, sems, local_sems)

    @pl.when(first)
    def _():
        greet(peers)
        for copy in copies:
            copy.start()

    @pl.when(last)
    def _():
        for copy in copies:
            copy.wait()


def exchange_kernel(moves, *refs):
    count = len(moves)
    peers, copies = make_moves(moves, refs[:count], refs[count : 2 * count], refs[2 * count], refs[2 * count + 1])
    greet(peers)
    for copy in copies:
        copy.start()
    for copy in copies:
        copy.wait()


def run_exchange(moves, values, number):
    return pl.pallas_call(
        functools.partial(exchange_kernel, tuple(moves)),
        in_specs=[pl.BlockSpec(memory_space=pl.ANY)] * len(moves),
        out_specs=[pl.BlockSpec(memory_space=pl.ANY)] * len(moves),
        out_shape=move_outs(moves, values),
        scratch_shapes=move_scratch(moves, values),
        compiler_params=pltpu.CompilerParams(collective_id=number, has_side_effects=True, vmem_limit_bytes=LIMIT),
        name="exchange",
    )(*values)


def sigmoid(v):
    return 1.0 / (1.0 + jnp.exp(-v))


def softplus(v):
    return jnp.maximum(v, 0.0) + jnp.log1p(jnp.exp(-jnp.abs(v)))


def to_col(row):
    return jnp.broadcast_to(row, (T, T)).T


def to_row(col):
    return jnp.broadcast_to(col, (T, T)).T[0:1]


def lanes(value, pick):
    return jnp.broadcast_to(value[:, pick : pick + 1], (value.shape[0], 128))


def step_terms(ubd, head_ref, heads):
    row, col = iotas(T, T)
    raw = jnp.where(col < heads, ubd[:, 2 * N :] + head_ref[0:1], 0.0)
    steps = jnp.where(col < heads, softplus(raw), 0.0)
    rates = -jnp.exp(head_ref[1:2])
    tril = (row >= col).astype(F32)
    logs = dot_exact(tril, steps * rates)
    return raw, steps, rates, logs


def forward_moves(steps, rows_ref, w_ref, full_ref, fw_ref, pass_sems, across_sems, side_sems, local_sems, rows_held, w_held):
    size, quarter = rows_ref.shape[0], rows_ref.shape[2]
    line = size // 2
    parts = w_ref.shape[0]
    me, own = lax.axis_index("dp"), lax.axis_index("head")
    step = pl.program_id(0) * pl.num_programs(1) + pl.program_id(1)
    far, near, back = row_forward(size, quarter, rows_ref, full_ref, pass_sems)
    across, side = shard_spread(w_ref, fw_ref, across_sems, side_sems)
    mine = pl.ds(pl.multiple_of(own * quarter, 128), quarter)
    into = [pltpu.make_async_copy(rows_ref, rows_held, local_sems.at[0]), pltpu.make_async_copy(w_ref, w_held, local_sems.at[1])]
    held = [
        pltpu.make_async_copy(rows_held, full_ref.at[:, :, mine], local_sems.at[2]),
        pltpu.make_async_copy(w_held, fw_ref.at[me], local_sems.at[3]),
    ]

    @pl.when(step == 0)
    def _():
        for copy in into:
            copy.start()
        greet([(me ^ 1, own)] + [(me ^ (2 * j), own) for j in range(1, line)] + [(me, own ^ 1), (me, own ^ 2)])
        for k in range(size):
            near(k).start()
        for k in range(size // 2):
            far(k).start()
        for part in range(parts):
            side(part, 0).start()
        for part in range(min(2, parts)):
            for j in range(1, line):
                across(part, j).start()

    for part in range(parts):

        @pl.when(step == min(steps - 1, (part + 2) * steps // (parts + 1)))
        def _():
            for j in range(1, line):
                across(part, j).wait_recv()
                side(part, j).start()
            if part + 2 < parts:
                for j in range(1, line):
                    across(part + 2, j).start()

    @pl.when(step == 1)
    def _():
        for first, second in zip(into, held):
            first.wait()
            second.start()

    groups = 4
    for group in range(groups):
        members = range(group * size // groups, (group + 1) * size // groups)

        @pl.when(step == min(steps - 1, ((group + 1) * 3 * steps) // (2 * groups)))
        def _():
            for k in members:
                far(k).wait_recv()
                back(k).start()
                if k < size // 2:
                    far(k + size // 2).start()

    @pl.when(step == steps - 1)
    def _():
        for copy in held:
            copy.wait()
        for k in range(size):
            near(k).wait()
            back(k).wait()
            far(k).wait_send()
        for part in range(parts):
            for j in range(line):
                side(part, j).wait()
                if j:
                    across(part, j).wait_send()


def forward_kernel(heads, steps, x_ref, z_ref, ubd_ref, par_ref, pbc_ref, head_ref, rows_ref, w_ref, y_ref, ss_ref, c_ref, cb_ref, st_ref, full_ref, fw_ref, ext_x, ext_b, state, *sems):
    forward_moves(steps, rows_ref, w_ref, full_ref, fw_ref, *sems)

    @pl.when(pl.program_id(1) == 0)
    def _():
        ext_x[0:8] = jnp.zeros_like(ext_x[0:8])
        ext_b[0:8] = jnp.zeros_like(ext_b[0:8])
        state[...] = jnp.zeros_like(state)

    def conv(ext, values, taps):
        ext[8 : 8 + T] = values
        total = taps[4:5] + taps[3:4] * values
        for k in range(3):
            total = total + taps[k : k + 1] * ext[5 + k : 5 + k + T]
        ext[0:8] = ext[T : T + 8]
        return total

    row, col = iotas(T, T)
    low = col < HEAD
    low_row = lax.broadcasted_iota(jnp.int32, (1, 128), 1) < HEAD
    causal = row >= col
    ubd = ubd_ref[...]
    c = conv(ext_x, x_ref[...].astype(F32), par_ref)
    c_ref[...] = c.astype(BF16)
    cb = conv(ext_b, ubd[:, : 2 * N], pbc_ref)
    cb_ref[...] = cb
    bc = cb * sigmoid(cb)
    b_rows = bc[:, :N]
    b_t = b_rows.T.astype(BF16)
    b_low, c_low = b_rows.astype(BF16), bc[:, N:].astype(BF16)
    _, steps, _, logs = step_terms(ubd, head_ref, heads)
    logs_t = logs.T
    scores = dot_nt(c_low, b_low)
    entering = state[...].astype(BF16)
    st_ref[0] = entering
    outer = dot(c_low, entering)
    squares = jnp.zeros((T, 128), F32)
    for pair in range(heads // 2):
        span = slice(128 * pair, 128 * pair + 128)
        h0, h1 = 2 * pair, 2 * pair + 1
        log0, log1 = lanes(logs, h0), lanes(logs, h1)
        log_pair = jnp.where(low, log0, log1)
        step_pair = jnp.where(low, lanes(steps, h0), lanes(steps, h1))
        last_pair = log_pair[T - 1 : T]
        cp = c[:, span]
        xp = cp * sigmoid(cp)
        xd = xp * step_pair
        m0 = (scores * jnp.exp(jnp.where(causal, log0 - logs_t[h0 : h0 + 1], NEG))).astype(BF16)
        m1 = (scores * jnp.exp(jnp.where(causal, log1 - logs_t[h1 : h1 + 1], NEG))).astype(BF16)
        stacked = jnp.concatenate([jnp.where(low, xd, 0.0).astype(BF16), jnp.where(low, 0.0, xd).astype(BF16)], axis=0)
        y = dot(jnp.concatenate([m0, m1], axis=1), stacked)
        y = y + jnp.exp(log_pair) * outer[:, span] + par_ref[5:6, span] * xp
        tail = (jnp.exp(last_pair - log_pair) * xd).astype(BF16)
        state[:, span] = jnp.exp(last_pair) * state[:, span] + dot(b_t, tail)
        y_ref[:, span] = y.astype(BF16)
        zp = z_ref[:, span].astype(F32)
        w = y * zp * sigmoid(zp)
        squares = squares + w * w
    ss_ref[0] = to_row(jnp.sum(squares, axis=1, keepdims=True))


def row_picks(order_ref, count):
    lane = lax.broadcasted_iota(jnp.int32, (T, T), 1).astype(F32)
    blocks = []
    for part in range(order_ref.shape[0]):
        wanted = to_col(order_ref[part])
        blocks.append(jnp.concatenate([(wanted == lane + float(T * j)).astype(F32).astype(BF16) for j in range(count)], axis=1))
    return jnp.concatenate(blocks, axis=0)


def project_kernel(heads, order_ref, x_ref, w_ref, out_ref, inv_ref, uzx_ref, ubd_ref, gain_ref):
    deep, width = x_ref.shape[1], 2 * heads * HEAD

    @pl.when(pl.program_id(0) == 0)
    def _():
        for j in range(deep // T):
            span = slice(j * T, j * T + T)
            gain_ref[0:1, span] = w_ref[span, width + 2 * N : width + 3 * N].astype(F32).T[heads : heads + 1]

    x = dot(row_picks(order_ref, x_ref.shape[0] // T), x_ref[...])
    inv = lax.rsqrt(jnp.sum(x * x, axis=1, keepdims=True) / deep + EPS)
    normed = (x * inv * gain_ref[0:1]).astype(BF16)
    out_ref[...] = normed
    for part in range(x.shape[0] // T):
        inv_ref[part] = to_row(inv[part * T : part * T + T])
    uzx_ref[...] = dot(normed, w_ref[:, :width]).astype(BF16)
    ubd_ref[...] = dot(normed, w_ref[:, width:])


def sort_kernel(order_ref, rows_ref, out_ref):
    out_ref[...] = dot(row_picks(order_ref, rows_ref.shape[0] // T), rows_ref[...]).astype(BF16)


def gate_kernel(g_ref, wo_ref, y_ref, z_ref, par_ref, mask_ref, dyn_ref, co_ref):
    dyn = dot(g_ref[...], wo_ref[...])
    for part in range(dyn.shape[0] // T):
        rows = slice(part * T, part * T + T)
        mask = to_col(mask_ref[part])[:, 0:1]
        own = dyn[rows] * mask
        dyn_ref[rows] = own.astype(BF16)
        z = z_ref[rows].astype(F32)
        w = y_ref[rows].astype(F32) * z * sigmoid(z)
        co_ref[part] = to_row(jnp.sum(own * w * par_ref[6:7], axis=1, keepdims=True))


def home_kernel(last, deep, order_ref, a_ref, b_ref, *refs):
    out_ref, held_ref = refs[-2:]
    step = pl.program_id(0)
    many = held_ref.shape[0] // a_ref.shape[0]
    size = a_ref.shape[0]

    @pl.when(step < many)
    def _():
        value = a_ref[...].astype(F32) + b_ref[...].astype(F32)
        if last:
            normed_ref, inv_ref, gain_ref, rdz_ref, rdx_ref, more_ref = refs[:6]
            gain = gain_ref[0:1]
            hat = normed_ref[...].astype(F32) / gain
            parts = []
            for part in range(size // T):
                inv_row = inv_ref[part]
                dots = rdz_ref[part] + rdx_ref[part] + more_ref[0, part] + more_ref[1, part] + more_ref[2, part]
                rows = slice(part * T, part * T + T)
                inv = to_col(inv_row)[:, 0:1]
                mean = to_col(dots / deep)[:, 0:1]
                parts.append(inv * (gain * value[rows] - hat[rows] * mean))
            value = jnp.concatenate(parts, axis=0)
        held_ref[pl.ds(pl.multiple_of(step * size, size), size), :] = value.astype(BF16)

    @pl.when(step >= many)
    def _():
        base = ((step - many) * size).astype(F32)
        row = lax.broadcasted_iota(jnp.int32, (size, T), 0).astype(F32) + base
        picks = jnp.concatenate([(row == order_ref[j]).astype(F32).astype(BF16) for j in range(order_ref.shape[0])], axis=1)
        out_ref[...] = dot(picks, held_ref[...]).astype(BF16)


def mid_kernel(width, moves, y_ref, z_ref, dyn_ref, par_ref, mask_ref, ss_ref, co_ref, yg_ref, dz_ref, dy_ref, gg_ref, rd_ref, got_ss, got_co, sems, local_sems):
    step = pl.program_id(0)

    @pl.when(step == 0)
    def _():
        gg_ref[...] = jnp.zeros_like(gg_ref)
        peers, copies = make_moves(moves, (ss_ref, co_ref), (got_ss, got_co), sems, local_sems)
        greet(peers)
        for copy in copies:
            copy.start()
        for copy in copies:
            copy.wait()

    gain = par_ref[6:7]
    parts = y_ref.shape[0] // T
    for part in range(parts):
        rows = slice(part * T, part * T + T)
        here = step * parts + part
        ss, co = ss_ref[here], co_ref[here]
        for other in range(got_ss.shape[0]):
            ss, co = ss + got_ss[other, here], co + got_co[other, here]
        mask = to_col(mask_ref[part])[:, 0:1]
        inv_row = lax.rsqrt(ss / width + EPS)
        inv = to_col(inv_row)[:, 0:1]
        cube = to_col(inv_row * inv_row * inv_row * (co / width))[:, 0:1]
        y = y_ref[rows].astype(F32)
        z = z_ref[rows].astype(F32)
        dyn = dyn_ref[rows].astype(F32)
        s = sigmoid(z)
        act = z * s
        w = y * act
        wi = w * inv
        yg_ref[rows] = (wi * gain * mask).astype(BF16)
        gg_ref[0:1] += jnp.sum(dyn * wi, axis=0, keepdims=True)
        dw = inv * gain * dyn - w * cube
        dy_ref[rows] = (dw * act).astype(BF16)
        dz = dw * y * (s * (1.0 + z * (1.0 - s)))
        dz_ref[rows] = dz.astype(BF16)
        rd_ref[part] = to_row(jnp.sum(dz * z, axis=1, keepdims=True))


def backward_kernel(heads, extra, moves, dy_ref, x_ref, c_ref, cb_ref, ubd_ref, st_ref, par_ref, pbc_ref, head_ref, *refs):
    count = len(moves)
    srcs, refs = refs[:count], refs[count + extra :]
    dx_ref, dbd_ref, rd_ref, gx_ref, gb_ref, gh_ref = refs[:6]
    dsts, refs = refs[6 : 6 + count], refs[6 + count :]
    d_state, ext_x, ext_b, rows_ref, prod, edy_ref, tail_ref = refs[:7]
    if moves:
        began = (pl.program_id(0) == 0) & (pl.program_id(1) == 0)
        ended = (pl.program_id(0) == pl.num_programs(0) - 1) & (pl.program_id(1) == pl.num_programs(1) - 1)
        background(began, ended, moves, srcs, dsts, *refs[7:])
    first = (pl.program_id(0) == 0) & (pl.program_id(1) == 0)

    @pl.when(first)
    def _():
        gx_ref[...] = jnp.zeros_like(gx_ref)
        gb_ref[...] = jnp.zeros_like(gb_ref)
        gh_ref[...] = jnp.zeros_like(gh_ref)
        rows_ref[...] = jnp.zeros_like(rows_ref)

    @pl.when(pl.program_id(1) == 0)
    def _():
        ext_x[T : T + 8] = jnp.zeros_like(ext_x[T : T + 8])
        ext_b[T : T + 8] = jnp.zeros_like(ext_b[T : T + 8])
        d_state[...] = jnp.zeros_like(d_state)

    row, col = iotas(T, T)
    low = col < HEAD
    upto = col >= row
    below = row < col
    reach = (row >= col).astype(BF16)
    ubd = ubd_ref[...]
    raw, steps, rates, logs = step_terms(ubd, head_ref, heads)
    logs_t = logs.T
    cb = cb_ref[...]
    sb = sigmoid(cb)
    bc = cb * sb
    b_low, c_low = bc[:, :N].astype(BF16), bc[:, N:].astype(BF16)
    c_t = bc[:, N:].T.astype(BF16)
    scores = dot_nt(b_low, c_low)
    entering = st_ref[0]
    outer = dot(c_low, entering)
    ds_low = d_state[...].astype(BF16)
    back = dot(b_low, ds_low)
    d_scores = jnp.zeros((T, T), F32)
    skip_parts, closing_parts = [], []
    for pair in range(heads // 2):
        span = slice(128 * pair, 128 * pair + 128)
        h0, h1 = 2 * pair, 2 * pair + 1
        log0, log1 = lanes(logs, h0), lanes(logs, h1)
        log_pair = jnp.where(low, log0, log1)
        step_pair = jnp.where(low, lanes(steps, h0), lanes(steps, h1))
        last_pair = log_pair[T - 1 : T]
        cp = c_ref[:, span].astype(F32)
        sp = sigmoid(cp)
        xp = cp * sp
        xd = xp * step_pair
        dy_low = dy_ref[:, span]
        dy = dy_low.astype(F32)
        decay0 = jnp.exp(jnp.where(upto, logs_t[h0 : h0 + 1] - log0, NEG))
        decay1 = jnp.exp(jnp.where(upto, logs_t[h1 : h1 + 1] - log1, NEG))
        m0, m1 = scores * decay0, scores * decay1
        zero = jnp.zeros_like(dy_low)
        x_stack = jnp.concatenate([jnp.where(low, xd, 0.0).astype(BF16), jnp.where(low, 0.0, xd).astype(BF16)], axis=0)
        dm = dot_nt(x_stack, dy_low)
        dm0, dm1 = dm[:T], dm[T:]
        d_scores = d_scores + dm0 * decay0 + dm1 * decay1
        dy_stack = jnp.concatenate([jnp.where(low, dy, 0.0).astype(BF16), jnp.where(low, 0.0, dy).astype(BF16)], axis=0)
        dxd = dot(jnp.concatenate([m0.astype(BF16), m1.astype(BF16)], axis=1), dy_stack)
        flow = jnp.concatenate([(dm0 * m0).astype(BF16), (dm1 * m1).astype(BF16)], axis=0)
        later = dot(flow, reach)
        rows_ref[h0 : h0 + 1] = jnp.sum(jnp.where(below, later[:T], 0.0), axis=0, keepdims=True)
        rows_ref[h1 : h1 + 1] = jnp.sum(jnp.where(below, later[T:], 0.0), axis=0, keepdims=True)
        grow = jnp.exp(log_pair)
        tail = jnp.exp(last_pair - log_pair)
        from_state = tail * back[:, span]
        dxd = dxd + from_state
        edy = grow * dy
        prod[0:T, span] = (edy * outer[:, span]).astype(BF16)
        prod[T : 2 * T, span] = (from_state * xd).astype(BF16)
        prod[2 * T : 3 * T, span] = (xp * dxd).astype(BF16)
        skip_parts.append(jnp.sum(xp * dy, axis=0, keepdims=True))
        edy_low = edy.astype(BF16)
        edy_ref[:, span] = edy_low
        tail_ref[:, span] = (tail * xd).astype(BF16)
        old = d_state[:, span]
        closing = jnp.exp(last_pair)
        closing_parts.append(closing * jnp.sum(old * entering[:, span].astype(F32), axis=0, keepdims=True))
        d_state[:, span] = closing * old + dot(c_t, edy_low)
        dx = dxd * step_pair + par_ref[5:6, span] * dy
        ext_x[0:T, span] = dx * (sp * (1.0 + cp * (1.0 - sp)))
    d_low = d_scores.astype(BF16)
    d_b = dot_nt(tail_ref[...], ds_low) + dot(d_low, c_low)
    d_c = dot_nt(edy_ref[...], entering) + dot(d_scores.T.astype(BF16), b_low)
    width = heads * HEAD
    lane_row, lane_col = iotas(width, 128)
    member = (lane_row // HEAD == lane_col).astype(BF16)
    sums = dot(prod[...], member)
    skip_all = jnp.concatenate(skip_parts, axis=1)
    closing_all = jnp.concatenate(closing_parts, axis=1)
    fill = jnp.zeros((6, width), F32)
    few = dot_exact(jnp.concatenate([skip_all, closing_all, fill], axis=0), member.astype(F32))
    d_logs = dot(upto.astype(BF16), sums[:T].astype(BF16)) + dot((col < row).astype(BF16), sums[T : 2 * T].astype(BF16))
    d_logs = d_logs + rows_ref[...].T + few[1:2]
    d_steps = sums[2 * T :] + rates * d_logs
    d_raw = jnp.where(col < heads, d_steps * sigmoid(raw), 0.0)
    gh_ref[0:1] += jnp.sum(d_raw, axis=0, keepdims=True)
    gh_ref[1:2] += rates * jnp.sum(steps * d_logs, axis=0, keepdims=True)
    gh_ref[2:3] += few[0:1]
    ext_b[0:T, 0:N] = d_b * (sb[:, :N] * (1.0 + cb[:, :N] * (1.0 - sb[:, :N])))
    ext_b[0:T, N:] = d_c * (sb[:, N:] * (1.0 + cb[:, N:] * (1.0 - sb[:, N:])))

    def conv_back(ext, values, taps, grads):
        now = ext[0:T]
        total = taps[3:4] * now
        grads[3:4] += jnp.sum(values * now, axis=0, keepdims=True)
        grads[4:5] += jnp.sum(now, axis=0, keepdims=True)
        for k in range(3):
            moved = ext[3 - k : 3 - k + T]
            total = total + taps[k : k + 1] * moved
            grads[k : k + 1] += jnp.sum(values * moved, axis=0, keepdims=True)
        ext[T : T + 8] = ext[0:8]
        return total

    ux = x_ref[...].astype(F32)
    dux = conv_back(ext_x, ux, par_ref, gx_ref)
    dx_ref[...] = dux.astype(BF16)
    ubc = ubd[:, : 2 * N]
    dubc = conv_back(ext_b, ubc, pbc_ref, gb_ref)
    dbd_ref[:, : 2 * N] = dubc.astype(BF16)
    dbd_ref[:, 2 * N :] = d_raw.astype(BF16)
    total = jnp.sum(dux * ux, axis=1, keepdims=True) + jnp.sum(dubc * ubc, axis=1, keepdims=True)
    total = total + jnp.sum(jnp.where(col < heads, d_raw * ubd[:, 2 * N :], 0.0), axis=1, keepdims=True)
    rd_ref[0] = to_row(total)


def params(*semantics, number=0):
    if number:
        return pltpu.CompilerParams(
            dimension_semantics=semantics, vmem_limit_bytes=LIMIT, collective_id=number, has_side_effects=True
        )
    return pltpu.CompilerParams(dimension_semantics=semantics, vmem_limit_bytes=LIMIT)


def run_forward(heads, u_zx, u_bd, par, pbc, hp, came, w_out, number):
    rows, width = u_zx.shape[0], heads * HEAD
    slots, chunks = rows // LEN, LEN // T
    at = lambda s, i: (s * chunks + i, 0)
    fixed = lambda s, i: (0, 0)
    size, block, quarter = came.shape
    line = size // 2
    anywhere = pl.BlockSpec(memory_space=pl.ANY)
    sems = pltpu.SemaphoreType.DMA
    return pl.pallas_call(
        functools.partial(forward_kernel, heads, slots * chunks),
        grid=(slots, chunks),
        in_specs=[
            pl.BlockSpec((T, width), lambda s, i: (s * chunks + i, 1)),
            pl.BlockSpec((T, width), at),
            pl.BlockSpec((T, 3 * N), at),
            pl.BlockSpec((8, width), fixed),
            pl.BlockSpec((8, 2 * N), fixed),
            pl.BlockSpec((8, 128), fixed),
            anywhere,
            anywhere,
        ],
        out_specs=[
            pl.BlockSpec((T, width), at),
            pl.BlockSpec((1, 1, T), lambda s, i: (s * chunks + i, 0, 0)),
            pl.BlockSpec((T, width), at),
            pl.BlockSpec((T, 2 * N), at),
            pl.BlockSpec((1, N, width), lambda s, i: (s * chunks + i, 0, 0)),
            anywhere,
            anywhere,
        ],
        out_shape=[
            jax.ShapeDtypeStruct((rows, width), BF16),
            jax.ShapeDtypeStruct((rows // T, 1, T), F32),
            jax.ShapeDtypeStruct((rows, width), BF16),
            jax.ShapeDtypeStruct((rows, 2 * N), F32),
            jax.ShapeDtypeStruct((rows // T, N, width), BF16),
            jax.ShapeDtypeStruct((size, block, quarter * 4), BF16),
            full_shape(size, w_out),
        ],
        scratch_shapes=[
            pltpu.VMEM((T + 8, width), F32),
            pltpu.VMEM((T + 8, 2 * N), F32),
            pltpu.VMEM((N, width), F32),
            sems((2, 3, size)),
            sems((2, PARTS, line)),
            sems((2, PARTS, line)),
            sems((4,)),
            pltpu.VMEM(came.shape, BF16),
            pltpu.VMEM((PARTS, w_out.shape[0] // PARTS, w_out.shape[1]), BF16),
        ],
        compiler_params=params("arbitrary", "arbitrary", number=number),
        cost_estimate=pl.CostEstimate(flops=rows * width * 2 * 1200, bytes_accessed=rows * width * 8, transcendentals=rows * width * 6),
        name="scan_forward",
    )(u_zx, u_zx, u_bd, par, pbc, hp, came, cut_shard(w_out))


def run_project(heads, order, x, w_in):
    rows, deep = x.shape
    wide = w_in.shape[1]
    width = 2 * heads * HEAD
    step = 256
    at = lambda i: (i, 0)
    fixed = lambda i: (0, 0)
    thin = pl.BlockSpec((step // T, 1, T), lambda i: (i, 0, 0))
    return pl.pallas_call(
        functools.partial(project_kernel, heads),
        grid=(rows // step,),
        in_specs=[thin, pl.BlockSpec((rows, deep), fixed), pl.BlockSpec((deep, wide), fixed)],
        out_specs=[pl.BlockSpec((step, deep), at), thin, pl.BlockSpec((step, width), at), pl.BlockSpec((step, wide - width), at)],
        out_shape=[
            jax.ShapeDtypeStruct((rows, deep), BF16),
            jax.ShapeDtypeStruct((rows // T, 1, T), F32),
            jax.ShapeDtypeStruct((rows, width), BF16),
            jax.ShapeDtypeStruct((rows, wide - width), F32),
        ],
        scratch_shapes=[pltpu.VMEM((8, deep), F32)],
        compiler_params=params("arbitrary"),
        cost_estimate=pl.CostEstimate(flops=LIGHT, bytes_accessed=LIGHT, transcendentals=0),
        name="project",
    )(order, x, w_in)


def run_sort(order, values):
    rows, wide = values.shape
    step = 512
    return pl.pallas_call(
        sort_kernel,
        grid=(rows // step,),
        in_specs=[pl.BlockSpec((step // T, 1, T), lambda i: (i, 0, 0)), pl.BlockSpec((rows, wide), lambda i: (0, 0))],
        out_specs=pl.BlockSpec((step, wide), lambda i: (i, 0)),
        out_shape=jax.ShapeDtypeStruct((rows, wide), BF16),
        compiler_params=params("arbitrary"),
        cost_estimate=pl.CostEstimate(flops=rows * rows * wide * 2, bytes_accessed=rows * wide * 4, transcendentals=0),
        name="sort_rows",
    )(order, values)


def run_gate(grads, w_out, y, u_zx, par, mask):
    rows, width = y.shape
    deep = grads.shape[1]
    step = 256
    at = lambda i: (i, 0)
    fixed = lambda i: (0, 0)
    thin = pl.BlockSpec((step // T, 1, T), lambda i: (i, 0, 0))
    return pl.pallas_call(
        gate_kernel,
        grid=(rows // step,),
        in_specs=[
            pl.BlockSpec((step, deep), at),
            pl.BlockSpec((deep, width), fixed),
            pl.BlockSpec((step, width), at),
            pl.BlockSpec((step, width), at),
            pl.BlockSpec((8, width), fixed),
            thin,
        ],
        out_specs=[pl.BlockSpec((step, width), at), thin],
        out_shape=[jax.ShapeDtypeStruct((rows, width), BF16), jax.ShapeDtypeStruct((rows // T, 1, T), F32)],
        compiler_params=params("arbitrary"),
        cost_estimate=pl.CostEstimate(flops=rows * deep * width * 2, bytes_accessed=rows * deep * 2 + rows * width * 6, transcendentals=rows * width),
        name="gate_back",
    )(grads, w_out, y, u_zx, par, mask)


def run_home(order, sums, extra, deep, name, after=()):
    rows, quarter = sums[0].shape
    step = 512
    many = rows // step
    into = lambda i: (jnp.minimum(i, many - 1), 0)
    into3 = lambda i: (jnp.minimum(i, many - 1), 0, 0)
    thin = pl.BlockSpec((step // T, 1, T), into3)
    specs = [pl.BlockSpec((rows // T, 1, T), lambda i: (0, 0, 0))] + [pl.BlockSpec((step, quarter), into)] * 2
    values = list(sums)
    if extra is not None:
        specs += [pl.BlockSpec((step, quarter), into), thin, pl.BlockSpec((8, quarter), lambda i: (0, 0)), thin, thin]
        specs += [pl.BlockSpec((3, step // T, 1, T), lambda i: (0, jnp.minimum(i, many - 1), 0, 0))]
        values += list(extra)
    values += list(after)
    specs += [pl.BlockSpec(memory_space=pl.ANY)] * len(after)
    return pl.pallas_call(
        functools.partial(home_kernel, extra is not None, float(deep)),
        grid=(2 * many,),
        in_specs=specs,
        out_specs=pl.BlockSpec((step, quarter), lambda i: (jnp.maximum(i - many, 0), 0)),
        out_shape=jax.ShapeDtypeStruct((rows, quarter), BF16),
        scratch_shapes=[pltpu.VMEM((rows, quarter), BF16)],
        compiler_params=params("arbitrary"),
        cost_estimate=pl.CostEstimate(flops=rows * rows * quarter * 2, bytes_accessed=rows * quarter * 10, transcendentals=0),
        name=name,
    )(order, *values)


def run_mid(all_width, y, u_zx, dyn, par, mask, ss, co, number):
    rows, width = y.shape
    step = 256
    at = lambda i: (i, 0)
    fixed = lambda i: (0, 0)
    thin = pl.BlockSpec((step // T, 1, T), lambda i: (i, 0, 0))
    whole = pl.BlockSpec((rows // T, 1, T), lambda i: (0, 0, 0))
    wide = pl.BlockSpec((step, width), at)
    moves = (("spread", "head"), ("spread", "head"))
    others = lax.axis_size("head") - 1
    return pl.pallas_call(
        functools.partial(mid_kernel, float(all_width), moves),
        grid=(rows // step,),
        in_specs=[wide, wide, wide, pl.BlockSpec((8, width), fixed), thin, whole, whole],
        out_specs=[wide, wide, wide, pl.BlockSpec((8, width), fixed), thin],
        out_shape=[jax.ShapeDtypeStruct((rows, width), BF16)] * 3
        + [jax.ShapeDtypeStruct((8, width), F32), jax.ShapeDtypeStruct((rows // T, 1, T), F32)],
        scratch_shapes=[pltpu.VMEM((others, rows // T, 1, T), F32)] * 2 + move_scratch(moves, (ss, co)),
        compiler_params=params("arbitrary", number=number),
        cost_estimate=pl.CostEstimate(flops=rows * width * 30, bytes_accessed=rows * width * 12, transcendentals=rows * width),
        name="gate_mid",
    )(y, u_zx, dyn, par, mask, ss, co)


def run_backward(heads, slot, dy, u_zx, c, cb, u_bd, st, par, pbc, hp, before, moves, values, number, after=()):
    rows, width = dy.shape
    chunks = LEN // T
    place = lambda s, i: slot * chunks + chunks - 1 - i
    at = lambda s, i: (place(s, i), 0)
    at3 = lambda s, i: (place(s, i), 0, 0)
    fixed = lambda s, i: (0, 0)
    anywhere = pl.BlockSpec(memory_space=pl.ANY)
    return pl.pallas_call(
        functools.partial(backward_kernel, heads, len(before) + len(after), tuple(moves)),
        grid=(1, chunks),
        in_specs=[
            pl.BlockSpec((T, width), at),
            pl.BlockSpec((T, width), lambda s, i: (place(s, i), 1)),
            pl.BlockSpec((T, width), at),
            pl.BlockSpec((T, 2 * N), at),
            pl.BlockSpec((T, 3 * N), at),
            pl.BlockSpec((1, N, width), at3),
            pl.BlockSpec((8, width), fixed),
            pl.BlockSpec((8, 2 * N), fixed),
            pl.BlockSpec((8, 128), fixed),
        ]
        + [anywhere] * (len(moves) + len(before) + len(after)),
        out_specs=[
            pl.BlockSpec((T, width), at),
            pl.BlockSpec((T, 3 * N), at),
            pl.BlockSpec((1, 1, T), at3),
            pl.BlockSpec((8, width), fixed),
            pl.BlockSpec((8, 2 * N), fixed),
            pl.BlockSpec((8, 128), fixed),
        ]
        + [anywhere] * len(moves),
        out_shape=[
            jax.ShapeDtypeStruct((rows, width), BF16),
            jax.ShapeDtypeStruct((rows, 3 * N), BF16),
            jax.ShapeDtypeStruct((rows // T, 1, T), F32),
            jax.ShapeDtypeStruct((8, width), F32),
            jax.ShapeDtypeStruct((8, 2 * N), F32),
            jax.ShapeDtypeStruct((8, 128), F32),
        ]
        + move_outs(moves, values),
        scratch_shapes=[
            pltpu.VMEM((N, width), F32),
            pltpu.VMEM((T + 8, width), F32),
            pltpu.VMEM((T + 8, 2 * N), F32),
            pltpu.VMEM((128, 128), F32),
            pltpu.VMEM((3 * T, width), BF16),
            pltpu.VMEM((T, width), BF16),
            pltpu.VMEM((T, width), BF16),
        ]
        + move_scratch(moves, values),
        input_output_aliases={9 + len(moves) + i: i for i in range(len(before))},
        compiler_params=params("arbitrary", "arbitrary", number=number),
        cost_estimate=pl.CostEstimate(flops=LIGHT, bytes_accessed=LIGHT, transcendentals=0),
        name="scan_backward",
    )(dy, u_zx, c, cb, u_bd, st, par, pbc, hp, *values, *before, *after)


def pieces_kernel(count, many, moves, extra, *refs):
    total = len(moves)
    values, weights, srcs = refs[:count], refs[count : 2 * count], refs[2 * count : 2 * count + total]
    refs = refs[2 * count + total + extra :]
    far_ref, own_ref = refs[:2]
    dsts, refs = refs[2 : 2 + total], refs[2 + total :]
    sent_ref, came_ref, near_sems = refs[:3]
    step = pl.program_id(0)
    rows, quarter = far_ref.shape
    dp, own = lax.axis_index("dp"), lax.axis_index("head")
    near = (dp, own ^ 1)
    peers, copies = make_moves(moves, srcs, dsts, *refs[3:]) if moves else ([], [])

    @pl.when(step == 0)
    def _():
        greet(peers if near_in(moves) else [near] + peers)
        for copy in copies:
            copy.start()

    def product(k):
        at = pl.ds(pl.multiple_of((own ^ k) * quarter, 128), quarter)
        out = None
        for value, weight in zip(values, weights):
            term = dot_nt(value[...], weight[at, :])
            out = term if out is None else out + term
        return out

    def near_copy(block):
        return pltpu.make_async_remote_copy(
            src_ref=sent_ref.at[block],
            dst_ref=came_ref.at[block],
            send_sem=near_sems.at[0, block],
            recv_sem=near_sems.at[1, block],
            device_id=near,
            device_id_type=MESH,
        )

    @pl.when(step < many)
    def _():
        sent_ref[step, :, :quarter] = product(3).astype(BF16)
        sent_ref[step, :, quarter:] = product(1).astype(BF16)
        near_copy(step).start()

    @pl.when(step >= many)
    def _():
        block = step - many
        far, mine = product(2), product(0)
        near_copy(block).wait_recv()
        far_ref[...] = (far + came_ref[block, :, :quarter].astype(F32)).astype(BF16)
        own_ref[...] = (mine + came_ref[block, :, quarter:].astype(F32)).astype(BF16)

    @pl.when(step == 2 * many - 1)
    def _():
        for block in range(many):
            near_copy(block).wait_send()
        for copy in copies:
            copy.wait()


def near_in(moves):
    return any(move[0] == "spread" and move[1] == "head" for move in moves)


def run_pieces(values, weights, quarter, name, moves, moved, number, after=()):
    rows = values[0].shape[0]
    step = 512
    many = rows // step
    anywhere = pl.BlockSpec(memory_space=pl.ANY)
    specs = [pl.BlockSpec((step, v.shape[1]), lambda i: (lax.rem(i, many), 0)) for v in values]
    for weight, block, wide in weights:
        specs.append(pl.BlockSpec((weight.shape[0], wide), lambda i, block=block: (0, block)))
    depth = sum(v.shape[1] for v in values)
    return pl.pallas_call(
        functools.partial(pieces_kernel, len(values), many, tuple(moves), len(after)),
        grid=(2 * many,),
        in_specs=specs + [anywhere] * (len(moves) + len(after)),
        out_specs=[pl.BlockSpec((step, quarter), lambda i: (jnp.maximum(i - many, 0), 0))] * 2 + [anywhere] * len(moves),
        out_shape=[jax.ShapeDtypeStruct((rows, quarter), BF16)] * 2 + move_outs(moves, moved),
        scratch_shapes=[pltpu.VMEM((many, step, 2 * quarter), BF16)] * 2 + [pltpu.SemaphoreType.DMA((2, many))] + move_scratch(moves, moved),
        compiler_params=params("arbitrary", number=number),
        cost_estimate=pl.CostEstimate(flops=LIGHT, bytes_accessed=LIGHT, transcendentals=0),
        name=name,
    )(*values, *[w for w, _, _ in weights], *moved, *after)


def grads_kernel(count, parts, moves, extra, *refs):
    total = len(moves)
    lefts, rights, srcs = refs[:count], refs[count : 2 * count], refs[2 * count : 2 * count + total]
    refs = refs[2 * count + total + extra :]
    outs, dsts, sems = refs[:count], refs[count : count + total], refs[count + total :]
    step = pl.program_id(0)
    if moves:
        background(step == 0, step == count * parts - 1, moves, srcs, dsts, *sems)
    for which in range(count):

        @pl.when((step >= which * parts) & (step < (which + 1) * parts))
        def _():
            out = lax.dot_general(lefts[which][...], rights[which][...], (((0,), (0,)), ((), ())), preferred_element_type=F32)
            outs[which][...] = out.astype(BF16)


def run_grads(pairs, name, moves=(), moved=(), number=0, after=()):
    rows, deep = pairs[0][0].shape
    step = 512
    parts = deep // step
    count = len(pairs)
    anywhere = pl.BlockSpec(memory_space=pl.ANY)
    into = lambda which: lambda i: jnp.clip(i - which * parts, 0, parts - 1)
    specs = [pl.BlockSpec((rows, step), lambda i, at=into(w): (0, at(i))) for w in range(count)]
    specs += [pl.BlockSpec(right.shape, lambda i: (0, 0)) for _, right in pairs]
    return pl.pallas_call(
        functools.partial(grads_kernel, count, parts, tuple(moves), len(after)),
        grid=(count * parts,),
        in_specs=specs + [anywhere] * (len(moves) + len(after)),
        out_specs=[pl.BlockSpec((step, right.shape[1]), lambda i, at=into(w): (at(i), 0)) for w, (_, right) in enumerate(pairs)]
        + [anywhere] * len(moves),
        out_shape=[jax.ShapeDtypeStruct((deep, right.shape[1]), BF16) for _, right in pairs] + move_outs(moves, moved),
        scratch_shapes=move_scratch(moves, moved),
        compiler_params=params("arbitrary", number=number),
        cost_estimate=pl.CostEstimate(flops=LIGHT, bytes_accessed=LIGHT, transcendentals=0),
        name=name,
    )(*[left for left, _ in pairs], *[right for _, right in pairs], *moved, *after)


def last_kernel(moves, *refs):
    count = len(moves)
    srcs, pair_ref = refs[:count], refs[count]
    dsts, out_ref = refs[count + 1 : 2 * count + 1], refs[2 * count + 1]
    kept_ref, line_ref, came_ref, own_ref, pair_sems, sems, local_sems = refs[2 * count + 2 :]
    me, head = lax.axis_index("dp"), lax.axis_index("head")
    peers, copies = make_moves(moves, srcs, dsts, sems, local_sems)

    def remote(src, dst, slot, peer):
        return pltpu.make_async_remote_copy(
            src_ref=src, dst_ref=dst, send_sem=pair_sems.at[0, slot], recv_sem=pair_sems.at[1, slot], device_id=(peer, head), device_id_type=MESH
        )

    high = me >> 1
    half = remote(pair_ref.at[:, 1 - (me & 1)], came_ref, 0, me ^ 1)
    line = [remote(kept_ref.at[high ^ j], line_ref.at[j - 1], j, me ^ (2 * j)) for j in range(1, own_ref.shape[0])]
    own = pltpu.make_async_copy(pair_ref.at[:, me & 1], own_ref, pair_sems.at[2, 0])
    greet(peers)
    half.start()
    own.start()
    for copy in copies:
        copy.start()
    own.wait()
    half.wait()
    for j in range(own_ref.shape[0]):
        kept_ref[j] = (own_ref[j].astype(F32) + came_ref[j].astype(F32)).astype(BF16)
    for copy in line:
        copy.start()
    for copy in line:
        copy.wait()
    total = kept_ref[high].astype(F32)
    for j in range(1, own_ref.shape[0]):
        total = total + line_ref[j - 1].astype(F32)
    out_ref[...] = total
    for copy in copies:
        copy.wait()


def run_last(moves, values, paired, number):
    many, _, block, wide = paired.shape
    anywhere = pl.BlockSpec(memory_space=pl.ANY)
    own = pltpu.VMEM((many, block, wide), BF16)
    return pl.pallas_call(
        functools.partial(last_kernel, tuple(moves)),
        in_specs=[anywhere] * (len(moves) + 1),
        out_specs=[anywhere] * len(moves) + [pl.BlockSpec(memory_space=pltpu.VMEM)],
        out_shape=move_outs(moves, values) + [jax.ShapeDtypeStruct((block, wide), F32)],
        scratch_shapes=[own, pltpu.VMEM((many - 1, block, wide), BF16), own, own, pltpu.SemaphoreType.DMA((3, many))] + move_scratch(moves, values),
        compiler_params=pltpu.CompilerParams(collective_id=number, has_side_effects=True, vmem_limit_bytes=LIMIT),
        name="last_exchange",
    )(*values, paired)


def row_forward(size, quarter, own_ref, full_ref, sems):
    me, own = lax.axis_index("dp"), lax.axis_index("head")
    columns = lambda head: pl.ds(pl.multiple_of(head * quarter, 128), quarter)

    def copy(src, dst, stage, k, head):
        return pltpu.make_async_remote_copy(
            src_ref=src, dst_ref=dst, send_sem=sems.at[0, stage, k], recv_sem=sems.at[1, stage, k], device_id=(me, head), device_id_type=MESH
        )

    def source(k):
        return full_ref.at[me ^ k, :, columns(own)] if own_ref is None else own_ref.at[me ^ k]

    def far(k):
        return copy(source(k), full_ref.at[me ^ k, :, columns(own)], 0, k, own ^ 2)

    def near(k):
        return copy(source(k), full_ref.at[me ^ k, :, columns(own)], 1, k, own ^ 1)

    def back(k):
        block = full_ref.at[me ^ k, :, columns(own ^ 2)]
        return copy(block, block, 2, k, own ^ 1)

    return far, near, back


def shard_spread(src, dst, across_sems, side_sems):
    me, own = lax.axis_index("dp"), lax.axis_index("head")

    def copy(a, b, sems, part, j, peer):
        return pltpu.make_async_remote_copy(
            src_ref=a, dst_ref=b, send_sem=sems.at[0, part, j], recv_sem=sems.at[1, part, j], device_id=(peer, own), device_id_type=MESH
        )

    def across(part, j):
        return copy(src.at[part], dst.at[me, part], across_sems, part, j, me ^ (2 * j))

    def side(part, j):
        here = dst.at[me ^ (2 * j), part]
        return copy(src.at[part] if j == 0 else here, here, side_sems, part, j, me ^ 1)

    return across, side


def entry_kernel(parts, x_ref, w_ref, fx_ref, fw_ref, row_sems, pass_sems, line_sems, side_sems, local_sems, x_held, w_held):
    size, quarter = x_ref.shape[0], x_ref.shape[2]
    line = size // 2
    me, own = lax.axis_index("dp"), lax.axis_index("head")
    spot = me >> 1
    mine = pl.ds(pl.multiple_of(own * quarter, 128), quarter)
    far, near, back = row_forward(size, quarter, None, fx_ref, pass_sems)

    def remote(src, dst, sems, slot, peer):
        return pltpu.make_async_remote_copy(
            src_ref=src, dst_ref=dst, send_sem=sems.at[(0,) + slot], recv_sem=sems.at[(1,) + slot], device_id=(peer, own), device_id_type=MESH
        )

    def rows(k):
        return remote(x_ref.at[me ^ k], fx_ref.at[me, :, mine], row_sems, (k,), me ^ k)

    def along(way, part, j):
        sign = 1 - 2 * way
        origin = jnp.clip(me - sign * 2 * (j - 1), 0, size - 1)
        peer = jnp.clip(me + sign * 2, 0, size - 1)
        here = fw_ref.at[origin, part]
        return remote(w_ref.at[part] if j == 1 else here, here, line_sems, (way, part, j - 1), peer)

    def came(way, part, j):
        sign = 1 - 2 * way
        here = fw_ref.at[jnp.clip(me - sign * 2 * j, 0, size - 1), part]
        return remote(here, here, line_sems, (way, part, j - 1), me)

    def side(way, part, j):
        sign = 1 - 2 * way
        here = fw_ref.at[jnp.clip(me - sign * 2 * j, 0, size - 1), part]
        return remote(w_ref.at[part] if j == 0 else here, here, side_sems, (way, part, j), me ^ 1)

    def goes_on(way):
        return spot < line - 1 if way == 0 else spot > 0

    def arrives(way, j):
        return spot >= j if way == 0 else spot < line - j

    greet_rows = [(me ^ k, own) for k in range(1, size)] + [(me, own ^ 1), (me, own ^ 2)]
    into = [pltpu.make_async_copy(x_ref.at[me], x_held, local_sems.at[0]), pltpu.make_async_copy(w_ref, w_held, local_sems.at[1])]
    held = [
        pltpu.make_async_copy(x_held, fx_ref.at[me, :, mine], local_sems.at[2]),
        pltpu.make_async_copy(w_held, fw_ref.at[me], local_sems.at[3]),
    ]
    for copy in into:
        copy.start()
    greet(greet_rows)
    order = turn_order(size)
    for k in order:
        rows(k).start()
    for part in range(parts):
        side(0, part, 0).start()
    for first, second in zip(into, held):
        first.wait()
        second.start()
    held[0].wait()
    far(0).start()
    near(0).start()
    for k in order:
        rows(k).wait_recv()
        far(k).start()
        near(k).start()
    for way in range(2):

        @pl.when(goes_on(way))
        def _():
            for part in range(parts):
                along(way, part, 1).start()

    for k in [0] + order:
        far(k).wait_recv()
        back(k).start()
    for j in range(1, line):
        for part in range(parts):
            for way in range(2):

                @pl.when(arrives(way, j))
                def _():
                    came(way, part, j).wait_recv()
                    side(way, part, j).start()

                if j + 1 < line:

                    @pl.when(arrives(way, j) & goes_on(way))
                    def _():
                        along(way, part, j + 1).start()

    held[1].wait()
    for k in range(size):
        near(k).wait()
        back(k).wait()
        far(k).wait_send()
        if k:
            rows(k).wait_send()
    for part in range(parts):
        side(0, part, 0).wait()
        for way in range(2):

            @pl.when(goes_on(way))
            def _():
                along(way, part, 1).wait_send()

            for j in range(1, line):

                @pl.when(arrives(way, j))
                def _():
                    side(way, part, j).wait()

                if j + 1 < line:

                    @pl.when(arrives(way, j) & goes_on(way))
                    def _():
                        along(way, part, j + 1).wait_send()


PARTS = 4


def cut_shard(w):
    return w.reshape(PARTS, w.shape[0] // PARTS, w.shape[1])


def full_shape(size, w):
    return jax.ShapeDtypeStruct((size, PARTS, w.shape[0] // PARTS, w.shape[1]), BF16)


def run_entry(tokens, w_in, number):
    size = lax.axis_size("dp")
    rows, quarter = tokens.shape
    line = size // 2
    anywhere = pl.BlockSpec(memory_space=pl.ANY)
    sems = pltpu.SemaphoreType.DMA
    came, full = pl.pallas_call(
        functools.partial(entry_kernel, PARTS),
        in_specs=[anywhere] * 2,
        out_specs=[anywhere] * 2,
        out_shape=[jax.ShapeDtypeStruct((size, rows // size, quarter * 4), BF16), full_shape(size, w_in)],
        scratch_shapes=[
            sems((2, size)),
            sems((2, 3, size)),
            sems((2, 2, PARTS, line)),
            sems((2, 2, PARTS, line)),
            sems((4,)),
            pltpu.VMEM((rows // size, quarter), BF16),
            pltpu.VMEM((PARTS, w_in.shape[0] // PARTS, w_in.shape[1]), BF16),
        ],
        compiler_params=pltpu.CompilerParams(collective_id=number, has_side_effects=True, vmem_limit_bytes=LIMIT),
        name="entry",
    )(tokens.reshape(size, rows // size, quarter), cut_shard(w_in))
    return came.reshape(rows, quarter * 4), full.reshape(size * w_in.shape[0], w_in.shape[1])


def mm(a, b, contract, kind):
    return lax.dot_general(a, b, (contract, ((), ())), preferred_element_type=F32).astype(kind)


def body(tokens, cotangent, order, lengths, norm_gain, w_zx, w_bc, w_dt, w_out, conv_x, conv_bc, head_params, gate_gain):
    rows, quarter = tokens.shape
    heads = head_params.shape[1]
    width = heads * HEAD
    place = lax.axis_index("head")
    size = lax.axis_size("dp")
    here = lax.axis_index("dp")
    all_width = width * lax.axis_size("head")
    deep = quarter * lax.axis_size("head")
    own_w = w_zx.shape[0]
    arrange = order.astype(F32).reshape(rows // T, 1, T)

    packed = jnp.concatenate(
        [w_zx.reshape(own_w, 2 * width), w_bc, w_dt, norm_gain[:, None], jnp.zeros((own_w, 127 - heads), BF16)], axis=1
    )
    blocks = lambda value: value.reshape(size, rows // size, quarter)
    came_x, w_in = run_entry(tokens, packed, 1)
    came_x, later = lax.optimization_barrier((came_x, cotangent))
    own_g = lax.all_to_all(later, "dp", split_axis=0, concat_axis=0, tiled=True)
    normed, inv_one, u_zx, u_bd = run_project(heads, arrange, came_x, w_in)

    par = jnp.concatenate([conv_x, jnp.repeat(head_params[2:3], HEAD, axis=1), gate_gain[None], jnp.zeros((1, width), F32)], axis=0)
    pbc = jnp.concatenate([conv_bc, jnp.zeros((3, 2 * N), F32)], axis=0)
    hp = jnp.pad(head_params, ((0, 5), (0, 128 - heads)))
    positions = lax.broadcasted_iota(jnp.int32, (lengths.shape[0], LEN), 1)
    mask = (positions < lengths[:, None]).astype(F32).reshape(rows // T, 1, T)

    sorted_g = run_sort(arrange, own_g)
    y, ss, c, cb, st, full_g, w_o = run_forward(heads, u_zx, u_bd, par, pbc, hp, blocks(sorted_g), w_out, 3)
    w_o = w_o.reshape(deep, width)
    full_g = full_g.reshape(rows, deep)
    dyn, co = run_gate(full_g, w_o, y, u_zx, par, mask)
    yg, dz, dy, gg, rd_z = run_mid(all_width, y, u_zx, dyn, par, mask, ss, co, 4)

    def keep(paired, came, bit):
        own = lax.dynamic_index_in_dim(paired, (here >> bit) & 1, 1, keepdims=False)
        return (own.astype(F32) + came.astype(F32)).astype(BF16)

    def total(kept, came, shift):
        own = lax.dynamic_index_in_dim(kept, here >> shift, 0, keepdims=False)
        return own.astype(F32) + jnp.sum(came.astype(F32), axis=0)

    def pairs(grads):
        return grads.reshape(size // 2, 2, own_w, grads.shape[1])

    def fours(grads):
        return grads.reshape(size // 4, 2, -1, own_w, grads.shape[-1])

    scan = functools.partial(run_backward, heads)
    shared = (dy, u_zx, c, cb, u_bd, st, par, pbc, hp)
    out_far, out_own = run_pieces([yg], [(w_o, 0, width)], quarter, "branch_pieces", [], [], 5)
    out_arrived = lax.ppermute(out_far, "head", [(i, i ^ 2) for i in range(lax.axis_size("head"))])
    grad_o, grad_z = run_grads([(full_g, yg), (normed, dz)], "gate_grads", after=[out_far])
    grad_o, grad_z = pairs(grad_o), fours(grad_z)
    *back0, gx0, gb0, gh0, came_o, came_z = scan(0, *shared, (), [("half", "dp", 0), ("half", "dp", 1)], [grad_o, grad_z], 7)
    sent_out = run_home(arrange, [out_own, out_arrived], None, deep, "home_out", [back0[0]])
    got_out = lax.all_to_all(sent_out, "dp", split_axis=0, concat_axis=0, tiled=True)
    kept_o = keep(grad_o, came_o, 0).reshape(size // 4, 2, own_w, width)
    kept_z = keep(grad_z, came_z, 1)
    *back1, gx1, gb1, gh1 = scan(1, *shared, back0, [], [], 0, [sent_out])
    dux, dbd, rd_x = back1
    grad_x, grad_bd, came_z, came_o = run_grads(
        [(normed, dux), (normed, dbd)], "scan_grads", [("half", "dp", 0), ("half", "dp", 1)], [kept_z, kept_o], 8
    )
    kept_z, kept_o = keep(kept_z, came_z, 0), keep(kept_o, came_o, 1)
    final_out = (tokens.astype(F32) + got_out.astype(F32)).astype(BF16)
    grad_x, grad_bd = pairs(grad_x), pairs(grad_bd)
    gb = gb0 + gb1
    d_far, d_own, line_o, line_z, came_x2, got_rows, got_gb = run_pieces(
        [dz, dux, dbd],
        [(w_in, 0, width), (w_in, 1, width), (w_in, 2 * width // (3 * N), 3 * N)],
        quarter,
        "input_pieces",
        [("direct", "dp", 2), ("direct", "dp", 2), ("half", "dp", 0), ("spread", "head"), ("spread", "head")],
        [kept_o, kept_z, grad_x, rd_z + rd_x, gb],
        9,
        [final_out],
    )
    kept_x = keep(grad_x, came_x2, 0)
    gb = gb[:5] + jnp.sum(got_gb, axis=0)[:5]
    gh = gh0 + gh1
    ends = jnp.concatenate([gb[3], gb[4]] + [gh[i, :32] for i in range(3)] + [jnp.zeros((width - 4 * N - 96,), F32)])
    small = jnp.concatenate([(gx0 + gx1)[:5], gg[:1], jnp.concatenate([gb[0], gb[1], gb[2]])[None], ends[None]], axis=0)
    d_arrived, line_x, got_small, grad_bd = run_last(
        [("whole", "head", 2), ("direct", "dp", 1), ("spread", "dp")], [d_far, kept_x, small], grad_bd, 10
    )

    gain_all = w_in[:, 2 * width + 2 * N + heads].astype(F32)
    gain_own = jnp.broadcast_to(lax.dynamic_slice_in_dim(gain_all, place * quarter, quarter, 0)[None], (8, quarter))
    normed_own = lax.dynamic_slice_in_dim(normed, place * quarter, quarter, 1)
    sent_back = run_home(arrange, [d_own, d_arrived], [normed_own, inv_one, gain_own, rd_z, rd_x, got_rows], deep, "home_back")
    got_back = lax.all_to_all(sent_back, "dp", split_axis=0, concat_axis=0, tiled=True)
    final_back = (cotangent.astype(F32) + got_back.astype(F32)).astype(BF16)

    grad_out, grad_z = total(kept_o, line_o, 2), total(kept_z, line_z, 2)
    grad_x = total(kept_x, line_x, 1)
    small = small + jnp.sum(got_small, axis=0)
    grad_zx = jnp.stack([grad_z, grad_x], axis=1)
    of_gain = jnp.sum(grad_z * w_zx[:, 0].astype(F32), axis=1) + jnp.sum(grad_x * w_zx[:, 1].astype(F32), axis=1)
    of_gain = of_gain + jnp.sum(grad_bd[:, : 2 * N] * w_bc.astype(F32), axis=1)
    of_gain = of_gain + jnp.sum(grad_bd[:, 2 * N : 2 * N + heads] * w_dt.astype(F32), axis=1)
    last = jnp.concatenate([grad_bd[:, : 2 * N], jnp.broadcast_to(of_gain[:, None], (own_w, 128))], axis=1)
    others, = run_exchange([("spread", "head")], [last], 11)
    last = last + jnp.sum(others, axis=0)
    grad_gain = last[:, 2 * N] / norm_gain.astype(F32)
    gx, gg = small[0:5], small[5]
    gb = jnp.concatenate([small[6].reshape(3, 2 * N), small[7, : 4 * N].reshape(2, 2 * N)], axis=0)
    gh = small[7, 4 * N : 4 * N + 96].reshape(3, 32)[:, :heads]
    return (final_out, final_back, grad_gain, grad_zx, last[:, : 2 * N], grad_bd[:, 2 * N : 2 * N + heads], grad_out, gx, gb, gh, gg)


def solution(mesh):
    return jax.shard_map(
        body,
        mesh=mesh,
        in_specs=(
            P("dp", "head"),
            P("dp", "head"),
            P("dp", None),
            P("dp"),
            P("dp"),
            P("dp", None, "head"),
            P("dp", None),
            P("dp", "head"),
            P("dp", "head"),
            P(None, "head"),
            P(),
            P(None, "head"),
            P("head"),
        ),
        out_specs=(
            P("dp", "head"),
            P("dp", "head"),
            P("dp"),
            P("dp", None, "head"),
            P("dp", None),
            P("dp", "head"),
            P("dp", "head"),
            P(None, "head"),
            P(),
            P(None, "head"),
            P("head"),
        ),
        check_vma=False,
    )
```

```python
import functools

import jax
import jax.numpy as jnp
from jax import lax
from jax.experimental import pallas as pl
from jax.experimental.pallas import tpu as pltpu
from jax.sharding import PartitionSpec as P

LEN = 1024
T = 128
N = 128
HEAD = 64
EPS = 1e-05
NEG = -1e30
LIGHT = 1000
LIMIT = 60 * 1024 * 1024
AXES = ("dp", "head")
F32 = jnp.float32
BF16 = jnp.bfloat16


def dot(a, b):
    return lax.dot_general(a, b, (((1,), (0,)), ((), ())), preferred_element_type=F32)


def dot_nt(a, b):
    return lax.dot_general(a, b, (((1,), (1,)), ((), ())), preferred_element_type=F32)


def dot_exact(a, b):
    return lax.dot_general(
        a, b, (((1,), (0,)), ((), ())), preferred_element_type=F32, precision=lax.Precision.HIGHEST
    )


def iotas(rows, cols):
    return (
        lax.broadcasted_iota(jnp.int32, (rows, cols), 0),
        lax.broadcasted_iota(jnp.int32, (rows, cols), 1),
    )


MESH = pl.DeviceIdType.MESH


def greet(peers):
    barrier = pltpu.get_barrier_semaphore()
    for peer in peers:
        pl.semaphore_signal(barrier, inc=1, device_id=peer, device_id_type=MESH)
    pl.semaphore_wait(barrier, len(peers))


def place_of():
    return {name: lax.axis_index(name) for name in AXES}


def move_copies(move, src, dst):
    kind, axis = move[0], move[1]
    place = place_of()
    me = place[axis]

    def peer(flip):
        return tuple(place[name] ^ flip if name == axis else place[name] for name in AXES)

    if kind == "whole":
        return [(peer(move[2]), src, dst)], []
    if kind == "rows":
        return [(peer(move[2]), src.at[pl.ds(move[3], move[4])], dst)], []
    if kind == "half":
        return [(peer(1 << move[2]), src.at[:, 1 - ((me >> move[2]) & 1)], dst)], []
    if kind == "direct":
        high = me >> move[2]
        return [(peer(j << move[2]), src.at[high ^ j], dst.at[j - 1]) for j in range(1, dst.shape[0] + 1)], []
    if kind == "all":
        groups = lax.axis_size("head")
        flips = [divmod(flat, groups) for flat in range(1, dst.shape[0] + 1)]
        return [((place["dp"] ^ f, place["head"] ^ e), src, dst.at[i]) for i, (f, e) in enumerate(flips)], []
    if kind == "spread":
        return [(peer(flip), src, dst.at[flip - 1]) for flip in range(1, dst.shape[0] + 1)], []
    remote = [(peer(k), src.at[me ^ k], dst.at[me]) for k in turn_order(src.shape[0])]
    return remote, [(src.at[me], dst.at[me])]


def turn_order(size):
    return sorted(range(1, size), key=lambda k: (-(k & ~1), k & 1))


def move_shape(move, shape):
    kind = move[0]
    if kind == "rows":
        return (move[4],) + shape[1:]
    if kind == "half":
        return (shape[0],) + shape[2:]
    if kind == "direct":
        return (shape[0] - 1,) + shape[1:]
    if kind == "spread":
        return (lax.axis_size(move[1]) - 1,) + shape
    if kind == "all":
        return (lax.axis_size("dp") * lax.axis_size("head") - 1,) + shape
    return shape


def move_counts(moves, values):
    remote = local = 0
    for move, value in zip(moves, values):
        size = lax.axis_size(move[1])
        world = lax.axis_size("dp") * lax.axis_size("head")
        count = {"direct": value.shape[0] - 1, "spread": size - 1, "turn": size - 1, "all": world - 1}.get(move[0], 1)
        remote, local = remote + count, local + (move[0] == "turn")
    return remote, local


def move_scratch(moves, values):
    remote, local = move_counts(moves, values)
    return [pltpu.SemaphoreType.DMA((2, remote)), pltpu.SemaphoreType.DMA((max(local, 1),))] if moves else []


def move_outs(moves, values):
    return [jax.ShapeDtypeStruct(move_shape(move, value.shape), value.dtype) for move, value in zip(moves, values)]


def make_moves(moves, srcs, dsts, sems, local_sems):
    remote, local = [], []
    for move, src, dst in zip(moves, srcs, dsts):
        here, there = move_copies(move, src, dst)
        remote += here
        local += there
    copies = [
        pltpu.make_async_remote_copy(src_ref=a, dst_ref=b, send_sem=sems.at[0, i], recv_sem=sems.at[1, i], device_id=peer, device_id_type=MESH)
        for i, (peer, a, b) in enumerate(remote)
    ]
    copies += [pltpu.make_async_copy(a, b, local_sems.at[i]) for i, (a, b) in enumerate(local)]
    return move_peers(moves, dsts), copies


def move_peers(moves, dsts):
    flips = {}
    for move, dst in zip(moves, dsts):
        kind, axis = move[0], move[1]
        if kind in ("whole", "rows"):
            own = [move[2]]
        elif kind == "half":
            own = [1 << move[2]]
        elif kind == "direct":
            own = [j << move[2] for j in range(1, dst.shape[0] + 1)]
        elif kind == "all":
            groups = lax.axis_size("head")
            for flat in range(1, dst.shape[0] + 1):
                flips[divmod(flat, groups)] = None
            continue
        elif kind == "spread":
            own = range(1, dst.shape[0] + 1)
        else:
            own = range(1, dst.shape[0])
        for flip in own:
            flips[(flip, 0) if axis == "dp" else (0, flip)] = None
    place = place_of()
    return [(place["dp"] ^ f, place["head"] ^ e) for f, e in flips]


def background(first, last, moves, srcs, dsts, sems, local_sems):
    peers, copies = make_moves(moves, srcs, dsts, sems, local_sems)

    @pl.when(first)
    def _():
        greet(peers)
        for copy in copies:
            copy.start()

    @pl.when(last)
    def _():
        for copy in copies:
            copy.wait()


def exchange_kernel(moves, *refs):
    count = len(moves)
    peers, copies = make_moves(moves, refs[:count], refs[count : 2 * count], refs[2 * count], refs[2 * count + 1])
    greet(peers)
    for copy in copies:
        copy.start()
    for copy in copies:
        copy.wait()


def run_exchange(moves, values, number):
    return pl.pallas_call(
        functools.partial(exchange_kernel, tuple(moves)),
        in_specs=[pl.BlockSpec(memory_space=pl.ANY)] * len(moves),
        out_specs=[pl.BlockSpec(memory_space=pl.ANY)] * len(moves),
        out_shape=move_outs(moves, values),
        scratch_shapes=move_scratch(moves, values),
        compiler_params=pltpu.CompilerParams(collective_id=number, has_side_effects=True, vmem_limit_bytes=LIMIT),
        name="exchange",
    )(*values)


def sigmoid(v):
    return 1.0 / (1.0 + jnp.exp(-v))


def softplus(v):
    return jnp.maximum(v, 0.0) + jnp.log1p(jnp.exp(-jnp.abs(v)))


def to_col(row):
    return jnp.broadcast_to(row, (T, T)).T


def to_row(col):
    return jnp.broadcast_to(col, (T, T)).T[0:1]


def lanes(value, pick):
    return jnp.broadcast_to(value[:, pick : pick + 1], (value.shape[0], 128))


def step_terms(ubd, head_ref, heads):
    row, col = iotas(T, T)
    raw = jnp.where(col < heads, ubd[:, 2 * N :] + head_ref[0:1], 0.0)
    steps = jnp.where(col < heads, softplus(raw), 0.0)
    rates = -jnp.exp(head_ref[1:2])
    tril = (row >= col).astype(F32)
    logs = dot_exact(tril, steps * rates)
    return raw, steps, rates, logs


def weight_moves(step, steps, parts, whole, w_ref, fw_ref, across_sems, side_sems, local_sems, w_held):
    line = fw_ref.shape[0] // 2
    me, own = lax.axis_index("dp"), lax.axis_index("head")
    across, side = shard_spread(w_ref, fw_ref, across_sems, side_sems)
    if whole:
        into = pltpu.make_async_copy(w_ref, w_held, local_sems.at[0])
        held = pltpu.make_async_copy(w_held, fw_ref.at[me], local_sems.at[1])

    @pl.when(step == 0)
    def _():
        if whole:
            into.start()
        greet([(me ^ 1, own)] + [(me ^ (2 * j), own) for j in range(1, line)])
        for part in parts:
            side(part, 0).start()
        if whole:
            into.wait()
            held.start()

    for i, part in enumerate(parts):
        begin = i * steps // len(parts)

        @pl.when(step == begin)
        def _():
            for j in range(1, line):
                across(part, j).start()

        @pl.when(step == min(steps - 1, begin + steps // 3 + 2))
        def _():
            for j in range(1, line):
                across(part, j).wait_recv()
                side(part, j).start()

    @pl.when(step == steps - 1)
    def _():
        if whole:
            held.wait()
        for part in parts:
            for j in range(line):
                side(part, j).wait()
                if j:
                    across(part, j).wait_send()


def weight_scratch(size, w):
    sems = pltpu.SemaphoreType.DMA
    return [sems((2, PARTS, size // 2)), sems((2, PARTS, size // 2)), sems((2,)), pltpu.VMEM((PARTS, w.shape[0] // PARTS, w.shape[1]), BF16)]


def forward_kernel(heads, steps, x_ref, z_ref, ubd_ref, par_ref, pbc_ref, head_ref, w_ref, before_ref, y_ref, ss_ref, c_ref, cb_ref, st_ref, fw_ref, ext_x, ext_b, state, *sems):
    weight_moves(pl.program_id(0) * pl.num_programs(1) + pl.program_id(1), steps, range(1, PARTS), False, w_ref, fw_ref, *sems)

    @pl.when(pl.program_id(1) == 0)
    def _():
        ext_x[0:8] = jnp.zeros_like(ext_x[0:8])
        ext_b[0:8] = jnp.zeros_like(ext_b[0:8])
        state[...] = jnp.zeros_like(state)

    def conv(ext, values, taps):
        ext[8 : 8 + T] = values
        total = taps[4:5] + taps[3:4] * values
        for k in range(3):
            total = total + taps[k : k + 1] * ext[5 + k : 5 + k + T]
        ext[0:8] = ext[T : T + 8]
        return total

    row, col = iotas(T, T)
    low = col < HEAD
    low_row = lax.broadcasted_iota(jnp.int32, (1, 128), 1) < HEAD
    causal = row >= col
    ubd = ubd_ref[...]
    c = conv(ext_x, x_ref[...].astype(F32), par_ref)
    c_ref[...] = c.astype(BF16)
    cb = conv(ext_b, ubd[:, : 2 * N], pbc_ref)
    cb_ref[...] = cb
    bc = cb * sigmoid(cb)
    b_rows = bc[:, :N]
    b_t = b_rows.T.astype(BF16)
    b_low, c_low = b_rows.astype(BF16), bc[:, N:].astype(BF16)
    _, steps, _, logs = step_terms(ubd, head_ref, heads)
    logs_t = logs.T
    scores = dot_nt(c_low, b_low)
    entering = state[...].astype(BF16)
    st_ref[0] = entering
    outer = dot(c_low, entering)
    squares = jnp.zeros((T, 128), F32)
    for pair in range(heads // 2):
        span = slice(128 * pair, 128 * pair + 128)
        h0, h1 = 2 * pair, 2 * pair + 1
        log0, log1 = lanes(logs, h0), lanes(logs, h1)
        log_pair = jnp.where(low, log0, log1)
        step_pair = jnp.where(low, lanes(steps, h0), lanes(steps, h1))
        last_pair = log_pair[T - 1 : T]
        skip_pair = jnp.where(low_row, lanes(head_ref[2:3], h0), lanes(head_ref[2:3], h1))
        cp = c[:, span]
        xp = cp * sigmoid(cp)
        xd = xp * step_pair
        m0 = (scores * jnp.exp(jnp.where(causal, log0 - logs_t[h0 : h0 + 1], NEG))).astype(BF16)
        m1 = (scores * jnp.exp(jnp.where(causal, log1 - logs_t[h1 : h1 + 1], NEG))).astype(BF16)
        stacked = jnp.concatenate([jnp.where(low, xd, 0.0).astype(BF16), jnp.where(low, 0.0, xd).astype(BF16)], axis=0)
        y = dot(jnp.concatenate([m0, m1], axis=1), stacked)
        y = y + jnp.exp(log_pair) * outer[:, span] + skip_pair * xp
        tail = (jnp.exp(last_pair - log_pair) * xd).astype(BF16)
        state[:, span] = jnp.exp(last_pair) * state[:, span] + dot(b_t, tail)
        y_ref[:, span] = y.astype(BF16)
        zp = z_ref[:, span].astype(F32)
        w = y * zp * sigmoid(zp)
        squares = squares + w * w
    ss_ref[0] = to_row(jnp.sum(squares, axis=1, keepdims=True))


def project_kernel(heads, steps, x_ref, w_ref, shard_ref, out_ref, inv_ref, uzx_ref, ubd_ref, gain_ref, fw_ref, *sems):
    deep, width = x_ref.shape[1], 2 * heads * HEAD
    weight_moves(pl.program_id(0), steps, range(1), True, shard_ref, fw_ref, *sems)

    @pl.when(pl.program_id(0) == 0)
    def _():
        for j in range(deep // T):
            span = slice(j * T, j * T + T)
            gain_ref[:, span] = jnp.broadcast_to(w_ref[span, width + 2 * N : width + 3 * N].astype(F32).T[heads : heads + 1], (8, T))

    x = x_ref[...].astype(F32)
    inv = lax.rsqrt(jnp.sum(x * x, axis=1, keepdims=True) / deep + EPS)
    normed = (x * inv * gain_ref[0:1]).astype(BF16)
    out_ref[...] = normed
    for part in range(x.shape[0] // T):
        inv_ref[part] = to_row(inv[part * T : part * T + T])
    uzx_ref[...] = dot(normed, w_ref[:, :width]).astype(BF16)
    ubd_ref[...] = dot(normed, w_ref[:, width:])


def gate_kernel(g_ref, wo_ref, y_ref, z_ref, par_ref, mask_ref, dyn_ref, co_ref):
    dyn = dot(g_ref[...], wo_ref[...])
    for part in range(dyn.shape[0] // T):
        rows = slice(part * T, part * T + T)
        mask = to_col(mask_ref[part])[:, 0:1]
        own = dyn[rows] * mask
        dyn_ref[rows] = own.astype(BF16)
        z = z_ref[rows].astype(F32)
        w = y_ref[rows].astype(F32) * z * sigmoid(z)
        co_ref[part] = to_row(jnp.sum(own * w * par_ref[0:1], axis=1, keepdims=True))


def home_kernel(last, deep, me_ref, order_ref, a_ref, b_ref, *refs):
    out_ref, held_ref = refs[-2:]
    step = pl.program_id(0)
    many = held_ref.shape[0] // a_ref.shape[0]
    size = a_ref.shape[0]

    @pl.when(step < many)
    def _():
        value = a_ref[...].astype(F32) + b_ref[...].astype(F32)
        if last:
            normed_ref, inv_ref, gain_ref, rdz_ref, rdx_ref, more_ref = refs[:6]
            gain = gain_ref[0:1]
            hat = normed_ref[...].astype(F32) / gain
            parts = []
            for part in range(size // T):
                inv_row = inv_ref[part]
                dots = rdz_ref[part] + rdx_ref[part] + more_ref[0, part] + more_ref[1, part] + more_ref[2, part]
                rows = slice(part * T, part * T + T)
                inv = to_col(inv_row)[:, 0:1]
                mean = to_col(dots / deep)[:, 0:1]
                parts.append(inv * (gain * value[rows] - hat[rows] * mean))
            value = jnp.concatenate(parts, axis=0)
        held_ref[pl.ds(pl.multiple_of(step * size, size), size), :] = value.astype(BF16)

    @pl.when(step >= many)
    def _():
        base = ((step - many) * size).astype(F32)
        row = lax.broadcasted_iota(jnp.int32, (size, T), 0).astype(F32) + base
        picks = jnp.concatenate([(row == order_ref[j]).astype(F32).astype(BF16) for j in range(order_ref.shape[0])], axis=1)
        out_ref[...] = dot(picks, held_ref[...]).astype(BF16)


def mid_kernel(width, moves, y_ref, z_ref, dyn_ref, par_ref, mask_ref, ss_ref, co_ref, yg_ref, dz_ref, dy_ref, gg_ref, rd_ref, got_ss, got_co, sems, local_sems):
    step = pl.program_id(0)

    @pl.when(step == 0)
    def _():
        gg_ref[...] = jnp.zeros_like(gg_ref)
        peers, copies = make_moves(moves, (ss_ref, co_ref), (got_ss, got_co), sems, local_sems)
        greet(peers)
        for copy in copies:
            copy.start()
        for copy in copies:
            copy.wait()

    gain = par_ref[0:1]
    parts = y_ref.shape[0] // T
    for part in range(parts):
        rows = slice(part * T, part * T + T)
        here = step * parts + part
        ss, co = ss_ref[here], co_ref[here]
        for other in range(got_ss.shape[0]):
            ss, co = ss + got_ss[other, here], co + got_co[other, here]
        mask = to_col(mask_ref[part])[:, 0:1]
        inv_row = lax.rsqrt(ss / width + EPS)
        inv = to_col(inv_row)[:, 0:1]
        cube = to_col(inv_row * inv_row * inv_row * (co / width))[:, 0:1]
        y = y_ref[rows].astype(F32)
        z = z_ref[rows].astype(F32)
        dyn = dyn_ref[rows].astype(F32)
        s = sigmoid(z)
        act = z * s
        w = y * act
        wi = w * inv
        yg_ref[rows] = (wi * gain * mask).astype(BF16)
        gg_ref[0:1] += jnp.sum(dyn * wi, axis=0, keepdims=True)
        dw = inv * gain * dyn - w * cube
        dy_ref[rows] = (dw * act).astype(BF16)
        dz = dw * y * (s * (1.0 + z * (1.0 - s)))
        dz_ref[rows] = dz.astype(BF16)
        rd_ref[part] = to_row(jnp.sum(dz * z, axis=1, keepdims=True))


def backward_kernel(heads, extra, moves, dy_ref, x_ref, c_ref, cb_ref, ubd_ref, st_ref, par_ref, pbc_ref, head_ref, *refs):
    count = len(moves)
    srcs, refs = refs[:count], refs[count + extra :]
    dx_ref, dbd_ref, rd_ref, gx_ref, gb_ref, gh_ref = refs[:6]
    dsts, refs = refs[6 : 6 + count], refs[6 + count :]
    d_state, ext_x, ext_b, rows_ref, prod, edy_ref, tail_ref = refs[:7]
    if moves:
        began = (pl.program_id(0) == 0) & (pl.program_id(1) == 0)
        ended = (pl.program_id(0) == pl.num_programs(0) - 1) & (pl.program_id(1) == pl.num_programs(1) - 1)
        background(began, ended, moves, srcs, dsts, *refs[7:])
    first = (pl.program_id(0) == 0) & (pl.program_id(1) == 0)

    @pl.when(first)
    def _():
        gx_ref[...] = jnp.zeros_like(gx_ref)
        gb_ref[...] = jnp.zeros_like(gb_ref)
        gh_ref[...] = jnp.zeros_like(gh_ref)
        rows_ref[...] = jnp.zeros_like(rows_ref)

    @pl.when(pl.program_id(1) == 0)
    def _():
        ext_x[T : T + 8] = jnp.zeros_like(ext_x[T : T + 8])
        ext_b[T : T + 8] = jnp.zeros_like(ext_b[T : T + 8])
        d_state[...] = jnp.zeros_like(d_state)

    row, col = iotas(T, T)
    low = col < HEAD
    low_row = lax.broadcasted_iota(jnp.int32, (1, 128), 1) < HEAD
    upto = col >= row
    below = row < col
    reach = (row >= col).astype(BF16)
    ubd = ubd_ref[...]
    raw, steps, rates, logs = step_terms(ubd, head_ref, heads)
    logs_t = logs.T
    cb = cb_ref[...]
    sb = sigmoid(cb)
    bc = cb * sb
    b_low, c_low = bc[:, :N].astype(BF16), bc[:, N:].astype(BF16)
    c_t = bc[:, N:].T.astype(BF16)
    scores = dot_nt(b_low, c_low)
    entering = st_ref[0]
    outer = dot(c_low, entering)
    ds_low = d_state[...].astype(BF16)
    back = dot(b_low, ds_low)
    d_scores = jnp.zeros((T, T), F32)
    skip_parts, closing_parts = [], []
    for pair in range(heads // 2):
        span = slice(128 * pair, 128 * pair + 128)
        h0, h1 = 2 * pair, 2 * pair + 1
        log0, log1 = lanes(logs, h0), lanes(logs, h1)
        log_pair = jnp.where(low, log0, log1)
        step_pair = jnp.where(low, lanes(steps, h0), lanes(steps, h1))
        last_pair = log_pair[T - 1 : T]
        skip_pair = jnp.where(low_row, lanes(head_ref[2:3], h0), lanes(head_ref[2:3], h1))
        cp = c_ref[:, span].astype(F32)
        sp = sigmoid(cp)
        xp = cp * sp
        xd = xp * step_pair
        dy_low = dy_ref[:, span]
        dy = dy_low.astype(F32)
        decay0 = jnp.exp(jnp.where(upto, logs_t[h0 : h0 + 1] - log0, NEG))
        decay1 = jnp.exp(jnp.where(upto, logs_t[h1 : h1 + 1] - log1, NEG))
        m0, m1 = scores * decay0, scores * decay1
        zero = jnp.zeros_like(dy_low)
        x_stack = jnp.concatenate([jnp.where(low, xd, 0.0).astype(BF16), jnp.where(low, 0.0, xd).astype(BF16)], axis=0)
        dm = dot_nt(x_stack, dy_low)
        dm0, dm1 = dm[:T], dm[T:]
        d_scores = d_scores + dm0 * decay0 + dm1 * decay1
        dy_stack = jnp.concatenate([jnp.where(low, dy, 0.0).astype(BF16), jnp.where(low, 0.0, dy).astype(BF16)], axis=0)
        dxd = dot(jnp.concatenate([m0.astype(BF16), m1.astype(BF16)], axis=1), dy_stack)
        flow = jnp.concatenate([(dm0 * m0).astype(BF16), (dm1 * m1).astype(BF16)], axis=0)
        later = dot(flow, reach)
        rows_ref[h0 : h0 + 1] = jnp.sum(jnp.where(below, later[:T], 0.0), axis=0, keepdims=True)
        rows_ref[h1 : h1 + 1] = jnp.sum(jnp.where(below, later[T:], 0.0), axis=0, keepdims=True)
        grow = jnp.exp(log_pair)
        tail = jnp.exp(last_pair - log_pair)
        from_state = tail * back[:, span]
        dxd = dxd + from_state
        edy = grow * dy
        prod[0:T, span] = (edy * outer[:, span]).astype(BF16)
        prod[T : 2 * T, span] = (from_state * xd).astype(BF16)
        prod[2 * T : 3 * T, span] = (xp * dxd).astype(BF16)
        skip_parts.append(jnp.sum(xp * dy, axis=0, keepdims=True))
        edy_low = edy.astype(BF16)
        edy_ref[:, span] = edy_low
        tail_ref[:, span] = (tail * xd).astype(BF16)
        old = d_state[:, span]
        closing = jnp.exp(last_pair)
        closing_parts.append(closing * jnp.sum(old * entering[:, span].astype(F32), axis=0, keepdims=True))
        d_state[:, span] = closing * old + dot(c_t, edy_low)
        dx = dxd * step_pair + skip_pair * dy
        ext_x[0:T, span] = dx * (sp * (1.0 + cp * (1.0 - sp)))
    d_low = d_scores.astype(BF16)
    d_b = dot_nt(tail_ref[...], ds_low) + dot(d_low, c_low)
    d_c = dot_nt(edy_ref[...], entering) + dot(d_scores.T.astype(BF16), b_low)
    width = heads * HEAD
    lane_row, lane_col = iotas(width, 128)
    member = (lane_row // HEAD == lane_col).astype(BF16)
    sums = dot(prod[...], member)
    skip_all = jnp.concatenate(skip_parts, axis=1)
    closing_all = jnp.concatenate(closing_parts, axis=1)
    fill = jnp.zeros((6, width), F32)
    few = dot_exact(jnp.concatenate([skip_all, closing_all, fill], axis=0), member.astype(F32))
    d_logs = dot(upto.astype(BF16), sums[:T].astype(BF16)) + dot((col < row).astype(BF16), sums[T : 2 * T].astype(BF16))
    d_logs = d_logs + rows_ref[...].T + few[1:2]
    d_steps = sums[2 * T :] + rates * d_logs
    d_raw = jnp.where(col < heads, d_steps * sigmoid(raw), 0.0)
    gh_ref[0:1] += jnp.sum(d_raw, axis=0, keepdims=True)
    gh_ref[1:2] += rates * jnp.sum(steps * d_logs, axis=0, keepdims=True)
    gh_ref[2:3] += few[0:1]
    ext_b[0:T, 0:N] = d_b * (sb[:, :N] * (1.0 + cb[:, :N] * (1.0 - sb[:, :N])))
    ext_b[0:T, N:] = d_c * (sb[:, N:] * (1.0 + cb[:, N:] * (1.0 - sb[:, N:])))

    def conv_back(ext, values, taps, grads):
        now = ext[0:T]
        total = taps[3:4] * now
        grads[3:4] += jnp.sum(values * now, axis=0, keepdims=True)
        grads[4:5] += jnp.sum(now, axis=0, keepdims=True)
        for k in range(3):
            moved = ext[3 - k : 3 - k + T]
            total = total + taps[k : k + 1] * moved
            grads[k : k + 1] += jnp.sum(values * moved, axis=0, keepdims=True)
        ext[T : T + 8] = ext[0:8]
        return total

    ux = x_ref[...].astype(F32)
    dux = conv_back(ext_x, ux, par_ref, gx_ref)
    dx_ref[...] = dux.astype(BF16)
    ubc = ubd[:, : 2 * N]
    dubc = conv_back(ext_b, ubc, pbc_ref, gb_ref)
    dbd_ref[:, : 2 * N] = dubc.astype(BF16)
    dbd_ref[:, 2 * N :] = d_raw.astype(BF16)
    total = jnp.sum(dux * ux, axis=1, keepdims=True) + jnp.sum(dubc * ubc, axis=1, keepdims=True)
    total = total + jnp.sum(jnp.where(col < heads, d_raw * ubd[:, 2 * N :], 0.0), axis=1, keepdims=True)
    rd_ref[0] = to_row(total)


def params(*semantics, number=0):
    if number:
        return pltpu.CompilerParams(
            dimension_semantics=semantics, vmem_limit_bytes=LIMIT, collective_id=number, has_side_effects=True
        )
    return pltpu.CompilerParams(dimension_semantics=semantics, vmem_limit_bytes=LIMIT)


def run_forward(heads, u_zx, u_bd, par, pbc, hp, w_out, before, number):
    rows, width = u_zx.shape[0], heads * HEAD
    slots, chunks = rows // LEN, LEN // T
    at = lambda s, i: (s * chunks + i, 0)
    fixed = lambda s, i: (0, 0)
    size = lax.axis_size("dp")
    anywhere = pl.BlockSpec(memory_space=pl.ANY)
    return pl.pallas_call(
        functools.partial(forward_kernel, heads, slots * chunks),
        grid=(slots, chunks),
        in_specs=[
            pl.BlockSpec((T, width), lambda s, i: (s * chunks + i, 1)),
            pl.BlockSpec((T, width), at),
            pl.BlockSpec((T, 3 * N), at),
            pl.BlockSpec((5, width), fixed),
            pl.BlockSpec((5, 2 * N), fixed),
            pl.BlockSpec((8, 128), fixed),
            anywhere,
            anywhere,
        ],
        out_specs=[
            pl.BlockSpec((T, width), at),
            pl.BlockSpec((1, 1, T), lambda s, i: (s * chunks + i, 0, 0)),
            pl.BlockSpec((T, width), at),
            pl.BlockSpec((T, 2 * N), at),
            pl.BlockSpec((1, N, width), lambda s, i: (s * chunks + i, 0, 0)),
            anywhere,
        ],
        out_shape=[
            jax.ShapeDtypeStruct((rows, width), BF16),
            jax.ShapeDtypeStruct((rows // T, 1, T), F32),
            jax.ShapeDtypeStruct((rows, width), BF16),
            jax.ShapeDtypeStruct((rows, 2 * N), F32),
            jax.ShapeDtypeStruct((rows // T, N, width), BF16),
            full_shape(size, w_out),
        ],
        scratch_shapes=[
            pltpu.VMEM((T + 8, width), F32),
            pltpu.VMEM((T + 8, 2 * N), F32),
            pltpu.VMEM((N, width), F32),
        ]
        + weight_scratch(size, w_out),
        input_output_aliases={7: 5},
        compiler_params=params("arbitrary", "arbitrary", number=number),
        cost_estimate=pl.CostEstimate(flops=rows * width * 2 * 1200, bytes_accessed=rows * width * 8, transcendentals=rows * width * 6),
        name="scan_forward",
    )(u_zx, u_zx, u_bd, par, pbc, hp, cut_shard(w_out), before)


def run_project(heads, x, w_in, w_out, number):
    rows, deep = x.shape
    wide = w_in.shape[1]
    width = 2 * heads * HEAD
    size = lax.axis_size("dp")
    step = 256
    at = lambda i: (i, 0)
    fixed = lambda i: (0, 0)
    anywhere = pl.BlockSpec(memory_space=pl.ANY)
    thin = pl.BlockSpec((step // T, 1, T), lambda i: (i, 0, 0))
    return pl.pallas_call(
        functools.partial(project_kernel, heads, rows // step),
        grid=(rows // step,),
        in_specs=[pl.BlockSpec((step, deep), at), pl.BlockSpec((deep, wide), fixed), anywhere],
        out_specs=[
            pl.BlockSpec((step, deep), at),
            thin,
            pl.BlockSpec((step, width), at),
            pl.BlockSpec((step, wide - width), at),
            pl.BlockSpec((8, deep), fixed),
            anywhere,
        ],
        out_shape=[
            jax.ShapeDtypeStruct((rows, deep), BF16),
            jax.ShapeDtypeStruct((rows // T, 1, T), F32),
            jax.ShapeDtypeStruct((rows, width), BF16),
            jax.ShapeDtypeStruct((rows, wide - width), F32),
            jax.ShapeDtypeStruct((8, deep), F32),
            full_shape(size, w_out),
        ],
        scratch_shapes=weight_scratch(size, w_out),
        compiler_params=params("arbitrary", number=number),
        cost_estimate=pl.CostEstimate(flops=LIGHT, bytes_accessed=LIGHT, transcendentals=0),
        name="project",
    )(x, w_in, cut_shard(w_out))


def run_gate(grads, w_out, y, u_zx, par, mask):
    rows, width = y.shape
    deep = grads.shape[1]
    step = 256
    at = lambda i: (i, 0)
    fixed = lambda i: (0, 0)
    thin = pl.BlockSpec((step // T, 1, T), lambda i: (i, 0, 0))
    return pl.pallas_call(
        gate_kernel,
        grid=(rows // step,),
        in_specs=[
            pl.BlockSpec((step, deep), at),
            pl.BlockSpec((deep, width), fixed),
            pl.BlockSpec((step, width), at),
            pl.BlockSpec((step, width), at),
            pl.BlockSpec((1, width), fixed),
            thin,
        ],
        out_specs=[pl.BlockSpec((step, width), at), thin],
        out_shape=[jax.ShapeDtypeStruct((rows, width), BF16), jax.ShapeDtypeStruct((rows // T, 1, T), F32)],
        compiler_params=params("arbitrary"),
        cost_estimate=pl.CostEstimate(flops=rows * deep * width * 2, bytes_accessed=rows * deep * 2 + rows * width * 6, transcendentals=rows * width),
        name="gate_back",
    )(grads, w_out, y, u_zx, par, mask)


def run_home(me, order, sums, extra, deep, name, after=()):
    rows, quarter = sums[0].shape
    step = 512
    many = rows // step
    into = lambda i, m: (jnp.minimum(i, many - 1), 0)
    thin = pl.BlockSpec((step // T, 1, T), lambda i, m: (jnp.minimum(i, many - 1), 0, 0))
    specs = [pl.BlockSpec((rows // T, 1, T), lambda i, m: (0, 0, 0))] + [pl.BlockSpec((step, quarter), into)] * 2
    values = list(sums)
    if extra is not None:
        specs += [pl.BlockSpec((step, quarter), lambda i, m: (jnp.minimum(i, many - 1), m[0])), thin]
        specs += [pl.BlockSpec((8, quarter), lambda i, m: (0, m[0])), thin, thin]
        specs += [pl.BlockSpec((3, step // T, 1, T), lambda i, m: (0, jnp.minimum(i, many - 1), 0, 0))]
        values += list(extra)
    values += list(after)
    specs += [pl.BlockSpec(memory_space=pl.ANY)] * len(after)
    return pl.pallas_call(
        functools.partial(home_kernel, extra is not None, float(deep)),
        grid_spec=pltpu.PrefetchScalarGridSpec(
            num_scalar_prefetch=1,
            grid=(2 * many,),
            in_specs=specs,
            out_specs=pl.BlockSpec((step, quarter), lambda i, m: (jnp.maximum(i - many, 0), 0)),
            scratch_shapes=[pltpu.VMEM((rows, quarter), BF16)],
        ),
        out_shape=jax.ShapeDtypeStruct((rows, quarter), BF16),
        compiler_params=params("arbitrary"),
        cost_estimate=pl.CostEstimate(flops=rows * rows * quarter * 2, bytes_accessed=rows * quarter * 10, transcendentals=0),
        name=name,
    )(me, order, *values)


def run_mid(all_width, y, u_zx, dyn, par, mask, ss, co, number):
    rows, width = y.shape
    step = 256
    at = lambda i: (i, 0)
    fixed = lambda i: (0, 0)
    thin = pl.BlockSpec((step // T, 1, T), lambda i: (i, 0, 0))
    whole = pl.BlockSpec((rows // T, 1, T), lambda i: (0, 0, 0))
    wide = pl.BlockSpec((step, width), at)
    moves = (("spread", "head"), ("spread", "head"))
    others = lax.axis_size("head") - 1
    return pl.pallas_call(
        functools.partial(mid_kernel, float(all_width), moves),
        grid=(rows // step,),
        in_specs=[wide, wide, wide, pl.BlockSpec((1, width), fixed), thin, whole, whole],
        out_specs=[wide, wide, wide, pl.BlockSpec((8, width), fixed), thin],
        out_shape=[jax.ShapeDtypeStruct((rows, width), BF16)] * 3
        + [jax.ShapeDtypeStruct((8, width), F32), jax.ShapeDtypeStruct((rows // T, 1, T), F32)],
        scratch_shapes=[pltpu.VMEM((others, rows // T, 1, T), F32)] * 2 + move_scratch(moves, (ss, co)),
        compiler_params=params("arbitrary", number=number),
        cost_estimate=pl.CostEstimate(flops=rows * width * 30, bytes_accessed=rows * width * 12, transcendentals=rows * width),
        name="gate_mid",
    )(y, u_zx, dyn, par, mask, ss, co)


def run_backward(heads, slot, dy, u_zx, c, cb, u_bd, st, par, pbc, hp, before, moves, values, number, after=()):
    rows, width = dy.shape
    chunks = LEN // T
    place = lambda s, i: slot * chunks + chunks - 1 - i
    at = lambda s, i: (place(s, i), 0)
    at3 = lambda s, i: (place(s, i), 0, 0)
    fixed = lambda s, i: (0, 0)
    anywhere = pl.BlockSpec(memory_space=pl.ANY)
    return pl.pallas_call(
        functools.partial(backward_kernel, heads, len(before) + len(after), tuple(moves)),
        grid=(1, chunks),
        in_specs=[
            pl.BlockSpec((T, width), at),
            pl.BlockSpec((T, width), lambda s, i: (place(s, i), 1)),
            pl.BlockSpec((T, width), at),
            pl.BlockSpec((T, 2 * N), at),
            pl.BlockSpec((T, 3 * N), at),
            pl.BlockSpec((1, N, width), at3),
            pl.BlockSpec((5, width), fixed),
            pl.BlockSpec((5, 2 * N), fixed),
            pl.BlockSpec((8, 128), fixed),
        ]
        + [anywhere] * (len(moves) + len(before) + len(after)),
        out_specs=[
            pl.BlockSpec((T, width), at),
            pl.BlockSpec((T, 3 * N), at),
            pl.BlockSpec((1, 1, T), at3),
            pl.BlockSpec((8, width), fixed),
            pl.BlockSpec((8, 2 * N), fixed),
            pl.BlockSpec((8, 128), fixed),
        ]
        + [anywhere] * len(moves),
        out_shape=[
            jax.ShapeDtypeStruct((rows, width), BF16),
            jax.ShapeDtypeStruct((rows, 3 * N), BF16),
            jax.ShapeDtypeStruct((rows // T, 1, T), F32),
            jax.ShapeDtypeStruct((8, width), F32),
            jax.ShapeDtypeStruct((8, 2 * N), F32),
            jax.ShapeDtypeStruct((8, 128), F32),
        ]
        + move_outs(moves, values),
        scratch_shapes=[
            pltpu.VMEM((N, width), F32),
            pltpu.VMEM((T + 8, width), F32),
            pltpu.VMEM((T + 8, 2 * N), F32),
            pltpu.VMEM((128, 128), F32),
            pltpu.VMEM((3 * T, width), BF16),
            pltpu.VMEM((T, width), BF16),
            pltpu.VMEM((T, width), BF16),
        ]
        + move_scratch(moves, values),
        input_output_aliases={9 + len(moves) + i: i for i in range(len(before))},
        compiler_params=params("arbitrary", "arbitrary", number=number),
        cost_estimate=pl.CostEstimate(flops=LIGHT, bytes_accessed=LIGHT, transcendentals=0),
        name="scan_backward",
    )(dy, u_zx, c, cb, u_bd, st, par, pbc, hp, *values, *before, *after)


def pieces_kernel(count, many, moves, extra, *refs):
    total = len(moves)
    values, weight_ref, srcs = refs[:count], refs[count], refs[count + 1 : count + 1 + total]
    refs = refs[count + 1 + total + extra :]
    far_ref, own_ref = refs[:2]
    dsts, refs = refs[2 : 2 + total], refs[2 + total :]
    sent_ref, came_ref, near_sems, joined_ref = refs[:4]
    step = pl.program_id(0)
    rows, quarter = far_ref.shape
    start = 0
    for value in values:
        joined_ref[:, start : start + value.shape[1]] = value[...]
        start += value.shape[1]
    dp, own = lax.axis_index("dp"), lax.axis_index("head")
    near = (dp, own ^ 1)
    peers, copies = make_moves(moves, srcs, dsts, *refs[4:]) if moves else ([], [])

    @pl.when(step == 0)
    def _():
        greet(peers if near_in(moves) else [near] + peers)
        for copy in copies:
            copy.start()

    def product(k):
        at = pl.ds(pl.multiple_of((own ^ k) * quarter, 128), quarter)
        return dot_nt(joined_ref[...], weight_ref[at, :])

    def near_copy(block):
        return pltpu.make_async_remote_copy(
            src_ref=sent_ref.at[block],
            dst_ref=came_ref.at[block],
            send_sem=near_sems.at[0, block],
            recv_sem=near_sems.at[1, block],
            device_id=near,
            device_id_type=MESH,
        )

    @pl.when(step < many)
    def _():
        sent_ref[step, :, :quarter] = product(3).astype(BF16)
        sent_ref[step, :, quarter:] = product(1).astype(BF16)
        near_copy(step).start()

    @pl.when(step >= many)
    def _():
        block = step - many
        far, mine = product(2), product(0)
        near_copy(block).wait_recv()
        far_ref[...] = (far + came_ref[block, :, :quarter].astype(F32)).astype(BF16)
        own_ref[...] = (mine + came_ref[block, :, quarter:].astype(F32)).astype(BF16)

    @pl.when(step == 2 * many - 1)
    def _():
        for block in range(many):
            near_copy(block).wait_send()
        for copy in copies:
            copy.wait()


def near_in(moves):
    return any(move[0] == "spread" and move[1] == "head" for move in moves)


def run_pieces(values, weight, quarter, name, moves, moved, number, after=()):
    rows = values[0].shape[0]
    step = 512
    many = rows // step
    anywhere = pl.BlockSpec(memory_space=pl.ANY)
    specs = [pl.BlockSpec((step, v.shape[1]), lambda i: (lax.rem(i, many), 0)) for v in values]
    specs.append(pl.BlockSpec(weight.shape, lambda i: (0, 0)))
    return pl.pallas_call(
        functools.partial(pieces_kernel, len(values), many, tuple(moves), len(after)),
        grid=(2 * many,),
        in_specs=specs + [anywhere] * (len(moves) + len(after)),
        out_specs=[pl.BlockSpec((step, quarter), lambda i: (jnp.maximum(i - many, 0), 0))] * 2 + [anywhere] * len(moves),
        out_shape=[jax.ShapeDtypeStruct((rows, quarter), BF16)] * 2 + move_outs(moves, moved),
        scratch_shapes=[pltpu.VMEM((many, step, 2 * quarter), BF16)] * 2 + [pltpu.SemaphoreType.DMA((2, many)), pltpu.VMEM((step, weight.shape[1]), BF16)] + move_scratch(moves, moved),
        compiler_params=params("arbitrary", number=number),
        cost_estimate=pl.CostEstimate(flops=LIGHT, bytes_accessed=LIGHT, transcendentals=0),
        name=name,
    )(*values, weight, *moved, *after)


def grads_kernel(count, parts, moves, extra, *refs):
    total = len(moves)
    lefts, rights, srcs = refs[:count], refs[count : 2 * count], refs[2 * count : 2 * count + total]
    refs = refs[2 * count + total + extra :]
    outs, dsts, sems = refs[:count], refs[count : count + total], refs[count + total :]
    step = pl.program_id(0)
    if moves:
        background(step == 0, step == count * parts - 1, moves, srcs, dsts, *sems)
    for which in range(count):

        @pl.when((step >= which * parts) & (step < (which + 1) * parts))
        def _():
            out = lax.dot_general(lefts[which][...], rights[which][...], (((0,), (0,)), ((), ())), preferred_element_type=F32)
            outs[which][...] = out.astype(BF16)


def run_grads(pairs, name, moves=(), moved=(), number=0, after=()):
    rows, deep = pairs[0][0].shape
    step = 512
    parts = deep // step
    count = len(pairs)
    anywhere = pl.BlockSpec(memory_space=pl.ANY)
    into = lambda which: lambda i: jnp.clip(i - which * parts, 0, parts - 1)
    specs = [pl.BlockSpec((rows, step), lambda i, at=into(w): (0, at(i))) for w in range(count)]
    specs += [pl.BlockSpec(right.shape, lambda i: (0, 0)) for _, right in pairs]
    return pl.pallas_call(
        functools.partial(grads_kernel, count, parts, tuple(moves), len(after)),
        grid=(count * parts,),
        in_specs=specs + [anywhere] * (len(moves) + len(after)),
        out_specs=[pl.BlockSpec((step, right.shape[1]), lambda i, at=into(w): (at(i), 0)) for w, (_, right) in enumerate(pairs)]
        + [anywhere] * len(moves),
        out_shape=[jax.ShapeDtypeStruct((deep, right.shape[1]), BF16) for _, right in pairs] + move_outs(moves, moved),
        scratch_shapes=move_scratch(moves, moved),
        compiler_params=params("arbitrary", number=number),
        cost_estimate=pl.CostEstimate(flops=LIGHT, bytes_accessed=LIGHT, transcendentals=0),
        name=name,
    )(*[left for left, _ in pairs], *[right for _, right in pairs], *moved, *after)


def last_kernel(moves, *refs):
    count = len(moves)
    srcs, pair_ref = refs[:count], refs[count]
    dsts, out_ref = refs[count + 1 : 2 * count + 1], refs[2 * count + 1]
    kept_ref, line_ref, came_ref, own_ref, pair_sems, sems, local_sems = refs[2 * count + 2 :]
    me, head = lax.axis_index("dp"), lax.axis_index("head")
    peers, copies = make_moves(moves, srcs, dsts, sems, local_sems)

    def remote(src, dst, slot, peer):
        return pltpu.make_async_remote_copy(
            src_ref=src, dst_ref=dst, send_sem=pair_sems.at[0, slot], recv_sem=pair_sems.at[1, slot], device_id=(peer, head), device_id_type=MESH
        )

    high = me >> 1
    half = remote(pair_ref.at[:, 1 - (me & 1)], came_ref, 0, me ^ 1)
    line = [remote(kept_ref.at[high ^ j], line_ref.at[j - 1], j, me ^ (2 * j)) for j in range(1, own_ref.shape[0])]
    own = pltpu.make_async_copy(pair_ref.at[:, me & 1], own_ref, pair_sems.at[2, 0])
    greet(peers)
    half.start()
    own.start()
    for copy in copies:
        copy.start()
    own.wait()
    half.wait()
    for j in range(own_ref.shape[0]):
        kept_ref[j] = (own_ref[j].astype(F32) + came_ref[j].astype(F32)).astype(BF16)
    for copy in line:
        copy.start()
    for copy in line:
        copy.wait()
    total = kept_ref[high].astype(F32)
    for j in range(1, own_ref.shape[0]):
        total = total + line_ref[j - 1].astype(F32)
    out_ref[...] = total
    for copy in copies:
        copy.wait()


def run_last(moves, values, paired, number):
    many, _, block, wide = paired.shape
    anywhere = pl.BlockSpec(memory_space=pl.ANY)
    own = pltpu.VMEM((many, block, wide), BF16)
    return pl.pallas_call(
        functools.partial(last_kernel, tuple(moves)),
        in_specs=[anywhere] * (len(moves) + 1),
        out_specs=[anywhere] * len(moves) + [pl.BlockSpec(memory_space=pltpu.VMEM)],
        out_shape=move_outs(moves, values) + [jax.ShapeDtypeStruct((block, wide), F32)],
        scratch_shapes=[own, pltpu.VMEM((many - 1, block, wide), BF16), own, own, pltpu.SemaphoreType.DMA((3, many))] + move_scratch(moves, values),
        compiler_params=pltpu.CompilerParams(collective_id=number, has_side_effects=True, vmem_limit_bytes=LIMIT),
        name="last_exchange",
    )(*values, paired)


def row_forward(size, quarter, own_ref, full_ref, sems):
    me, own = lax.axis_index("dp"), lax.axis_index("head")
    columns = lambda head: pl.ds(pl.multiple_of(head * quarter, 128), quarter)

    def copy(src, dst, stage, k, head):
        return pltpu.make_async_remote_copy(
            src_ref=src, dst_ref=dst, send_sem=sems.at[0, stage, k], recv_sem=sems.at[1, stage, k], device_id=(me, head), device_id_type=MESH
        )

    def source(k):
        return full_ref.at[me ^ k, :, columns(own)] if own_ref is None else own_ref.at[me ^ k]

    def far(k):
        return copy(source(k), full_ref.at[me ^ k, :, columns(own)], 0, k, own ^ 2)

    def near(k):
        return copy(source(k), full_ref.at[me ^ k, :, columns(own)], 1, k, own ^ 1)

    def back(k):
        block = full_ref.at[me ^ k, :, columns(own ^ 2)]
        return copy(block, block, 2, k, own ^ 1)

    return far, near, back


def shard_spread(src, dst, across_sems, side_sems):
    me, own = lax.axis_index("dp"), lax.axis_index("head")

    def copy(a, b, sems, part, j, peer):
        return pltpu.make_async_remote_copy(
            src_ref=a, dst_ref=b, send_sem=sems.at[0, part, j], recv_sem=sems.at[1, part, j], device_id=(peer, own), device_id_type=MESH
        )

    def across(part, j):
        return copy(src.at[part], dst.at[me, part], across_sems, part, j, me ^ (2 * j))

    def side(part, j):
        here = dst.at[me ^ (2 * j), part]
        return copy(src.at[part] if j == 0 else here, here, side_sems, part, j, me ^ 1)

    return across, side


def entry_kernel(parts, order_ref, x_ref, g_ref, w_ref, fx_ref, fg_ref, fw_ref, row_sems, x_sems, g_sems, line_sems, side_sems, local_sems, land, ready, picks, w_held):
    size, block, quarter = x_ref.shape
    line = size // 2
    me, own = lax.axis_index("dp"), lax.axis_index("head")
    spot = me >> 1
    mine = pl.ds(pl.multiple_of(own * quarter, 128), quarter)
    sources, fulls = (x_ref, g_ref), (fx_ref, fg_ref)
    forwards = [row_forward(size, quarter, ready.at[i], fulls[i], sems) for i, sems in enumerate((x_sems, g_sems))]

    def remote(src, dst, sems, slot, peer):
        return pltpu.make_async_remote_copy(
            src_ref=src, dst_ref=dst, send_sem=sems.at[(0,) + slot], recv_sem=sems.at[(1,) + slot], device_id=(peer, own), device_id_type=MESH
        )

    def rows(which, k):
        return remote(sources[which].at[me ^ k], land.at[which, me], row_sems, (which, k), me ^ k)

    def along(way, part, j):
        sign = 1 - 2 * way
        origin = jnp.clip(me - sign * 2 * (j - 1), 0, size - 1)
        peer = jnp.clip(me + sign * 2, 0, size - 1)
        here = fw_ref.at[origin, part]
        return remote(w_ref.at[part] if j == 1 else here, here, line_sems, (way, part, j - 1), peer)

    def came(way, part, j):
        sign = 1 - 2 * way
        here = fw_ref.at[jnp.clip(me - sign * 2 * j, 0, size - 1), part]
        return remote(here, here, line_sems, (way, part, j - 1), me)

    def side(way, part, j):
        sign = 1 - 2 * way
        here = fw_ref.at[jnp.clip(me - sign * 2 * j, 0, size - 1), part]
        return remote(w_ref.at[part] if j == 0 else here, here, side_sems, (way, part, j), me ^ 1)

    def goes_on(way):
        return spot < line - 1 if way == 0 else spot > 0

    def arrives(way, j):
        return spot >= j if way == 0 else spot < line - j

    into = [pltpu.make_async_copy(sources[i].at[me], land.at[i, me], local_sems.at[i]) for i in range(2)]
    into.append(pltpu.make_async_copy(w_ref, w_held, local_sems.at[2]))
    held = [pltpu.make_async_copy(ready.at[i], fulls[i].at[:, :, mine], local_sems.at[3 + i]) for i in range(2)]
    held.append(pltpu.make_async_copy(w_held, fw_ref.at[me], local_sems.at[5]))
    for copy in into:
        copy.start()
    greet([(me ^ k, own) for k in range(1, size)] + [(me, own ^ 1), (me, own ^ 2)])
    order = turn_order(size)
    for k in order:
        rows(0, k).start()
    for part in range(parts):
        side(0, part, 0).start()
    for copy in into:
        copy.wait()
    held[2].start()
    total = size * block
    lane = lax.broadcasted_iota(jnp.int32, (T, T), 1).astype(F32)

    def pick(i, carry):
        wanted = to_col(order_ref[i])
        at = pl.ds(pl.multiple_of(i * T, T), T)
        for j in range(total // T):
            picks[at, j * T : j * T + T] = (wanted == lane + float(T * j)).astype(F32).astype(BF16)
        return carry

    lax.fori_loop(0, total // T, pick, 0)

    def arrange(which):
        step = min(512, total)
        for i in range(total // step):
            value = dot(picks[i * step : (i + 1) * step, :], land[which].reshape(total, quarter)).astype(BF16)
            ready[which, i * step // block : (i + 1) * step // block] = value.reshape(step // block, block, quarter)
        held[which].start()
        far, near, _ = forwards[which]
        for k in range(size):
            far(k).start()
            near(k).start()

    def backs(which, some):
        far, _, back = forwards[which]
        for k in some:
            far(k).wait_recv()
            back(k).start()

    for k in order:
        rows(0, k).wait_recv()
    for k in order:
        rows(1, k).start()
    arrange(0)
    for k in order:
        rows(1, k).wait_recv()
    for way in range(2):

        @pl.when(goes_on(way))
        def _():
            for part in range(parts):
                along(way, part, 1).start()

    arrange(1)
    backs(0, range(size))
    for j in range(1, line):
        for part in range(parts):
            if j == line - 1:
                backs(1, range(part * size // parts, (part + 1) * size // parts))
            for way in range(2):

                @pl.when(arrives(way, j))
                def _():
                    came(way, part, j).wait_recv()
                    side(way, part, j).start()

                if j + 1 < line:

                    @pl.when(arrives(way, j) & goes_on(way))
                    def _():
                        along(way, part, j + 1).start()

    for copy in held:
        copy.wait()
    for which in range(2):
        far, near, back = forwards[which]
        for k in range(size):
            near(k).wait()
            back(k).wait()
            far(k).wait_send()
            if k:
                rows(which, k).wait_send()
    for part in range(parts):
        side(0, part, 0).wait()
        for way in range(2):

            @pl.when(goes_on(way))
            def _():
                along(way, part, 1).wait_send()

            for j in range(1, line):

                @pl.when(arrives(way, j))
                def _():
                    side(way, part, j).wait()

                if j + 1 < line:

                    @pl.when(arrives(way, j) & goes_on(way))
                    def _():
                        along(way, part, j + 1).wait_send()


PARTS = 4


def cut_shard(w):
    return w.reshape(PARTS, w.shape[0] // PARTS, w.shape[1])


def full_shape(size, w):
    return jax.ShapeDtypeStruct((size, PARTS, w.shape[0] // PARTS, w.shape[1]), BF16)


def run_entry(order, tokens, cotangent, w_in, number):
    size = lax.axis_size("dp")
    rows, quarter = tokens.shape
    block = rows // size
    line = size // 2
    anywhere = pl.BlockSpec(memory_space=pl.ANY)
    sems = pltpu.SemaphoreType.DMA
    full = jax.ShapeDtypeStruct((size, block, quarter * 4), BF16)
    came_x, came_g, came_w = pl.pallas_call(
        functools.partial(entry_kernel, PARTS),
        in_specs=[pl.BlockSpec(memory_space=pltpu.VMEM)] + [anywhere] * 3,
        out_specs=[anywhere] * 3,
        out_shape=[full, full, full_shape(size, w_in)],
        scratch_shapes=[
            sems((2, 2, size)),
            sems((2, 3, size)),
            sems((2, 3, size)),
            sems((2, 2, PARTS, line)),
            sems((2, 2, PARTS, line)),
            sems((6,)),
            pltpu.VMEM((2, size, block, quarter), BF16),
            pltpu.VMEM((2, size, block, quarter), BF16),
            pltpu.VMEM((rows, rows), BF16),
            pltpu.VMEM((PARTS, w_in.shape[0] // PARTS, w_in.shape[1]), BF16),
        ],
        compiler_params=pltpu.CompilerParams(collective_id=number, has_side_effects=True, vmem_limit_bytes=LIMIT),
        name="entry",
    )(order, tokens.reshape(size, block, quarter), cotangent.reshape(size, block, quarter), cut_shard(w_in))
    return came_x.reshape(rows, quarter * 4), came_g.reshape(rows, quarter * 4), came_w.reshape(size * w_in.shape[0], w_in.shape[1])


def mm(a, b, contract, kind):
    return lax.dot_general(a, b, (contract, ((), ())), preferred_element_type=F32).astype(kind)


def body(tokens, cotangent, order, lengths, norm_gain, w_zx, w_bc, w_dt, w_out, conv_x, conv_bc, head_params, gate_gain):
    rows, quarter = tokens.shape
    heads = head_params.shape[1]
    width = heads * HEAD
    me = lax.axis_index("head").astype(jnp.int32).reshape(1)
    size = lax.axis_size("dp")
    here = lax.axis_index("dp")
    all_width = width * lax.axis_size("head")
    deep = quarter * lax.axis_size("head")
    own_w = w_zx.shape[0]
    arrange = order.astype(F32).reshape(rows // T, 1, T)

    packed = jnp.concatenate(
        [w_zx.reshape(own_w, 2 * width), w_bc, w_dt, norm_gain[:, None], jnp.zeros((own_w, 127 - heads), BF16)], axis=1
    )
    blocks = lambda value: value.reshape(size, rows // size, quarter)
    full_x, full_g, w_in = run_entry(arrange, tokens, cotangent, packed, 1)
    normed, inv_one, u_zx, u_bd, gain, w_o = run_project(heads, full_x, w_in, w_out, 2)

    gated = gate_gain.reshape(1, width)
    hp = jnp.pad(head_params, ((0, 5), (0, 128 - heads)))
    positions = lax.broadcasted_iota(jnp.int32, (lengths.shape[0], LEN), 1)
    mask = (positions < lengths[:, None]).astype(F32).reshape(rows // T, 1, T)

    y, ss, c, cb, st, w_o = run_forward(heads, u_zx, u_bd, conv_x, conv_bc, hp, w_out, w_o, 3)
    w_o = w_o.reshape(deep, width)
    dyn, co = run_gate(full_g, w_o, y, u_zx, gated, mask)
    yg, dz, dy, gg, rd_z = run_mid(all_width, y, u_zx, dyn, gated, mask, ss, co, 4)

    def keep(paired, came, bit):
        own = lax.dynamic_index_in_dim(paired, (here >> bit) & 1, 1, keepdims=False)
        return (own.astype(F32) + came.astype(F32)).astype(BF16)

    def total(kept, came, shift):
        own = lax.dynamic_index_in_dim(kept, here >> shift, 0, keepdims=False)
        return own.astype(F32) + jnp.sum(came.astype(F32), axis=0)

    def pairs(grads):
        return grads.reshape(size // 2, 2, own_w, grads.shape[1])

    def fours(grads):
        return grads.reshape(size // 4, 2, -1, own_w, grads.shape[-1])

    scan = functools.partial(run_backward, heads)
    shared = (dy, u_zx, c, cb, u_bd, st, conv_x, conv_bc, hp)
    out_far, out_own = run_pieces([yg], w_o, quarter, "branch_pieces", [], [], 5)
    out_arrived = lax.ppermute(out_far, "head", [(i, i ^ 2) for i in range(lax.axis_size("head"))])
    grad_o, grad_z = run_grads([(full_g, yg), (normed, dz)], "gate_grads", after=[out_far])
    grad_o, grad_z = pairs(grad_o), fours(grad_z)
    *back0, gx0, gb0, gh0, came_o, came_z = scan(0, *shared, (), [("half", "dp", 0), ("half", "dp", 1)], [grad_o, grad_z], 7)
    sent_out = run_home(me, arrange, [out_own, out_arrived], None, deep, "home_out", [back0[0]])
    got_out = lax.all_to_all(sent_out, "dp", split_axis=0, concat_axis=0, tiled=True)
    *back1, gx1, gb1, gh1 = scan(1, *shared, back0, [], [], 0, [sent_out])
    kept_z = keep(grad_z, came_z, 1)
    kept_o = keep(grad_o, came_o, 0).reshape(size // 4, 2, own_w, width)
    dux, dbd, rd_x = back1
    grad_x, grad_bd, came_z, came_o = run_grads(
        [(normed, dux), (normed, dbd)], "scan_grads", [("half", "dp", 0), ("half", "dp", 1)], [kept_z, kept_o], 8
    )
    kept_z, kept_o = keep(kept_z, came_z, 0), keep(kept_o, came_o, 1)
    grad_x, grad_bd = pairs(grad_x), pairs(grad_bd)
    gb = gb0 + gb1
    d_far, d_own, line_o, line_z, came_x2, got_rows, got_gb = run_pieces(
        [dz, dux, dbd],
        w_in,
        quarter,
        "input_pieces",
        [("direct", "dp", 2), ("direct", "dp", 2), ("half", "dp", 0), ("spread", "head"), ("spread", "head")],
        [kept_o, kept_z, grad_x, rd_z + rd_x, gb],
        9,
        [got_out],
    )
    kept_x = keep(grad_x, came_x2, 0)
    gb = gb[:5] + jnp.sum(got_gb, axis=0)[:5]
    gh = gh0 + gh1
    ends = jnp.concatenate([gb[3], gb[4]] + [gh[i, :32] for i in range(3)] + [jnp.zeros((width - 4 * N - 96,), F32)])
    small = jnp.concatenate([(gx0 + gx1)[:5], gg[:1], jnp.concatenate([gb[0], gb[1], gb[2]])[None], ends[None]], axis=0)
    d_arrived, line_x, got_small, grad_bd = run_last(
        [("whole", "head", 2), ("direct", "dp", 1), ("spread", "dp")], [d_far, kept_x, small], grad_bd, 10
    )

    sent_back = run_home(me, arrange, [d_own, d_arrived], [normed, inv_one, gain, rd_z, rd_x, got_rows], deep, "home_back")
    got_back = lax.all_to_all(sent_back, "dp", split_axis=0, concat_axis=0, tiled=True)
    final_out = (tokens.astype(F32) + got_out.astype(F32)).astype(BF16)
    final_back = (cotangent.astype(F32) + got_back.astype(F32)).astype(BF16)

    grad_out, grad_z = total(kept_o, line_o, 2), total(kept_z, line_z, 2)
    grad_x = total(kept_x, line_x, 1)
    small = small + jnp.sum(got_small, axis=0)
    grad_zx = jnp.stack([grad_z, grad_x], axis=1)
    of_gain = jnp.sum(grad_z * w_zx[:, 0].astype(F32), axis=1) + jnp.sum(grad_x * w_zx[:, 1].astype(F32), axis=1)
    of_gain = of_gain + jnp.sum(grad_bd[:, : 2 * N] * w_bc.astype(F32), axis=1)
    of_gain = of_gain + jnp.sum(grad_bd[:, 2 * N : 2 * N + heads] * w_dt.astype(F32), axis=1)
    last = jnp.concatenate([grad_bd[:, : 2 * N], jnp.broadcast_to(of_gain[:, None], (own_w, 128))], axis=1)
    others, = run_exchange([("spread", "head")], [last], 11)
    last = last + jnp.sum(others, axis=0)
    grad_gain = last[:, 2 * N] / norm_gain.astype(F32)
    gx, gg = small[0:5], small[5]
    gb = jnp.concatenate([small[6].reshape(3, 2 * N), small[7, : 4 * N].reshape(2, 2 * N)], axis=0)
    gh = small[7, 4 * N : 4 * N + 96].reshape(3, 32)[:, :heads]
    return (final_out, final_back, grad_gain, grad_zx, last[:, : 2 * N], grad_bd[:, 2 * N : 2 * N + heads], grad_out, gx, gb, gh, gg)


def solution(mesh):
    return jax.shard_map(
        body,
        mesh=mesh,
        in_specs=(
            P("dp", "head"),
            P("dp", "head"),
            P("dp", None),
            P("dp"),
            P("dp"),
            P("dp", None, "head"),
            P("dp", None),
            P("dp", "head"),
            P("dp", "head"),
            P(None, "head"),
            P(),
            P(None, "head"),
            P("head"),
        ),
        out_specs=(
            P("dp", "head"),
            P("dp", "head"),
            P("dp"),
            P("dp", None, "head"),
            P("dp", None),
            P("dp", "head"),
            P("dp", "head"),
            P(None, "head"),
            P(),
            P(None, "head"),
            P("head"),
        ),
        check_vma=False,
    )
```

```python
import functools

import jax
import jax.numpy as jnp
from jax import lax
from jax.experimental import pallas as pl
from jax.experimental.pallas import tpu as pltpu
from jax.sharding import PartitionSpec as P

LEN = 1024
T = 128
N = 128
HEAD = 64
EPS = 1e-05
NEG = -1e30
LIGHT = 1000
LIMIT = 60 * 1024 * 1024
AXES = ("dp", "head")
F32 = jnp.float32
BF16 = jnp.bfloat16


def dot(a, b):
    return lax.dot_general(a, b, (((1,), (0,)), ((), ())), preferred_element_type=F32)


def dot_nt(a, b):
    return lax.dot_general(a, b, (((1,), (1,)), ((), ())), preferred_element_type=F32)


def dot_exact(a, b):
    return lax.dot_general(
        a, b, (((1,), (0,)), ((), ())), preferred_element_type=F32, precision=lax.Precision.HIGHEST
    )


def iotas(rows, cols):
    return (
        lax.broadcasted_iota(jnp.int32, (rows, cols), 0),
        lax.broadcasted_iota(jnp.int32, (rows, cols), 1),
    )


MESH = pl.DeviceIdType.MESH


def greet(peers):
    barrier = pltpu.get_barrier_semaphore()
    for peer in peers:
        pl.semaphore_signal(barrier, inc=1, device_id=peer, device_id_type=MESH)
    pl.semaphore_wait(barrier, len(peers))


def place_of():
    return {name: lax.axis_index(name) for name in AXES}


def move_copies(move, src, dst):
    kind, axis = move[0], move[1]
    place = place_of()
    me = place[axis]

    def peer(flip):
        return tuple(place[name] ^ flip if name == axis else place[name] for name in AXES)

    if kind == "whole":
        return [(peer(move[2]), src, dst)], []
    if kind == "rows":
        return [(peer(move[2]), src.at[pl.ds(move[3], move[4])], dst)], []
    if kind == "half":
        return [(peer(1 << move[2]), src.at[:, 1 - ((me >> move[2]) & 1)], dst)], []
    if kind == "direct":
        high = me >> move[2]
        return [(peer(j << move[2]), src.at[high ^ j], dst.at[j - 1]) for j in range(1, dst.shape[0] + 1)], []
    if kind == "all":
        groups = lax.axis_size("head")
        flips = [divmod(flat, groups) for flat in range(1, dst.shape[0] + 1)]
        return [((place["dp"] ^ f, place["head"] ^ e), src, dst.at[i]) for i, (f, e) in enumerate(flips)], []
    if kind == "spread":
        return [(peer(flip), src, dst.at[flip - 1]) for flip in range(1, dst.shape[0] + 1)], []
    remote = [(peer(k), src.at[me ^ k], dst.at[me]) for k in turn_order(src.shape[0])]
    return remote, [(src.at[me], dst.at[me])]


def turn_order(size):
    return sorted(range(1, size), key=lambda k: (-(k & ~1), k & 1))


def move_shape(move, shape):
    kind = move[0]
    if kind == "rows":
        return (move[4],) + shape[1:]
    if kind == "half":
        return (shape[0],) + shape[2:]
    if kind == "direct":
        return (shape[0] - 1,) + shape[1:]
    if kind == "spread":
        return (lax.axis_size(move[1]) - 1,) + shape
    if kind == "all":
        return (lax.axis_size("dp") * lax.axis_size("head") - 1,) + shape
    return shape


def move_counts(moves, values):
    remote = local = 0
    for move, value in zip(moves, values):
        size = lax.axis_size(move[1])
        world = lax.axis_size("dp") * lax.axis_size("head")
        count = {"direct": value.shape[0] - 1, "spread": size - 1, "turn": size - 1, "all": world - 1}.get(move[0], 1)
        remote, local = remote + count, local + (move[0] == "turn")
    return remote, local


def move_scratch(moves, values):
    remote, local = move_counts(moves, values)
    return [pltpu.SemaphoreType.DMA((2, remote)), pltpu.SemaphoreType.DMA((max(local, 1),))] if moves else []


def move_outs(moves, values):
    return [jax.ShapeDtypeStruct(move_shape(move, value.shape), value.dtype) for move, value in zip(moves, values)]


def make_moves(moves, srcs, dsts, sems, local_sems):
    remote, local = [], []
    for move, src, dst in zip(moves, srcs, dsts):
        here, there = move_copies(move, src, dst)
        remote += here
        local += there
    copies = [
        pltpu.make_async_remote_copy(src_ref=a, dst_ref=b, send_sem=sems.at[0, i], recv_sem=sems.at[1, i], device_id=peer, device_id_type=MESH)
        for i, (peer, a, b) in enumerate(remote)
    ]
    copies += [pltpu.make_async_copy(a, b, local_sems.at[i]) for i, (a, b) in enumerate(local)]
    return move_peers(moves, dsts), copies


def move_peers(moves, dsts):
    flips = {}
    for move, dst in zip(moves, dsts):
        kind, axis = move[0], move[1]
        if kind in ("whole", "rows"):
            own = [move[2]]
        elif kind == "half":
            own = [1 << move[2]]
        elif kind == "direct":
            own = [j << move[2] for j in range(1, dst.shape[0] + 1)]
        elif kind == "all":
            groups = lax.axis_size("head")
            for flat in range(1, dst.shape[0] + 1):
                flips[divmod(flat, groups)] = None
            continue
        elif kind == "spread":
            own = range(1, dst.shape[0] + 1)
        else:
            own = range(1, dst.shape[0])
        for flip in own:
            flips[(flip, 0) if axis == "dp" else (0, flip)] = None
    place = place_of()
    return [(place["dp"] ^ f, place["head"] ^ e) for f, e in flips]


def background(first, last, moves, srcs, dsts, sems, local_sems):
    peers, copies = make_moves(moves, srcs, dsts, sems, local_sems)

    @pl.when(first)
    def _():
        greet(peers)
        for copy in copies:
            copy.start()

    @pl.when(last)
    def _():
        for copy in copies:
            copy.wait()


def exchange_kernel(moves, *refs):
    count = len(moves)
    peers, copies = make_moves(moves, refs[:count], refs[count : 2 * count], refs[2 * count], refs[2 * count + 1])
    greet(peers)
    for copy in copies:
        copy.start()
    for copy in copies:
        copy.wait()


def run_exchange(moves, values, number):
    return pl.pallas_call(
        functools.partial(exchange_kernel, tuple(moves)),
        in_specs=[pl.BlockSpec(memory_space=pl.ANY)] * len(moves),
        out_specs=[pl.BlockSpec(memory_space=pl.ANY)] * len(moves),
        out_shape=move_outs(moves, values),
        scratch_shapes=move_scratch(moves, values),
        compiler_params=pltpu.CompilerParams(collective_id=number, has_side_effects=True, vmem_limit_bytes=LIMIT),
        name="exchange",
    )(*values)


def sigmoid(v):
    return 1.0 / (1.0 + jnp.exp(-v))


def softplus(v):
    return jnp.maximum(v, 0.0) + jnp.log1p(jnp.exp(-jnp.abs(v)))


def to_col(row):
    return jnp.broadcast_to(row, (T, T)).T


def to_row(col):
    return jnp.broadcast_to(col, (T, T)).T[0:1]


def lanes(value, pick):
    return jnp.broadcast_to(value[:, pick : pick + 1], (value.shape[0], 128))


def step_terms(ubd, head_ref, heads):
    row, col = iotas(T, T)
    raw = jnp.where(col < heads, ubd[:, 2 * N :] + head_ref[0:1], 0.0)
    steps = jnp.where(col < heads, softplus(raw), 0.0)
    rates = -jnp.exp(head_ref[1:2])
    tril = (row >= col).astype(F32)
    logs = dot_exact(tril, steps * rates)
    return raw, steps, rates, logs


def weight_moves(step, steps, parts, whole, w_ref, fw_ref, across_sems, side_sems, local_sems, w_held):
    line = fw_ref.shape[0] // 2
    me, own = lax.axis_index("dp"), lax.axis_index("head")
    across, side = shard_spread(w_ref, fw_ref, across_sems, side_sems)
    if whole:
        into = pltpu.make_async_copy(w_ref, w_held, local_sems.at[0])
        held = pltpu.make_async_copy(w_held, fw_ref.at[me], local_sems.at[1])

    @pl.when(step == 0)
    def _():
        if whole:
            into.start()
        greet([(me ^ 1, own)] + [(me ^ (2 * j), own) for j in range(1, line)])
        for part in parts:
            side(part, 0).start()
        if whole:
            into.wait()
            held.start()

    for i, part in enumerate(parts):
        begin = i * steps // len(parts)

        @pl.when(step == begin)
        def _():
            for j in range(1, line):
                across(part, j).start()

        @pl.when(step == min(steps - 1, begin + steps // 3 + 2))
        def _():
            for j in range(1, line):
                across(part, j).wait_recv()
                side(part, j).start()

    @pl.when(step == steps - 1)
    def _():
        if whole:
            held.wait()
        for part in parts:
            for j in range(line):
                side(part, j).wait()
                if j:
                    across(part, j).wait_send()


def weight_scratch(size, w):
    sems = pltpu.SemaphoreType.DMA
    return [sems((2, PARTS, size // 2)), sems((2, PARTS, size // 2)), sems((2,)), pltpu.VMEM((PARTS, w.shape[0] // PARTS, w.shape[1]), BF16)]


def forward_kernel(heads, steps, x_ref, z_ref, ubd_ref, par_ref, pbc_ref, head_ref, w_ref, before_ref, y_ref, ss_ref, c_ref, cb_ref, st_ref, fw_ref, ext_x, ext_b, state, *sems):
    weight_moves(pl.program_id(0) * pl.num_programs(1) + pl.program_id(1), steps, range(1, PARTS), False, w_ref, fw_ref, *sems)

    @pl.when(pl.program_id(1) == 0)
    def _():
        ext_x[0:8] = jnp.zeros_like(ext_x[0:8])
        ext_b[0:8] = jnp.zeros_like(ext_b[0:8])
        state[...] = jnp.zeros_like(state)

    def conv(ext, values, taps):
        ext[8 : 8 + T] = values
        total = taps[4:5] + taps[3:4] * values
        for k in range(3):
            total = total + taps[k : k + 1] * ext[5 + k : 5 + k + T]
        ext[0:8] = ext[T : T + 8]
        return total

    row, col = iotas(T, T)
    low = col < HEAD
    low_row = lax.broadcasted_iota(jnp.int32, (1, 128), 1) < HEAD
    causal = row >= col
    ubd = ubd_ref[...]
    c = conv(ext_x, x_ref[...].astype(F32), par_ref)
    c_ref[...] = c.astype(BF16)
    cb = conv(ext_b, ubd[:, : 2 * N], pbc_ref)
    cb_ref[...] = cb
    bc = cb * sigmoid(cb)
    b_rows = bc[:, :N]
    b_t = b_rows.T.astype(BF16)
    b_low, c_low = b_rows.astype(BF16), bc[:, N:].astype(BF16)
    _, steps, _, logs = step_terms(ubd, head_ref, heads)
    logs_t = logs.T
    scores = dot_nt(c_low, b_low)
    entering = state[...].astype(BF16)
    st_ref[0] = entering
    outer = dot(c_low, entering)
    squares = jnp.zeros((T, 128), F32)
    for pair in range(heads // 2):
        span = slice(128 * pair, 128 * pair + 128)
        h0, h1 = 2 * pair, 2 * pair + 1
        log0, log1 = lanes(logs, h0), lanes(logs, h1)
        log_pair = jnp.where(low, log0, log1)
        step_pair = jnp.where(low, lanes(steps, h0), lanes(steps, h1))
        last_pair = log_pair[T - 1 : T]
        skip_pair = jnp.where(low_row, lanes(head_ref[2:3], h0), lanes(head_ref[2:3], h1))
        cp = c[:, span]
        xp = cp * sigmoid(cp)
        xd = xp * step_pair
        m0 = (scores * jnp.exp(jnp.where(causal, log0 - logs_t[h0 : h0 + 1], NEG))).astype(BF16)
        m1 = (scores * jnp.exp(jnp.where(causal, log1 - logs_t[h1 : h1 + 1], NEG))).astype(BF16)
        stacked = jnp.concatenate([jnp.where(low, xd, 0.0).astype(BF16), jnp.where(low, 0.0, xd).astype(BF16)], axis=0)
        y = dot(jnp.concatenate([m0, m1], axis=1), stacked)
        y = y + jnp.exp(log_pair) * outer[:, span] + skip_pair * xp
        tail = (jnp.exp(last_pair - log_pair) * xd).astype(BF16)
        state[:, span] = jnp.exp(last_pair) * state[:, span] + dot(b_t, tail)
        y_ref[:, span] = y.astype(BF16)
        zp = z_ref[:, span].astype(F32)
        w = y * zp * sigmoid(zp)
        squares = squares + w * w
    ss_ref[0] = to_row(jnp.sum(squares, axis=1, keepdims=True))


def project_kernel(heads, steps, x_ref, w_ref, shard_ref, out_ref, inv_ref, uzx_ref, ubd_ref, gain_ref, fw_ref, *sems):
    deep, width = x_ref.shape[1], 2 * heads * HEAD
    weight_moves(pl.program_id(0), steps, range(1), True, shard_ref, fw_ref, *sems)

    @pl.when(pl.program_id(0) == 0)
    def _():
        for j in range(deep // T):
            span = slice(j * T, j * T + T)
            gain_ref[:, span] = jnp.broadcast_to(w_ref[span, width + 2 * N : width + 3 * N].astype(F32).T[heads : heads + 1], (8, T))

    x = x_ref[...].astype(F32)
    inv = lax.rsqrt(jnp.sum(x * x, axis=1, keepdims=True) / deep + EPS)
    normed = (x * inv * gain_ref[0:1]).astype(BF16)
    out_ref[...] = normed
    for part in range(x.shape[0] // T):
        inv_ref[part] = to_row(inv[part * T : part * T + T])
    uzx_ref[...] = dot(normed, w_ref[:, :width]).astype(BF16)
    ubd_ref[...] = dot(normed, w_ref[:, width:])


def gate_kernel(g_ref, wo_ref, y_ref, z_ref, par_ref, mask_ref, dyn_ref, co_ref):
    dyn = dot(g_ref[...], wo_ref[...])
    for part in range(dyn.shape[0] // T):
        rows = slice(part * T, part * T + T)
        mask = to_col(mask_ref[part])[:, 0:1]
        own = dyn[rows] * mask
        dyn_ref[rows] = own.astype(BF16)
        z = z_ref[rows].astype(F32)
        w = y_ref[rows].astype(F32) * z * sigmoid(z)
        co_ref[part] = to_row(jnp.sum(own * w * par_ref[0:1], axis=1, keepdims=True))


def home_kernel(last, deep, me_ref, order_ref, a_ref, b_ref, *refs):
    out_ref, held_ref = refs[-2:]
    step = pl.program_id(0)
    many = held_ref.shape[0] // a_ref.shape[0]
    size = a_ref.shape[0]

    @pl.when(step < many)
    def _():
        value = a_ref[...].astype(F32) + b_ref[...].astype(F32)
        if last:
            normed_ref, inv_ref, gain_ref, rdz_ref, rdx_ref, more_ref = refs[:6]
            gain = gain_ref[0:1]
            hat = normed_ref[...].astype(F32) / gain
            parts = []
            for part in range(size // T):
                inv_row = inv_ref[part]
                dots = rdz_ref[part] + rdx_ref[part] + more_ref[0, part] + more_ref[1, part] + more_ref[2, part]
                rows = slice(part * T, part * T + T)
                inv = to_col(inv_row)[:, 0:1]
                mean = to_col(dots / deep)[:, 0:1]
                parts.append(inv * (gain * value[rows] - hat[rows] * mean))
            value = jnp.concatenate(parts, axis=0)
        held_ref[pl.ds(pl.multiple_of(step * size, size), size), :] = value.astype(BF16)

    @pl.when(step >= many)
    def _():
        base = ((step - many) * size).astype(F32)
        row = lax.broadcasted_iota(jnp.int32, (size, T), 0).astype(F32) + base
        picks = jnp.concatenate([(row == order_ref[j]).astype(F32).astype(BF16) for j in range(order_ref.shape[0])], axis=1)
        out_ref[...] = dot(picks, held_ref[...]).astype(BF16)


def mid_kernel(width, moves, y_ref, z_ref, dyn_ref, par_ref, mask_ref, ss_ref, co_ref, yg_ref, dz_ref, dy_ref, gg_ref, rd_ref, got_ss, got_co, sems, local_sems):
    step = pl.program_id(0)

    @pl.when(step == 0)
    def _():
        gg_ref[...] = jnp.zeros_like(gg_ref)
        peers, copies = make_moves(moves, (ss_ref, co_ref), (got_ss, got_co), sems, local_sems)
        greet(peers)
        for copy in copies:
            copy.start()
        for copy in copies:
            copy.wait()

    gain = par_ref[0:1]
    parts = y_ref.shape[0] // T
    for part in range(parts):
        rows = slice(part * T, part * T + T)
        here = step * parts + part
        ss, co = ss_ref[here], co_ref[here]
        for other in range(got_ss.shape[0]):
            ss, co = ss + got_ss[other, here], co + got_co[other, here]
        mask = to_col(mask_ref[part])[:, 0:1]
        inv_row = lax.rsqrt(ss / width + EPS)
        inv = to_col(inv_row)[:, 0:1]
        cube = to_col(inv_row * inv_row * inv_row * (co / width))[:, 0:1]
        y = y_ref[rows].astype(F32)
        z = z_ref[rows].astype(F32)
        dyn = dyn_ref[rows].astype(F32)
        s = sigmoid(z)
        act = z * s
        w = y * act
        wi = w * inv
        yg_ref[rows] = (wi * gain * mask).astype(BF16)
        gg_ref[0:1] += jnp.sum(dyn * wi, axis=0, keepdims=True)
        dw = inv * gain * dyn - w * cube
        dy_ref[rows] = (dw * act).astype(BF16)
        dz = dw * y * (s * (1.0 + z * (1.0 - s)))
        dz_ref[rows] = dz.astype(BF16)
        rd_ref[part] = to_row(jnp.sum(dz * z, axis=1, keepdims=True))


def backward_kernel(heads, extra, moves, dy_ref, x_ref, c_ref, cb_ref, ubd_ref, st_ref, par_ref, pbc_ref, head_ref, *refs):
    count = len(moves)
    srcs, refs = refs[:count], refs[count + extra :]
    dx_ref, dbd_ref, rd_ref, gx_ref, gb_ref, gh_ref = refs[:6]
    dsts, refs = refs[6 : 6 + count], refs[6 + count :]
    d_state, ext_x, ext_b, rows_ref, prod, edy_ref, tail_ref = refs[:7]
    if moves:
        began = (pl.program_id(0) == 0) & (pl.program_id(1) == 0)
        ended = (pl.program_id(0) == pl.num_programs(0) - 1) & (pl.program_id(1) == pl.num_programs(1) - 1)
        background(began, ended, moves, srcs, dsts, *refs[7:])
    first = (pl.program_id(0) == 0) & (pl.program_id(1) == 0)

    @pl.when(first)
    def _():
        gx_ref[...] = jnp.zeros_like(gx_ref)
        gb_ref[...] = jnp.zeros_like(gb_ref)
        gh_ref[...] = jnp.zeros_like(gh_ref)
        rows_ref[...] = jnp.zeros_like(rows_ref)

    @pl.when(pl.program_id(1) == 0)
    def _():
        ext_x[T : T + 8] = jnp.zeros_like(ext_x[T : T + 8])
        ext_b[T : T + 8] = jnp.zeros_like(ext_b[T : T + 8])
        d_state[...] = jnp.zeros_like(d_state)

    row, col = iotas(T, T)
    low = col < HEAD
    low_row = lax.broadcasted_iota(jnp.int32, (1, 128), 1) < HEAD
    upto = col >= row
    below = row < col
    reach = (row >= col).astype(BF16)
    ubd = ubd_ref[...]
    raw, steps, rates, logs = step_terms(ubd, head_ref, heads)
    logs_t = logs.T
    cb = cb_ref[...]
    sb = sigmoid(cb)
    bc = cb * sb
    b_low, c_low = bc[:, :N].astype(BF16), bc[:, N:].astype(BF16)
    c_t = bc[:, N:].T.astype(BF16)
    scores = dot_nt(b_low, c_low)
    entering = st_ref[0]
    outer = dot(c_low, entering)
    ds_low = d_state[...].astype(BF16)
    back = dot(b_low, ds_low)
    d_scores = jnp.zeros((T, T), F32)
    skip_parts, closing_parts = [], []
    for pair in range(heads // 2):
        span = slice(128 * pair, 128 * pair + 128)
        h0, h1 = 2 * pair, 2 * pair + 1
        log0, log1 = lanes(logs, h0), lanes(logs, h1)
        log_pair = jnp.where(low, log0, log1)
        step_pair = jnp.where(low, lanes(steps, h0), lanes(steps, h1))
        last_pair = log_pair[T - 1 : T]
        skip_pair = jnp.where(low_row, lanes(head_ref[2:3], h0), lanes(head_ref[2:3], h1))
        cp = c_ref[:, span].astype(F32)
        sp = sigmoid(cp)
        xp = cp * sp
        xd = xp * step_pair
        dy_low = dy_ref[:, span]
        dy = dy_low.astype(F32)
        decay0 = jnp.exp(jnp.where(upto, logs_t[h0 : h0 + 1] - log0, NEG))
        decay1 = jnp.exp(jnp.where(upto, logs_t[h1 : h1 + 1] - log1, NEG))
        m0, m1 = scores * decay0, scores * decay1
        zero = jnp.zeros_like(dy_low)
        x_stack = jnp.concatenate([jnp.where(low, xd, 0.0).astype(BF16), jnp.where(low, 0.0, xd).astype(BF16)], axis=0)
        dm = dot_nt(x_stack, dy_low)
        dm0, dm1 = dm[:T], dm[T:]
        d_scores = d_scores + dm0 * decay0 + dm1 * decay1
        dy_stack = jnp.concatenate([jnp.where(low, dy, 0.0).astype(BF16), jnp.where(low, 0.0, dy).astype(BF16)], axis=0)
        dxd = dot(jnp.concatenate([m0.astype(BF16), m1.astype(BF16)], axis=1), dy_stack)
        flow = jnp.concatenate([(dm0 * m0).astype(BF16), (dm1 * m1).astype(BF16)], axis=0)
        later = dot(flow, reach)
        rows_ref[h0 : h0 + 1] = jnp.sum(jnp.where(below, later[:T], 0.0), axis=0, keepdims=True)
        rows_ref[h1 : h1 + 1] = jnp.sum(jnp.where(below, later[T:], 0.0), axis=0, keepdims=True)
        grow = jnp.exp(log_pair)
        tail = jnp.exp(last_pair - log_pair)
        from_state = tail * back[:, span]
        dxd = dxd + from_state
        edy = grow * dy
        prod[0:T, span] = (edy * outer[:, span]).astype(BF16)
        prod[T : 2 * T, span] = (from_state * xd).astype(BF16)
        prod[2 * T : 3 * T, span] = (xp * dxd).astype(BF16)
        skip_parts.append(jnp.sum(xp * dy, axis=0, keepdims=True))
        edy_low = edy.astype(BF16)
        edy_ref[:, span] = edy_low
        tail_ref[:, span] = (tail * xd).astype(BF16)
        old = d_state[:, span]
        closing = jnp.exp(last_pair)
        closing_parts.append(closing * jnp.sum(old * entering[:, span].astype(F32), axis=0, keepdims=True))
        d_state[:, span] = closing * old + dot(c_t, edy_low)
        dx = dxd * step_pair + skip_pair * dy
        ext_x[0:T, span] = dx * (sp * (1.0 + cp * (1.0 - sp)))
    d_low = d_scores.astype(BF16)
    d_b = dot_nt(tail_ref[...], ds_low) + dot(d_low, c_low)
    d_c = dot_nt(edy_ref[...], entering) + dot(d_scores.T.astype(BF16), b_low)
    width = heads * HEAD
    lane_row, lane_col = iotas(width, 128)
    member = (lane_row // HEAD == lane_col).astype(BF16)
    sums = dot(prod[...], member)
    skip_all = jnp.concatenate(skip_parts, axis=1)
    closing_all = jnp.concatenate(closing_parts, axis=1)
    fill = jnp.zeros((6, width), F32)
    few = dot_exact(jnp.concatenate([skip_all, closing_all, fill], axis=0), member.astype(F32))
    d_logs = dot(upto.astype(BF16), sums[:T].astype(BF16)) + dot((col < row).astype(BF16), sums[T : 2 * T].astype(BF16))
    d_logs = d_logs + rows_ref[...].T + few[1:2]
    d_steps = sums[2 * T :] + rates * d_logs
    d_raw = jnp.where(col < heads, d_steps * sigmoid(raw), 0.0)
    gh_ref[0:1] += jnp.sum(d_raw, axis=0, keepdims=True)
    gh_ref[1:2] += rates * jnp.sum(steps * d_logs, axis=0, keepdims=True)
    gh_ref[2:3] += few[0:1]
    ext_b[0:T, 0:N] = d_b * (sb[:, :N] * (1.0 + cb[:, :N] * (1.0 - sb[:, :N])))
    ext_b[0:T, N:] = d_c * (sb[:, N:] * (1.0 + cb[:, N:] * (1.0 - sb[:, N:])))

    def conv_back(ext, values, taps, grads):
        now = ext[0:T]
        total = taps[3:4] * now
        grads[3:4] += jnp.sum(values * now, axis=0, keepdims=True)
        grads[4:5] += jnp.sum(now, axis=0, keepdims=True)
        for k in range(3):
            moved = ext[3 - k : 3 - k + T]
            total = total + taps[k : k + 1] * moved
            grads[k : k + 1] += jnp.sum(values * moved, axis=0, keepdims=True)
        ext[T : T + 8] = ext[0:8]
        return total

    ux = x_ref[...].astype(F32)
    dux = conv_back(ext_x, ux, par_ref, gx_ref)
    dx_ref[...] = dux.astype(BF16)
    ubc = ubd[:, : 2 * N]
    dubc = conv_back(ext_b, ubc, pbc_ref, gb_ref)
    dbd_ref[:, : 2 * N] = dubc.astype(BF16)
    dbd_ref[:, 2 * N :] = d_raw.astype(BF16)
    total = jnp.sum(dux * ux, axis=1, keepdims=True) + jnp.sum(dubc * ubc, axis=1, keepdims=True)
    total = total + jnp.sum(jnp.where(col < heads, d_raw * ubd[:, 2 * N :], 0.0), axis=1, keepdims=True)
    rd_ref[0] = to_row(total)


def params(*semantics, number=0):
    if number:
        return pltpu.CompilerParams(
            dimension_semantics=semantics, vmem_limit_bytes=LIMIT, collective_id=number, has_side_effects=True
        )
    return pltpu.CompilerParams(dimension_semantics=semantics, vmem_limit_bytes=LIMIT)


def run_forward(heads, u_zx, u_bd, par, pbc, hp, w_out, before, number):
    rows, width = u_zx.shape[0], heads * HEAD
    slots, chunks = rows // LEN, LEN // T
    at = lambda s, i: (s * chunks + i, 0)
    fixed = lambda s, i: (0, 0)
    size = lax.axis_size("dp")
    anywhere = pl.BlockSpec(memory_space=pl.ANY)
    return pl.pallas_call(
        functools.partial(forward_kernel, heads, slots * chunks),
        grid=(slots, chunks),
        in_specs=[
            pl.BlockSpec((T, width), lambda s, i: (s * chunks + i, 1)),
            pl.BlockSpec((T, width), at),
            pl.BlockSpec((T, 3 * N), at),
            pl.BlockSpec((5, width), fixed),
            pl.BlockSpec((5, 2 * N), fixed),
            pl.BlockSpec((8, 128), fixed),
            anywhere,
            anywhere,
        ],
        out_specs=[
            pl.BlockSpec((T, width), at),
            pl.BlockSpec((1, 1, T), lambda s, i: (s * chunks + i, 0, 0)),
            pl.BlockSpec((T, width), at),
            pl.BlockSpec((T, 2 * N), at),
            pl.BlockSpec((1, N, width), lambda s, i: (s * chunks + i, 0, 0)),
            anywhere,
        ],
        out_shape=[
            jax.ShapeDtypeStruct((rows, width), BF16),
            jax.ShapeDtypeStruct((rows // T, 1, T), F32),
            jax.ShapeDtypeStruct((rows, width), BF16),
            jax.ShapeDtypeStruct((rows, 2 * N), F32),
            jax.ShapeDtypeStruct((rows // T, N, width), BF16),
            full_shape(size, w_out),
        ],
        scratch_shapes=[
            pltpu.VMEM((T + 8, width), F32),
            pltpu.VMEM((T + 8, 2 * N), F32),
            pltpu.VMEM((N, width), F32),
        ]
        + weight_scratch(size, w_out),
        input_output_aliases={7: 5},
        compiler_params=params("arbitrary", "arbitrary", number=number),
        cost_estimate=pl.CostEstimate(flops=rows * width * 2 * 1200, bytes_accessed=rows * width * 8, transcendentals=rows * width * 6),
        name="scan_forward",
    )(u_zx, u_zx, u_bd, par, pbc, hp, cut_shard(w_out), before)


def run_project(heads, x, w_in, w_out, number):
    rows, deep = x.shape
    wide = w_in.shape[1]
    width = 2 * heads * HEAD
    size = lax.axis_size("dp")
    step = 256
    at = lambda i: (i, 0)
    fixed = lambda i: (0, 0)
    anywhere = pl.BlockSpec(memory_space=pl.ANY)
    thin = pl.BlockSpec((step // T, 1, T), lambda i: (i, 0, 0))
    return pl.pallas_call(
        functools.partial(project_kernel, heads, rows // step),
        grid=(rows // step,),
        in_specs=[pl.BlockSpec((step, deep), at), pl.BlockSpec((deep, wide), fixed), anywhere],
        out_specs=[
            pl.BlockSpec((step, deep), at),
            thin,
            pl.BlockSpec((step, width), at),
            pl.BlockSpec((step, wide - width), at),
            pl.BlockSpec((8, deep), fixed),
            anywhere,
        ],
        out_shape=[
            jax.ShapeDtypeStruct((rows, deep), BF16),
            jax.ShapeDtypeStruct((rows // T, 1, T), F32),
            jax.ShapeDtypeStruct((rows, width), BF16),
            jax.ShapeDtypeStruct((rows, wide - width), F32),
            jax.ShapeDtypeStruct((8, deep), F32),
            full_shape(size, w_out),
        ],
        scratch_shapes=weight_scratch(size, w_out),
        compiler_params=params("arbitrary", number=number),
        cost_estimate=pl.CostEstimate(flops=LIGHT, bytes_accessed=LIGHT, transcendentals=0),
        name="project",
    )(x, w_in, cut_shard(w_out))


def run_gate(grads, w_out, y, u_zx, par, mask):
    rows, width = y.shape
    deep = grads.shape[1]
    step = 256
    at = lambda i: (i, 0)
    fixed = lambda i: (0, 0)
    thin = pl.BlockSpec((step // T, 1, T), lambda i: (i, 0, 0))
    return pl.pallas_call(
        gate_kernel,
        grid=(rows // step,),
        in_specs=[
            pl.BlockSpec((step, deep), at),
            pl.BlockSpec((deep, width), fixed),
            pl.BlockSpec((step, width), at),
            pl.BlockSpec((step, width), at),
            pl.BlockSpec((1, width), fixed),
            thin,
        ],
        out_specs=[pl.BlockSpec((step, width), at), thin],
        out_shape=[jax.ShapeDtypeStruct((rows, width), BF16), jax.ShapeDtypeStruct((rows // T, 1, T), F32)],
        compiler_params=params("arbitrary"),
        cost_estimate=pl.CostEstimate(flops=rows * deep * width * 2, bytes_accessed=rows * deep * 2 + rows * width * 6, transcendentals=rows * width),
        name="gate_back",
    )(grads, w_out, y, u_zx, par, mask)


def run_home(me, order, sums, extra, deep, name, after=()):
    rows, quarter = sums[0].shape
    step = 512
    many = rows // step
    into = lambda i, m: (jnp.minimum(i, many - 1), 0)
    thin = pl.BlockSpec((step // T, 1, T), lambda i, m: (jnp.minimum(i, many - 1), 0, 0))
    specs = [pl.BlockSpec((rows // T, 1, T), lambda i, m: (0, 0, 0))] + [pl.BlockSpec((step, quarter), into)] * 2
    values = list(sums)
    if extra is not None:
        specs += [pl.BlockSpec((step, quarter), lambda i, m: (jnp.minimum(i, many - 1), m[0])), thin]
        specs += [pl.BlockSpec((8, quarter), lambda i, m: (0, m[0])), thin, thin]
        specs += [pl.BlockSpec((3, step // T, 1, T), lambda i, m: (0, jnp.minimum(i, many - 1), 0, 0))]
        values += list(extra)
    values += list(after)
    specs += [pl.BlockSpec(memory_space=pl.ANY)] * len(after)
    return pl.pallas_call(
        functools.partial(home_kernel, extra is not None, float(deep)),
        grid_spec=pltpu.PrefetchScalarGridSpec(
            num_scalar_prefetch=1,
            grid=(2 * many,),
            in_specs=specs,
            out_specs=pl.BlockSpec((step, quarter), lambda i, m: (jnp.maximum(i - many, 0), 0)),
            scratch_shapes=[pltpu.VMEM((rows, quarter), BF16)],
        ),
        out_shape=jax.ShapeDtypeStruct((rows, quarter), BF16),
        compiler_params=params("arbitrary"),
        cost_estimate=pl.CostEstimate(flops=rows * rows * quarter * 2, bytes_accessed=rows * quarter * 10, transcendentals=0),
        name=name,
    )(me, order, *values)


def run_mid(all_width, y, u_zx, dyn, par, mask, ss, co, number):
    rows, width = y.shape
    step = 256
    at = lambda i: (i, 0)
    fixed = lambda i: (0, 0)
    thin = pl.BlockSpec((step // T, 1, T), lambda i: (i, 0, 0))
    whole = pl.BlockSpec((rows // T, 1, T), lambda i: (0, 0, 0))
    wide = pl.BlockSpec((step, width), at)
    moves = (("spread", "head"), ("spread", "head"))
    others = lax.axis_size("head") - 1
    return pl.pallas_call(
        functools.partial(mid_kernel, float(all_width), moves),
        grid=(rows // step,),
        in_specs=[wide, wide, wide, pl.BlockSpec((1, width), fixed), thin, whole, whole],
        out_specs=[wide, wide, wide, pl.BlockSpec((8, width), fixed), thin],
        out_shape=[jax.ShapeDtypeStruct((rows, width), BF16)] * 3
        + [jax.ShapeDtypeStruct((8, width), F32), jax.ShapeDtypeStruct((rows // T, 1, T), F32)],
        scratch_shapes=[pltpu.VMEM((others, rows // T, 1, T), F32)] * 2 + move_scratch(moves, (ss, co)),
        compiler_params=params("arbitrary", number=number),
        cost_estimate=pl.CostEstimate(flops=rows * width * 30, bytes_accessed=rows * width * 12, transcendentals=rows * width),
        name="gate_mid",
    )(y, u_zx, dyn, par, mask, ss, co)


def run_backward(heads, slot, dy, u_zx, c, cb, u_bd, st, par, pbc, hp, before, moves, values, number, after=()):
    rows, width = dy.shape
    chunks = LEN // T
    place = lambda s, i: slot * chunks + chunks - 1 - i
    at = lambda s, i: (place(s, i), 0)
    at3 = lambda s, i: (place(s, i), 0, 0)
    fixed = lambda s, i: (0, 0)
    anywhere = pl.BlockSpec(memory_space=pl.ANY)
    return pl.pallas_call(
        functools.partial(backward_kernel, heads, len(before) + len(after), tuple(moves)),
        grid=(1, chunks),
        in_specs=[
            pl.BlockSpec((T, width), at),
            pl.BlockSpec((T, width), lambda s, i: (place(s, i), 1)),
            pl.BlockSpec((T, width), at),
            pl.BlockSpec((T, 2 * N), at),
            pl.BlockSpec((T, 3 * N), at),
            pl.BlockSpec((1, N, width), at3),
            pl.BlockSpec((5, width), fixed),
            pl.BlockSpec((5, 2 * N), fixed),
            pl.BlockSpec((8, 128), fixed),
        ]
        + [anywhere] * (len(moves) + len(before) + len(after)),
        out_specs=[
            pl.BlockSpec((T, width), at),
            pl.BlockSpec((T, 3 * N), at),
            pl.BlockSpec((1, 1, T), at3),
            pl.BlockSpec((8, width), fixed),
            pl.BlockSpec((8, 2 * N), fixed),
            pl.BlockSpec((8, 128), fixed),
        ]
        + [anywhere] * len(moves),
        out_shape=[
            jax.ShapeDtypeStruct((rows, width), BF16),
            jax.ShapeDtypeStruct((rows, 3 * N), BF16),
            jax.ShapeDtypeStruct((rows // T, 1, T), F32),
            jax.ShapeDtypeStruct((8, width), F32),
            jax.ShapeDtypeStruct((8, 2 * N), F32),
            jax.ShapeDtypeStruct((8, 128), F32),
        ]
        + move_outs(moves, values),
        scratch_shapes=[
            pltpu.VMEM((N, width), F32),
            pltpu.VMEM((T + 8, width), F32),
            pltpu.VMEM((T + 8, 2 * N), F32),
            pltpu.VMEM((128, 128), F32),
            pltpu.VMEM((3 * T, width), BF16),
            pltpu.VMEM((T, width), BF16),
            pltpu.VMEM((T, width), BF16),
        ]
        + move_scratch(moves, values),
        input_output_aliases={9 + len(moves) + i: i for i in range(len(before))},
        compiler_params=params("arbitrary", "arbitrary", number=number),
        cost_estimate=pl.CostEstimate(flops=LIGHT, bytes_accessed=LIGHT, transcendentals=0),
        name="scan_backward",
    )(dy, u_zx, c, cb, u_bd, st, par, pbc, hp, *values, *before, *after)


def pieces_kernel(count, many, moves, extra, *refs):
    total = len(moves)
    values, weight_ref, srcs = refs[:count], refs[count], refs[count + 1 : count + 1 + total]
    refs = refs[count + 1 + total + extra :]
    far_ref, own_ref = refs[:2]
    dsts, refs = refs[2 : 2 + total], refs[2 + total :]
    sent_ref, came_ref, near_sems, joined_ref = refs[:4]
    step = pl.program_id(0)
    rows, quarter = far_ref.shape
    start = 0
    for value in values:
        joined_ref[:, start : start + value.shape[1]] = value[...]
        start += value.shape[1]
    dp, own = lax.axis_index("dp"), lax.axis_index("head")
    near = (dp, own ^ 1)
    peers, copies = make_moves(moves, srcs, dsts, *refs[4:]) if moves else ([], [])

    @pl.when(step == 0)
    def _():
        greet(peers if near_in(moves) else [near] + peers)
        for copy in copies:
            copy.start()

    def product(k):
        at = pl.ds(pl.multiple_of((own ^ k) * quarter, 128), quarter)
        return dot_nt(joined_ref[...], weight_ref[at, :])

    def near_copy(block):
        return pltpu.make_async_remote_copy(
            src_ref=sent_ref.at[block],
            dst_ref=came_ref.at[block],
            send_sem=near_sems.at[0, block],
            recv_sem=near_sems.at[1, block],
            device_id=near,
            device_id_type=MESH,
        )

    @pl.when(step < many)
    def _():
        sent_ref[step, :, :quarter] = product(3).astype(BF16)
        sent_ref[step, :, quarter:] = product(1).astype(BF16)
        near_copy(step).start()

    @pl.when(step >= many)
    def _():
        block = step - many
        far, mine = product(2), product(0)
        near_copy(block).wait_recv()
        far_ref[...] = (far + came_ref[block, :, :quarter].astype(F32)).astype(BF16)
        own_ref[...] = (mine + came_ref[block, :, quarter:].astype(F32)).astype(BF16)

    @pl.when(step == 2 * many - 1)
    def _():
        for block in range(many):
            near_copy(block).wait_send()
        for copy in copies:
            copy.wait()


def near_in(moves):
    return any(move[0] == "spread" and move[1] == "head" for move in moves)


def run_pieces(values, weight, quarter, name, moves, moved, number, after=()):
    rows = values[0].shape[0]
    step = 512
    many = rows // step
    anywhere = pl.BlockSpec(memory_space=pl.ANY)
    specs = [pl.BlockSpec((step, v.shape[1]), lambda i: (lax.rem(i, many), 0)) for v in values]
    specs.append(pl.BlockSpec(weight.shape, lambda i: (0, 0)))
    return pl.pallas_call(
        functools.partial(pieces_kernel, len(values), many, tuple(moves), len(after)),
        grid=(2 * many,),
        in_specs=specs + [anywhere] * (len(moves) + len(after)),
        out_specs=[pl.BlockSpec((step, quarter), lambda i: (jnp.maximum(i - many, 0), 0))] * 2 + [anywhere] * len(moves),
        out_shape=[jax.ShapeDtypeStruct((rows, quarter), BF16)] * 2 + move_outs(moves, moved),
        scratch_shapes=[pltpu.VMEM((many, step, 2 * quarter), BF16)] * 2 + [pltpu.SemaphoreType.DMA((2, many)), pltpu.VMEM((step, weight.shape[1]), BF16)] + move_scratch(moves, moved),
        compiler_params=params("arbitrary", number=number),
        cost_estimate=pl.CostEstimate(flops=LIGHT, bytes_accessed=LIGHT, transcendentals=0),
        name=name,
    )(*values, weight, *moved, *after)


def second_bits(step, last, paired, came, kept, holds, halves, quarters, bit_sems, load_sems):
    me, head = lax.axis_index("dp"), lax.axis_index("head")
    side, mid = me & 1, (me >> 1) & 1
    own = [paired[0].at[:, :, side], paired[1].at[:, mid]]
    loads = [pltpu.make_async_copy(own[i], holds[i], load_sems.at[0, i]) for i in range(2)]
    loads += [pltpu.make_async_copy(came[i], halves[i], load_sems.at[1, i]) for i in range(2)]
    picks, peers = (mid, side), ((me ^ 2, head), (me ^ 1, head))
    sends = [
        pltpu.make_async_remote_copy(
            src_ref=holds[i].at[:, 1 - picks[i]],
            dst_ref=quarters[i],
            send_sem=bit_sems.at[0, i],
            recv_sem=bit_sems.at[1, i],
            device_id=peers[i],
            device_id_type=MESH,
        )
        for i in range(2)
    ]

    @pl.when(step == 0)
    def _():
        for copy in loads:
            copy.start()
        greet(peers)
        for copy in loads:
            copy.wait()
        for i in range(2):
            for j in range(holds[i].shape[0]):
                for k in range(2):
                    holds[i][j, k] = (holds[i][j, k].astype(F32) + halves[i][j, k].astype(F32)).astype(BF16)
            sends[i].start()

    @pl.when(step == last)
    def _():
        for i in range(2):
            sends[i].wait()
            for j in range(holds[i].shape[0]):
                kept[i][j] = (holds[i][j, picks[i]].astype(F32) + quarters[i][j].astype(F32)).astype(BF16)


def grads_kernel(count, parts, extra, reduce, *refs):
    lefts, rights = refs[:count], refs[count : 2 * count]
    paired, came = refs[2 * count : 2 * count + 2], refs[2 * count + 2 : 2 * count + 4]
    refs = refs[2 * count + extra + (4 if reduce else 0) :]
    outs, refs = refs[:count], refs[count:]
    step = pl.program_id(0)
    if reduce:
        second_bits(step, count * parts - 1, paired, came, refs[0:2], refs[2:4], refs[4:6], refs[6:8], refs[8], refs[9])
    for which in range(count):

        @pl.when((step >= which * parts) & (step < (which + 1) * parts))
        def _():
            out = lax.dot_general(lefts[which][...], rights[which][...], (((0,), (0,)), ((), ())), preferred_element_type=F32)
            outs[which][...] = out.astype(BF16)


def run_grads(pairs, name, paired=(), came=(), number=0, after=()):
    rows, deep = pairs[0][0].shape
    step = 512
    parts = deep // step
    count = len(pairs)
    anywhere = pl.BlockSpec(memory_space=pl.ANY)
    into = lambda which: lambda i: jnp.clip(i - which * parts, 0, parts - 1)
    specs = [pl.BlockSpec((rows, step), lambda i, at=into(w): (0, at(i))) for w in range(count)]
    specs += [pl.BlockSpec(right.shape, lambda i: (0, 0)) for _, right in pairs]
    kept = [(p.shape[0], p.shape[3], p.shape[4]) for p in paired]
    twice = [pltpu.VMEM((m, 2, r, c), BF16) for m, r, c in kept]
    sems = pltpu.SemaphoreType.DMA
    return pl.pallas_call(
        functools.partial(grads_kernel, count, parts, len(after), bool(paired)),
        grid=(count * parts,),
        in_specs=specs + [anywhere] * (len(paired) + len(came) + len(after)),
        out_specs=[pl.BlockSpec((step, right.shape[1]), lambda i, at=into(w): (at(i), 0)) for w, (_, right) in enumerate(pairs)]
        + [pl.BlockSpec(shape, lambda i: (0, 0, 0)) for shape in kept],
        out_shape=[jax.ShapeDtypeStruct((deep, right.shape[1]), BF16) for _, right in pairs] + [jax.ShapeDtypeStruct(shape, BF16) for shape in kept],
        scratch_shapes=twice + twice + [pltpu.VMEM(shape, BF16) for shape in kept] + ([sems((2, 2)), sems((2, 2))] if paired else []),
        compiler_params=params("arbitrary", number=number),
        cost_estimate=pl.CostEstimate(flops=LIGHT, bytes_accessed=LIGHT, transcendentals=0),
        name=name,
    )(*[left for left, _ in pairs], *[right for _, right in pairs], *paired, *came, *after)


def last_kernel(moves, *refs):
    count = len(moves)
    srcs, thin_ref, wide_ref, half_ref = refs[:count], *refs[count : count + 3]
    refs = refs[count + 3 :]
    dsts, thin_out, wide_out = refs[:count], refs[count], refs[count + 1]
    thin_own, thin_came, thin_line, wide_own, wide_came, wide_line, load_sems, pair_sems, sems, local_sems = refs[count + 2 :]
    me, head = lax.axis_index("dp"), lax.axis_index("head")
    side, high = me & 1, me >> 1
    many = thin_own.shape[0]
    peers, copies = make_moves(moves, srcs, dsts, sems, local_sems)

    def remote(src, dst, which, slot, peer):
        return pltpu.make_async_remote_copy(
            src_ref=src,
            dst_ref=dst,
            send_sem=pair_sems.at[0, which, slot],
            recv_sem=pair_sems.at[1, which, slot],
            device_id=(peer, head),
            device_id_type=MESH,
        )

    def blocks(own, line, which):
        return [remote(own.at[high ^ j], line.at[j - 1], which, j, me ^ (2 * j)) for j in range(1, many)]

    half = remote(thin_ref.at[:, 1 - side], thin_came, 0, 0, me ^ 1)
    thin_blocks, wide_blocks = blocks(thin_own, thin_line, 0), blocks(wide_own, wide_line, 1)
    loads = [
        pltpu.make_async_copy(wide_ref.at[:, side], wide_own, load_sems.at[0]),
        pltpu.make_async_copy(half_ref, wide_came, load_sems.at[1]),
        pltpu.make_async_copy(thin_ref.at[:, side], thin_own, load_sems.at[2]),
    ]
    for copy in loads:
        copy.start()
    greet(peers)
    half.start()
    for copy in copies:
        copy.start()
    for copy in loads:
        copy.wait()
    for j in range(many):
        wide_own[j] = (wide_own[j].astype(F32) + wide_came[j].astype(F32)).astype(BF16)
    for copy in wide_blocks:
        copy.start()
    half.wait()
    for j in range(many):
        thin_own[j] = (thin_own[j].astype(F32) + thin_came[j].astype(F32)).astype(BF16)
    for copy in thin_blocks:
        copy.start()
    for copy in wide_blocks + thin_blocks:
        copy.wait()
    thin, wide = thin_own[high].astype(F32), wide_own[high].astype(F32)
    for j in range(many - 1):
        thin, wide = thin + thin_line[j].astype(F32), wide + wide_line[j].astype(F32)
    thin_out[...] = thin
    wide_out[...] = wide
    for copy in copies:
        copy.wait()


def run_last(moves, values, thin, wide, half, number):
    many, _, block, slim = thin.shape
    broad = wide.shape[3]
    anywhere = pl.BlockSpec(memory_space=pl.ANY)
    inside = pl.BlockSpec(memory_space=pltpu.VMEM)
    space = lambda count, columns: pltpu.VMEM((count, block, columns), BF16)
    sems = pltpu.SemaphoreType.DMA
    return pl.pallas_call(
        functools.partial(last_kernel, tuple(moves)),
        in_specs=[anywhere] * (len(moves) + 3),
        out_specs=[anywhere] * len(moves) + [inside] * 2,
        out_shape=move_outs(moves, values) + [jax.ShapeDtypeStruct((block, slim), F32), jax.ShapeDtypeStruct((block, broad), F32)],
        scratch_shapes=[space(many, slim), space(many, slim), space(many - 1, slim), space(many, broad), space(many, broad), space(many - 1, broad)]
        + [sems((3,)), sems((2, 2, many))]
        + move_scratch(moves, values),
        compiler_params=pltpu.CompilerParams(collective_id=number, has_side_effects=True, vmem_limit_bytes=LIMIT),
        name="last_exchange",
    )(*values, thin, wide, half)


def row_forward(size, quarter, own_ref, full_ref, sems):
    me, own = lax.axis_index("dp"), lax.axis_index("head")
    columns = lambda head: pl.ds(pl.multiple_of(head * quarter, 128), quarter)

    def copy(src, dst, stage, k, head):
        return pltpu.make_async_remote_copy(
            src_ref=src, dst_ref=dst, send_sem=sems.at[0, stage, k], recv_sem=sems.at[1, stage, k], device_id=(me, head), device_id_type=MESH
        )

    def source(k):
        return full_ref.at[me ^ k, :, columns(own)] if own_ref is None else own_ref.at[me ^ k]

    def far(k):
        return copy(source(k), full_ref.at[me ^ k, :, columns(own)], 0, k, own ^ 2)

    def near(k):
        return copy(source(k), full_ref.at[me ^ k, :, columns(own)], 1, k, own ^ 1)

    def back(k):
        block = full_ref.at[me ^ k, :, columns(own ^ 2)]
        return copy(block, block, 2, k, own ^ 1)

    return far, near, back


def shard_spread(src, dst, across_sems, side_sems):
    me, own = lax.axis_index("dp"), lax.axis_index("head")

    def copy(a, b, sems, part, j, peer):
        return pltpu.make_async_remote_copy(
            src_ref=a, dst_ref=b, send_sem=sems.at[0, part, j], recv_sem=sems.at[1, part, j], device_id=(peer, own), device_id_type=MESH
        )

    def across(part, j):
        return copy(src.at[part], dst.at[me, part], across_sems, part, j, me ^ (2 * j))

    def side(part, j):
        here = dst.at[me ^ (2 * j), part]
        return copy(src.at[part] if j == 0 else here, here, side_sems, part, j, me ^ 1)

    return across, side


def entry_kernel(parts, order_ref, x_ref, g_ref, w_ref, fx_ref, fg_ref, fw_ref, row_sems, x_sems, g_sems, line_sems, side_sems, local_sems, land, ready, picks, w_held):
    size, block, quarter = x_ref.shape
    line = size // 2
    me, own = lax.axis_index("dp"), lax.axis_index("head")
    spot = me >> 1
    mine = pl.ds(pl.multiple_of(own * quarter, 128), quarter)
    sources, fulls = (x_ref, g_ref), (fx_ref, fg_ref)
    forwards = [row_forward(size, quarter, ready.at[i], fulls[i], sems) for i, sems in enumerate((x_sems, g_sems))]

    def remote(src, dst, sems, slot, peer):
        return pltpu.make_async_remote_copy(
            src_ref=src, dst_ref=dst, send_sem=sems.at[(0,) + slot], recv_sem=sems.at[(1,) + slot], device_id=(peer, own), device_id_type=MESH
        )

    def rows(which, k):
        return remote(sources[which].at[me ^ k], land.at[which, me], row_sems, (which, k), me ^ k)

    def along(way, part, j):
        sign = 1 - 2 * way
        origin = jnp.clip(me - sign * 2 * (j - 1), 0, size - 1)
        peer = jnp.clip(me + sign * 2, 0, size - 1)
        here = fw_ref.at[origin, part]
        return remote(w_ref.at[part] if j == 1 else here, here, line_sems, (way, part, j - 1), peer)

    def came(way, part, j):
        sign = 1 - 2 * way
        here = fw_ref.at[jnp.clip(me - sign * 2 * j, 0, size - 1), part]
        return remote(here, here, line_sems, (way, part, j - 1), me)

    def side(way, part, j):
        sign = 1 - 2 * way
        here = fw_ref.at[jnp.clip(me - sign * 2 * j, 0, size - 1), part]
        return remote(w_ref.at[part] if j == 0 else here, here, side_sems, (way, part, j), me ^ 1)

    def goes_on(way):
        return spot < line - 1 if way == 0 else spot > 0

    def arrives(way, j):
        return spot >= j if way == 0 else spot < line - j

    into = [pltpu.make_async_copy(sources[i].at[me], land.at[i, me], local_sems.at[i]) for i in range(2)]
    into.append(pltpu.make_async_copy(w_ref, w_held, local_sems.at[2]))
    held = [pltpu.make_async_copy(ready.at[i], fulls[i].at[:, :, mine], local_sems.at[3 + i]) for i in range(2)]
    held.append(pltpu.make_async_copy(w_held, fw_ref.at[me], local_sems.at[5]))
    for copy in into:
        copy.start()
    greet([(me ^ k, own) for k in range(1, size)] + [(me, own ^ 1), (me, own ^ 2)])
    order = turn_order(size)
    for k in order:
        rows(0, k).start()
    for part in range(parts):
        side(0, part, 0).start()
    for copy in into:
        copy.wait()
    held[2].start()
    total = size * block
    lane = lax.broadcasted_iota(jnp.int32, (T, T), 1).astype(F32)

    def pick(i, carry):
        wanted = to_col(order_ref[i])
        at = pl.ds(pl.multiple_of(i * T, T), T)
        for j in range(total // T):
            picks[at, j * T : j * T + T] = (wanted == lane + float(T * j)).astype(F32).astype(BF16)
        return carry

    lax.fori_loop(0, total // T, pick, 0)

    def arrange(which):
        step = min(512, total)
        for i in range(total // step):
            value = dot(picks[i * step : (i + 1) * step, :], land[which].reshape(total, quarter)).astype(BF16)
            ready[which, i * step // block : (i + 1) * step // block] = value.reshape(step // block, block, quarter)
        held[which].start()
        far, near, _ = forwards[which]
        for k in range(size):
            far(k).start()
            near(k).start()

    def backs(which, some):
        far, _, back = forwards[which]
        for k in some:
            far(k).wait_recv()
            back(k).start()

    for k in order:
        rows(0, k).wait_recv()
    for k in order:
        rows(1, k).start()
    arrange(0)
    for k in order:
        rows(1, k).wait_recv()
    for way in range(2):

        @pl.when(goes_on(way))
        def _():
            for part in range(parts):
                along(way, part, 1).start()

    arrange(1)
    backs(0, range(size))
    for j in range(1, line):
        for part in range(parts):
            if j == line - 1:
                backs(1, range(part * size // parts, (part + 1) * size // parts))
            for way in range(2):

                @pl.when(arrives(way, j))
                def _():
                    came(way, part, j).wait_recv()
                    side(way, part, j).start()

                if j + 1 < line:

                    @pl.when(arrives(way, j) & goes_on(way))
                    def _():
                        along(way, part, j + 1).start()

    for copy in held:
        copy.wait()
    for which in range(2):
        far, near, back = forwards[which]
        for k in range(size):
            near(k).wait()
            back(k).wait()
            far(k).wait_send()
            if k:
                rows(which, k).wait_send()
    for part in range(parts):
        side(0, part, 0).wait()
        for way in range(2):

            @pl.when(goes_on(way))
            def _():
                along(way, part, 1).wait_send()

            for j in range(1, line):

                @pl.when(arrives(way, j))
                def _():
                    side(way, part, j).wait()

                if j + 1 < line:

                    @pl.when(arrives(way, j) & goes_on(way))
                    def _():
                        along(way, part, j + 1).wait_send()


PARTS = 4


def cut_shard(w):
    return w.reshape(PARTS, w.shape[0] // PARTS, w.shape[1])


def full_shape(size, w):
    return jax.ShapeDtypeStruct((size, PARTS, w.shape[0] // PARTS, w.shape[1]), BF16)


def run_entry(order, tokens, cotangent, w_in, number):
    size = lax.axis_size("dp")
    rows, quarter = tokens.shape
    block = rows // size
    line = size // 2
    anywhere = pl.BlockSpec(memory_space=pl.ANY)
    sems = pltpu.SemaphoreType.DMA
    full = jax.ShapeDtypeStruct((size, block, quarter * 4), BF16)
    came_x, came_g, came_w = pl.pallas_call(
        functools.partial(entry_kernel, PARTS),
        in_specs=[pl.BlockSpec(memory_space=pltpu.VMEM)] + [anywhere] * 3,
        out_specs=[anywhere] * 3,
        out_shape=[full, full, full_shape(size, w_in)],
        scratch_shapes=[
            sems((2, 2, size)),
            sems((2, 3, size)),
            sems((2, 3, size)),
            sems((2, 2, PARTS, line)),
            sems((2, 2, PARTS, line)),
            sems((6,)),
            pltpu.VMEM((2, size, block, quarter), BF16),
            pltpu.VMEM((2, size, block, quarter), BF16),
            pltpu.VMEM((rows, rows), BF16),
            pltpu.VMEM((PARTS, w_in.shape[0] // PARTS, w_in.shape[1]), BF16),
        ],
        compiler_params=pltpu.CompilerParams(collective_id=number, has_side_effects=True, vmem_limit_bytes=LIMIT),
        name="entry",
    )(order, tokens.reshape(size, block, quarter), cotangent.reshape(size, block, quarter), cut_shard(w_in))
    return came_x.reshape(rows, quarter * 4), came_g.reshape(rows, quarter * 4), came_w.reshape(size * w_in.shape[0], w_in.shape[1])


def mm(a, b, contract, kind):
    return lax.dot_general(a, b, (contract, ((), ())), preferred_element_type=F32).astype(kind)


def body(tokens, cotangent, order, lengths, norm_gain, w_zx, w_bc, w_dt, w_out, conv_x, conv_bc, head_params, gate_gain):
    rows, quarter = tokens.shape
    heads = head_params.shape[1]
    width = heads * HEAD
    me = lax.axis_index("head").astype(jnp.int32).reshape(1)
    size = lax.axis_size("dp")
    here = lax.axis_index("dp")
    all_width = width * lax.axis_size("head")
    deep = quarter * lax.axis_size("head")
    own_w = w_zx.shape[0]
    arrange = order.astype(F32).reshape(rows // T, 1, T)

    packed = jnp.concatenate(
        [w_zx.reshape(own_w, 2 * width), w_bc, w_dt, norm_gain[:, None], jnp.zeros((own_w, 127 - heads), BF16)], axis=1
    )
    blocks = lambda value: value.reshape(size, rows // size, quarter)
    full_x, full_g, w_in = run_entry(arrange, tokens, cotangent, packed, 1)
    normed, inv_one, u_zx, u_bd, gain, w_o = run_project(heads, full_x, w_in, w_out, 2)

    gated = gate_gain.reshape(1, width)
    hp = jnp.pad(head_params, ((0, 5), (0, 128 - heads)))
    positions = lax.broadcasted_iota(jnp.int32, (lengths.shape[0], LEN), 1)
    mask = (positions < lengths[:, None]).astype(F32).reshape(rows // T, 1, T)

    y, ss, c, cb, st, w_o = run_forward(heads, u_zx, u_bd, conv_x, conv_bc, hp, w_out, w_o, 3)
    w_o = w_o.reshape(deep, width)
    dyn, co = run_gate(full_g, w_o, y, u_zx, gated, mask)
    yg, dz, dy, gg, rd_z = run_mid(all_width, y, u_zx, dyn, gated, mask, ss, co, 4)

    def total(kept, came, shift):
        own = lax.dynamic_index_in_dim(kept, here >> shift, 0, keepdims=False)
        return own.astype(F32) + jnp.sum(came.astype(F32), axis=0)

    def pairs(grads):
        return grads.reshape(size // 2, 2, own_w, grads.shape[1])

    def fours(grads):
        return grads.reshape(size // 4, 2, -1, own_w, grads.shape[-1])

    scan = functools.partial(run_backward, heads)
    shared = (dy, u_zx, c, cb, u_bd, st, conv_x, conv_bc, hp)
    out_far, out_own = run_pieces([yg], w_o, quarter, "branch_pieces", [], [], 5)
    out_arrived = lax.ppermute(out_far, "head", [(i, i ^ 2) for i in range(lax.axis_size("head"))])
    grad_o, grad_z = run_grads([(full_g, yg), (normed, dz)], "gate_grads", after=[out_far])
    grad_o, grad_z = pairs(grad_o), fours(grad_z)
    *back0, gx0, gb0, gh0, came_o, came_z = scan(0, *shared, (), [("half", "dp", 0), ("half", "dp", 1)], [grad_o, grad_z], 7)
    sent_out = run_home(me, arrange, [out_own, out_arrived], None, deep, "home_out", [back0[0]])
    got_out = lax.all_to_all(sent_out, "dp", split_axis=0, concat_axis=0, tiled=True)
    *back1, gx1, gb1, gh1 = scan(1, *shared, back0, [], [], 0, [sent_out])
    dux, dbd, rd_x = back1
    grad_x, grad_bd, kept_o, kept_z = run_grads(
        [(normed, dux), (normed, dbd)], "scan_grads", [fours(grad_o), grad_z], [came_o.reshape(came_z.shape), came_z], 8
    )
    grad_x, grad_bd = pairs(grad_x), pairs(grad_bd)
    gb = gb0 + gb1
    d_far, d_own, line_o, line_z, came_x2, got_rows, got_gb = run_pieces(
        [dz, dux, dbd],
        w_in,
        quarter,
        "input_pieces",
        [("direct", "dp", 2), ("direct", "dp", 2), ("half", "dp", 0), ("spread", "head"), ("spread", "head")],
        [kept_o, kept_z, grad_x, rd_z + rd_x, gb],
        9,
        [got_out],
    )
    gb = gb[:5] + jnp.sum(got_gb, axis=0)[:5]
    gh = gh0 + gh1
    ends = jnp.concatenate([gb[3], gb[4]] + [gh[i, :32] for i in range(3)] + [jnp.zeros((width - 4 * N - 96,), F32)])
    small = jnp.concatenate([(gx0 + gx1)[:5], gg[:1], jnp.concatenate([gb[0], gb[1], gb[2]])[None], ends[None]], axis=0)
    d_arrived, got_small, grad_bd, grad_x = run_last([("whole", "head", 2), ("spread", "dp")], [d_far, small], grad_bd, grad_x, came_x2, 10)

    sent_back = run_home(me, arrange, [d_own, d_arrived], [normed, inv_one, gain, rd_z, rd_x, got_rows], deep, "home_back")
    got_back = lax.all_to_all(sent_back, "dp", split_axis=0, concat_axis=0, tiled=True)
    final_out = (tokens.astype(F32) + got_out.astype(F32)).astype(BF16)
    final_back = (cotangent.astype(F32) + got_back.astype(F32)).astype(BF16)

    grad_out, grad_z = total(kept_o, line_o, 2), total(kept_z, line_z, 2)
    small = small + jnp.sum(got_small, axis=0)
    grad_zx = jnp.stack([grad_z, grad_x], axis=1)
    of_gain = jnp.sum(grad_z * w_zx[:, 0].astype(F32), axis=1) + jnp.sum(grad_x * w_zx[:, 1].astype(F32), axis=1)
    of_gain = of_gain + jnp.sum(grad_bd[:, : 2 * N] * w_bc.astype(F32), axis=1)
    of_gain = of_gain + jnp.sum(grad_bd[:, 2 * N : 2 * N + heads] * w_dt.astype(F32), axis=1)
    last = jnp.concatenate([grad_bd[:, : 2 * N], jnp.broadcast_to(of_gain[:, None], (own_w, 128))], axis=1)
    others, = run_exchange([("spread", "head")], [last], 11)
    last = last + jnp.sum(others, axis=0)
    grad_gain = last[:, 2 * N] / norm_gain.astype(F32)
    gx, gg = small[0:5], small[5]
    gb = jnp.concatenate([small[6].reshape(3, 2 * N), small[7, : 4 * N].reshape(2, 2 * N)], axis=0)
    gh = small[7, 4 * N : 4 * N + 96].reshape(3, 32)[:, :heads]
    return (final_out, final_back, grad_gain, grad_zx, last[:, : 2 * N], grad_bd[:, 2 * N : 2 * N + heads], grad_out, gx, gb, gh, gg)


def solution(mesh):
    return jax.shard_map(
        body,
        mesh=mesh,
        in_specs=(
            P("dp", "head"),
            P("dp", "head"),
            P("dp", None),
            P("dp"),
            P("dp"),
            P("dp", None, "head"),
            P("dp", None),
            P("dp", "head"),
            P("dp", "head"),
            P(None, "head"),
            P(),
            P(None, "head"),
            P("head"),
        ),
        out_specs=(
            P("dp", "head"),
            P("dp", "head"),
            P("dp"),
            P("dp", None, "head"),
            P("dp", None),
            P("dp", "head"),
            P("dp", "head"),
            P(None, "head"),
            P(),
            P(None, "head"),
            P("head"),
        ),
        check_vma=False,
    )
```

```python
import functools

import jax
import jax.numpy as jnp
from jax import lax
from jax.experimental import pallas as pl
from jax.experimental.pallas import tpu as pltpu
from jax.sharding import PartitionSpec as P

LEN = 1024
T = 128
N = 128
HEAD = 64
EPS = 1e-05
NEG = -1e30
LIGHT = 1000
LIMIT = 60 * 1024 * 1024
AXES = ("dp", "head")
F32 = jnp.float32
BF16 = jnp.bfloat16


def dot(a, b):
    return lax.dot_general(a, b, (((1,), (0,)), ((), ())), preferred_element_type=F32)


def dot_nt(a, b):
    return lax.dot_general(a, b, (((1,), (1,)), ((), ())), preferred_element_type=F32)


def dot_exact(a, b):
    return lax.dot_general(
        a, b, (((1,), (0,)), ((), ())), preferred_element_type=F32, precision=lax.Precision.HIGHEST
    )


def iotas(rows, cols):
    return (
        lax.broadcasted_iota(jnp.int32, (rows, cols), 0),
        lax.broadcasted_iota(jnp.int32, (rows, cols), 1),
    )


MESH = pl.DeviceIdType.MESH


def greet(peers):
    barrier = pltpu.get_barrier_semaphore()
    for peer in peers:
        pl.semaphore_signal(barrier, inc=1, device_id=peer, device_id_type=MESH)
    pl.semaphore_wait(barrier, len(peers))


def place_of():
    return {name: lax.axis_index(name) for name in AXES}


def move_copies(move, src, dst):
    kind, axis = move[0], move[1]
    place = place_of()
    me = place[axis]

    def peer(flip):
        return tuple(place[name] ^ flip if name == axis else place[name] for name in AXES)

    if kind == "whole":
        return [(peer(move[2]), src, dst)], []
    if kind == "rows":
        return [(peer(move[2]), src.at[pl.ds(move[3], move[4])], dst)], []
    if kind == "half":
        return [(peer(1 << move[2]), src.at[:, 1 - ((me >> move[2]) & 1)], dst)], []
    if kind == "direct":
        high = me >> move[2]
        return [(peer(j << move[2]), src.at[high ^ j], dst.at[j - 1]) for j in range(1, dst.shape[0] + 1)], []
    if kind == "all":
        groups = lax.axis_size("head")
        flips = [divmod(flat, groups) for flat in range(1, dst.shape[0] + 1)]
        return [((place["dp"] ^ f, place["head"] ^ e), src, dst.at[i]) for i, (f, e) in enumerate(flips)], []
    if kind == "spread":
        return [(peer(flip), src, dst.at[flip - 1]) for flip in range(1, dst.shape[0] + 1)], []
    remote = [(peer(k), src.at[me ^ k], dst.at[me]) for k in turn_order(src.shape[0])]
    return remote, [(src.at[me], dst.at[me])]


def turn_order(size):
    return sorted(range(1, size), key=lambda k: (-(k & ~1), k & 1))


def move_shape(move, shape):
    kind = move[0]
    if kind == "rows":
        return (move[4],) + shape[1:]
    if kind == "half":
        return (shape[0],) + shape[2:]
    if kind == "direct":
        return (shape[0] - 1,) + shape[1:]
    if kind == "spread":
        return (lax.axis_size(move[1]) - 1,) + shape
    if kind == "all":
        return (lax.axis_size("dp") * lax.axis_size("head") - 1,) + shape
    return shape


def move_counts(moves, values):
    remote = local = 0
    for move, value in zip(moves, values):
        size = lax.axis_size(move[1])
        world = lax.axis_size("dp") * lax.axis_size("head")
        count = {"direct": value.shape[0] - 1, "spread": size - 1, "turn": size - 1, "all": world - 1}.get(move[0], 1)
        remote, local = remote + count, local + (move[0] == "turn")
    return remote, local


def move_scratch(moves, values):
    remote, local = move_counts(moves, values)
    return [pltpu.SemaphoreType.DMA((2, remote)), pltpu.SemaphoreType.DMA((max(local, 1),))] if moves else []


def move_outs(moves, values):
    return [jax.ShapeDtypeStruct(move_shape(move, value.shape), value.dtype) for move, value in zip(moves, values)]


def make_moves(moves, srcs, dsts, sems, local_sems):
    remote, local = [], []
    for move, src, dst in zip(moves, srcs, dsts):
        here, there = move_copies(move, src, dst)
        remote += here
        local += there
    copies = [
        pltpu.make_async_remote_copy(src_ref=a, dst_ref=b, send_sem=sems.at[0, i], recv_sem=sems.at[1, i], device_id=peer, device_id_type=MESH)
        for i, (peer, a, b) in enumerate(remote)
    ]
    copies += [pltpu.make_async_copy(a, b, local_sems.at[i]) for i, (a, b) in enumerate(local)]
    return move_peers(moves, dsts), copies


def move_peers(moves, dsts):
    flips = {}
    for move, dst in zip(moves, dsts):
        kind, axis = move[0], move[1]
        if kind in ("whole", "rows"):
            own = [move[2]]
        elif kind == "half":
            own = [1 << move[2]]
        elif kind == "direct":
            own = [j << move[2] for j in range(1, dst.shape[0] + 1)]
        elif kind == "all":
            groups = lax.axis_size("head")
            for flat in range(1, dst.shape[0] + 1):
                flips[divmod(flat, groups)] = None
            continue
        elif kind == "spread":
            own = range(1, dst.shape[0] + 1)
        else:
            own = range(1, dst.shape[0])
        for flip in own:
            flips[(flip, 0) if axis == "dp" else (0, flip)] = None
    place = place_of()
    return [(place["dp"] ^ f, place["head"] ^ e) for f, e in flips]


def background(first, last, moves, srcs, dsts, sems, local_sems):
    peers, copies = make_moves(moves, srcs, dsts, sems, local_sems)

    @pl.when(first)
    def _():
        greet(peers)
        for copy in copies:
            copy.start()

    @pl.when(last)
    def _():
        for copy in copies:
            copy.wait()


def exchange_kernel(moves, *refs):
    count = len(moves)
    peers, copies = make_moves(moves, refs[:count], refs[count : 2 * count], refs[2 * count], refs[2 * count + 1])
    greet(peers)
    for copy in copies:
        copy.start()
    for copy in copies:
        copy.wait()


def run_exchange(moves, values, number):
    return pl.pallas_call(
        functools.partial(exchange_kernel, tuple(moves)),
        in_specs=[pl.BlockSpec(memory_space=pl.ANY)] * len(moves),
        out_specs=[pl.BlockSpec(memory_space=pl.ANY)] * len(moves),
        out_shape=move_outs(moves, values),
        scratch_shapes=move_scratch(moves, values),
        compiler_params=pltpu.CompilerParams(collective_id=number, has_side_effects=True, vmem_limit_bytes=LIMIT),
        name="exchange",
    )(*values)


def sigmoid(v):
    return 1.0 / (1.0 + jnp.exp(-v))


def softplus(v):
    return jnp.maximum(v, 0.0) + jnp.log1p(jnp.exp(-jnp.abs(v)))


def to_col(row):
    return jnp.broadcast_to(row, (T, T)).T


def to_row(col):
    return jnp.broadcast_to(col, (T, T)).T[0:1]


def lanes(value, pick):
    return jnp.broadcast_to(value[:, pick : pick + 1], (value.shape[0], 128))


def step_terms(ubd, head_ref, heads):
    row, col = iotas(T, T)
    raw = jnp.where(col < heads, ubd[:, 2 * N :] + head_ref[0:1], 0.0)
    steps = jnp.where(col < heads, softplus(raw), 0.0)
    rates = -jnp.exp(head_ref[1:2])
    tril = (row >= col).astype(F32)
    logs = dot_exact(tril, steps * rates)
    return raw, steps, rates, logs


def weight_moves(step, steps, parts, whole, w_ref, fw_ref, across_sems, side_sems, local_sems, w_held):
    line = fw_ref.shape[0] // 2
    me, own = lax.axis_index("dp"), lax.axis_index("head")
    across, side = shard_spread(w_ref, fw_ref, across_sems, side_sems)
    if whole:
        into = pltpu.make_async_copy(w_ref, w_held, local_sems.at[0])
        held = pltpu.make_async_copy(w_held, fw_ref.at[me], local_sems.at[1])

    @pl.when(step == 0)
    def _():
        if whole:
            into.start()
        greet([(me ^ 1, own)] + [(me ^ (2 * j), own) for j in range(1, line)])
        for part in parts:
            side(part, 0).start()
        if whole:
            into.wait()
            held.start()

    for i, part in enumerate(parts):
        begin = i * steps // len(parts)

        @pl.when(step == begin)
        def _():
            for j in range(1, line):
                across(part, j).start()

        @pl.when(step == min(steps - 1, begin + steps // 3 + 2))
        def _():
            for j in range(1, line):
                across(part, j).wait_recv()
                side(part, j).start()

    @pl.when(step == steps - 1)
    def _():
        if whole:
            held.wait()
        for part in parts:
            for j in range(line):
                side(part, j).wait()
                if j:
                    across(part, j).wait_send()


def weight_scratch(size, w):
    sems = pltpu.SemaphoreType.DMA
    return [sems((2, PARTS, size // 2)), sems((2, PARTS, size // 2)), sems((2,)), pltpu.VMEM((PARTS, w.shape[0] // PARTS, w.shape[1]), BF16)]


def forward_kernel(heads, steps, x_ref, z_ref, ubd_ref, par_ref, pbc_ref, head_ref, w_ref, before_ref, y_ref, ss_ref, c_ref, cb_ref, st_ref, fw_ref, ext_x, ext_b, state, *sems):
    weight_moves(pl.program_id(0) * pl.num_programs(1) + pl.program_id(1), steps, range(1, PARTS), False, w_ref, fw_ref, *sems)

    @pl.when(pl.program_id(1) == 0)
    def _():
        ext_x[0:8] = jnp.zeros_like(ext_x[0:8])
        ext_b[0:8] = jnp.zeros_like(ext_b[0:8])
        state[...] = jnp.zeros_like(state)

    def conv(ext, values, taps):
        ext[8 : 8 + T] = values
        total = taps[4:5] + taps[3:4] * values
        for k in range(3):
            total = total + taps[k : k + 1] * ext[5 + k : 5 + k + T]
        ext[0:8] = ext[T : T + 8]
        return total

    row, col = iotas(T, T)
    low = col < HEAD
    low_row = lax.broadcasted_iota(jnp.int32, (1, 128), 1) < HEAD
    causal = row >= col
    ubd = ubd_ref[...]
    c = conv(ext_x, x_ref[...].astype(F32), par_ref)
    c_ref[...] = c.astype(BF16)
    cb = conv(ext_b, ubd[:, : 2 * N], pbc_ref)
    cb_ref[...] = cb
    bc = cb * sigmoid(cb)
    b_rows = bc[:, :N]
    b_t = b_rows.T.astype(BF16)
    b_low, c_low = b_rows.astype(BF16), bc[:, N:].astype(BF16)
    _, steps, _, logs = step_terms(ubd, head_ref, heads)
    logs_t = logs.T
    scores = dot_nt(c_low, b_low)
    entering = state[...].astype(BF16)
    st_ref[0] = entering
    outer = dot(c_low, entering)
    squares = jnp.zeros((T, 128), F32)
    for pair in range(heads // 2):
        span = slice(128 * pair, 128 * pair + 128)
        h0, h1 = 2 * pair, 2 * pair + 1
        log0, log1 = lanes(logs, h0), lanes(logs, h1)
        log_pair = jnp.where(low, log0, log1)
        step_pair = jnp.where(low, lanes(steps, h0), lanes(steps, h1))
        last_pair = log_pair[T - 1 : T]
        skip_pair = jnp.where(low_row, lanes(head_ref[2:3], h0), lanes(head_ref[2:3], h1))
        cp = c[:, span]
        xp = cp * sigmoid(cp)
        xd = xp * step_pair
        m0 = (scores * jnp.exp(jnp.where(causal, log0 - logs_t[h0 : h0 + 1], NEG))).astype(BF16)
        m1 = (scores * jnp.exp(jnp.where(causal, log1 - logs_t[h1 : h1 + 1], NEG))).astype(BF16)
        stacked = jnp.concatenate([jnp.where(low, xd, 0.0).astype(BF16), jnp.where(low, 0.0, xd).astype(BF16)], axis=0)
        y = dot(jnp.concatenate([m0, m1], axis=1), stacked)
        y = y + jnp.exp(log_pair) * outer[:, span] + skip_pair * xp
        tail = (jnp.exp(last_pair - log_pair) * xd).astype(BF16)
        state[:, span] = jnp.exp(last_pair) * state[:, span] + dot(b_t, tail)
        y_ref[:, span] = y.astype(BF16)
        zp = z_ref[:, span].astype(F32)
        w = y * zp * sigmoid(zp)
        squares = squares + w * w
    ss_ref[0] = to_row(jnp.sum(squares, axis=1, keepdims=True))


def project_kernel(heads, steps, x_ref, w_ref, shard_ref, out_ref, inv_ref, uzx_ref, ubd_ref, gain_ref, fw_ref, *sems):
    deep, width = x_ref.shape[1], 2 * heads * HEAD
    weight_moves(pl.program_id(0), steps, range(1), True, shard_ref, fw_ref, *sems)

    @pl.when(pl.program_id(0) == 0)
    def _():
        for j in range(deep // T):
            span = slice(j * T, j * T + T)
            gain_ref[:, span] = jnp.broadcast_to(w_ref[span, width + 2 * N : width + 3 * N].astype(F32).T[heads : heads + 1], (8, T))

    x = x_ref[...].astype(F32)
    inv = lax.rsqrt(jnp.sum(x * x, axis=1, keepdims=True) / deep + EPS)
    normed = (x * inv * gain_ref[0:1]).astype(BF16)
    out_ref[...] = normed
    for part in range(x.shape[0] // T):
        inv_ref[part] = to_row(inv[part * T : part * T + T])
    uzx_ref[...] = dot(normed, w_ref[:, :width]).astype(BF16)
    ubd_ref[...] = dot(normed, w_ref[:, width:])


def home_kernel(last, deep, me_ref, order_ref, a_ref, b_ref, *refs):
    out_ref, held_ref = refs[-2:]
    step = pl.program_id(0)
    many = held_ref.shape[0] // a_ref.shape[0]
    size = a_ref.shape[0]

    @pl.when(step < many)
    def _():
        value = a_ref[...].astype(F32) + b_ref[...].astype(F32)
        if last:
            normed_ref, inv_ref, gain_ref, rdz_ref, rdx_ref, more_ref = refs[:6]
            gain = gain_ref[0:1]
            hat = normed_ref[...].astype(F32) / gain
            parts = []
            for part in range(size // T):
                inv_row = inv_ref[part]
                dots = rdz_ref[part] + rdx_ref[part] + more_ref[0, part] + more_ref[1, part] + more_ref[2, part]
                rows = slice(part * T, part * T + T)
                inv = to_col(inv_row)[:, 0:1]
                mean = to_col(dots / deep)[:, 0:1]
                parts.append(inv * (gain * value[rows] - hat[rows] * mean))
            value = jnp.concatenate(parts, axis=0)
        held_ref[pl.ds(pl.multiple_of(step * size, size), size), :] = value.astype(BF16)

    @pl.when(step >= many)
    def _():
        base = ((step - many) * size).astype(F32)
        row = lax.broadcasted_iota(jnp.int32, (size, T), 0).astype(F32) + base
        picks = jnp.concatenate([(row == order_ref[j].astype(F32)).astype(F32).astype(BF16) for j in range(order_ref.shape[0])], axis=1)
        out_ref[...] = dot(picks, held_ref[...]).astype(BF16)


def gate_kernel(width, moves, g_ref, wo_ref, y_ref, z_ref, gain_ref, mask_ref, ss_ref, yg_ref, dz_ref, dy_ref, gg_ref, rd_ref, held, co_held, got_ss, got_co, sems, local_sems):
    step = pl.program_id(0)
    many = pl.num_programs(0) // 2
    size = y_ref.shape[0]
    parts = size // T
    others = got_ss.shape[0]
    peers, copies = make_moves(moves, (ss_ref, co_held), (got_ss, got_co), sems, local_sems)
    gain = gain_ref[0:1]

    @pl.when(step == 0)
    def _():
        gg_ref[...] = jnp.zeros_like(gg_ref)
        greet(peers)
        for copy in copies[:others]:
            copy.start()

    @pl.when(step < many)
    def _():
        dyn = dot(g_ref[...], wo_ref[...])
        for part in range(parts):
            rows = slice(part * T, part * T + T)
            mask = to_col(mask_ref[part])[:, 0:1]
            own = dyn[rows] * mask
            held[step, rows] = own.astype(BF16)
            z = z_ref[rows].astype(F32)
            w = y_ref[rows].astype(F32) * z * sigmoid(z)
            co_held[step * parts + part] = to_row(jnp.sum(own * w * gain, axis=1, keepdims=True))

    @pl.when(step == many - 1)
    def _():
        for copy in copies[others:]:
            copy.start()

    @pl.when(step == many)
    def _():
        for copy in copies:
            copy.wait()

    @pl.when(step >= many)
    def _():
        for part in range(parts):
            rows = slice(part * T, part * T + T)
            block = step - many
            here = block * parts + part
            ss, co = ss_ref[here], co_held[here]
            for other in range(others):
                ss, co = ss + got_ss[other, here], co + got_co[other, here]
            mask = to_col(mask_ref[part])[:, 0:1]
            inv_row = lax.rsqrt(ss / width + EPS)
            inv = to_col(inv_row)[:, 0:1]
            cube = to_col(inv_row * inv_row * inv_row * (co / width))[:, 0:1]
            y = y_ref[rows].astype(F32)
            z = z_ref[rows].astype(F32)
            dyn = held[block, rows].astype(F32)
            s = sigmoid(z)
            act = z * s
            w = y * act
            wi = w * inv
            yg_ref[rows] = (wi * gain * mask).astype(BF16)
            gg_ref[0:1] += jnp.sum(dyn * wi, axis=0, keepdims=True)
            dw = inv * gain * dyn - w * cube
            dy_ref[rows] = (dw * act).astype(BF16)
            dz = dw * y * (s * (1.0 + z * (1.0 - s)))
            dz_ref[rows] = dz.astype(BF16)
            rd_ref[part] = to_row(jnp.sum(dz * z, axis=1, keepdims=True))


def backward_kernel(heads, extra, moves, dy_ref, x_ref, c_ref, cb_ref, ubd_ref, st_ref, par_ref, pbc_ref, head_ref, *refs):
    count = len(moves)
    srcs, refs = refs[:count], refs[count + extra :]
    dx_ref, dbd_ref, rd_ref, gx_ref, gb_ref, gh_ref = refs[:6]
    dsts, refs = refs[6 : 6 + count], refs[6 + count :]
    d_state, ext_x, ext_b, rows_ref, prod, edy_ref, tail_ref = refs[:7]
    if moves:
        began = (pl.program_id(0) == 0) & (pl.program_id(1) == 0)
        ended = (pl.program_id(0) == pl.num_programs(0) - 1) & (pl.program_id(1) == pl.num_programs(1) - 1)
        background(began, ended, moves, srcs, dsts, *refs[7:])
    first = (pl.program_id(0) == 0) & (pl.program_id(1) == 0)

    @pl.when(first)
    def _():
        gx_ref[...] = jnp.zeros_like(gx_ref)
        gb_ref[...] = jnp.zeros_like(gb_ref)
        gh_ref[...] = jnp.zeros_like(gh_ref)
        rows_ref[...] = jnp.zeros_like(rows_ref)

    @pl.when(pl.program_id(1) == 0)
    def _():
        ext_x[T : T + 8] = jnp.zeros_like(ext_x[T : T + 8])
        ext_b[T : T + 8] = jnp.zeros_like(ext_b[T : T + 8])
        d_state[...] = jnp.zeros_like(d_state)

    row, col = iotas(T, T)
    low = col < HEAD
    low_row = lax.broadcasted_iota(jnp.int32, (1, 128), 1) < HEAD
    upto = col >= row
    below = row < col
    reach = (row >= col).astype(BF16)
    ubd = ubd_ref[...]
    raw, steps, rates, logs = step_terms(ubd, head_ref, heads)
    logs_t = logs.T
    cb = cb_ref[...]
    sb = sigmoid(cb)
    bc = cb * sb
    b_low, c_low = bc[:, :N].astype(BF16), bc[:, N:].astype(BF16)
    c_t = bc[:, N:].T.astype(BF16)
    scores = dot_nt(b_low, c_low)
    entering = st_ref[0]
    outer = dot(c_low, entering)
    ds_low = d_state[...].astype(BF16)
    back = dot(b_low, ds_low)
    d_scores = jnp.zeros((T, T), F32)
    skip_parts, closing_parts = [], []
    for pair in range(heads // 2):
        span = slice(128 * pair, 128 * pair + 128)
        h0, h1 = 2 * pair, 2 * pair + 1
        log0, log1 = lanes(logs, h0), lanes(logs, h1)
        log_pair = jnp.where(low, log0, log1)
        step_pair = jnp.where(low, lanes(steps, h0), lanes(steps, h1))
        last_pair = log_pair[T - 1 : T]
        skip_pair = jnp.where(low_row, lanes(head_ref[2:3], h0), lanes(head_ref[2:3], h1))
        cp = c_ref[:, span].astype(F32)
        sp = sigmoid(cp)
        xp = cp * sp
        xd = xp * step_pair
        dy_low = dy_ref[:, span]
        dy = dy_low.astype(F32)
        decay0 = jnp.exp(jnp.where(upto, logs_t[h0 : h0 + 1] - log0, NEG))
        decay1 = jnp.exp(jnp.where(upto, logs_t[h1 : h1 + 1] - log1, NEG))
        m0, m1 = scores * decay0, scores * decay1
        zero = jnp.zeros_like(dy_low)
        x_stack = jnp.concatenate([jnp.where(low, xd, 0.0).astype(BF16), jnp.where(low, 0.0, xd).astype(BF16)], axis=0)
        dm = dot_nt(x_stack, dy_low)
        dm0, dm1 = dm[:T], dm[T:]
        d_scores = d_scores + dm0 * decay0 + dm1 * decay1
        dy_stack = jnp.concatenate([jnp.where(low, dy, 0.0).astype(BF16), jnp.where(low, 0.0, dy).astype(BF16)], axis=0)
        dxd = dot(jnp.concatenate([m0.astype(BF16), m1.astype(BF16)], axis=1), dy_stack)
        flow = jnp.concatenate([(dm0 * m0).astype(BF16), (dm1 * m1).astype(BF16)], axis=0)
        later = dot(flow, reach)
        rows_ref[h0 : h0 + 1] = jnp.sum(jnp.where(below, later[:T], 0.0), axis=0, keepdims=True)
        rows_ref[h1 : h1 + 1] = jnp.sum(jnp.where(below, later[T:], 0.0), axis=0, keepdims=True)
        grow = jnp.exp(log_pair)
        tail = jnp.exp(last_pair - log_pair)
        from_state = tail * back[:, span]
        dxd = dxd + from_state
        edy = grow * dy
        prod[0:T, span] = (edy * outer[:, span]).astype(BF16)
        prod[T : 2 * T, span] = (from_state * xd).astype(BF16)
        prod[2 * T : 3 * T, span] = (xp * dxd).astype(BF16)
        skip_parts.append(jnp.sum(xp * dy, axis=0, keepdims=True))
        edy_low = edy.astype(BF16)
        edy_ref[:, span] = edy_low
        tail_ref[:, span] = (tail * xd).astype(BF16)
        old = d_state[:, span]
        closing = jnp.exp(last_pair)
        closing_parts.append(closing * jnp.sum(old * entering[:, span].astype(F32), axis=0, keepdims=True))
        d_state[:, span] = closing * old + dot(c_t, edy_low)
        dx = dxd * step_pair + skip_pair * dy
        ext_x[0:T, span] = dx * (sp * (1.0 + cp * (1.0 - sp)))
    d_low = d_scores.astype(BF16)
    d_b = dot_nt(tail_ref[...], ds_low) + dot(d_low, c_low)
    d_c = dot_nt(edy_ref[...], entering) + dot(d_scores.T.astype(BF16), b_low)
    width = heads * HEAD
    lane_row, lane_col = iotas(width, 128)
    member = (lane_row // HEAD == lane_col).astype(BF16)
    sums = dot(prod[...], member)
    skip_all = jnp.concatenate(skip_parts, axis=1)
    closing_all = jnp.concatenate(closing_parts, axis=1)
    fill = jnp.zeros((6, width), F32)
    few = dot_exact(jnp.concatenate([skip_all, closing_all, fill], axis=0), member.astype(F32))
    d_logs = dot(upto.astype(BF16), sums[:T].astype(BF16)) + dot((col < row).astype(BF16), sums[T : 2 * T].astype(BF16))
    d_logs = d_logs + rows_ref[...].T + few[1:2]
    d_steps = sums[2 * T :] + rates * d_logs
    d_raw = jnp.where(col < heads, d_steps * sigmoid(raw), 0.0)
    gh_ref[0:1] += jnp.sum(d_raw, axis=0, keepdims=True)
    gh_ref[1:2] += rates * jnp.sum(steps * d_logs, axis=0, keepdims=True)
    gh_ref[2:3] += few[0:1]
    ext_b[0:T, 0:N] = d_b * (sb[:, :N] * (1.0 + cb[:, :N] * (1.0 - sb[:, :N])))
    ext_b[0:T, N:] = d_c * (sb[:, N:] * (1.0 + cb[:, N:] * (1.0 - sb[:, N:])))

    def conv_back(ext, values, taps, grads):
        now = ext[0:T]
        total = taps[3:4] * now
        grads[3:4] += jnp.sum(values * now, axis=0, keepdims=True)
        grads[4:5] += jnp.sum(now, axis=0, keepdims=True)
        for k in range(3):
            moved = ext[3 - k : 3 - k + T]
            total = total + taps[k : k + 1] * moved
            grads[k : k + 1] += jnp.sum(values * moved, axis=0, keepdims=True)
        ext[T : T + 8] = ext[0:8]
        return total

    ux = x_ref[...].astype(F32)
    dux = conv_back(ext_x, ux, par_ref, gx_ref)
    dx_ref[...] = dux.astype(BF16)
    ubc = ubd[:, : 2 * N]
    dubc = conv_back(ext_b, ubc, pbc_ref, gb_ref)
    dbd_ref[:, : 2 * N] = dubc.astype(BF16)
    dbd_ref[:, 2 * N :] = d_raw.astype(BF16)
    total = jnp.sum(dux * ux, axis=1, keepdims=True) + jnp.sum(dubc * ubc, axis=1, keepdims=True)
    total = total + jnp.sum(jnp.where(col < heads, d_raw * ubd[:, 2 * N :], 0.0), axis=1, keepdims=True)
    rd_ref[0] = to_row(total)


def params(*semantics, number=0):
    if number:
        return pltpu.CompilerParams(
            dimension_semantics=semantics, vmem_limit_bytes=LIMIT, collective_id=number, has_side_effects=True
        )
    return pltpu.CompilerParams(dimension_semantics=semantics, vmem_limit_bytes=LIMIT)


def run_forward(heads, u_zx, u_bd, par, pbc, hp, w_out, before, number):
    rows, width = u_zx.shape[0], heads * HEAD
    slots, chunks = rows // LEN, LEN // T
    at = lambda s, i: (s * chunks + i, 0)
    fixed = lambda s, i: (0, 0)
    size = lax.axis_size("dp")
    anywhere = pl.BlockSpec(memory_space=pl.ANY)
    return pl.pallas_call(
        functools.partial(forward_kernel, heads, slots * chunks),
        grid=(slots, chunks),
        in_specs=[
            pl.BlockSpec((T, width), lambda s, i: (s * chunks + i, 1)),
            pl.BlockSpec((T, width), at),
            pl.BlockSpec((T, 3 * N), at),
            pl.BlockSpec((5, width), fixed),
            pl.BlockSpec((5, 2 * N), fixed),
            pl.BlockSpec((8, 128), fixed),
            anywhere,
            anywhere,
        ],
        out_specs=[
            pl.BlockSpec((T, width), at),
            pl.BlockSpec((1, 1, T), lambda s, i: (s * chunks + i, 0, 0)),
            pl.BlockSpec((T, width), at),
            pl.BlockSpec((T, 2 * N), at),
            pl.BlockSpec((1, N, width), lambda s, i: (s * chunks + i, 0, 0)),
            anywhere,
        ],
        out_shape=[
            jax.ShapeDtypeStruct((rows, width), BF16),
            jax.ShapeDtypeStruct((rows // T, 1, T), F32),
            jax.ShapeDtypeStruct((rows, width), BF16),
            jax.ShapeDtypeStruct((rows, 2 * N), F32),
            jax.ShapeDtypeStruct((rows // T, N, width), BF16),
            full_shape(size, w_out),
        ],
        scratch_shapes=[
            pltpu.VMEM((T + 8, width), F32),
            pltpu.VMEM((T + 8, 2 * N), F32),
            pltpu.VMEM((N, width), F32),
        ]
        + weight_scratch(size, w_out),
        input_output_aliases={7: 5},
        compiler_params=params("arbitrary", "arbitrary", number=number),
        cost_estimate=pl.CostEstimate(flops=rows * width * 2 * 1200, bytes_accessed=rows * width * 8, transcendentals=rows * width * 6),
        name="scan_forward",
    )(u_zx, u_zx, u_bd, par, pbc, hp, cut_shard(w_out), before)


def run_project(heads, x, w_in, w_out, number):
    rows, deep = x.shape
    wide = w_in.shape[1]
    width = 2 * heads * HEAD
    size = lax.axis_size("dp")
    step = 256
    at = lambda i: (i, 0)
    fixed = lambda i: (0, 0)
    anywhere = pl.BlockSpec(memory_space=pl.ANY)
    thin = pl.BlockSpec((step // T, 1, T), lambda i: (i, 0, 0))
    return pl.pallas_call(
        functools.partial(project_kernel, heads, rows // step),
        grid=(rows // step,),
        in_specs=[pl.BlockSpec((step, deep), at), pl.BlockSpec((deep, wide), fixed), anywhere],
        out_specs=[
            pl.BlockSpec((step, deep), at),
            thin,
            pl.BlockSpec((step, width), at),
            pl.BlockSpec((step, wide - width), at),
            pl.BlockSpec((8, deep), fixed),
            anywhere,
        ],
        out_shape=[
            jax.ShapeDtypeStruct((rows, deep), BF16),
            jax.ShapeDtypeStruct((rows // T, 1, T), F32),
            jax.ShapeDtypeStruct((rows, width), BF16),
            jax.ShapeDtypeStruct((rows, wide - width), F32),
            jax.ShapeDtypeStruct((8, deep), F32),
            full_shape(size, w_out),
        ],
        scratch_shapes=weight_scratch(size, w_out),
        compiler_params=params("arbitrary", number=number),
        cost_estimate=pl.CostEstimate(flops=LIGHT, bytes_accessed=LIGHT, transcendentals=0),
        name="project",
    )(x, w_in, cut_shard(w_out))


def run_home(me, order, sums, extra, deep, name, after=()):
    rows, quarter = sums[0].shape
    step = 512
    many = rows // step
    into = lambda i, m: (jnp.minimum(i, many - 1), 0)
    thin = pl.BlockSpec((step // T, 1, T), lambda i, m: (jnp.minimum(i, many - 1), 0, 0))
    specs = [pl.BlockSpec((rows // T, 1, T), lambda i, m: (0, 0, 0))] + [pl.BlockSpec((step, quarter), into)] * 2
    values = list(sums)
    if extra is not None:
        specs += [pl.BlockSpec((step, quarter), lambda i, m: (jnp.minimum(i, many - 1), m[0])), thin]
        specs += [pl.BlockSpec((8, quarter), lambda i, m: (0, m[0])), thin, thin]
        specs += [pl.BlockSpec((3, step // T, 1, T), lambda i, m: (0, jnp.minimum(i, many - 1), 0, 0))]
        values += list(extra)
    values += list(after)
    specs += [pl.BlockSpec(memory_space=pl.ANY)] * len(after)
    return pl.pallas_call(
        functools.partial(home_kernel, extra is not None, float(deep)),
        grid_spec=pltpu.PrefetchScalarGridSpec(
            num_scalar_prefetch=1,
            grid=(2 * many,),
            in_specs=specs,
            out_specs=pl.BlockSpec((step, quarter), lambda i, m: (jnp.maximum(i - many, 0), 0)),
            scratch_shapes=[pltpu.VMEM((rows, quarter), BF16)],
        ),
        out_shape=jax.ShapeDtypeStruct((rows, quarter), BF16),
        compiler_params=params("arbitrary"),
        cost_estimate=pl.CostEstimate(flops=rows * rows * quarter * 2, bytes_accessed=rows * quarter * 10, transcendentals=0),
        name=name,
    )(me, order, *values)


def run_gate(all_width, grads, w_out, y, u_zx, gain, mask, ss, number):
    rows, width = y.shape
    deep = grads.shape[1]
    step = 256
    many = rows // step
    both = lambda i: (lax.rem(i, many), 0)
    late = lambda i: (jnp.maximum(i - many, 0), 0)
    fixed = lambda i: (0, 0)
    wide, out = pl.BlockSpec((step, width), both), pl.BlockSpec((step, width), late)
    moves = (("spread", "head"), ("spread", "head"))
    others = lax.axis_size("head") - 1
    return pl.pallas_call(
        functools.partial(gate_kernel, float(all_width), moves),
        grid=(2 * many,),
        in_specs=[
            pl.BlockSpec((step, deep), lambda i: (jnp.minimum(i, many - 1), 0)),
            pl.BlockSpec((deep, width), fixed),
            wide,
            wide,
            pl.BlockSpec((1, width), fixed),
            pl.BlockSpec((step // T, 1, T), lambda i: (lax.rem(i, many), 0, 0)),
            pl.BlockSpec((rows // T, 1, T), lambda i: (0, 0, 0)),
        ],
        out_specs=[out, out, out, pl.BlockSpec((8, width), fixed), pl.BlockSpec((step // T, 1, T), lambda i: (jnp.maximum(i - many, 0), 0, 0))],
        out_shape=[jax.ShapeDtypeStruct((rows, width), BF16)] * 3
        + [jax.ShapeDtypeStruct((8, width), F32), jax.ShapeDtypeStruct((rows // T, 1, T), F32)],
        scratch_shapes=[pltpu.VMEM((many, step, width), BF16), pltpu.VMEM((rows // T, 1, T), F32)]
        + [pltpu.VMEM((others, rows // T, 1, T), F32)] * 2
        + move_scratch(moves, (ss, ss)),
        compiler_params=params("arbitrary", number=number),
        cost_estimate=pl.CostEstimate(flops=LIGHT, bytes_accessed=LIGHT, transcendentals=0),
        name="gate",
    )(grads, w_out, y, u_zx, gain, mask, ss)


def run_backward(heads, slot, dy, u_zx, c, cb, u_bd, st, par, pbc, hp, before, moves, values, number, after=()):
    rows, width = dy.shape
    chunks = LEN // T
    place = lambda s, i: slot * chunks + chunks - 1 - i
    at = lambda s, i: (place(s, i), 0)
    at3 = lambda s, i: (place(s, i), 0, 0)
    fixed = lambda s, i: (0, 0)
    anywhere = pl.BlockSpec(memory_space=pl.ANY)
    return pl.pallas_call(
        functools.partial(backward_kernel, heads, len(before) + len(after), tuple(moves)),
        grid=(1, chunks),
        in_specs=[
            pl.BlockSpec((T, width), at),
            pl.BlockSpec((T, width), lambda s, i: (place(s, i), 1)),
            pl.BlockSpec((T, width), at),
            pl.BlockSpec((T, 2 * N), at),
            pl.BlockSpec((T, 3 * N), at),
            pl.BlockSpec((1, N, width), at3),
            pl.BlockSpec((5, width), fixed),
            pl.BlockSpec((5, 2 * N), fixed),
            pl.BlockSpec((8, 128), fixed),
        ]
        + [anywhere] * (len(moves) + len(before) + len(after)),
        out_specs=[
            pl.BlockSpec((T, width), at),
            pl.BlockSpec((T, 3 * N), at),
            pl.BlockSpec((1, 1, T), at3),
            pl.BlockSpec((8, width), fixed),
            pl.BlockSpec((8, 2 * N), fixed),
            pl.BlockSpec((8, 128), fixed),
        ]
        + [anywhere] * len(moves),
        out_shape=[
            jax.ShapeDtypeStruct((rows, width), BF16),
            jax.ShapeDtypeStruct((rows, 3 * N), BF16),
            jax.ShapeDtypeStruct((rows // T, 1, T), F32),
            jax.ShapeDtypeStruct((8, width), F32),
            jax.ShapeDtypeStruct((8, 2 * N), F32),
            jax.ShapeDtypeStruct((8, 128), F32),
        ]
        + move_outs(moves, values),
        scratch_shapes=[
            pltpu.VMEM((N, width), F32),
            pltpu.VMEM((T + 8, width), F32),
            pltpu.VMEM((T + 8, 2 * N), F32),
            pltpu.VMEM((128, 128), F32),
            pltpu.VMEM((3 * T, width), BF16),
            pltpu.VMEM((T, width), BF16),
            pltpu.VMEM((T, width), BF16),
        ]
        + move_scratch(moves, values),
        input_output_aliases={9 + len(moves) + i: i for i in range(len(before))},
        compiler_params=params("arbitrary", "arbitrary", number=number),
        cost_estimate=pl.CostEstimate(flops=LIGHT, bytes_accessed=LIGHT, transcendentals=0),
        name="scan_backward",
    )(dy, u_zx, c, cb, u_bd, st, par, pbc, hp, *values, *before, *after)


def pieces_kernel(count, many, moves, extra, *refs):
    total = len(moves)
    values, weight_ref, srcs = refs[:count], refs[count], refs[count + 1 : count + 1 + total]
    refs = refs[count + 1 + total + extra :]
    far_ref, own_ref = refs[:2]
    dsts, refs = refs[2 : 2 + total], refs[2 + total :]
    sent_ref, came_ref, near_sems, joined_ref = refs[:4]
    step = pl.program_id(0)
    rows, quarter = far_ref.shape
    start = 0
    for value in values:
        joined_ref[:, start : start + value.shape[1]] = value[...]
        start += value.shape[1]
    dp, own = lax.axis_index("dp"), lax.axis_index("head")
    near = (dp, own ^ 1)
    peers, copies = make_moves(moves, srcs, dsts, *refs[4:]) if moves else ([], [])

    @pl.when(step == 0)
    def _():
        greet(peers if near_in(moves) else [near] + peers)
        for copy in copies:
            copy.start()

    def product(k):
        at = pl.ds(pl.multiple_of((own ^ k) * quarter, 128), quarter)
        return dot_nt(joined_ref[...], weight_ref[at, :])

    def near_copy(block):
        return pltpu.make_async_remote_copy(
            src_ref=sent_ref.at[block],
            dst_ref=came_ref.at[block],
            send_sem=near_sems.at[0, block],
            recv_sem=near_sems.at[1, block],
            device_id=near,
            device_id_type=MESH,
        )

    @pl.when(step < many)
    def _():
        sent_ref[step, :, :quarter] = product(3).astype(BF16)
        sent_ref[step, :, quarter:] = product(1).astype(BF16)
        near_copy(step).start()

    @pl.when(step >= many)
    def _():
        block = step - many
        far, mine = product(2), product(0)
        near_copy(block).wait_recv()
        far_ref[...] = (far + came_ref[block, :, :quarter].astype(F32)).astype(BF16)
        own_ref[...] = (mine + came_ref[block, :, quarter:].astype(F32)).astype(BF16)

    @pl.when(step == 2 * many - 1)
    def _():
        for block in range(many):
            near_copy(block).wait_send()
        for copy in copies:
            copy.wait()


def near_in(moves):
    return any(move[0] == "spread" and move[1] == "head" for move in moves)


def run_pieces(values, weight, quarter, name, moves, moved, number, after=()):
    rows = values[0].shape[0]
    step = 512
    many = rows // step
    anywhere = pl.BlockSpec(memory_space=pl.ANY)
    specs = [pl.BlockSpec((step, v.shape[1]), lambda i: (lax.rem(i, many), 0)) for v in values]
    specs.append(pl.BlockSpec(weight.shape, lambda i: (0, 0)))
    return pl.pallas_call(
        functools.partial(pieces_kernel, len(values), many, tuple(moves), len(after)),
        grid=(2 * many,),
        in_specs=specs + [anywhere] * (len(moves) + len(after)),
        out_specs=[pl.BlockSpec((step, quarter), lambda i: (jnp.maximum(i - many, 0), 0))] * 2 + [anywhere] * len(moves),
        out_shape=[jax.ShapeDtypeStruct((rows, quarter), BF16)] * 2 + move_outs(moves, moved),
        scratch_shapes=[pltpu.VMEM((many, step, 2 * quarter), BF16)] * 2 + [pltpu.SemaphoreType.DMA((2, many)), pltpu.VMEM((step, weight.shape[1]), BF16)] + move_scratch(moves, moved),
        compiler_params=params("arbitrary", number=number),
        cost_estimate=pl.CostEstimate(flops=LIGHT, bytes_accessed=LIGHT, transcendentals=0),
        name=name,
    )(*values, weight, *moved, *after)


def second_bits(step, last, paired, came, kept, holds, halves, quarters, bit_sems, load_sems):
    me, head = lax.axis_index("dp"), lax.axis_index("head")
    side, mid = me & 1, (me >> 1) & 1
    own = [paired[0].at[:, :, side], paired[1].at[:, mid]]
    loads = [pltpu.make_async_copy(own[i], holds[i], load_sems.at[0, i]) for i in range(2)]
    loads += [pltpu.make_async_copy(came[i], halves[i], load_sems.at[1, i]) for i in range(2)]
    picks, peers = (mid, side), ((me ^ 2, head), (me ^ 1, head))
    sends = [
        pltpu.make_async_remote_copy(
            src_ref=holds[i].at[:, 1 - picks[i]],
            dst_ref=quarters[i],
            send_sem=bit_sems.at[0, i],
            recv_sem=bit_sems.at[1, i],
            device_id=peers[i],
            device_id_type=MESH,
        )
        for i in range(2)
    ]

    @pl.when(step == 0)
    def _():
        for copy in loads:
            copy.start()
        greet(peers)
        for copy in loads:
            copy.wait()
        for i in range(2):
            for j in range(holds[i].shape[0]):
                for k in range(2):
                    holds[i][j, k] = (holds[i][j, k].astype(F32) + halves[i][j, k].astype(F32)).astype(BF16)
            sends[i].start()

    @pl.when(step == last)
    def _():
        for i in range(2):
            sends[i].wait()
            for j in range(holds[i].shape[0]):
                kept[i][j] = (holds[i][j, picks[i]].astype(F32) + quarters[i][j].astype(F32)).astype(BF16)


def grads_kernel(count, parts, extra, reduce, *refs):
    lefts, rights = refs[:count], refs[count : 2 * count]
    paired, came = refs[2 * count : 2 * count + 2], refs[2 * count + 2 : 2 * count + 4]
    refs = refs[2 * count + extra + (4 if reduce else 0) :]
    outs, refs = refs[:count], refs[count:]
    step = pl.program_id(0)
    if reduce:
        second_bits(step, count * parts - 1, paired, came, refs[0:2], refs[2:4], refs[4:6], refs[6:8], refs[8], refs[9])
    for which in range(count):

        @pl.when((step >= which * parts) & (step < (which + 1) * parts))
        def _():
            out = lax.dot_general(lefts[which][...], rights[which][...], (((0,), (0,)), ((), ())), preferred_element_type=F32)
            outs[which][...] = out.astype(BF16)


def run_grads(pairs, name, paired=(), came=(), number=0, after=()):
    rows, deep = pairs[0][0].shape
    step = 512
    parts = deep // step
    count = len(pairs)
    anywhere = pl.BlockSpec(memory_space=pl.ANY)
    into = lambda which: lambda i: jnp.clip(i - which * parts, 0, parts - 1)
    specs = [pl.BlockSpec((rows, step), lambda i, at=into(w): (0, at(i))) for w in range(count)]
    specs += [pl.BlockSpec(right.shape, lambda i: (0, 0)) for _, right in pairs]
    kept = [(p.shape[0], p.shape[3], p.shape[4]) for p in paired]
    twice = [pltpu.VMEM((m, 2, r, c), BF16) for m, r, c in kept]
    sems = pltpu.SemaphoreType.DMA
    return pl.pallas_call(
        functools.partial(grads_kernel, count, parts, len(after), bool(paired)),
        grid=(count * parts,),
        in_specs=specs + [anywhere] * (len(paired) + len(came) + len(after)),
        out_specs=[pl.BlockSpec((step, right.shape[1]), lambda i, at=into(w): (at(i), 0)) for w, (_, right) in enumerate(pairs)]
        + [pl.BlockSpec(shape, lambda i: (0, 0, 0)) for shape in kept],
        out_shape=[jax.ShapeDtypeStruct((deep, right.shape[1]), BF16) for _, right in pairs] + [jax.ShapeDtypeStruct(shape, BF16) for shape in kept],
        scratch_shapes=twice + twice + [pltpu.VMEM(shape, BF16) for shape in kept] + ([sems((2, 2)), sems((2, 2))] if paired else []),
        compiler_params=params("arbitrary", number=number),
        cost_estimate=pl.CostEstimate(flops=LIGHT, bytes_accessed=LIGHT, transcendentals=0),
        name=name,
    )(*[left for left, _ in pairs], *[right for _, right in pairs], *paired, *came, *after)


def last_kernel(moves, *refs):
    count = len(moves)
    srcs, thin_ref, wide_ref, half_ref = refs[:count], *refs[count : count + 3]
    refs = refs[count + 3 :]
    dsts, thin_out, wide_out = refs[:count], refs[count], refs[count + 1]
    thin_own, thin_came, thin_line, wide_own, wide_came, wide_line, load_sems, pair_sems, sems, local_sems = refs[count + 2 :]
    me, head = lax.axis_index("dp"), lax.axis_index("head")
    side, high = me & 1, me >> 1
    many = thin_own.shape[0]
    peers, copies = make_moves(moves, srcs, dsts, sems, local_sems)

    def remote(src, dst, which, slot, peer):
        return pltpu.make_async_remote_copy(
            src_ref=src,
            dst_ref=dst,
            send_sem=pair_sems.at[0, which, slot],
            recv_sem=pair_sems.at[1, which, slot],
            device_id=(peer, head),
            device_id_type=MESH,
        )

    def blocks(own, line, which):
        return [remote(own.at[high ^ j], line.at[j - 1], which, j, me ^ (2 * j)) for j in range(1, many)]

    half = remote(thin_ref.at[:, 1 - side], thin_came, 0, 0, me ^ 1)
    thin_blocks, wide_blocks = blocks(thin_own, thin_line, 0), blocks(wide_own, wide_line, 1)
    loads = [
        pltpu.make_async_copy(wide_ref.at[:, side], wide_own, load_sems.at[0]),
        pltpu.make_async_copy(half_ref, wide_came, load_sems.at[1]),
        pltpu.make_async_copy(thin_ref.at[:, side], thin_own, load_sems.at[2]),
    ]
    for copy in loads:
        copy.start()
    greet(peers)
    half.start()
    for copy in copies:
        copy.start()
    for copy in loads:
        copy.wait()
    for j in range(many):
        wide_own[j] = (wide_own[j].astype(F32) + wide_came[j].astype(F32)).astype(BF16)
    for copy in wide_blocks:
        copy.start()
    half.wait()
    for j in range(many):
        thin_own[j] = (thin_own[j].astype(F32) + thin_came[j].astype(F32)).astype(BF16)
    for copy in thin_blocks:
        copy.start()
    for copy in wide_blocks + thin_blocks:
        copy.wait()
    thin, wide = thin_own[high].astype(F32), wide_own[high].astype(F32)
    for j in range(many - 1):
        thin, wide = thin + thin_line[j].astype(F32), wide + wide_line[j].astype(F32)
    thin_out[...] = thin
    wide_out[...] = wide
    for copy in copies:
        copy.wait()


def run_last(moves, values, thin, wide, half, number):
    many, _, block, slim = thin.shape
    broad = wide.shape[3]
    anywhere = pl.BlockSpec(memory_space=pl.ANY)
    inside = pl.BlockSpec(memory_space=pltpu.VMEM)
    space = lambda count, columns: pltpu.VMEM((count, block, columns), BF16)
    sems = pltpu.SemaphoreType.DMA
    return pl.pallas_call(
        functools.partial(last_kernel, tuple(moves)),
        in_specs=[anywhere] * (len(moves) + 3),
        out_specs=[anywhere] * len(moves) + [inside] * 2,
        out_shape=move_outs(moves, values) + [jax.ShapeDtypeStruct((block, slim), F32), jax.ShapeDtypeStruct((block, broad), F32)],
        scratch_shapes=[space(many, slim), space(many, slim), space(many - 1, slim), space(many, broad), space(many, broad), space(many - 1, broad)]
        + [sems((3,)), sems((2, 2, many))]
        + move_scratch(moves, values),
        compiler_params=pltpu.CompilerParams(collective_id=number, has_side_effects=True, vmem_limit_bytes=LIMIT),
        name="last_exchange",
    )(*values, thin, wide, half)


def row_forward(size, quarter, own_ref, full_ref, sems):
    me, own = lax.axis_index("dp"), lax.axis_index("head")
    columns = lambda head: pl.ds(pl.multiple_of(head * quarter, 128), quarter)

    def copy(src, dst, stage, k, head):
        return pltpu.make_async_remote_copy(
            src_ref=src, dst_ref=dst, send_sem=sems.at[0, stage, k], recv_sem=sems.at[1, stage, k], device_id=(me, head), device_id_type=MESH
        )

    def source(k):
        return full_ref.at[me ^ k, :, columns(own)] if own_ref is None else own_ref.at[me ^ k]

    def far(k):
        return copy(source(k), full_ref.at[me ^ k, :, columns(own)], 0, k, own ^ 2)

    def near(k):
        return copy(source(k), full_ref.at[me ^ k, :, columns(own)], 1, k, own ^ 1)

    def back(k):
        block = full_ref.at[me ^ k, :, columns(own ^ 2)]
        return copy(block, block, 2, k, own ^ 1)

    return far, near, back


def shard_spread(src, dst, across_sems, side_sems):
    me, own = lax.axis_index("dp"), lax.axis_index("head")

    def copy(a, b, sems, part, j, peer):
        return pltpu.make_async_remote_copy(
            src_ref=a, dst_ref=b, send_sem=sems.at[0, part, j], recv_sem=sems.at[1, part, j], device_id=(peer, own), device_id_type=MESH
        )

    def across(part, j):
        return copy(src.at[part], dst.at[me, part], across_sems, part, j, me ^ (2 * j))

    def side(part, j):
        here = dst.at[me ^ (2 * j), part]
        return copy(src.at[part] if j == 0 else here, here, side_sems, part, j, me ^ 1)

    return across, side


def entry_kernel(parts, order_ref, x_ref, g_ref, zx_ref, rest_ref, fx_ref, fg_ref, fw_ref, row_sems, x_sems, g_sems, line_sems, side_sems, local_sems, land, ready, picks, w_held):
    size, block, quarter = x_ref.shape
    line = size // 2
    me, own = lax.axis_index("dp"), lax.axis_index("head")
    spot = me >> 1
    mine = pl.ds(pl.multiple_of(own * quarter, 128), quarter)
    sources, fulls = (x_ref, g_ref), (fx_ref, fg_ref)
    forwards = [row_forward(size, quarter, ready.at[i], fulls[i], sems) for i, sems in enumerate((x_sems, g_sems))]

    def remote(src, dst, sems, slot, peer):
        return pltpu.make_async_remote_copy(
            src_ref=src, dst_ref=dst, send_sem=sems.at[(0,) + slot], recv_sem=sems.at[(1,) + slot], device_id=(peer, own), device_id_type=MESH
        )

    def rows(which, k):
        return remote(sources[which].at[me ^ k], land.at[which, me], row_sems, (which, k), me ^ k)

    def along(way, part, j):
        sign = 1 - 2 * way
        origin = jnp.clip(me - sign * 2 * (j - 1), 0, size - 1)
        peer = jnp.clip(me + sign * 2, 0, size - 1)
        here = fw_ref.at[origin, part]
        return remote(w_held.at[part] if j == 1 else here, here, line_sems, (way, part, j - 1), peer)

    def came(way, part, j):
        sign = 1 - 2 * way
        here = fw_ref.at[jnp.clip(me - sign * 2 * j, 0, size - 1), part]
        return remote(here, here, line_sems, (way, part, j - 1), me)

    def side(way, part, j):
        sign = 1 - 2 * way
        here = fw_ref.at[jnp.clip(me - sign * 2 * j, 0, size - 1), part]
        return remote(w_held.at[part] if j == 0 else here, here, side_sems, (way, part, j), me ^ 1)

    def goes_on(way):
        return spot < line - 1 if way == 0 else spot > 0

    def arrives(way, j):
        return spot >= j if way == 0 else spot < line - j

    into = [pltpu.make_async_copy(sources[i].at[me], land.at[i, me], local_sems.at[i]) for i in range(2)]
    edge = zx_ref.shape[2]
    into.append(pltpu.make_async_copy(zx_ref, w_held.at[:, :, pl.ds(0, edge)], local_sems.at[2]))
    into.append(pltpu.make_async_copy(rest_ref, w_held.at[:, :, pl.ds(edge, rest_ref.shape[2])], local_sems.at[6]))
    held = [pltpu.make_async_copy(ready.at[i], fulls[i].at[:, :, mine], local_sems.at[3 + i]) for i in range(2)]
    held.append(pltpu.make_async_copy(w_held, fw_ref.at[me], local_sems.at[5]))
    for copy in into:
        copy.start()
    greet([(me ^ k, own) for k in range(1, size)] + [(me, own ^ 1), (me, own ^ 2)])
    order = turn_order(size)
    for k in order:
        rows(0, k).start()
    for copy in into:
        copy.wait()
    for part in range(parts):
        side(0, part, 0).start()
    held[2].start()
    total = size * block
    lane = lax.broadcasted_iota(jnp.int32, (T, T), 1).astype(F32)

    def pick(i, carry):
        wanted = to_col(order_ref[i].astype(F32))
        at = pl.ds(pl.multiple_of(i * T, T), T)
        for j in range(total // T):
            picks[at, j * T : j * T + T] = (wanted == lane + float(T * j)).astype(F32).astype(BF16)
        return carry

    lax.fori_loop(0, total // T, pick, 0)

    def arrange(which):
        step = min(512, total)
        for i in range(total // step):
            value = dot(picks[i * step : (i + 1) * step, :], land[which].reshape(total, quarter)).astype(BF16)
            ready[which, i * step // block : (i + 1) * step // block] = value.reshape(step // block, block, quarter)
        held[which].start()
        far, near, _ = forwards[which]
        for k in range(size):
            far(k).start()
            near(k).start()

    def backs(which, some):
        far, _, back = forwards[which]
        for k in some:
            far(k).wait_recv()
            back(k).start()

    for k in order:
        rows(0, k).wait_recv()
    for k in order:
        rows(1, k).start()
    arrange(0)
    for k in order:
        rows(1, k).wait_recv()
    for way in range(2):

        @pl.when(goes_on(way))
        def _():
            for part in range(parts):
                along(way, part, 1).start()

    arrange(1)
    backs(0, range(size))
    for j in range(1, line):
        for part in range(parts):
            if j == line - 1:
                backs(1, range(part * size // parts, (part + 1) * size // parts))
            for way in range(2):

                @pl.when(arrives(way, j))
                def _():
                    came(way, part, j).wait_recv()
                    side(way, part, j).start()

                if j + 1 < line:

                    @pl.when(arrives(way, j) & goes_on(way))
                    def _():
                        along(way, part, j + 1).start()

    for copy in held:
        copy.wait()
    for which in range(2):
        far, near, back = forwards[which]
        for k in range(size):
            near(k).wait()
            back(k).wait()
            far(k).wait_send()
            if k:
                rows(which, k).wait_send()
    for part in range(parts):
        side(0, part, 0).wait()
        for way in range(2):

            @pl.when(goes_on(way))
            def _():
                along(way, part, 1).wait_send()

            for j in range(1, line):

                @pl.when(arrives(way, j))
                def _():
                    side(way, part, j).wait()

                if j + 1 < line:

                    @pl.when(arrives(way, j) & goes_on(way))
                    def _():
                        along(way, part, j + 1).wait_send()


PARTS = 4


def cut_shard(w):
    return w.reshape(PARTS, w.shape[0] // PARTS, w.shape[1])


def full_shape(size, w):
    return jax.ShapeDtypeStruct((size, PARTS, w.shape[0] // PARTS, w.shape[1]), BF16)


def run_entry(order, tokens, cotangent, w_zx, w_rest, number):
    size = lax.axis_size("dp")
    shard, wide = w_zx.shape[0], w_zx.shape[1] + w_rest.shape[1]
    rows, quarter = tokens.shape
    block = rows // size
    line = size // 2
    anywhere = pl.BlockSpec(memory_space=pl.ANY)
    sems = pltpu.SemaphoreType.DMA
    full = jax.ShapeDtypeStruct((size, block, quarter * 4), BF16)
    came_x, came_g, came_w = pl.pallas_call(
        functools.partial(entry_kernel, PARTS),
        in_specs=[pl.BlockSpec(memory_space=pltpu.VMEM)] + [anywhere] * 4,
        out_specs=[anywhere] * 3,
        out_shape=[full, full, jax.ShapeDtypeStruct((size, PARTS, shard // PARTS, wide), BF16)],
        scratch_shapes=[
            sems((2, 2, size)),
            sems((2, 3, size)),
            sems((2, 3, size)),
            sems((2, 2, PARTS, line)),
            sems((2, 2, PARTS, line)),
            sems((7,)),
            pltpu.VMEM((2, size, block, quarter), BF16),
            pltpu.VMEM((2, size, block, quarter), BF16),
            pltpu.VMEM((rows, rows), BF16),
            pltpu.VMEM((PARTS, shard // PARTS, wide), BF16),
        ],
        compiler_params=pltpu.CompilerParams(collective_id=number, has_side_effects=True, vmem_limit_bytes=LIMIT),
        name="entry",
    )(order, tokens.reshape(size, block, quarter), cotangent.reshape(size, block, quarter), cut_shard(w_zx), cut_shard(w_rest))
    return came_x.reshape(rows, quarter * 4), came_g.reshape(rows, quarter * 4), came_w.reshape(size * shard, wide)


def mm(a, b, contract, kind):
    return lax.dot_general(a, b, (contract, ((), ())), preferred_element_type=F32).astype(kind)


def body(tokens, cotangent, order, lengths, norm_gain, w_zx, w_bc, w_dt, w_out, conv_x, conv_bc, head_params, gate_gain):
    rows, quarter = tokens.shape
    heads = head_params.shape[1]
    width = heads * HEAD
    me = lax.axis_index("head").astype(jnp.int32).reshape(1)
    size = lax.axis_size("dp")
    here = lax.axis_index("dp")
    all_width = width * lax.axis_size("head")
    deep = quarter * lax.axis_size("head")
    own_w = w_zx.shape[0]
    arrange = order.reshape(rows // T, 1, T)

    rest = jnp.concatenate([w_bc, w_dt, norm_gain[:, None], jnp.zeros((own_w, 127 - heads), BF16)], axis=1)
    blocks = lambda value: value.reshape(size, rows // size, quarter)
    full_x, full_g, w_in = run_entry(arrange, tokens, cotangent, w_zx.reshape(own_w, 2 * width), rest, 1)
    normed, inv_one, u_zx, u_bd, gain, w_o = run_project(heads, full_x, w_in, w_out, 2)

    gated = gate_gain.reshape(1, width)
    hp = jnp.pad(head_params, ((0, 5), (0, 128 - heads)))
    positions = lax.broadcasted_iota(jnp.int32, (lengths.shape[0], LEN), 1)
    mask = (positions < lengths[:, None]).astype(F32).reshape(rows // T, 1, T)

    y, ss, c, cb, st, w_o = run_forward(heads, u_zx, u_bd, conv_x, conv_bc, hp, w_out, w_o, 3)
    w_o = w_o.reshape(deep, width)
    yg, dz, dy, gg, rd_z = run_gate(all_width, full_g, w_o, y, u_zx, gated, mask, ss, 4)

    def total(kept, came, shift):
        own = lax.dynamic_index_in_dim(kept, here >> shift, 0, keepdims=False)
        return own.astype(F32) + jnp.sum(came.astype(F32), axis=0)

    def pairs(grads):
        return grads.reshape(size // 2, 2, own_w, grads.shape[1])

    def fours(grads):
        return grads.reshape(size // 4, 2, -1, own_w, grads.shape[-1])

    scan = functools.partial(run_backward, heads)
    shared = (dy, u_zx, c, cb, u_bd, st, conv_x, conv_bc, hp)
    out_far, out_own = run_pieces([yg], w_o, quarter, "branch_pieces", [], [], 5)
    out_arrived = lax.ppermute(out_far, "head", [(i, i ^ 2) for i in range(lax.axis_size("head"))])
    grad_o, grad_z = run_grads([(full_g, yg), (normed, dz)], "gate_grads", after=[out_far])
    grad_o, grad_z = pairs(grad_o), fours(grad_z)
    def other_half(paired, bit):
        send = lax.dynamic_index_in_dim(paired, 1 - ((here >> bit) & 1), 1, keepdims=False)
        return send, lax.ppermute(send, "dp", [(i, i ^ (1 << bit)) for i in range(size)])

    send_o, came_o = other_half(grad_o, 0)
    send_z, came_z = other_half(grad_z, 1)
    *back0, gx0, gb0, gh0 = scan(0, *shared, (), [], [], 0, [send_o, send_z])
    sent_out = run_home(me, arrange, [out_own, out_arrived], None, deep, "home_out", [back0[0], came_o, came_z])
    got_out = lax.all_to_all(sent_out, "dp", split_axis=0, concat_axis=0, tiled=True)
    *back1, gx1, gb1, gh1 = scan(1, *shared, back0, [], [], 0, [sent_out])
    dux, dbd, rd_x = back1
    grad_x, grad_bd, kept_o, kept_z = run_grads(
        [(normed, dux), (normed, dbd)], "scan_grads", [fours(grad_o), grad_z], [came_o.reshape(came_z.shape), came_z], 8
    )
    grad_x, grad_bd = pairs(grad_x), pairs(grad_bd)
    gb = gb0 + gb1
    d_far, d_own, line_o, line_z, came_x2, got_rows, got_gb = run_pieces(
        [dz, dux, dbd],
        w_in,
        quarter,
        "input_pieces",
        [("direct", "dp", 2), ("direct", "dp", 2), ("half", "dp", 0), ("spread", "head"), ("spread", "head")],
        [kept_o, kept_z, grad_x, rd_z + rd_x, gb],
        9,
        [got_out],
    )
    gb = gb[:5] + jnp.sum(got_gb, axis=0)[:5]
    gh = gh0 + gh1
    ends = jnp.concatenate([gb[3], gb[4]] + [gh[i, :32] for i in range(3)] + [jnp.zeros((width - 4 * N - 96,), F32)])
    small = jnp.concatenate([(gx0 + gx1)[:5], gg[:1], jnp.concatenate([gb[0], gb[1], gb[2]])[None], ends[None]], axis=0)
    d_arrived, got_small, grad_bd, grad_x = run_last([("whole", "head", 2), ("spread", "dp")], [d_far, small], grad_bd, grad_x, came_x2, 10)

    sent_back = run_home(me, arrange, [d_own, d_arrived], [normed, inv_one, gain, rd_z, rd_x, got_rows], deep, "home_back")
    got_back = lax.all_to_all(sent_back, "dp", split_axis=0, concat_axis=0, tiled=True)
    final_out = (tokens.astype(F32) + got_out.astype(F32)).astype(BF16)
    final_back = (cotangent.astype(F32) + got_back.astype(F32)).astype(BF16)

    grad_out, grad_z = total(kept_o, line_o, 2), total(kept_z, line_z, 2)
    small = small + jnp.sum(got_small, axis=0)
    grad_zx = jnp.stack([grad_z, grad_x], axis=1)
    of_gain = jnp.sum(grad_z * w_zx[:, 0].astype(F32), axis=1) + jnp.sum(grad_x * w_zx[:, 1].astype(F32), axis=1)
    of_gain = of_gain + jnp.sum(grad_bd[:, : 2 * N] * w_bc.astype(F32), axis=1)
    of_gain = of_gain + jnp.sum(grad_bd[:, 2 * N : 2 * N + heads] * w_dt.astype(F32), axis=1)
    last = jnp.concatenate([grad_bd[:, : 2 * N], jnp.broadcast_to(of_gain[:, None], (own_w, 128))], axis=1)
    others, = run_exchange([("spread", "head")], [last], 11)
    last = last + jnp.sum(others, axis=0)
    grad_gain = last[:, 2 * N] / norm_gain.astype(F32)
    gx, gg = small[0:5], small[5]
    gb = jnp.concatenate([small[6].reshape(3, 2 * N), small[7, : 4 * N].reshape(2, 2 * N)], axis=0)
    gh = small[7, 4 * N : 4 * N + 96].reshape(3, 32)[:, :heads]
    return (final_out, final_back, grad_gain, grad_zx, last[:, : 2 * N], grad_bd[:, 2 * N : 2 * N + heads], grad_out, gx, gb, gh, gg)


def solution(mesh):
    return jax.shard_map(
        body,
        mesh=mesh,
        in_specs=(
            P("dp", "head"),
            P("dp", "head"),
            P("dp", None),
            P("dp"),
            P("dp"),
            P("dp", None, "head"),
            P("dp", None),
            P("dp", "head"),
            P("dp", "head"),
            P(None, "head"),
            P(),
            P(None, "head"),
            P("head"),
        ),
        out_specs=(
            P("dp", "head"),
            P("dp", "head"),
            P("dp"),
            P("dp", None, "head"),
            P("dp", None),
            P("dp", "head"),
            P("dp", "head"),
            P(None, "head"),
            P(),
            P(None, "head"),
            P("head"),
        ),
        check_vma=False,
    )
```

```python
import functools

import jax
import jax.numpy as jnp
from jax import lax
from jax.experimental import pallas as pl
from jax.experimental.pallas import tpu as pltpu
from jax.sharding import PartitionSpec as P

LEN = 1024
T = 128
N = 128
HEAD = 64
EPS = 1e-05
NEG = -1e30
LIGHT = 1000
LIMIT = 60 * 1024 * 1024
AXES = ("dp", "head")
F32 = jnp.float32
BF16 = jnp.bfloat16


def dot(a, b):
    return lax.dot_general(a, b, (((1,), (0,)), ((), ())), preferred_element_type=F32)


def dot_nt(a, b):
    return lax.dot_general(a, b, (((1,), (1,)), ((), ())), preferred_element_type=F32)


def dot_exact(a, b):
    return lax.dot_general(
        a, b, (((1,), (0,)), ((), ())), preferred_element_type=F32, precision=lax.Precision.HIGHEST
    )


def iotas(rows, cols):
    return (
        lax.broadcasted_iota(jnp.int32, (rows, cols), 0),
        lax.broadcasted_iota(jnp.int32, (rows, cols), 1),
    )


MESH = pl.DeviceIdType.MESH


def greet(peers):
    barrier = pltpu.get_barrier_semaphore()
    for peer in peers:
        pl.semaphore_signal(barrier, inc=1, device_id=peer, device_id_type=MESH)
    pl.semaphore_wait(barrier, len(peers))


def place_of():
    return {name: lax.axis_index(name) for name in AXES}


def move_copies(move, src, dst):
    kind, axis = move[0], move[1]
    place = place_of()
    me = place[axis]

    def peer(flip):
        return tuple(place[name] ^ flip if name == axis else place[name] for name in AXES)

    if kind == "whole":
        return [(peer(move[2]), src, dst)], []
    if kind == "rows":
        return [(peer(move[2]), src.at[pl.ds(move[3], move[4])], dst)], []
    if kind == "half":
        return [(peer(1 << move[2]), src.at[:, 1 - ((me >> move[2]) & 1)], dst)], []
    if kind == "direct":
        high = me >> move[2]
        return [(peer(j << move[2]), src.at[high ^ j], dst.at[j - 1]) for j in range(1, dst.shape[0] + 1)], []
    if kind == "all":
        groups = lax.axis_size("head")
        flips = [divmod(flat, groups) for flat in range(1, dst.shape[0] + 1)]
        return [((place["dp"] ^ f, place["head"] ^ e), src, dst.at[i]) for i, (f, e) in enumerate(flips)], []
    if kind == "spread":
        return [(peer(flip), src, dst.at[flip - 1]) for flip in range(1, dst.shape[0] + 1)], []
    remote = [(peer(k), src.at[me ^ k], dst.at[me]) for k in turn_order(src.shape[0])]
    return remote, [(src.at[me], dst.at[me])]


def turn_order(size):
    return sorted(range(1, size), key=lambda k: (-(k & ~1), k & 1))


def move_shape(move, shape):
    kind = move[0]
    if kind == "rows":
        return (move[4],) + shape[1:]
    if kind == "half":
        return (shape[0],) + shape[2:]
    if kind == "direct":
        return (shape[0] - 1,) + shape[1:]
    if kind == "spread":
        return (lax.axis_size(move[1]) - 1,) + shape
    if kind == "all":
        return (lax.axis_size("dp") * lax.axis_size("head") - 1,) + shape
    return shape


def move_counts(moves, values):
    remote = local = 0
    for move, value in zip(moves, values):
        size = lax.axis_size(move[1])
        world = lax.axis_size("dp") * lax.axis_size("head")
        count = {"direct": value.shape[0] - 1, "spread": size - 1, "turn": size - 1, "all": world - 1}.get(move[0], 1)
        remote, local = remote + count, local + (move[0] == "turn")
    return remote, local


def move_scratch(moves, values):
    remote, local = move_counts(moves, values)
    return [pltpu.SemaphoreType.DMA((2, remote)), pltpu.SemaphoreType.DMA((max(local, 1),))] if moves else []


def move_outs(moves, values):
    return [jax.ShapeDtypeStruct(move_shape(move, value.shape), value.dtype) for move, value in zip(moves, values)]


def make_moves(moves, srcs, dsts, sems, local_sems):
    remote, local = [], []
    for move, src, dst in zip(moves, srcs, dsts):
        here, there = move_copies(move, src, dst)
        remote += here
        local += there
    copies = [
        pltpu.make_async_remote_copy(src_ref=a, dst_ref=b, send_sem=sems.at[0, i], recv_sem=sems.at[1, i], device_id=peer, device_id_type=MESH)
        for i, (peer, a, b) in enumerate(remote)
    ]
    copies += [pltpu.make_async_copy(a, b, local_sems.at[i]) for i, (a, b) in enumerate(local)]
    return move_peers(moves, dsts), copies


def move_peers(moves, dsts):
    flips = {}
    for move, dst in zip(moves, dsts):
        kind, axis = move[0], move[1]
        if kind in ("whole", "rows"):
            own = [move[2]]
        elif kind == "half":
            own = [1 << move[2]]
        elif kind == "direct":
            own = [j << move[2] for j in range(1, dst.shape[0] + 1)]
        elif kind == "all":
            groups = lax.axis_size("head")
            for flat in range(1, dst.shape[0] + 1):
                flips[divmod(flat, groups)] = None
            continue
        elif kind == "spread":
            own = range(1, dst.shape[0] + 1)
        else:
            own = range(1, dst.shape[0])
        for flip in own:
            flips[(flip, 0) if axis == "dp" else (0, flip)] = None
    place = place_of()
    return [(place["dp"] ^ f, place["head"] ^ e) for f, e in flips]


def background(first, last, moves, srcs, dsts, sems, local_sems):
    peers, copies = make_moves(moves, srcs, dsts, sems, local_sems)

    @pl.when(first)
    def _():
        greet(peers)
        for copy in copies:
            copy.start()

    @pl.when(last)
    def _():
        for copy in copies:
            copy.wait()


def exchange_kernel(moves, *refs):
    count = len(moves)
    peers, copies = make_moves(moves, refs[:count], refs[count : 2 * count], refs[2 * count], refs[2 * count + 1])
    greet(peers)
    for copy in copies:
        copy.start()
    for copy in copies:
        copy.wait()


def run_exchange(moves, values, number):
    return pl.pallas_call(
        functools.partial(exchange_kernel, tuple(moves)),
        in_specs=[pl.BlockSpec(memory_space=pl.ANY)] * len(moves),
        out_specs=[pl.BlockSpec(memory_space=pl.ANY)] * len(moves),
        out_shape=move_outs(moves, values),
        scratch_shapes=move_scratch(moves, values),
        compiler_params=pltpu.CompilerParams(collective_id=number, has_side_effects=True, vmem_limit_bytes=LIMIT),
        name="exchange",
    )(*values)


def sigmoid(v):
    return 1.0 / (1.0 + jnp.exp(-v))


def softplus(v):
    return jnp.maximum(v, 0.0) + jnp.log1p(jnp.exp(-jnp.abs(v)))


def to_col(row):
    return jnp.broadcast_to(row, (T, T)).T


def to_row(col):
    return jnp.broadcast_to(col, (T, T)).T[0:1]


def lanes(value, pick):
    return jnp.broadcast_to(value[:, pick : pick + 1], (value.shape[0], 128))


def step_terms(ubd, head_ref, heads):
    fill = jnp.zeros((1, 128 - heads), F32)
    wide_row = lambda i: jnp.concatenate([head_ref[i : i + 1], fill], axis=1)
    row, col = iotas(T, T)
    raw = jnp.where(col < heads, ubd[:, 2 * N :] + wide_row(0), 0.0)
    steps = jnp.where(col < heads, softplus(raw), 0.0)
    rates = -jnp.exp(wide_row(1))
    tril = (row >= col).astype(F32)
    logs = dot_exact(tril, steps * rates)
    return raw, steps, rates, logs


def weight_moves(step, steps, parts, whole, w_ref, fw_ref, across_sems, side_sems, local_sems, w_held):
    line = fw_ref.shape[0] // 2
    me, own = lax.axis_index("dp"), lax.axis_index("head")
    across, side = shard_spread(w_ref, fw_ref, across_sems, side_sems)
    if whole:
        into = pltpu.make_async_copy(w_ref, w_held, local_sems.at[0])
        held = pltpu.make_async_copy(w_held, fw_ref.at[me], local_sems.at[1])

    @pl.when(step == 0)
    def _():
        if whole:
            into.start()
        greet([(me ^ 1, own)] + [(me ^ (2 * j), own) for j in range(1, line)])
        for part in parts:
            side(part, 0).start()
        if whole:
            into.wait()
            held.start()

    for i, part in enumerate(parts):
        begin = i * steps // len(parts)

        @pl.when(step == begin)
        def _():
            for j in range(1, line):
                across(part, j).start()

        @pl.when(step == min(steps - 1, begin + steps // 3 + 2))
        def _():
            for j in range(1, line):
                across(part, j).wait_recv()
                side(part, j).start()

    @pl.when(step == steps - 1)
    def _():
        if whole:
            held.wait()
        for part in parts:
            for j in range(line):
                side(part, j).wait()
                if j:
                    across(part, j).wait_send()


def weight_scratch(size, w):
    sems = pltpu.SemaphoreType.DMA
    return [sems((2, PARTS, size // 2)), sems((2, PARTS, size // 2)), sems((2,)), pltpu.VMEM((PARTS, w.shape[0] // PARTS, w.shape[1]), BF16)]


def forward_kernel(heads, steps, x_ref, z_ref, ubd_ref, par_ref, pbc_ref, head_ref, w_ref, before_ref, y_ref, ss_ref, c_ref, cb_ref, st_ref, fw_ref, ext_x, ext_b, state, *sems):
    weight_moves(pl.program_id(0) * pl.num_programs(1) + pl.program_id(1), steps, range(1, PARTS), False, w_ref, fw_ref, *sems)

    @pl.when(pl.program_id(1) == 0)
    def _():
        ext_x[0:8] = jnp.zeros_like(ext_x[0:8])
        ext_b[0:8] = jnp.zeros_like(ext_b[0:8])
        state[...] = jnp.zeros_like(state)

    def conv(ext, values, taps):
        ext[8 : 8 + T] = values
        total = taps[4:5] + taps[3:4] * values
        for k in range(3):
            total = total + taps[k : k + 1] * ext[5 + k : 5 + k + T]
        ext[0:8] = ext[T : T + 8]
        return total

    row, col = iotas(T, T)
    low = col < HEAD
    low_row = lax.broadcasted_iota(jnp.int32, (1, 128), 1) < HEAD
    causal = row >= col
    ubd = ubd_ref[...]
    c = conv(ext_x, x_ref[...].astype(F32), par_ref)
    c_ref[...] = c.astype(BF16)
    cb = conv(ext_b, ubd[:, : 2 * N], pbc_ref)
    cb_ref[...] = cb
    bc = cb * sigmoid(cb)
    b_rows = bc[:, :N]
    b_t = b_rows.T.astype(BF16)
    b_low, c_low = b_rows.astype(BF16), bc[:, N:].astype(BF16)
    _, steps, _, logs = step_terms(ubd, head_ref, heads)
    logs_t = logs.T
    scores = dot_nt(c_low, b_low)
    entering = state[...].astype(BF16)
    st_ref[0] = entering
    outer = dot(c_low, entering)
    squares = jnp.zeros((T, 128), F32)
    for pair in range(heads // 2):
        span = slice(128 * pair, 128 * pair + 128)
        h0, h1 = 2 * pair, 2 * pair + 1
        log0, log1 = lanes(logs, h0), lanes(logs, h1)
        log_pair = jnp.where(low, log0, log1)
        step_pair = jnp.where(low, lanes(steps, h0), lanes(steps, h1))
        last_pair = log_pair[T - 1 : T]
        skip_pair = jnp.where(low_row, lanes(head_ref[2:3], h0), lanes(head_ref[2:3], h1))
        cp = c[:, span]
        xp = cp * sigmoid(cp)
        xd = xp * step_pair
        m0 = (scores * jnp.exp(jnp.where(causal, log0 - logs_t[h0 : h0 + 1], NEG))).astype(BF16)
        m1 = (scores * jnp.exp(jnp.where(causal, log1 - logs_t[h1 : h1 + 1], NEG))).astype(BF16)
        stacked = jnp.concatenate([jnp.where(low, xd, 0.0).astype(BF16), jnp.where(low, 0.0, xd).astype(BF16)], axis=0)
        y = dot(jnp.concatenate([m0, m1], axis=1), stacked)
        y = y + jnp.exp(log_pair) * outer[:, span] + skip_pair * xp
        tail = (jnp.exp(last_pair - log_pair) * xd).astype(BF16)
        state[:, span] = jnp.exp(last_pair) * state[:, span] + dot(b_t, tail)
        y_ref[:, span] = y.astype(BF16)
        zp = z_ref[:, span].astype(F32)
        w = y * zp * sigmoid(zp)
        squares = squares + w * w
    ss_ref[0] = to_row(jnp.sum(squares, axis=1, keepdims=True))


def project_kernel(heads, steps, x_ref, w_ref, shard_ref, out_ref, inv_ref, uzx_ref, ubd_ref, gain_ref, fw_ref, *sems):
    deep, width = x_ref.shape[1], 2 * heads * HEAD
    weight_moves(pl.program_id(0), steps, range(1), True, shard_ref, fw_ref, *sems)

    @pl.when(pl.program_id(0) == 0)
    def _():
        for j in range(deep // T):
            span = slice(j * T, j * T + T)
            gain_ref[:, span] = jnp.broadcast_to(w_ref[span, width + 2 * N : width + 3 * N].astype(F32).T[heads : heads + 1], (8, T))

    x = x_ref[...].astype(F32)
    inv = lax.rsqrt(jnp.sum(x * x, axis=1, keepdims=True) / deep + EPS)
    normed = (x * inv * gain_ref[0:1]).astype(BF16)
    out_ref[...] = normed
    for part in range(x.shape[0] // T):
        inv_ref[part] = to_row(inv[part * T : part * T + T])
    uzx_ref[...] = dot(normed, w_ref[:, :width]).astype(BF16)
    ubd_ref[...] = dot(normed, w_ref[:, width:])


def home_kernel(last, deep, me_ref, order_ref, a_ref, b_ref, *refs):
    out_ref, held_ref = refs[-2:]
    step = pl.program_id(0)
    many = held_ref.shape[0] // a_ref.shape[0]
    size = a_ref.shape[0]

    @pl.when(step < many)
    def _():
        value = a_ref[...].astype(F32) + b_ref[...].astype(F32)
        if last:
            normed_ref, inv_ref, gain_ref, rdz_ref, rdx_ref, more_ref = refs[:6]
            gain = gain_ref[0:1]
            hat = normed_ref[...].astype(F32) / gain
            parts = []
            for part in range(size // T):
                inv_row = inv_ref[part]
                dots = rdz_ref[part] + rdx_ref[part] + more_ref[0, part] + more_ref[1, part] + more_ref[2, part]
                rows = slice(part * T, part * T + T)
                inv = to_col(inv_row)[:, 0:1]
                mean = to_col(dots / deep)[:, 0:1]
                parts.append(inv * (gain * value[rows] - hat[rows] * mean))
            value = jnp.concatenate(parts, axis=0)
        held_ref[pl.ds(pl.multiple_of(step * size, size), size), :] = value.astype(BF16)

    @pl.when(step >= many)
    def _():
        base = ((step - many) * size).astype(F32)
        row = lax.broadcasted_iota(jnp.int32, (size, T), 0).astype(F32) + base
        picks = jnp.concatenate([(row == order_ref[j].astype(F32)).astype(F32).astype(BF16) for j in range(order_ref.shape[0])], axis=1)
        out_ref[...] = dot(picks, held_ref[...]).astype(BF16)


def gate_kernel(width, moves, g_ref, wo_ref, y_ref, z_ref, gain_ref, mask_ref, ss_ref, yg_ref, dz_ref, dy_ref, gg_ref, rd_ref, held, co_held, got_ss, got_co, sems, local_sems):
    step = pl.program_id(0)
    many = pl.num_programs(0) // 2
    size = y_ref.shape[0]
    parts = size // T
    others = got_ss.shape[0]
    peers, copies = make_moves(moves, (ss_ref, co_held), (got_ss, got_co), sems, local_sems)
    gain = gain_ref[...][None]

    @pl.when(step == 0)
    def _():
        gg_ref[...] = jnp.zeros_like(gg_ref)
        greet(peers)
        for copy in copies[:others]:
            copy.start()

    @pl.when(step < many)
    def _():
        dyn = dot(g_ref[...], wo_ref[...])
        for part in range(parts):
            rows = slice(part * T, part * T + T)
            mask = to_col(mask_ref[part])[:, 0:1]
            own = dyn[rows] * mask
            held[step, rows] = own.astype(BF16)
            z = z_ref[rows].astype(F32)
            w = y_ref[rows].astype(F32) * z * sigmoid(z)
            co_held[step * parts + part] = to_row(jnp.sum(own * w * gain, axis=1, keepdims=True))

    @pl.when(step == many - 1)
    def _():
        for copy in copies[others:]:
            copy.start()

    @pl.when(step == many)
    def _():
        for copy in copies:
            copy.wait()

    @pl.when(step >= many)
    def _():
        for part in range(parts):
            rows = slice(part * T, part * T + T)
            block = step - many
            here = block * parts + part
            ss, co = ss_ref[here], co_held[here]
            for other in range(others):
                ss, co = ss + got_ss[other, here], co + got_co[other, here]
            mask = to_col(mask_ref[part])[:, 0:1]
            inv_row = lax.rsqrt(ss / width + EPS)
            inv = to_col(inv_row)[:, 0:1]
            cube = to_col(inv_row * inv_row * inv_row * (co / width))[:, 0:1]
            y = y_ref[rows].astype(F32)
            z = z_ref[rows].astype(F32)
            dyn = held[block, rows].astype(F32)
            s = sigmoid(z)
            act = z * s
            w = y * act
            wi = w * inv
            yg_ref[rows] = (wi * gain * mask).astype(BF16)
            gg_ref[0:1] += jnp.sum(dyn * wi, axis=0, keepdims=True)
            dw = inv * gain * dyn - w * cube
            dy_ref[rows] = (dw * act).astype(BF16)
            dz = dw * y * (s * (1.0 + z * (1.0 - s)))
            dz_ref[rows] = dz.astype(BF16)
            rd_ref[part] = to_row(jnp.sum(dz * z, axis=1, keepdims=True))


def backward_kernel(heads, extra, moves, dy_ref, x_ref, c_ref, cb_ref, ubd_ref, st_ref, par_ref, pbc_ref, head_ref, *refs):
    count = len(moves)
    srcs, refs = refs[:count], refs[count + extra :]
    dx_ref, dbd_ref, rd_ref, gx_ref, gb_ref, gh_ref = refs[:6]
    dsts, refs = refs[6 : 6 + count], refs[6 + count :]
    d_state, ext_x, ext_b, rows_ref, prod, edy_ref, tail_ref = refs[:7]
    if moves:
        began = (pl.program_id(0) == 0) & (pl.program_id(1) == 0)
        ended = (pl.program_id(0) == pl.num_programs(0) - 1) & (pl.program_id(1) == pl.num_programs(1) - 1)
        background(began, ended, moves, srcs, dsts, *refs[7:])
    first = (pl.program_id(0) == 0) & (pl.program_id(1) == 0)

    @pl.when(first)
    def _():
        gx_ref[...] = jnp.zeros_like(gx_ref)
        gb_ref[...] = jnp.zeros_like(gb_ref)
        gh_ref[...] = jnp.zeros_like(gh_ref)
        rows_ref[...] = jnp.zeros_like(rows_ref)

    @pl.when(pl.program_id(1) == 0)
    def _():
        ext_x[T : T + 8] = jnp.zeros_like(ext_x[T : T + 8])
        ext_b[T : T + 8] = jnp.zeros_like(ext_b[T : T + 8])
        d_state[...] = jnp.zeros_like(d_state)

    row, col = iotas(T, T)
    low = col < HEAD
    low_row = lax.broadcasted_iota(jnp.int32, (1, 128), 1) < HEAD
    upto = col >= row
    below = row < col
    reach = (row >= col).astype(BF16)
    ubd = ubd_ref[...]
    raw, steps, rates, logs = step_terms(ubd, head_ref, heads)
    logs_t = logs.T
    cb = cb_ref[...]
    sb = sigmoid(cb)
    bc = cb * sb
    b_low, c_low = bc[:, :N].astype(BF16), bc[:, N:].astype(BF16)
    c_t = bc[:, N:].T.astype(BF16)
    scores = dot_nt(b_low, c_low)
    entering = st_ref[0]
    outer = dot(c_low, entering)
    ds_low = d_state[...].astype(BF16)
    back = dot(b_low, ds_low)
    d_scores = jnp.zeros((T, T), F32)
    skip_parts, closing_parts = [], []
    for pair in range(heads // 2):
        span = slice(128 * pair, 128 * pair + 128)
        h0, h1 = 2 * pair, 2 * pair + 1
        log0, log1 = lanes(logs, h0), lanes(logs, h1)
        log_pair = jnp.where(low, log0, log1)
        step_pair = jnp.where(low, lanes(steps, h0), lanes(steps, h1))
        last_pair = log_pair[T - 1 : T]
        skip_pair = jnp.where(low_row, lanes(head_ref[2:3], h0), lanes(head_ref[2:3], h1))
        cp = c_ref[:, span].astype(F32)
        sp = sigmoid(cp)
        xp = cp * sp
        xd = xp * step_pair
        dy_low = dy_ref[:, span]
        dy = dy_low.astype(F32)
        decay0 = jnp.exp(jnp.where(upto, logs_t[h0 : h0 + 1] - log0, NEG))
        decay1 = jnp.exp(jnp.where(upto, logs_t[h1 : h1 + 1] - log1, NEG))
        m0, m1 = scores * decay0, scores * decay1
        zero = jnp.zeros_like(dy_low)
        x_stack = jnp.concatenate([jnp.where(low, xd, 0.0).astype(BF16), jnp.where(low, 0.0, xd).astype(BF16)], axis=0)
        dm = dot_nt(x_stack, dy_low)
        dm0, dm1 = dm[:T], dm[T:]
        d_scores = d_scores + dm0 * decay0 + dm1 * decay1
        dy_stack = jnp.concatenate([jnp.where(low, dy, 0.0).astype(BF16), jnp.where(low, 0.0, dy).astype(BF16)], axis=0)
        dxd = dot(jnp.concatenate([m0.astype(BF16), m1.astype(BF16)], axis=1), dy_stack)
        flow = jnp.concatenate([(dm0 * m0).astype(BF16), (dm1 * m1).astype(BF16)], axis=0)
        later = dot(flow, reach)
        rows_ref[h0 : h0 + 1] = jnp.sum(jnp.where(below, later[:T], 0.0), axis=0, keepdims=True)
        rows_ref[h1 : h1 + 1] = jnp.sum(jnp.where(below, later[T:], 0.0), axis=0, keepdims=True)
        grow = jnp.exp(log_pair)
        tail = jnp.exp(last_pair - log_pair)
        from_state = tail * back[:, span]
        dxd = dxd + from_state
        edy = grow * dy
        prod[0:T, span] = (edy * outer[:, span]).astype(BF16)
        prod[T : 2 * T, span] = (from_state * xd).astype(BF16)
        prod[2 * T : 3 * T, span] = (xp * dxd).astype(BF16)
        skip_parts.append(jnp.sum(xp * dy, axis=0, keepdims=True))
        edy_low = edy.astype(BF16)
        edy_ref[:, span] = edy_low
        tail_ref[:, span] = (tail * xd).astype(BF16)
        old = d_state[:, span]
        closing = jnp.exp(last_pair)
        closing_parts.append(closing * jnp.sum(old * entering[:, span].astype(F32), axis=0, keepdims=True))
        d_state[:, span] = closing * old + dot(c_t, edy_low)
        dx = dxd * step_pair + skip_pair * dy
        ext_x[0:T, span] = dx * (sp * (1.0 + cp * (1.0 - sp)))
    d_low = d_scores.astype(BF16)
    d_b = dot_nt(tail_ref[...], ds_low) + dot(d_low, c_low)
    d_c = dot_nt(edy_ref[...], entering) + dot(d_scores.T.astype(BF16), b_low)
    width = heads * HEAD
    lane_row, lane_col = iotas(width, 128)
    member = (lane_row // HEAD == lane_col).astype(BF16)
    sums = dot(prod[...], member)
    skip_all = jnp.concatenate(skip_parts, axis=1)
    closing_all = jnp.concatenate(closing_parts, axis=1)
    fill = jnp.zeros((6, width), F32)
    few = dot_exact(jnp.concatenate([skip_all, closing_all, fill], axis=0), member.astype(F32))
    d_logs = dot(upto.astype(BF16), sums[:T].astype(BF16)) + dot((col < row).astype(BF16), sums[T : 2 * T].astype(BF16))
    d_logs = d_logs + rows_ref[...].T + few[1:2]
    d_steps = sums[2 * T :] + rates * d_logs
    d_raw = jnp.where(col < heads, d_steps * sigmoid(raw), 0.0)
    gh_ref[0:1] += jnp.sum(d_raw, axis=0, keepdims=True)
    gh_ref[1:2] += rates * jnp.sum(steps * d_logs, axis=0, keepdims=True)
    gh_ref[2:3] += few[0:1]
    ext_b[0:T, 0:N] = d_b * (sb[:, :N] * (1.0 + cb[:, :N] * (1.0 - sb[:, :N])))
    ext_b[0:T, N:] = d_c * (sb[:, N:] * (1.0 + cb[:, N:] * (1.0 - sb[:, N:])))

    def conv_back(ext, values, taps, grads):
        now = ext[0:T]
        total = taps[3:4] * now
        grads[3:4] += jnp.sum(values * now, axis=0, keepdims=True)
        grads[4:5] += jnp.sum(now, axis=0, keepdims=True)
        for k in range(3):
            moved = ext[3 - k : 3 - k + T]
            total = total + taps[k : k + 1] * moved
            grads[k : k + 1] += jnp.sum(values * moved, axis=0, keepdims=True)
        ext[T : T + 8] = ext[0:8]
        return total

    ux = x_ref[...].astype(F32)
    dux = conv_back(ext_x, ux, par_ref, gx_ref)
    dx_ref[...] = dux.astype(BF16)
    ubc = ubd[:, : 2 * N]
    dubc = conv_back(ext_b, ubc, pbc_ref, gb_ref)
    dbd_ref[:, : 2 * N] = dubc.astype(BF16)
    dbd_ref[:, 2 * N :] = d_raw.astype(BF16)
    total = jnp.sum(dux * ux, axis=1, keepdims=True) + jnp.sum(dubc * ubc, axis=1, keepdims=True)
    total = total + jnp.sum(jnp.where(col < heads, d_raw * ubd[:, 2 * N :], 0.0), axis=1, keepdims=True)
    rd_ref[0] = to_row(total)


def params(*semantics, number=0):
    if number:
        return pltpu.CompilerParams(
            dimension_semantics=semantics, vmem_limit_bytes=LIMIT, collective_id=number, has_side_effects=True
        )
    return pltpu.CompilerParams(dimension_semantics=semantics, vmem_limit_bytes=LIMIT)


def run_forward(heads, u_zx, u_bd, par, pbc, hp, w_out, before, number):
    rows, width = u_zx.shape[0], heads * HEAD
    slots, chunks = rows // LEN, LEN // T
    at = lambda s, i: (s * chunks + i, 0)
    fixed = lambda s, i: (0, 0)
    size = lax.axis_size("dp")
    anywhere = pl.BlockSpec(memory_space=pl.ANY)
    return pl.pallas_call(
        functools.partial(forward_kernel, heads, slots * chunks),
        grid=(slots, chunks),
        in_specs=[
            pl.BlockSpec((T, width), lambda s, i: (s * chunks + i, 1)),
            pl.BlockSpec((T, width), at),
            pl.BlockSpec((T, 3 * N), at),
            pl.BlockSpec((5, width), fixed),
            pl.BlockSpec((5, 2 * N), fixed),
            pl.BlockSpec((3, heads), fixed),
            anywhere,
            anywhere,
        ],
        out_specs=[
            pl.BlockSpec((T, width), at),
            pl.BlockSpec((1, 1, T), lambda s, i: (s * chunks + i, 0, 0)),
            pl.BlockSpec((T, width), at),
            pl.BlockSpec((T, 2 * N), at),
            pl.BlockSpec((1, N, width), lambda s, i: (s * chunks + i, 0, 0)),
            anywhere,
        ],
        out_shape=[
            jax.ShapeDtypeStruct((rows, width), BF16),
            jax.ShapeDtypeStruct((rows // T, 1, T), F32),
            jax.ShapeDtypeStruct((rows, width), BF16),
            jax.ShapeDtypeStruct((rows, 2 * N), F32),
            jax.ShapeDtypeStruct((rows // T, N, width), BF16),
            full_shape(size, w_out),
        ],
        scratch_shapes=[
            pltpu.VMEM((T + 8, width), F32),
            pltpu.VMEM((T + 8, 2 * N), F32),
            pltpu.VMEM((N, width), F32),
        ]
        + weight_scratch(size, w_out),
        input_output_aliases={7: 5},
        compiler_params=params("arbitrary", "arbitrary", number=number),
        cost_estimate=pl.CostEstimate(flops=rows * width * 2 * 1200, bytes_accessed=rows * width * 8, transcendentals=rows * width * 6),
        name="scan_forward",
    )(u_zx, u_zx, u_bd, par, pbc, hp, cut_shard(w_out), before)


def run_project(heads, x, w_in, w_out, number):
    rows, deep = x.shape
    wide = w_in.shape[1]
    width = 2 * heads * HEAD
    size = lax.axis_size("dp")
    step = 256
    at = lambda i: (i, 0)
    fixed = lambda i: (0, 0)
    anywhere = pl.BlockSpec(memory_space=pl.ANY)
    thin = pl.BlockSpec((step // T, 1, T), lambda i: (i, 0, 0))
    return pl.pallas_call(
        functools.partial(project_kernel, heads, rows // step),
        grid=(rows // step,),
        in_specs=[pl.BlockSpec((step, deep), at), pl.BlockSpec((deep, wide), fixed), anywhere],
        out_specs=[
            pl.BlockSpec((step, deep), at),
            thin,
            pl.BlockSpec((step, width), at),
            pl.BlockSpec((step, wide - width), at),
            pl.BlockSpec((8, deep), fixed),
            anywhere,
        ],
        out_shape=[
            jax.ShapeDtypeStruct((rows, deep), BF16),
            jax.ShapeDtypeStruct((rows // T, 1, T), F32),
            jax.ShapeDtypeStruct((rows, width), BF16),
            jax.ShapeDtypeStruct((rows, wide - width), F32),
            jax.ShapeDtypeStruct((8, deep), F32),
            full_shape(size, w_out),
        ],
        scratch_shapes=weight_scratch(size, w_out),
        compiler_params=params("arbitrary", number=number),
        cost_estimate=pl.CostEstimate(flops=LIGHT, bytes_accessed=LIGHT, transcendentals=0),
        name="project",
    )(x, w_in, cut_shard(w_out))


def run_home(me, order, sums, extra, deep, name, after=()):
    rows, quarter = sums[0].shape
    step = 512
    many = rows // step
    into = lambda i, m: (jnp.minimum(i, many - 1), 0)
    thin = pl.BlockSpec((step // T, 1, T), lambda i, m: (jnp.minimum(i, many - 1), 0, 0))
    specs = [pl.BlockSpec((rows // T, 1, T), lambda i, m: (0, 0, 0))] + [pl.BlockSpec((step, quarter), into)] * 2
    values = list(sums)
    if extra is not None:
        specs += [pl.BlockSpec((step, quarter), lambda i, m: (jnp.minimum(i, many - 1), m[0])), thin]
        specs += [pl.BlockSpec((8, quarter), lambda i, m: (0, m[0])), thin, thin]
        specs += [pl.BlockSpec((3, step // T, 1, T), lambda i, m: (0, jnp.minimum(i, many - 1), 0, 0))]
        values += list(extra)
    values += list(after)
    specs += [pl.BlockSpec(memory_space=pl.ANY)] * len(after)
    return pl.pallas_call(
        functools.partial(home_kernel, extra is not None, float(deep)),
        grid_spec=pltpu.PrefetchScalarGridSpec(
            num_scalar_prefetch=1,
            grid=(2 * many,),
            in_specs=specs,
            out_specs=pl.BlockSpec((step, quarter), lambda i, m: (jnp.maximum(i - many, 0), 0)),
            scratch_shapes=[pltpu.VMEM((rows, quarter), BF16)],
        ),
        out_shape=jax.ShapeDtypeStruct((rows, quarter), BF16),
        compiler_params=params("arbitrary"),
        cost_estimate=pl.CostEstimate(flops=rows * rows * quarter * 2, bytes_accessed=rows * quarter * 10, transcendentals=0),
        name=name,
    )(me, order, *values)


def run_gate(all_width, grads, w_out, y, u_zx, gain, mask, ss, number):
    rows, width = y.shape
    deep = grads.shape[1]
    step = 256
    many = rows // step
    both = lambda i: (lax.rem(i, many), 0)
    late = lambda i: (jnp.maximum(i - many, 0), 0)
    fixed = lambda i: (0, 0)
    wide, out = pl.BlockSpec((step, width), both), pl.BlockSpec((step, width), late)
    moves = (("spread", "head"), ("spread", "head"))
    others = lax.axis_size("head") - 1
    return pl.pallas_call(
        functools.partial(gate_kernel, float(all_width), moves),
        grid=(2 * many,),
        in_specs=[
            pl.BlockSpec((step, deep), lambda i: (jnp.minimum(i, many - 1), 0)),
            pl.BlockSpec((deep, width), fixed),
            wide,
            wide,
            pl.BlockSpec((width,), lambda i: (0,)),
            pl.BlockSpec((step // T, 1, T), lambda i: (lax.rem(i, many), 0, 0)),
            pl.BlockSpec((rows // T, 1, T), lambda i: (0, 0, 0)),
        ],
        out_specs=[out, out, out, pl.BlockSpec((8, width), fixed), pl.BlockSpec((step // T, 1, T), lambda i: (jnp.maximum(i - many, 0), 0, 0))],
        out_shape=[jax.ShapeDtypeStruct((rows, width), BF16)] * 3
        + [jax.ShapeDtypeStruct((8, width), F32), jax.ShapeDtypeStruct((rows // T, 1, T), F32)],
        scratch_shapes=[pltpu.VMEM((many, step, width), BF16), pltpu.VMEM((rows // T, 1, T), F32)]
        + [pltpu.VMEM((others, rows // T, 1, T), F32)] * 2
        + move_scratch(moves, (ss, ss)),
        compiler_params=params("arbitrary", number=number),
        cost_estimate=pl.CostEstimate(flops=LIGHT, bytes_accessed=LIGHT, transcendentals=0),
        name="gate",
    )(grads, w_out, y, u_zx, gain, mask, ss)


def run_backward(heads, slot, dy, u_zx, c, cb, u_bd, st, par, pbc, hp, before, moves, values, number, after=()):
    rows, width = dy.shape
    chunks = LEN // T
    place = lambda s, i: slot * chunks + chunks - 1 - i
    at = lambda s, i: (place(s, i), 0)
    at3 = lambda s, i: (place(s, i), 0, 0)
    fixed = lambda s, i: (0, 0)
    anywhere = pl.BlockSpec(memory_space=pl.ANY)
    return pl.pallas_call(
        functools.partial(backward_kernel, heads, len(before) + len(after), tuple(moves)),
        grid=(1, chunks),
        in_specs=[
            pl.BlockSpec((T, width), at),
            pl.BlockSpec((T, width), lambda s, i: (place(s, i), 1)),
            pl.BlockSpec((T, width), at),
            pl.BlockSpec((T, 2 * N), at),
            pl.BlockSpec((T, 3 * N), at),
            pl.BlockSpec((1, N, width), at3),
            pl.BlockSpec((5, width), fixed),
            pl.BlockSpec((5, 2 * N), fixed),
            pl.BlockSpec((3, heads), fixed),
        ]
        + [anywhere] * (len(moves) + len(before) + len(after)),
        out_specs=[
            pl.BlockSpec((T, width), at),
            pl.BlockSpec((T, 3 * N), at),
            pl.BlockSpec((1, 1, T), at3),
            pl.BlockSpec((8, width), fixed),
            pl.BlockSpec((8, 2 * N), fixed),
            pl.BlockSpec((8, 128), fixed),
        ]
        + [anywhere] * len(moves),
        out_shape=[
            jax.ShapeDtypeStruct((rows, width), BF16),
            jax.ShapeDtypeStruct((rows, 3 * N), BF16),
            jax.ShapeDtypeStruct((rows // T, 1, T), F32),
            jax.ShapeDtypeStruct((8, width), F32),
            jax.ShapeDtypeStruct((8, 2 * N), F32),
            jax.ShapeDtypeStruct((8, 128), F32),
        ]
        + move_outs(moves, values),
        scratch_shapes=[
            pltpu.VMEM((N, width), F32),
            pltpu.VMEM((T + 8, width), F32),
            pltpu.VMEM((T + 8, 2 * N), F32),
            pltpu.VMEM((128, 128), F32),
            pltpu.VMEM((3 * T, width), BF16),
            pltpu.VMEM((T, width), BF16),
            pltpu.VMEM((T, width), BF16),
        ]
        + move_scratch(moves, values),
        input_output_aliases={9 + len(moves) + i: i for i in range(len(before))},
        compiler_params=params("arbitrary", "arbitrary", number=number),
        cost_estimate=pl.CostEstimate(flops=LIGHT, bytes_accessed=LIGHT, transcendentals=0),
        name="scan_backward",
    )(dy, u_zx, c, cb, u_bd, st, par, pbc, hp, *values, *before, *after)


def pieces_kernel(count, many, moves, extra, *refs):
    total = len(moves)
    values, weight_ref, srcs = refs[:count], refs[count], refs[count + 1 : count + 1 + total]
    refs = refs[count + 1 + total + extra :]
    far_ref, own_ref = refs[:2]
    dsts, refs = refs[2 : 2 + total], refs[2 + total :]
    sent_ref, came_ref, near_sems, joined_ref = refs[:4]
    step = pl.program_id(0)
    rows, quarter = far_ref.shape
    start = 0
    for value in values:
        joined_ref[:, start : start + value.shape[1]] = value[...]
        start += value.shape[1]
    dp, own = lax.axis_index("dp"), lax.axis_index("head")
    near = (dp, own ^ 1)
    peers, copies = make_moves(moves, srcs, dsts, *refs[4:]) if moves else ([], [])

    @pl.when(step == 0)
    def _():
        greet(peers if near_in(moves) else [near] + peers)
        for copy in copies:
            copy.start()

    def product(k):
        at = pl.ds(pl.multiple_of((own ^ k) * quarter, 128), quarter)
        return dot_nt(joined_ref[...], weight_ref[at, :])

    def near_copy(block):
        return pltpu.make_async_remote_copy(
            src_ref=sent_ref.at[block],
            dst_ref=came_ref.at[block],
            send_sem=near_sems.at[0, block],
            recv_sem=near_sems.at[1, block],
            device_id=near,
            device_id_type=MESH,
        )

    @pl.when(step < many)
    def _():
        sent_ref[step, :, :quarter] = product(3).astype(BF16)
        sent_ref[step, :, quarter:] = product(1).astype(BF16)
        near_copy(step).start()

    @pl.when(step >= many)
    def _():
        block = step - many
        far, mine = product(2), product(0)
        near_copy(block).wait_recv()
        far_ref[...] = (far + came_ref[block, :, :quarter].astype(F32)).astype(BF16)
        own_ref[...] = (mine + came_ref[block, :, quarter:].astype(F32)).astype(BF16)

    @pl.when(step == 2 * many - 1)
    def _():
        for block in range(many):
            near_copy(block).wait_send()
        for copy in copies:
            copy.wait()


def near_in(moves):
    return any(move[0] == "spread" and move[1] == "head" for move in moves)


def run_pieces(values, weight, quarter, name, moves, moved, number, after=()):
    rows = values[0].shape[0]
    step = 512
    many = rows // step
    anywhere = pl.BlockSpec(memory_space=pl.ANY)
    specs = [pl.BlockSpec((step, v.shape[1]), lambda i: (lax.rem(i, many), 0)) for v in values]
    specs.append(pl.BlockSpec(weight.shape, lambda i: (0, 0)))
    return pl.pallas_call(
        functools.partial(pieces_kernel, len(values), many, tuple(moves), len(after)),
        grid=(2 * many,),
        in_specs=specs + [anywhere] * (len(moves) + len(after)),
        out_specs=[pl.BlockSpec((step, quarter), lambda i: (jnp.maximum(i - many, 0), 0))] * 2 + [anywhere] * len(moves),
        out_shape=[jax.ShapeDtypeStruct((rows, quarter), BF16)] * 2 + move_outs(moves, moved),
        scratch_shapes=[pltpu.VMEM((many, step, 2 * quarter), BF16)] * 2 + [pltpu.SemaphoreType.DMA((2, many)), pltpu.VMEM((step, weight.shape[1]), BF16)] + move_scratch(moves, moved),
        compiler_params=params("arbitrary", number=number),
        cost_estimate=pl.CostEstimate(flops=LIGHT, bytes_accessed=LIGHT, transcendentals=0),
        name=name,
    )(*values, weight, *moved, *after)


def second_bits(step, last, paired, came, kept, holds, halves, quarters, bit_sems, load_sems):
    me, head = lax.axis_index("dp"), lax.axis_index("head")
    side, mid = me & 1, (me >> 1) & 1
    own = [paired[0].at[:, :, side], paired[1].at[:, mid]]
    loads = [pltpu.make_async_copy(own[i], holds[i], load_sems.at[0, i]) for i in range(2)]
    loads += [pltpu.make_async_copy(came[i], halves[i], load_sems.at[1, i]) for i in range(2)]
    picks, peers = (mid, side), ((me ^ 2, head), (me ^ 1, head))
    sends = [
        pltpu.make_async_remote_copy(
            src_ref=holds[i].at[:, 1 - picks[i]],
            dst_ref=quarters[i],
            send_sem=bit_sems.at[0, i],
            recv_sem=bit_sems.at[1, i],
            device_id=peers[i],
            device_id_type=MESH,
        )
        for i in range(2)
    ]

    @pl.when(step == 0)
    def _():
        for copy in loads:
            copy.start()
        greet(peers)
        for copy in loads:
            copy.wait()
        for i in range(2):
            for j in range(holds[i].shape[0]):
                for k in range(2):
                    holds[i][j, k] = (holds[i][j, k].astype(F32) + halves[i][j, k].astype(F32)).astype(BF16)
            sends[i].start()

    @pl.when(step == last)
    def _():
        for i in range(2):
            sends[i].wait()
            for j in range(holds[i].shape[0]):
                kept[i][j] = (holds[i][j, picks[i]].astype(F32) + quarters[i][j].astype(F32)).astype(BF16)


def grads_kernel(count, parts, extra, reduce, *refs):
    lefts, rights = refs[:count], refs[count : 2 * count]
    paired, came = refs[2 * count : 2 * count + 2], refs[2 * count + 2 : 2 * count + 4]
    refs = refs[2 * count + extra + (4 if reduce else 0) :]
    outs, refs = refs[:count], refs[count:]
    step = pl.program_id(0)
    if reduce:
        second_bits(step, count * parts - 1, paired, came, refs[0:2], refs[2:4], refs[4:6], refs[6:8], refs[8], refs[9])
    for which in range(count):

        @pl.when((step >= which * parts) & (step < (which + 1) * parts))
        def _():
            out = lax.dot_general(lefts[which][...], rights[which][...], (((0,), (0,)), ((), ())), preferred_element_type=F32)
            outs[which][...] = out.astype(BF16)


def run_grads(pairs, name, paired=(), came=(), number=0, after=()):
    rows, deep = pairs[0][0].shape
    step = 512
    parts = deep // step
    count = len(pairs)
    anywhere = pl.BlockSpec(memory_space=pl.ANY)
    into = lambda which: lambda i: jnp.clip(i - which * parts, 0, parts - 1)
    specs = [pl.BlockSpec((rows, step), lambda i, at=into(w): (0, at(i))) for w in range(count)]
    specs += [pl.BlockSpec(right.shape, lambda i: (0, 0)) for _, right in pairs]
    kept = [(p.shape[0], p.shape[3], p.shape[4]) for p in paired]
    twice = [pltpu.VMEM((m, 2, r, c), BF16) for m, r, c in kept]
    sems = pltpu.SemaphoreType.DMA
    return pl.pallas_call(
        functools.partial(grads_kernel, count, parts, len(after), bool(paired)),
        grid=(count * parts,),
        in_specs=specs + [anywhere] * (len(paired) + len(came) + len(after)),
        out_specs=[pl.BlockSpec((step, right.shape[1]), lambda i, at=into(w): (at(i), 0)) for w, (_, right) in enumerate(pairs)]
        + [pl.BlockSpec(shape, lambda i: (0, 0, 0)) for shape in kept],
        out_shape=[jax.ShapeDtypeStruct((deep, right.shape[1]), BF16) for _, right in pairs] + [jax.ShapeDtypeStruct(shape, BF16) for shape in kept],
        scratch_shapes=twice + twice + [pltpu.VMEM(shape, BF16) for shape in kept] + ([sems((2, 2)), sems((2, 2))] if paired else []),
        compiler_params=params("arbitrary", number=number),
        cost_estimate=pl.CostEstimate(flops=LIGHT, bytes_accessed=LIGHT, transcendentals=0),
        name=name,
    )(*[left for left, _ in pairs], *[right for _, right in pairs], *paired, *came, *after)


def last_kernel(moves, *refs):
    count = len(moves)
    srcs, thin_ref, wide_ref, half_ref = refs[:count], *refs[count : count + 3]
    refs = refs[count + 3 :]
    dsts, thin_out, wide_out = refs[:count], refs[count], refs[count + 1]
    thin_own, thin_came, thin_line, wide_own, wide_came, wide_line, load_sems, pair_sems, sems, local_sems = refs[count + 2 :]
    me, head = lax.axis_index("dp"), lax.axis_index("head")
    side, high = me & 1, me >> 1
    many = thin_own.shape[0]
    peers, copies = make_moves(moves, srcs, dsts, sems, local_sems)

    def remote(src, dst, which, slot, peer):
        return pltpu.make_async_remote_copy(
            src_ref=src,
            dst_ref=dst,
            send_sem=pair_sems.at[0, which, slot],
            recv_sem=pair_sems.at[1, which, slot],
            device_id=(peer, head),
            device_id_type=MESH,
        )

    def blocks(own, line, which):
        return [remote(own.at[high ^ j], line.at[j - 1], which, j, me ^ (2 * j)) for j in range(1, many)]

    half = remote(thin_ref.at[:, 1 - side], thin_came, 0, 0, me ^ 1)
    thin_blocks, wide_blocks = blocks(thin_own, thin_line, 0), blocks(wide_own, wide_line, 1)
    loads = [
        pltpu.make_async_copy(wide_ref.at[:, side], wide_own, load_sems.at[0]),
        pltpu.make_async_copy(half_ref, wide_came, load_sems.at[1]),
        pltpu.make_async_copy(thin_ref.at[:, side], thin_own, load_sems.at[2]),
    ]
    for copy in loads:
        copy.start()
    greet(peers)
    half.start()
    for copy in copies:
        copy.start()
    for copy in loads:
        copy.wait()
    for j in range(many):
        wide_own[j] = (wide_own[j].astype(F32) + wide_came[j].astype(F32)).astype(BF16)
    for copy in wide_blocks:
        copy.start()
    half.wait()
    for j in range(many):
        thin_own[j] = (thin_own[j].astype(F32) + thin_came[j].astype(F32)).astype(BF16)
    for copy in thin_blocks:
        copy.start()
    for copy in wide_blocks + thin_blocks:
        copy.wait()
    thin, wide = thin_own[high].astype(F32), wide_own[high].astype(F32)
    for j in range(many - 1):
        thin, wide = thin + thin_line[j].astype(F32), wide + wide_line[j].astype(F32)
    thin_out[...] = thin
    wide_out[...] = wide
    for copy in copies:
        copy.wait()


def run_last(moves, values, thin, wide, half, number):
    many, _, block, slim = thin.shape
    broad = wide.shape[3]
    anywhere = pl.BlockSpec(memory_space=pl.ANY)
    inside = pl.BlockSpec(memory_space=pltpu.VMEM)
    space = lambda count, columns: pltpu.VMEM((count, block, columns), BF16)
    sems = pltpu.SemaphoreType.DMA
    return pl.pallas_call(
        functools.partial(last_kernel, tuple(moves)),
        in_specs=[anywhere] * (len(moves) + 3),
        out_specs=[anywhere] * len(moves) + [inside] * 2,
        out_shape=move_outs(moves, values) + [jax.ShapeDtypeStruct((block, slim), F32), jax.ShapeDtypeStruct((block, broad), F32)],
        scratch_shapes=[space(many, slim), space(many, slim), space(many - 1, slim), space(many, broad), space(many, broad), space(many - 1, broad)]
        + [sems((3,)), sems((2, 2, many))]
        + move_scratch(moves, values),
        compiler_params=pltpu.CompilerParams(collective_id=number, has_side_effects=True, vmem_limit_bytes=LIMIT),
        name="last_exchange",
    )(*values, thin, wide, half)


def row_forward(size, quarter, own_ref, full_ref, sems):
    me, own = lax.axis_index("dp"), lax.axis_index("head")
    columns = lambda head: pl.ds(pl.multiple_of(head * quarter, 128), quarter)

    def copy(src, dst, stage, k, head):
        return pltpu.make_async_remote_copy(
            src_ref=src, dst_ref=dst, send_sem=sems.at[0, stage, k], recv_sem=sems.at[1, stage, k], device_id=(me, head), device_id_type=MESH
        )

    def source(k):
        return full_ref.at[me ^ k, :, columns(own)] if own_ref is None else own_ref.at[me ^ k]

    def far(k):
        return copy(source(k), full_ref.at[me ^ k, :, columns(own)], 0, k, own ^ 2)

    def near(k):
        return copy(source(k), full_ref.at[me ^ k, :, columns(own)], 1, k, own ^ 1)

    def back(k):
        block = full_ref.at[me ^ k, :, columns(own ^ 2)]
        return copy(block, block, 2, k, own ^ 1)

    return far, near, back


def shard_spread(src, dst, across_sems, side_sems):
    me, own = lax.axis_index("dp"), lax.axis_index("head")

    def copy(a, b, sems, part, j, peer):
        return pltpu.make_async_remote_copy(
            src_ref=a, dst_ref=b, send_sem=sems.at[0, part, j], recv_sem=sems.at[1, part, j], device_id=(peer, own), device_id_type=MESH
        )

    def across(part, j):
        return copy(src.at[part], dst.at[me, part], across_sems, part, j, me ^ (2 * j))

    def side(part, j):
        here = dst.at[me ^ (2 * j), part]
        return copy(src.at[part] if j == 0 else here, here, side_sems, part, j, me ^ 1)

    return across, side


def entry_kernel(parts, order_ref, x_ref, g_ref, zx_ref, rest_ref, fx_ref, fg_ref, fw_ref, row_sems, x_sems, g_sems, line_sems, side_sems, local_sems, land, ready, picks, w_held):
    size, block, quarter = x_ref.shape
    line = size // 2
    me, own = lax.axis_index("dp"), lax.axis_index("head")
    spot = me >> 1
    mine = pl.ds(pl.multiple_of(own * quarter, 128), quarter)
    sources, fulls = (x_ref, g_ref), (fx_ref, fg_ref)
    forwards = [row_forward(size, quarter, ready.at[i], fulls[i], sems) for i, sems in enumerate((x_sems, g_sems))]

    def remote(src, dst, sems, slot, peer):
        return pltpu.make_async_remote_copy(
            src_ref=src, dst_ref=dst, send_sem=sems.at[(0,) + slot], recv_sem=sems.at[(1,) + slot], device_id=(peer, own), device_id_type=MESH
        )

    def rows(which, k):
        return remote(sources[which].at[me ^ k], land.at[which, me], row_sems, (which, k), me ^ k)

    def along(way, part, j):
        sign = 1 - 2 * way
        origin = jnp.clip(me - sign * 2 * (j - 1), 0, size - 1)
        peer = jnp.clip(me + sign * 2, 0, size - 1)
        here = fw_ref.at[origin, part]
        return remote(w_held.at[part] if j == 1 else here, here, line_sems, (way, part, j - 1), peer)

    def came(way, part, j):
        sign = 1 - 2 * way
        here = fw_ref.at[jnp.clip(me - sign * 2 * j, 0, size - 1), part]
        return remote(here, here, line_sems, (way, part, j - 1), me)

    def side(way, part, j):
        sign = 1 - 2 * way
        here = fw_ref.at[jnp.clip(me - sign * 2 * j, 0, size - 1), part]
        return remote(w_held.at[part] if j == 0 else here, here, side_sems, (way, part, j), me ^ 1)

    def goes_on(way):
        return spot < line - 1 if way == 0 else spot > 0

    def arrives(way, j):
        return spot >= j if way == 0 else spot < line - j

    into = [pltpu.make_async_copy(sources[i].at[me], land.at[i, me], local_sems.at[i]) for i in range(2)]
    edge = zx_ref.shape[2]
    into.append(pltpu.make_async_copy(zx_ref, w_held.at[:, :, pl.ds(0, edge)], local_sems.at[2]))
    into.append(pltpu.make_async_copy(rest_ref, w_held.at[:, :, pl.ds(edge, rest_ref.shape[2])], local_sems.at[6]))
    held = [pltpu.make_async_copy(ready.at[i], fulls[i].at[:, :, mine], local_sems.at[3 + i]) for i in range(2)]
    held.append(pltpu.make_async_copy(w_held, fw_ref.at[me], local_sems.at[5]))
    for copy in into:
        copy.start()
    greet([(me ^ k, own) for k in range(1, size)] + [(me, own ^ 1), (me, own ^ 2)])
    order = turn_order(size)
    for k in order:
        rows(0, k).start()
    for copy in into:
        copy.wait()
    for part in range(parts):
        side(0, part, 0).start()
    held[2].start()
    total = size * block
    lane = lax.broadcasted_iota(jnp.int32, (T, T), 1).astype(F32)

    def pick(i, carry):
        wanted = to_col(order_ref[i].astype(F32))
        at = pl.ds(pl.multiple_of(i * T, T), T)
        for j in range(total // T):
            picks[at, j * T : j * T + T] = (wanted == lane + float(T * j)).astype(F32).astype(BF16)
        return carry

    lax.fori_loop(0, total // T, pick, 0)

    def arrange(which):
        step = min(512, total)
        for i in range(total // step):
            value = dot(picks[i * step : (i + 1) * step, :], land[which].reshape(total, quarter)).astype(BF16)
            ready[which, i * step // block : (i + 1) * step // block] = value.reshape(step // block, block, quarter)
        held[which].start()
        far, near, _ = forwards[which]
        for k in range(size):
            far(k).start()
            near(k).start()

    def backs(which, some):
        far, _, back = forwards[which]
        for k in some:
            far(k).wait_recv()
            back(k).start()

    for k in order:
        rows(0, k).wait_recv()
    for k in order:
        rows(1, k).start()
    arrange(0)
    for k in order:
        rows(1, k).wait_recv()
    for way in range(2):

        @pl.when(goes_on(way))
        def _():
            for part in range(parts):
                along(way, part, 1).start()

    arrange(1)
    backs(0, range(size))
    for j in range(1, line):
        for part in range(parts):
            if j == line - 1:
                backs(1, range(part * size // parts, (part + 1) * size // parts))
            for way in range(2):

                @pl.when(arrives(way, j))
                def _():
                    came(way, part, j).wait_recv()
                    side(way, part, j).start()

                if j + 1 < line:

                    @pl.when(arrives(way, j) & goes_on(way))
                    def _():
                        along(way, part, j + 1).start()

    for copy in held:
        copy.wait()
    for which in range(2):
        far, near, back = forwards[which]
        for k in range(size):
            near(k).wait()
            back(k).wait()
            far(k).wait_send()
            if k:
                rows(which, k).wait_send()
    for part in range(parts):
        side(0, part, 0).wait()
        for way in range(2):

            @pl.when(goes_on(way))
            def _():
                along(way, part, 1).wait_send()

            for j in range(1, line):

                @pl.when(arrives(way, j))
                def _():
                    side(way, part, j).wait()

                if j + 1 < line:

                    @pl.when(arrives(way, j) & goes_on(way))
                    def _():
                        along(way, part, j + 1).wait_send()


PARTS = 4


def cut_shard(w):
    return w.reshape(PARTS, w.shape[0] // PARTS, w.shape[1])


def full_shape(size, w):
    return jax.ShapeDtypeStruct((size, PARTS, w.shape[0] // PARTS, w.shape[1]), BF16)


def run_entry(order, tokens, cotangent, w_zx, w_rest, number):
    size = lax.axis_size("dp")
    shard, wide = w_zx.shape[0], w_zx.shape[1] + w_rest.shape[1]
    rows, quarter = tokens.shape
    block = rows // size
    line = size // 2
    anywhere = pl.BlockSpec(memory_space=pl.ANY)
    sems = pltpu.SemaphoreType.DMA
    full = jax.ShapeDtypeStruct((size, block, quarter * 4), BF16)
    came_x, came_g, came_w = pl.pallas_call(
        functools.partial(entry_kernel, PARTS),
        in_specs=[pl.BlockSpec(memory_space=pltpu.VMEM)] + [anywhere] * 4,
        out_specs=[anywhere] * 3,
        out_shape=[full, full, jax.ShapeDtypeStruct((size, PARTS, shard // PARTS, wide), BF16)],
        scratch_shapes=[
            sems((2, 2, size)),
            sems((2, 3, size)),
            sems((2, 3, size)),
            sems((2, 2, PARTS, line)),
            sems((2, 2, PARTS, line)),
            sems((7,)),
            pltpu.VMEM((2, size, block, quarter), BF16),
            pltpu.VMEM((2, size, block, quarter), BF16),
            pltpu.VMEM((rows, rows), BF16),
            pltpu.VMEM((PARTS, shard // PARTS, wide), BF16),
        ],
        compiler_params=pltpu.CompilerParams(collective_id=number, has_side_effects=True, vmem_limit_bytes=LIMIT),
        name="entry",
    )(order, tokens.reshape(size, block, quarter), cotangent.reshape(size, block, quarter), cut_shard(w_zx), cut_shard(w_rest))
    return came_x.reshape(rows, quarter * 4), came_g.reshape(rows, quarter * 4), came_w.reshape(size * shard, wide)


def mm(a, b, contract, kind):
    return lax.dot_general(a, b, (contract, ((), ())), preferred_element_type=F32).astype(kind)


def body(tokens, cotangent, order, lengths, norm_gain, w_zx, w_bc, w_dt, w_out, conv_x, conv_bc, head_params, gate_gain):
    rows, quarter = tokens.shape
    heads = head_params.shape[1]
    width = heads * HEAD
    me = lax.axis_index("head").astype(jnp.int32).reshape(1)
    size = lax.axis_size("dp")
    here = lax.axis_index("dp")
    all_width = width * lax.axis_size("head")
    deep = quarter * lax.axis_size("head")
    own_w = w_zx.shape[0]
    arrange = order.reshape(rows // T, 1, T)

    rest = jnp.concatenate([w_bc, w_dt, norm_gain[:, None], jnp.zeros((own_w, 127 - heads), BF16)], axis=1)
    blocks = lambda value: value.reshape(size, rows // size, quarter)
    full_x, full_g, w_in = run_entry(arrange, tokens, cotangent, w_zx.reshape(own_w, 2 * width), rest, 1)
    normed, inv_one, u_zx, u_bd, gain, w_o = run_project(heads, full_x, w_in, w_out, 2)

    gated = gate_gain
    hp = head_params
    positions = lax.broadcasted_iota(jnp.int32, (lengths.shape[0], LEN), 1)
    mask = (positions < lengths[:, None]).astype(F32).reshape(rows // T, 1, T)

    y, ss, c, cb, st, w_o = run_forward(heads, u_zx, u_bd, conv_x, conv_bc, hp, w_out, w_o, 3)
    w_o = w_o.reshape(deep, width)
    yg, dz, dy, gg, rd_z = run_gate(all_width, full_g, w_o, y, u_zx, gated, mask, ss, 4)

    def total(kept, came, shift):
        own = lax.dynamic_index_in_dim(kept, here >> shift, 0, keepdims=False)
        return own.astype(F32) + jnp.sum(came.astype(F32), axis=0)

    def pairs(grads):
        return grads.reshape(size // 2, 2, own_w, grads.shape[1])

    def fours(grads):
        return grads.reshape(size // 4, 2, -1, own_w, grads.shape[-1])

    scan = functools.partial(run_backward, heads)
    shared = (dy, u_zx, c, cb, u_bd, st, conv_x, conv_bc, hp)
    out_far, out_own = run_pieces([yg], w_o, quarter, "branch_pieces", [], [], 5)
    out_arrived = lax.ppermute(out_far, "head", [(i, i ^ 2) for i in range(lax.axis_size("head"))])
    grad_o, grad_z = run_grads([(full_g, yg), (normed, dz)], "gate_grads", after=[out_far])
    grad_o, grad_z = pairs(grad_o), fours(grad_z)
    def other_half(paired, bit):
        send = lax.dynamic_index_in_dim(paired, 1 - ((here >> bit) & 1), 1, keepdims=False)
        return send, lax.ppermute(send, "dp", [(i, i ^ (1 << bit)) for i in range(size)])

    send_o, came_o = other_half(grad_o, 0)
    send_z, came_z = other_half(grad_z, 1)
    *back0, gx0, gb0, gh0 = scan(0, *shared, (), [], [], 0, [send_o, send_z])
    sent_out = run_home(me, arrange, [out_own, out_arrived], None, deep, "home_out", [back0[0], came_o, came_z])
    got_out = lax.all_to_all(sent_out, "dp", split_axis=0, concat_axis=0, tiled=True)
    *back1, gx1, gb1, gh1 = scan(1, *shared, back0, [], [], 0, [sent_out])
    dux, dbd, rd_x = back1
    grad_x, grad_bd, kept_o, kept_z = run_grads(
        [(normed, dux), (normed, dbd)], "scan_grads", [fours(grad_o), grad_z], [came_o.reshape(came_z.shape), came_z], 8
    )
    grad_x, grad_bd = pairs(grad_x), pairs(grad_bd)
    gb = gb0 + gb1
    d_far, d_own, line_o, line_z, came_x2, got_rows, got_gb = run_pieces(
        [dz, dux, dbd],
        w_in,
        quarter,
        "input_pieces",
        [("direct", "dp", 2), ("direct", "dp", 2), ("half", "dp", 0), ("spread", "head"), ("spread", "head")],
        [kept_o, kept_z, grad_x, rd_z + rd_x, gb],
        9,
        [got_out],
    )
    gb = gb[:5] + jnp.sum(got_gb, axis=0)[:5]
    gh = gh0 + gh1
    ends = jnp.concatenate([gb[3], gb[4]] + [gh[i, :32] for i in range(3)] + [jnp.zeros((width - 4 * N - 96,), F32)])
    small = jnp.concatenate([(gx0 + gx1)[:5], gg[:1], jnp.concatenate([gb[0], gb[1], gb[2]])[None], ends[None]], axis=0)
    d_arrived, got_small, grad_bd, grad_x = run_last([("whole", "head", 2), ("spread", "dp")], [d_far, small], grad_bd, grad_x, came_x2, 10)

    sent_back = run_home(me, arrange, [d_own, d_arrived], [normed, inv_one, gain, rd_z, rd_x, got_rows], deep, "home_back")
    got_back = lax.all_to_all(sent_back, "dp", split_axis=0, concat_axis=0, tiled=True)
    final_out = (tokens.astype(F32) + got_out.astype(F32)).astype(BF16)
    final_back = (cotangent.astype(F32) + got_back.astype(F32)).astype(BF16)

    grad_out, grad_z = total(kept_o, line_o, 2), total(kept_z, line_z, 2)
    small = small + jnp.sum(got_small, axis=0)
    grad_zx = jnp.stack([grad_z, grad_x], axis=1)
    of_gain = jnp.sum(grad_z * w_zx[:, 0].astype(F32), axis=1) + jnp.sum(grad_x * w_zx[:, 1].astype(F32), axis=1)
    of_gain = of_gain + jnp.sum(grad_bd[:, : 2 * N] * w_bc.astype(F32), axis=1)
    of_gain = of_gain + jnp.sum(grad_bd[:, 2 * N : 2 * N + heads] * w_dt.astype(F32), axis=1)
    last = jnp.concatenate([grad_bd[:, : 2 * N], jnp.broadcast_to(of_gain[:, None], (own_w, 128))], axis=1)
    others, = run_exchange([("spread", "head")], [last], 11)
    last = last + jnp.sum(others, axis=0)
    grad_gain = last[:, 2 * N] / norm_gain.astype(F32)
    gx, gg = small[0:5], small[5]
    gb = jnp.concatenate([small[6].reshape(3, 2 * N), small[7, : 4 * N].reshape(2, 2 * N)], axis=0)
    gh = small[7, 4 * N : 4 * N + 96].reshape(3, 32)[:, :heads]
    return (final_out, final_back, grad_gain, grad_zx, last[:, : 2 * N], grad_bd[:, 2 * N : 2 * N + heads], grad_out, gx, gb, gh, gg)


def solution(mesh):
    return jax.shard_map(
        body,
        mesh=mesh,
        in_specs=(
            P("dp", "head"),
            P("dp", "head"),
            P("dp", None),
            P("dp"),
            P("dp"),
            P("dp", None, "head"),
            P("dp", None),
            P("dp", "head"),
            P("dp", "head"),
            P(None, "head"),
            P(),
            P(None, "head"),
            P("head"),
        ),
        out_specs=(
            P("dp", "head"),
            P("dp", "head"),
            P("dp"),
            P("dp", None, "head"),
            P("dp", None),
            P("dp", "head"),
            P("dp", "head"),
            P(None, "head"),
            P(),
            P(None, "head"),
            P("head"),
        ),
        check_vma=False,
    )
```

```python
import functools

import jax
import jax.numpy as jnp
from jax import lax
from jax.experimental import pallas as pl
from jax.experimental.pallas import tpu as pltpu
from jax.sharding import PartitionSpec as P

LEN = 1024
T = 128
N = 128
HEAD = 64
EPS = 1e-05
NEG = -1e30
LIGHT = 1000
LIMIT = 60 * 1024 * 1024
AXES = ("dp", "head")
F32 = jnp.float32
BF16 = jnp.bfloat16


def dot(a, b):
    return lax.dot_general(a, b, (((1,), (0,)), ((), ())), preferred_element_type=F32)


def dot_nt(a, b):
    return lax.dot_general(a, b, (((1,), (1,)), ((), ())), preferred_element_type=F32)


def dot_exact(a, b):
    return lax.dot_general(
        a, b, (((1,), (0,)), ((), ())), preferred_element_type=F32, precision=lax.Precision.HIGHEST
    )


def iotas(rows, cols):
    return (
        lax.broadcasted_iota(jnp.int32, (rows, cols), 0),
        lax.broadcasted_iota(jnp.int32, (rows, cols), 1),
    )


MESH = pl.DeviceIdType.MESH


def greet(peers):
    barrier = pltpu.get_barrier_semaphore()
    for peer in peers:
        pl.semaphore_signal(barrier, inc=1, device_id=peer, device_id_type=MESH)
    pl.semaphore_wait(barrier, len(peers))


def place_of():
    return {name: lax.axis_index(name) for name in AXES}


def move_copies(move, src, dst):
    kind, axis = move[0], move[1]
    place = place_of()
    me = place[axis]

    def peer(flip):
        return tuple(place[name] ^ flip if name == axis else place[name] for name in AXES)

    if kind == "whole":
        return [(peer(move[2]), src, dst)], []
    if kind == "rows":
        return [(peer(move[2]), src.at[pl.ds(move[3], move[4])], dst)], []
    if kind == "half":
        return [(peer(1 << move[2]), src.at[:, 1 - ((me >> move[2]) & 1)], dst)], []
    if kind == "direct":
        high = me >> move[2]
        return [(peer(j << move[2]), src.at[high ^ j], dst.at[j - 1]) for j in range(1, dst.shape[0] + 1)], []
    if kind == "all":
        groups = lax.axis_size("head")
        flips = [divmod(flat, groups) for flat in range(1, dst.shape[0] + 1)]
        return [((place["dp"] ^ f, place["head"] ^ e), src, dst.at[i]) for i, (f, e) in enumerate(flips)], []
    if kind == "spread":
        return [(peer(flip), src, dst.at[flip - 1]) for flip in range(1, dst.shape[0] + 1)], []
    remote = [(peer(k), src.at[me ^ k], dst.at[me]) for k in turn_order(src.shape[0])]
    return remote, [(src.at[me], dst.at[me])]


def turn_order(size):
    return sorted(range(1, size), key=lambda k: (-(k & ~1), k & 1))


def move_shape(move, shape):
    kind = move[0]
    if kind == "rows":
        return (move[4],) + shape[1:]
    if kind == "half":
        return (shape[0],) + shape[2:]
    if kind == "direct":
        return (shape[0] - 1,) + shape[1:]
    if kind == "spread":
        return (lax.axis_size(move[1]) - 1,) + shape
    if kind == "all":
        return (lax.axis_size("dp") * lax.axis_size("head") - 1,) + shape
    return shape


def move_counts(moves, values):
    remote = local = 0
    for move, value in zip(moves, values):
        size = lax.axis_size(move[1])
        world = lax.axis_size("dp") * lax.axis_size("head")
        count = {"direct": value.shape[0] - 1, "spread": size - 1, "turn": size - 1, "all": world - 1}.get(move[0], 1)
        remote, local = remote + count, local + (move[0] == "turn")
    return remote, local


def move_scratch(moves, values):
    remote, local = move_counts(moves, values)
    return [pltpu.SemaphoreType.DMA((2, remote)), pltpu.SemaphoreType.DMA((max(local, 1),))] if moves else []


def move_outs(moves, values):
    return [jax.ShapeDtypeStruct(move_shape(move, value.shape), value.dtype) for move, value in zip(moves, values)]


def make_moves(moves, srcs, dsts, sems, local_sems):
    remote, local = [], []
    for move, src, dst in zip(moves, srcs, dsts):
        here, there = move_copies(move, src, dst)
        remote += here
        local += there
    copies = [
        pltpu.make_async_remote_copy(src_ref=a, dst_ref=b, send_sem=sems.at[0, i], recv_sem=sems.at[1, i], device_id=peer, device_id_type=MESH)
        for i, (peer, a, b) in enumerate(remote)
    ]
    copies += [pltpu.make_async_copy(a, b, local_sems.at[i]) for i, (a, b) in enumerate(local)]
    return move_peers(moves, dsts), copies


def move_peers(moves, dsts):
    flips = {}
    for move, dst in zip(moves, dsts):
        kind, axis = move[0], move[1]
        if kind in ("whole", "rows"):
            own = [move[2]]
        elif kind == "half":
            own = [1 << move[2]]
        elif kind == "direct":
            own = [j << move[2] for j in range(1, dst.shape[0] + 1)]
        elif kind == "all":
            groups = lax.axis_size("head")
            for flat in range(1, dst.shape[0] + 1):
                flips[divmod(flat, groups)] = None
            continue
        elif kind == "spread":
            own = range(1, dst.shape[0] + 1)
        else:
            own = range(1, dst.shape[0])
        for flip in own:
            flips[(flip, 0) if axis == "dp" else (0, flip)] = None
    place = place_of()
    return [(place["dp"] ^ f, place["head"] ^ e) for f, e in flips]


def background(first, last, moves, srcs, dsts, sems, local_sems):
    peers, copies = make_moves(moves, srcs, dsts, sems, local_sems)

    @pl.when(first)
    def _():
        greet(peers)
        for copy in copies:
            copy.start()

    @pl.when(last)
    def _():
        for copy in copies:
            copy.wait()


def exchange_kernel(moves, *refs):
    count = len(moves)
    peers, copies = make_moves(moves, refs[:count], refs[count : 2 * count], refs[2 * count], refs[2 * count + 1])
    greet(peers)
    for copy in copies:
        copy.start()
    for copy in copies:
        copy.wait()


def run_exchange(moves, values, number):
    return pl.pallas_call(
        functools.partial(exchange_kernel, tuple(moves)),
        in_specs=[pl.BlockSpec(memory_space=pl.ANY)] * len(moves),
        out_specs=[pl.BlockSpec(memory_space=pl.ANY)] * len(moves),
        out_shape=move_outs(moves, values),
        scratch_shapes=move_scratch(moves, values),
        compiler_params=pltpu.CompilerParams(collective_id=number, has_side_effects=True, vmem_limit_bytes=LIMIT),
        name="exchange",
    )(*values)


def sigmoid(v):
    return 1.0 / (1.0 + jnp.exp(-v))


def softplus(v):
    return jnp.maximum(v, 0.0) + jnp.log1p(jnp.exp(-jnp.abs(v)))


def to_col(row):
    return jnp.broadcast_to(row, (T, T)).T


def to_row(col):
    return jnp.broadcast_to(col, (T, T)).T[0:1]


def lanes(value, pick):
    return jnp.broadcast_to(value[:, pick : pick + 1], (value.shape[0], 128))


def step_terms(ubd, head_ref, heads):
    fill = jnp.zeros((1, 128 - heads), F32)
    wide_row = lambda i: jnp.concatenate([head_ref[i : i + 1], fill], axis=1)
    row, col = iotas(T, T)
    raw = jnp.where(col < heads, ubd[:, 2 * N :] + wide_row(0), 0.0)
    steps = jnp.where(col < heads, softplus(raw), 0.0)
    rates = -jnp.exp(wide_row(1))
    tril = (row >= col).astype(F32)
    logs = dot_exact(tril, steps * rates)
    return raw, steps, rates, logs


def weight_moves(step, steps, parts, whole, w_ref, fw_ref, across_sems, side_sems, local_sems, w_held):
    line = fw_ref.shape[0] // 2
    me, own = lax.axis_index("dp"), lax.axis_index("head")
    across, side = shard_spread(w_ref, fw_ref, across_sems, side_sems)
    if whole:
        into = pltpu.make_async_copy(w_ref, w_held, local_sems.at[0])
        held = pltpu.make_async_copy(w_held, fw_ref.at[me], local_sems.at[1])

    @pl.when(step == 0)
    def _():
        if whole:
            into.start()
        greet([(me ^ 1, own)] + [(me ^ (2 * j), own) for j in range(1, line)])
        for part in parts:
            side(part, 0).start()
        if whole:
            into.wait()
            held.start()

    for i, part in enumerate(parts):
        begin = i * steps // len(parts)

        @pl.when(step == begin)
        def _():
            for j in range(1, line):
                across(part, j).start()

        @pl.when(step == min(steps - 1, begin + steps // 3 + 2))
        def _():
            for j in range(1, line):
                across(part, j).wait_recv()
                side(part, j).start()

    @pl.when(step == steps - 1)
    def _():
        if whole:
            held.wait()
        for part in parts:
            for j in range(line):
                side(part, j).wait()
                if j:
                    across(part, j).wait_send()


def weight_scratch(size, w):
    sems = pltpu.SemaphoreType.DMA
    return [sems((2, PARTS, size // 2)), sems((2, PARTS, size // 2)), sems((2,)), pltpu.VMEM((PARTS, w.shape[0] // PARTS, w.shape[1]), BF16)]


def forward_kernel(heads, steps, x_ref, z_ref, ubd_ref, par_ref, pbc_ref, head_ref, w_ref, before_ref, y_ref, ss_ref, c_ref, cb_ref, st_ref, fw_ref, ext_x, ext_b, state, *sems):
    weight_moves(pl.program_id(0) * pl.num_programs(1) + pl.program_id(1), steps, range(1, PARTS), False, w_ref, fw_ref, *sems)

    @pl.when(pl.program_id(1) == 0)
    def _():
        ext_x[0:8] = jnp.zeros_like(ext_x[0:8])
        ext_b[0:8] = jnp.zeros_like(ext_b[0:8])
        state[...] = jnp.zeros_like(state)

    def conv(ext, values, taps):
        ext[8 : 8 + T] = values
        total = taps[4:5] + taps[3:4] * values
        for k in range(3):
            total = total + taps[k : k + 1] * ext[5 + k : 5 + k + T]
        ext[0:8] = ext[T : T + 8]
        return total

    row, col = iotas(T, T)
    low = col < HEAD
    low_row = lax.broadcasted_iota(jnp.int32, (1, 128), 1) < HEAD
    causal = row >= col
    ubd = ubd_ref[...]
    c = conv(ext_x, x_ref[...].astype(F32), par_ref)
    c_ref[...] = c.astype(BF16)
    cb = conv(ext_b, ubd[:, : 2 * N], pbc_ref)
    cb_ref[...] = cb
    bc = cb * sigmoid(cb)
    b_rows = bc[:, :N]
    b_t = b_rows.T.astype(BF16)
    b_low, c_low = b_rows.astype(BF16), bc[:, N:].astype(BF16)
    _, steps, _, logs = step_terms(ubd, head_ref, heads)
    logs_t = logs.T
    scores = dot_nt(c_low, b_low)
    entering = state[...].astype(BF16)
    st_ref[0] = entering
    outer = dot(c_low, entering)
    squares = jnp.zeros((T, 128), F32)
    for pair in range(heads // 2):
        span = slice(128 * pair, 128 * pair + 128)
        h0, h1 = 2 * pair, 2 * pair + 1
        log0, log1 = lanes(logs, h0), lanes(logs, h1)
        log_pair = jnp.where(low, log0, log1)
        step_pair = jnp.where(low, lanes(steps, h0), lanes(steps, h1))
        last_pair = log_pair[T - 1 : T]
        skip_pair = jnp.where(low_row, lanes(head_ref[2:3], h0), lanes(head_ref[2:3], h1))
        cp = c[:, span]
        xp = cp * sigmoid(cp)
        xd = xp * step_pair
        m0 = (scores * jnp.exp(jnp.where(causal, log0 - logs_t[h0 : h0 + 1], NEG))).astype(BF16)
        m1 = (scores * jnp.exp(jnp.where(causal, log1 - logs_t[h1 : h1 + 1], NEG))).astype(BF16)
        stacked = jnp.concatenate([jnp.where(low, xd, 0.0).astype(BF16), jnp.where(low, 0.0, xd).astype(BF16)], axis=0)
        y = dot(jnp.concatenate([m0, m1], axis=1), stacked)
        y = y + jnp.exp(log_pair) * outer[:, span] + skip_pair * xp
        tail = (jnp.exp(last_pair - log_pair) * xd).astype(BF16)
        state[:, span] = jnp.exp(last_pair) * state[:, span] + dot(b_t, tail)
        y_ref[:, span] = y.astype(BF16)
        zp = z_ref[:, span].astype(F32)
        w = y * zp * sigmoid(zp)
        squares = squares + w * w
    ss_ref[0] = to_row(jnp.sum(squares, axis=1, keepdims=True))


def project_kernel(heads, steps, x_ref, w_ref, shard_ref, out_ref, inv_ref, uzx_ref, ubd_ref, gain_ref, fw_ref, *sems):
    deep, width = x_ref.shape[1], 2 * heads * HEAD
    weight_moves(pl.program_id(0), steps, range(1), True, shard_ref, fw_ref, *sems)

    @pl.when(pl.program_id(0) == 0)
    def _():
        for j in range(deep // T):
            span = slice(j * T, j * T + T)
            gain_ref[:, span] = jnp.broadcast_to(w_ref[span, width + 2 * N : width + 3 * N].astype(F32).T[heads : heads + 1], (8, T))

    x = x_ref[...].astype(F32)
    inv = lax.rsqrt(jnp.sum(x * x, axis=1, keepdims=True) / deep + EPS)
    normed = (x * inv * gain_ref[0:1]).astype(BF16)
    out_ref[...] = normed
    for part in range(x.shape[0] // T):
        inv_ref[part] = to_row(inv[part * T : part * T + T])
    uzx_ref[...] = dot(normed, w_ref[:, :width]).astype(BF16)
    ubd_ref[...] = dot(normed, w_ref[:, width:])


def home_kernel(last, deep, me_ref, order_ref, a_ref, b_ref, *refs):
    out_ref, held_ref = refs[-2:]
    step = pl.program_id(0)
    many = held_ref.shape[0] // a_ref.shape[0]
    size = a_ref.shape[0]

    @pl.when(step < many)
    def _():
        value = a_ref[...].astype(F32) + b_ref[...].astype(F32)
        if last:
            normed_ref, inv_ref, gain_ref, rdz_ref, rdx_ref, more_ref = refs[:6]
            gain = gain_ref[0:1]
            hat = normed_ref[...].astype(F32) / gain
            parts = []
            for part in range(size // T):
                inv_row = inv_ref[part]
                dots = rdz_ref[part] + rdx_ref[part] + more_ref[0, part] + more_ref[1, part] + more_ref[2, part]
                rows = slice(part * T, part * T + T)
                inv = to_col(inv_row)[:, 0:1]
                mean = to_col(dots / deep)[:, 0:1]
                parts.append(inv * (gain * value[rows] - hat[rows] * mean))
            value = jnp.concatenate(parts, axis=0)
        held_ref[pl.ds(pl.multiple_of(step * size, size), size), :] = value.astype(BF16)

    @pl.when(step >= many)
    def _():
        base = ((step - many) * size).astype(F32)
        row = lax.broadcasted_iota(jnp.int32, (size, T), 0).astype(F32) + base
        picks = jnp.concatenate([(row == order_ref[j].astype(F32)).astype(F32).astype(BF16) for j in range(order_ref.shape[0])], axis=1)
        out_ref[...] = dot(picks, held_ref[...]).astype(BF16)


def gate_kernel(width, moves, g_ref, wo_ref, y_ref, z_ref, gain_ref, mask_ref, ss_ref, yg_ref, dz_ref, dy_ref, gg_ref, rd_ref, held, co_held, got_ss, got_co, sems, local_sems):
    step = pl.program_id(0)
    many = pl.num_programs(0) // 2
    size = y_ref.shape[0]
    parts = size // T
    others = got_ss.shape[0]
    peers, copies = make_moves(moves, (ss_ref, co_held), (got_ss, got_co), sems, local_sems)
    gain = gain_ref[...][None]

    @pl.when(step == 0)
    def _():
        gg_ref[...] = jnp.zeros_like(gg_ref)
        greet(peers)
        for copy in copies[:others]:
            copy.start()

    @pl.when(step < many)
    def _():
        dyn = dot(g_ref[...], wo_ref[...])
        for part in range(parts):
            rows = slice(part * T, part * T + T)
            mask = to_col(mask_ref[part])[:, 0:1]
            own = dyn[rows] * mask
            held[step, rows] = own.astype(BF16)
            z = z_ref[rows].astype(F32)
            w = y_ref[rows].astype(F32) * z * sigmoid(z)
            co_held[step * parts + part] = to_row(jnp.sum(own * w * gain, axis=1, keepdims=True))

    @pl.when(step == many - 1)
    def _():
        for copy in copies[others:]:
            copy.start()

    @pl.when(step == many)
    def _():
        for copy in copies:
            copy.wait()

    @pl.when(step >= many)
    def _():
        for part in range(parts):
            rows = slice(part * T, part * T + T)
            block = step - many
            here = block * parts + part
            ss, co = ss_ref[here], co_held[here]
            for other in range(others):
                ss, co = ss + got_ss[other, here], co + got_co[other, here]
            mask = to_col(mask_ref[part])[:, 0:1]
            inv_row = lax.rsqrt(ss / width + EPS)
            inv = to_col(inv_row)[:, 0:1]
            cube = to_col(inv_row * inv_row * inv_row * (co / width))[:, 0:1]
            y = y_ref[rows].astype(F32)
            z = z_ref[rows].astype(F32)
            dyn = held[block, rows].astype(F32)
            s = sigmoid(z)
            act = z * s
            w = y * act
            wi = w * inv
            yg_ref[rows] = (wi * gain * mask).astype(BF16)
            gg_ref[0:1] += jnp.sum(dyn * wi, axis=0, keepdims=True)
            dw = inv * gain * dyn - w * cube
            dy_ref[rows] = (dw * act).astype(BF16)
            dz = dw * y * (s * (1.0 + z * (1.0 - s)))
            dz_ref[rows] = dz.astype(BF16)
            rd_ref[part] = to_row(jnp.sum(dz * z, axis=1, keepdims=True))


def backward_kernel(heads, extra, moves, dy_ref, x_ref, c_ref, cb_ref, ubd_ref, st_ref, par_ref, pbc_ref, head_ref, *refs):
    count = len(moves)
    srcs, refs = refs[:count], refs[count + extra :]
    dx_ref, dbd_ref, rd_ref, gx_ref, gb_ref, gh_ref = refs[:6]
    dsts, refs = refs[6 : 6 + count], refs[6 + count :]
    d_state, ext_x, ext_b, rows_ref, prod, edy_ref, tail_ref = refs[:7]
    if moves:
        began = (pl.program_id(0) == 0) & (pl.program_id(1) == 0)
        ended = (pl.program_id(0) == pl.num_programs(0) - 1) & (pl.program_id(1) == pl.num_programs(1) - 1)
        background(began, ended, moves, srcs, dsts, *refs[7:])
    first = (pl.program_id(0) == 0) & (pl.program_id(1) == 0)

    @pl.when(first)
    def _():
        gx_ref[...] = jnp.zeros_like(gx_ref)
        gb_ref[...] = jnp.zeros_like(gb_ref)
        gh_ref[...] = jnp.zeros_like(gh_ref)
        rows_ref[...] = jnp.zeros_like(rows_ref)

    @pl.when(pl.program_id(1) == 0)
    def _():
        ext_x[T : T + 8] = jnp.zeros_like(ext_x[T : T + 8])
        ext_b[T : T + 8] = jnp.zeros_like(ext_b[T : T + 8])
        d_state[...] = jnp.zeros_like(d_state)

    row, col = iotas(T, T)
    low = col < HEAD
    low_row = lax.broadcasted_iota(jnp.int32, (1, 128), 1) < HEAD
    upto = col >= row
    below = row < col
    reach = (row >= col).astype(BF16)
    ubd = ubd_ref[...]
    raw, steps, rates, logs = step_terms(ubd, head_ref, heads)
    logs_t = logs.T
    cb = cb_ref[...]
    sb = sigmoid(cb)
    bc = cb * sb
    b_low, c_low = bc[:, :N].astype(BF16), bc[:, N:].astype(BF16)
    c_t = bc[:, N:].T.astype(BF16)
    scores = dot_nt(b_low, c_low)
    entering = st_ref[0]
    outer = dot(c_low, entering)
    ds_low = d_state[...].astype(BF16)
    back = dot(b_low, ds_low)
    d_scores = jnp.zeros((T, T), F32)
    skip_parts, closing_parts = [], []
    for pair in range(heads // 2):
        span = slice(128 * pair, 128 * pair + 128)
        h0, h1 = 2 * pair, 2 * pair + 1
        log0, log1 = lanes(logs, h0), lanes(logs, h1)
        log_pair = jnp.where(low, log0, log1)
        step_pair = jnp.where(low, lanes(steps, h0), lanes(steps, h1))
        last_pair = log_pair[T - 1 : T]
        skip_pair = jnp.where(low_row, lanes(head_ref[2:3], h0), lanes(head_ref[2:3], h1))
        cp = c_ref[:, span].astype(F32)
        sp = sigmoid(cp)
        xp = cp * sp
        xd = xp * step_pair
        dy_low = dy_ref[:, span]
        dy = dy_low.astype(F32)
        decay0 = jnp.exp(jnp.where(upto, logs_t[h0 : h0 + 1] - log0, NEG))
        decay1 = jnp.exp(jnp.where(upto, logs_t[h1 : h1 + 1] - log1, NEG))
        m0, m1 = scores * decay0, scores * decay1
        zero = jnp.zeros_like(dy_low)
        x_stack = jnp.concatenate([jnp.where(low, xd, 0.0).astype(BF16), jnp.where(low, 0.0, xd).astype(BF16)], axis=0)
        dm = dot_nt(x_stack, dy_low)
        dm0, dm1 = dm[:T], dm[T:]
        d_scores = d_scores + dm0 * decay0 + dm1 * decay1
        dy_stack = jnp.concatenate([jnp.where(low, dy, 0.0).astype(BF16), jnp.where(low, 0.0, dy).astype(BF16)], axis=0)
        dxd = dot(jnp.concatenate([m0.astype(BF16), m1.astype(BF16)], axis=1), dy_stack)
        flow = jnp.concatenate([(dm0 * m0).astype(BF16), (dm1 * m1).astype(BF16)], axis=0)
        later = dot(flow, reach)
        rows_ref[h0 : h0 + 1] = jnp.sum(jnp.where(below, later[:T], 0.0), axis=0, keepdims=True)
        rows_ref[h1 : h1 + 1] = jnp.sum(jnp.where(below, later[T:], 0.0), axis=0, keepdims=True)
        grow = jnp.exp(log_pair)
        tail = jnp.exp(last_pair - log_pair)
        from_state = tail * back[:, span]
        dxd = dxd + from_state
        edy = grow * dy
        prod[0:T, span] = (edy * outer[:, span]).astype(BF16)
        prod[T : 2 * T, span] = (from_state * xd).astype(BF16)
        prod[2 * T : 3 * T, span] = (xp * dxd).astype(BF16)
        skip_parts.append(jnp.sum(xp * dy, axis=0, keepdims=True))
        edy_low = edy.astype(BF16)
        edy_ref[:, span] = edy_low
        tail_ref[:, span] = (tail * xd).astype(BF16)
        old = d_state[:, span]
        closing = jnp.exp(last_pair)
        closing_parts.append(closing * jnp.sum(old * entering[:, span].astype(F32), axis=0, keepdims=True))
        d_state[:, span] = closing * old + dot(c_t, edy_low)
        dx = dxd * step_pair + skip_pair * dy
        ext_x[0:T, span] = dx * (sp * (1.0 + cp * (1.0 - sp)))
    d_low = d_scores.astype(BF16)
    d_b = dot_nt(tail_ref[...], ds_low) + dot(d_low, c_low)
    d_c = dot_nt(edy_ref[...], entering) + dot(d_scores.T.astype(BF16), b_low)
    width = heads * HEAD
    lane_row, lane_col = iotas(width, 128)
    member = (lane_row // HEAD == lane_col).astype(BF16)
    sums = dot(prod[...], member)
    skip_all = jnp.concatenate(skip_parts, axis=1)
    closing_all = jnp.concatenate(closing_parts, axis=1)
    fill = jnp.zeros((6, width), F32)
    few = dot_exact(jnp.concatenate([skip_all, closing_all, fill], axis=0), member.astype(F32))
    d_logs = dot(upto.astype(BF16), sums[:T].astype(BF16)) + dot((col < row).astype(BF16), sums[T : 2 * T].astype(BF16))
    d_logs = d_logs + rows_ref[...].T + few[1:2]
    d_steps = sums[2 * T :] + rates * d_logs
    d_raw = jnp.where(col < heads, d_steps * sigmoid(raw), 0.0)
    gh_ref[0:1] += jnp.sum(d_raw, axis=0, keepdims=True)
    gh_ref[1:2] += rates * jnp.sum(steps * d_logs, axis=0, keepdims=True)
    gh_ref[2:3] += few[0:1]
    ext_b[0:T, 0:N] = d_b * (sb[:, :N] * (1.0 + cb[:, :N] * (1.0 - sb[:, :N])))
    ext_b[0:T, N:] = d_c * (sb[:, N:] * (1.0 + cb[:, N:] * (1.0 - sb[:, N:])))

    def conv_back(ext, values, taps, grads):
        now = ext[0:T]
        total = taps[3:4] * now
        grads[3:4] += jnp.sum(values * now, axis=0, keepdims=True)
        grads[4:5] += jnp.sum(now, axis=0, keepdims=True)
        for k in range(3):
            moved = ext[3 - k : 3 - k + T]
            total = total + taps[k : k + 1] * moved
            grads[k : k + 1] += jnp.sum(values * moved, axis=0, keepdims=True)
        ext[T : T + 8] = ext[0:8]
        return total

    ux = x_ref[...].astype(F32)
    dux = conv_back(ext_x, ux, par_ref, gx_ref)
    dx_ref[...] = dux.astype(BF16)
    ubc = ubd[:, : 2 * N]
    dubc = conv_back(ext_b, ubc, pbc_ref, gb_ref)
    dbd_ref[:, : 2 * N] = dubc.astype(BF16)
    dbd_ref[:, 2 * N :] = d_raw.astype(BF16)
    total = jnp.sum(dux * ux, axis=1, keepdims=True) + jnp.sum(dubc * ubc, axis=1, keepdims=True)
    total = total + jnp.sum(jnp.where(col < heads, d_raw * ubd[:, 2 * N :], 0.0), axis=1, keepdims=True)
    rd_ref[0] = to_row(total)


def params(*semantics, number=0):
    if number:
        return pltpu.CompilerParams(
            dimension_semantics=semantics, vmem_limit_bytes=LIMIT, collective_id=number, has_side_effects=True
        )
    return pltpu.CompilerParams(dimension_semantics=semantics, vmem_limit_bytes=LIMIT)


def run_forward(heads, u_zx, u_bd, par, pbc, hp, w_out, before, number):
    rows, width = u_zx.shape[0], heads * HEAD
    slots, chunks = rows // LEN, LEN // T
    at = lambda s, i: (s * chunks + i, 0)
    fixed = lambda s, i: (0, 0)
    size = lax.axis_size("dp")
    anywhere = pl.BlockSpec(memory_space=pl.ANY)
    return pl.pallas_call(
        functools.partial(forward_kernel, heads, slots * chunks),
        grid=(slots, chunks),
        in_specs=[
            pl.BlockSpec((T, width), lambda s, i: (s * chunks + i, 1)),
            pl.BlockSpec((T, width), at),
            pl.BlockSpec((T, 3 * N), at),
            pl.BlockSpec((5, width), fixed),
            pl.BlockSpec((5, 2 * N), fixed),
            pl.BlockSpec((3, heads), fixed),
            anywhere,
            anywhere,
        ],
        out_specs=[
            pl.BlockSpec((T, width), at),
            pl.BlockSpec((1, 1, T), lambda s, i: (s * chunks + i, 0, 0)),
            pl.BlockSpec((T, width), at),
            pl.BlockSpec((T, 2 * N), at),
            pl.BlockSpec((1, N, width), lambda s, i: (s * chunks + i, 0, 0)),
            anywhere,
        ],
        out_shape=[
            jax.ShapeDtypeStruct((rows, width), BF16),
            jax.ShapeDtypeStruct((rows // T, 1, T), F32),
            jax.ShapeDtypeStruct((rows, width), BF16),
            jax.ShapeDtypeStruct((rows, 2 * N), F32),
            jax.ShapeDtypeStruct((rows // T, N, width), BF16),
            full_shape(size, w_out),
        ],
        scratch_shapes=[
            pltpu.VMEM((T + 8, width), F32),
            pltpu.VMEM((T + 8, 2 * N), F32),
            pltpu.VMEM((N, width), F32),
        ]
        + weight_scratch(size, w_out),
        input_output_aliases={7: 5},
        compiler_params=params("arbitrary", "arbitrary", number=number),
        cost_estimate=pl.CostEstimate(flops=rows * width * 2 * 1200, bytes_accessed=rows * width * 8, transcendentals=rows * width * 6),
        name="scan_forward",
    )(u_zx, u_zx, u_bd, par, pbc, hp, cut_shard(w_out), before)


def run_project(heads, x, w_in, w_out, number):
    rows, deep = x.shape
    wide = w_in.shape[1]
    width = 2 * heads * HEAD
    size = lax.axis_size("dp")
    step = 256
    at = lambda i: (i, 0)
    fixed = lambda i: (0, 0)
    anywhere = pl.BlockSpec(memory_space=pl.ANY)
    thin = pl.BlockSpec((step // T, 1, T), lambda i: (i, 0, 0))
    return pl.pallas_call(
        functools.partial(project_kernel, heads, rows // step),
        grid=(rows // step,),
        in_specs=[pl.BlockSpec((step, deep), at), pl.BlockSpec((deep, wide), fixed), anywhere],
        out_specs=[
            pl.BlockSpec((step, deep), at),
            thin,
            pl.BlockSpec((step, width), at),
            pl.BlockSpec((step, wide - width), at),
            pl.BlockSpec((8, deep), fixed),
            anywhere,
        ],
        out_shape=[
            jax.ShapeDtypeStruct((rows, deep), BF16),
            jax.ShapeDtypeStruct((rows // T, 1, T), F32),
            jax.ShapeDtypeStruct((rows, width), BF16),
            jax.ShapeDtypeStruct((rows, wide - width), F32),
            jax.ShapeDtypeStruct((8, deep), F32),
            full_shape(size, w_out),
        ],
        scratch_shapes=weight_scratch(size, w_out),
        compiler_params=params("arbitrary", number=number),
        cost_estimate=pl.CostEstimate(flops=LIGHT, bytes_accessed=LIGHT, transcendentals=0),
        name="project",
    )(x, w_in, cut_shard(w_out))


def run_home(me, order, sums, extra, deep, name, after=()):
    rows, quarter = sums[0].shape
    step = 512
    many = rows // step
    into = lambda i, m: (jnp.minimum(i, many - 1), 0)
    thin = pl.BlockSpec((step // T, 1, T), lambda i, m: (jnp.minimum(i, many - 1), 0, 0))
    specs = [pl.BlockSpec((rows // T, 1, T), lambda i, m: (0, 0, 0))] + [pl.BlockSpec((step, quarter), into)] * 2
    values = list(sums)
    if extra is not None:
        specs += [pl.BlockSpec((step, quarter), lambda i, m: (jnp.minimum(i, many - 1), m[0])), thin]
        specs += [pl.BlockSpec((8, quarter), lambda i, m: (0, m[0])), thin, thin]
        specs += [pl.BlockSpec((3, step // T, 1, T), lambda i, m: (0, jnp.minimum(i, many - 1), 0, 0))]
        values += list(extra)
    values += list(after)
    specs += [pl.BlockSpec(memory_space=pl.ANY)] * len(after)
    return pl.pallas_call(
        functools.partial(home_kernel, extra is not None, float(deep)),
        grid_spec=pltpu.PrefetchScalarGridSpec(
            num_scalar_prefetch=1,
            grid=(2 * many,),
            in_specs=specs,
            out_specs=pl.BlockSpec((step, quarter), lambda i, m: (jnp.maximum(i - many, 0), 0)),
            scratch_shapes=[pltpu.VMEM((rows, quarter), BF16)],
        ),
        out_shape=jax.ShapeDtypeStruct((rows, quarter), BF16),
        compiler_params=params("arbitrary"),
        cost_estimate=pl.CostEstimate(flops=rows * rows * quarter * 2, bytes_accessed=rows * quarter * 10, transcendentals=0),
        name=name,
    )(me, order, *values)


def run_gate(all_width, grads, w_out, y, u_zx, gain, mask, ss, number):
    rows, width = y.shape
    deep = grads.shape[1]
    step = 256
    many = rows // step
    both = lambda i: (lax.rem(i, many), 0)
    late = lambda i: (jnp.maximum(i - many, 0), 0)
    fixed = lambda i: (0, 0)
    wide, out = pl.BlockSpec((step, width), both), pl.BlockSpec((step, width), late)
    moves = (("spread", "head"), ("spread", "head"))
    others = lax.axis_size("head") - 1
    return pl.pallas_call(
        functools.partial(gate_kernel, float(all_width), moves),
        grid=(2 * many,),
        in_specs=[
            pl.BlockSpec((step, deep), lambda i: (jnp.minimum(i, many - 1), 0)),
            pl.BlockSpec((deep, width), fixed),
            wide,
            wide,
            pl.BlockSpec((width,), lambda i: (0,)),
            pl.BlockSpec((step // T, 1, T), lambda i: (lax.rem(i, many), 0, 0)),
            pl.BlockSpec((rows // T, 1, T), lambda i: (0, 0, 0)),
        ],
        out_specs=[out, out, out, pl.BlockSpec((8, width), fixed), pl.BlockSpec((step // T, 1, T), lambda i: (jnp.maximum(i - many, 0), 0, 0))],
        out_shape=[jax.ShapeDtypeStruct((rows, width), BF16)] * 3
        + [jax.ShapeDtypeStruct((8, width), F32), jax.ShapeDtypeStruct((rows // T, 1, T), F32)],
        scratch_shapes=[pltpu.VMEM((many, step, width), BF16), pltpu.VMEM((rows // T, 1, T), F32)]
        + [pltpu.VMEM((others, rows // T, 1, T), F32)] * 2
        + move_scratch(moves, (ss, ss)),
        compiler_params=params("arbitrary", number=number),
        cost_estimate=pl.CostEstimate(flops=LIGHT, bytes_accessed=LIGHT, transcendentals=0),
        name="gate",
    )(grads, w_out, y, u_zx, gain, mask, ss)


def run_backward(heads, slot, dy, u_zx, c, cb, u_bd, st, par, pbc, hp, before, moves, values, number, after=()):
    rows, width = dy.shape
    chunks = LEN // T
    place = lambda s, i: slot * chunks + chunks - 1 - i
    at = lambda s, i: (place(s, i), 0)
    at3 = lambda s, i: (place(s, i), 0, 0)
    fixed = lambda s, i: (0, 0)
    anywhere = pl.BlockSpec(memory_space=pl.ANY)
    return pl.pallas_call(
        functools.partial(backward_kernel, heads, len(before) + len(after), tuple(moves)),
        grid=(1, chunks),
        in_specs=[
            pl.BlockSpec((T, width), at),
            pl.BlockSpec((T, width), lambda s, i: (place(s, i), 1)),
            pl.BlockSpec((T, width), at),
            pl.BlockSpec((T, 2 * N), at),
            pl.BlockSpec((T, 3 * N), at),
            pl.BlockSpec((1, N, width), at3),
            pl.BlockSpec((5, width), fixed),
            pl.BlockSpec((5, 2 * N), fixed),
            pl.BlockSpec((3, heads), fixed),
        ]
        + [anywhere] * (len(moves) + len(before) + len(after)),
        out_specs=[
            pl.BlockSpec((T, width), at),
            pl.BlockSpec((T, 3 * N), at),
            pl.BlockSpec((1, 1, T), at3),
            pl.BlockSpec((8, width), fixed),
            pl.BlockSpec((8, 2 * N), fixed),
            pl.BlockSpec((8, 128), fixed),
        ]
        + [anywhere] * len(moves),
        out_shape=[
            jax.ShapeDtypeStruct((rows, width), BF16),
            jax.ShapeDtypeStruct((rows, 3 * N), BF16),
            jax.ShapeDtypeStruct((rows // T, 1, T), F32),
            jax.ShapeDtypeStruct((8, width), F32),
            jax.ShapeDtypeStruct((8, 2 * N), F32),
            jax.ShapeDtypeStruct((8, 128), F32),
        ]
        + move_outs(moves, values),
        scratch_shapes=[
            pltpu.VMEM((N, width), F32),
            pltpu.VMEM((T + 8, width), F32),
            pltpu.VMEM((T + 8, 2 * N), F32),
            pltpu.VMEM((128, 128), F32),
            pltpu.VMEM((3 * T, width), BF16),
            pltpu.VMEM((T, width), BF16),
            pltpu.VMEM((T, width), BF16),
        ]
        + move_scratch(moves, values),
        input_output_aliases={9 + len(moves) + i: i for i in range(len(before))},
        compiler_params=params("arbitrary", "arbitrary", number=number),
        cost_estimate=pl.CostEstimate(flops=LIGHT, bytes_accessed=LIGHT, transcendentals=0),
        name="scan_backward",
    )(dy, u_zx, c, cb, u_bd, st, par, pbc, hp, *values, *before, *after)


def pieces_kernel(count, many, moves, extra, *refs):
    total = len(moves)
    values, weight_ref, srcs = refs[:count], refs[count], refs[count + 1 : count + 1 + total]
    refs = refs[count + 1 + total + extra :]
    far_ref, own_ref = refs[:2]
    dsts, refs = refs[2 : 2 + total], refs[2 + total :]
    sent_ref, came_ref, near_sems, joined_ref = refs[:4]
    step = pl.program_id(0)
    rows, quarter = far_ref.shape
    start = 0
    for value in values:
        joined_ref[:, start : start + value.shape[1]] = value[...]
        start += value.shape[1]
    dp, own = lax.axis_index("dp"), lax.axis_index("head")
    near = (dp, own ^ 1)
    peers, copies = make_moves(moves, srcs, dsts, *refs[4:]) if moves else ([], [])

    @pl.when(step == 0)
    def _():
        greet(peers if near_in(moves) else [near] + peers)
        for copy in copies:
            copy.start()

    def product(k):
        at = pl.ds(pl.multiple_of((own ^ k) * quarter, 128), quarter)
        return dot_nt(joined_ref[...], weight_ref[at, :])

    def near_copy(block):
        return pltpu.make_async_remote_copy(
            src_ref=sent_ref.at[block],
            dst_ref=came_ref.at[block],
            send_sem=near_sems.at[0, block],
            recv_sem=near_sems.at[1, block],
            device_id=near,
            device_id_type=MESH,
        )

    @pl.when(step < many)
    def _():
        sent_ref[step, :, :quarter] = product(3).astype(BF16)
        sent_ref[step, :, quarter:] = product(1).astype(BF16)
        near_copy(step).start()

    @pl.when(step >= many)
    def _():
        block = step - many
        far, mine = product(2), product(0)
        near_copy(block).wait_recv()
        far_ref[...] = (far + came_ref[block, :, :quarter].astype(F32)).astype(BF16)
        own_ref[...] = (mine + came_ref[block, :, quarter:].astype(F32)).astype(BF16)

    @pl.when(step == 2 * many - 1)
    def _():
        for block in range(many):
            near_copy(block).wait_send()
        for copy in copies:
            copy.wait()


def near_in(moves):
    return any(move[0] == "spread" and move[1] == "head" for move in moves)


def run_pieces(values, weight, quarter, name, moves, moved, number, after=()):
    rows = values[0].shape[0]
    step = 512
    many = rows // step
    anywhere = pl.BlockSpec(memory_space=pl.ANY)
    specs = [pl.BlockSpec((step, v.shape[1]), lambda i: (lax.rem(i, many), 0)) for v in values]
    specs.append(pl.BlockSpec(weight.shape, lambda i: (0, 0)))
    return pl.pallas_call(
        functools.partial(pieces_kernel, len(values), many, tuple(moves), len(after)),
        grid=(2 * many,),
        in_specs=specs + [anywhere] * (len(moves) + len(after)),
        out_specs=[pl.BlockSpec((step, quarter), lambda i: (jnp.maximum(i - many, 0), 0))] * 2 + [anywhere] * len(moves),
        out_shape=[jax.ShapeDtypeStruct((rows, quarter), BF16)] * 2 + move_outs(moves, moved),
        scratch_shapes=[pltpu.VMEM((many, step, 2 * quarter), BF16)] * 2 + [pltpu.SemaphoreType.DMA((2, many)), pltpu.VMEM((step, weight.shape[1]), BF16)] + move_scratch(moves, moved),
        compiler_params=params("arbitrary", number=number),
        cost_estimate=pl.CostEstimate(flops=LIGHT, bytes_accessed=LIGHT, transcendentals=0),
        name=name,
    )(*values, weight, *moved, *after)


def second_bits(step, last, paired, came, kept, holds, halves, quarters, bit_sems, load_sems):
    me, head = lax.axis_index("dp"), lax.axis_index("head")
    side, mid = me & 1, (me >> 1) & 1
    own = [paired[0].at[:, :, side], paired[1].at[:, mid]]
    loads = [pltpu.make_async_copy(own[i], holds[i], load_sems.at[0, i]) for i in range(2)]
    loads += [pltpu.make_async_copy(came[i], halves[i], load_sems.at[1, i]) for i in range(2)]
    picks, peers = (mid, side), ((me ^ 2, head), (me ^ 1, head))
    sends = [
        pltpu.make_async_remote_copy(
            src_ref=holds[i].at[:, 1 - picks[i]],
            dst_ref=quarters[i],
            send_sem=bit_sems.at[0, i],
            recv_sem=bit_sems.at[1, i],
            device_id=peers[i],
            device_id_type=MESH,
        )
        for i in range(2)
    ]

    @pl.when(step == 0)
    def _():
        for copy in loads:
            copy.start()
        greet(peers)
        for copy in loads:
            copy.wait()
        for i in range(2):
            for j in range(holds[i].shape[0]):
                for k in range(2):
                    holds[i][j, k] = (holds[i][j, k].astype(F32) + halves[i][j, k].astype(F32)).astype(BF16)
            sends[i].start()

    @pl.when(step == last)
    def _():
        for i in range(2):
            sends[i].wait()
            for j in range(holds[i].shape[0]):
                kept[i][j] = (holds[i][j, picks[i]].astype(F32) + quarters[i][j].astype(F32)).astype(BF16)


def grads_kernel(count, parts, extra, reduce, *refs):
    lefts, rights = refs[:count], refs[count : 2 * count]
    paired, came = refs[2 * count : 2 * count + 2], refs[2 * count + 2 : 2 * count + 4]
    refs = refs[2 * count + extra + (4 if reduce else 0) :]
    outs, refs = refs[:count], refs[count:]
    step = pl.program_id(0)
    if reduce:
        second_bits(step, count * parts - 1, paired, came, refs[0:2], refs[2:4], refs[4:6], refs[6:8], refs[8], refs[9])
    for which in range(count):

        @pl.when((step >= which * parts) & (step < (which + 1) * parts))
        def _():
            out = lax.dot_general(lefts[which][...], rights[which][...], (((0,), (0,)), ((), ())), preferred_element_type=F32)
            outs[which][...] = out.astype(BF16)


def run_grads(pairs, name, paired=(), came=(), number=0, after=()):
    rows, deep = pairs[0][0].shape
    step = 512
    parts = deep // step
    count = len(pairs)
    anywhere = pl.BlockSpec(memory_space=pl.ANY)
    into = lambda which: lambda i: jnp.clip(i - which * parts, 0, parts - 1)
    specs = [pl.BlockSpec((rows, step), lambda i, at=into(w): (0, at(i))) for w in range(count)]
    specs += [pl.BlockSpec(right.shape, lambda i: (0, 0)) for _, right in pairs]
    kept = [(p.shape[0], p.shape[3], p.shape[4]) for p in paired]
    twice = [pltpu.VMEM((m, 2, r, c), BF16) for m, r, c in kept]
    sems = pltpu.SemaphoreType.DMA
    return pl.pallas_call(
        functools.partial(grads_kernel, count, parts, len(after), bool(paired)),
        grid=(count * parts,),
        in_specs=specs + [anywhere] * (len(paired) + len(came) + len(after)),
        out_specs=[pl.BlockSpec((step, right.shape[1]), lambda i, at=into(w): (at(i), 0)) for w, (_, right) in enumerate(pairs)]
        + [pl.BlockSpec(shape, lambda i: (0, 0, 0)) for shape in kept],
        out_shape=[jax.ShapeDtypeStruct((deep, right.shape[1]), BF16) for _, right in pairs] + [jax.ShapeDtypeStruct(shape, BF16) for shape in kept],
        scratch_shapes=twice + twice + [pltpu.VMEM(shape, BF16) for shape in kept] + ([sems((2, 2)), sems((2, 2))] if paired else []),
        compiler_params=params("arbitrary", number=number),
        cost_estimate=pl.CostEstimate(flops=LIGHT, bytes_accessed=LIGHT, transcendentals=0),
        name=name,
    )(*[left for left, _ in pairs], *[right for _, right in pairs], *paired, *came, *after)


def last_kernel(moves, *refs):
    count = len(moves)
    srcs, thin_ref, wide_ref, half_ref = refs[:count], *refs[count : count + 3]
    refs = refs[count + 3 :]
    dsts, thin_out, wide_out = refs[:count], refs[count], refs[count + 1]
    thin_own, thin_came, thin_line, wide_own, wide_came, wide_line, load_sems, pair_sems, sems, local_sems = refs[count + 2 :]
    me, head = lax.axis_index("dp"), lax.axis_index("head")
    side, high = me & 1, me >> 1
    many = thin_own.shape[0]
    peers, copies = make_moves(moves, srcs, dsts, sems, local_sems)

    def remote(src, dst, which, slot, peer):
        return pltpu.make_async_remote_copy(
            src_ref=src,
            dst_ref=dst,
            send_sem=pair_sems.at[0, which, slot],
            recv_sem=pair_sems.at[1, which, slot],
            device_id=(peer, head),
            device_id_type=MESH,
        )

    def blocks(own, line, which):
        return [remote(own.at[high ^ j], line.at[j - 1], which, j, me ^ (2 * j)) for j in range(1, many)]

    half = remote(thin_ref.at[:, 1 - side], thin_came, 0, 0, me ^ 1)
    thin_blocks, wide_blocks = blocks(thin_own, thin_line, 0), blocks(wide_own, wide_line, 1)
    loads = [
        pltpu.make_async_copy(wide_ref.at[:, side], wide_own, load_sems.at[0]),
        pltpu.make_async_copy(half_ref, wide_came, load_sems.at[1]),
        pltpu.make_async_copy(thin_ref.at[:, side], thin_own, load_sems.at[2]),
    ]
    for copy in loads:
        copy.start()
    greet(peers)
    half.start()
    for copy in copies:
        copy.start()
    for copy in loads:
        copy.wait()
    for j in range(many):
        wide_own[j] = (wide_own[j].astype(F32) + wide_came[j].astype(F32)).astype(BF16)
    for copy in wide_blocks:
        copy.start()
    half.wait()
    for j in range(many):
        thin_own[j] = (thin_own[j].astype(F32) + thin_came[j].astype(F32)).astype(BF16)
    for copy in thin_blocks:
        copy.start()
    for copy in wide_blocks + thin_blocks:
        copy.wait()
    thin, wide = thin_own[high].astype(F32), wide_own[high].astype(F32)
    for j in range(many - 1):
        thin, wide = thin + thin_line[j].astype(F32), wide + wide_line[j].astype(F32)
    thin_out[...] = thin
    wide_out[...] = wide
    for copy in copies:
        copy.wait()


def run_last(moves, values, thin, wide, half, number):
    many, _, block, slim = thin.shape
    broad = wide.shape[3]
    anywhere = pl.BlockSpec(memory_space=pl.ANY)
    inside = pl.BlockSpec(memory_space=pltpu.VMEM)
    space = lambda count, columns: pltpu.VMEM((count, block, columns), BF16)
    sems = pltpu.SemaphoreType.DMA
    return pl.pallas_call(
        functools.partial(last_kernel, tuple(moves)),
        in_specs=[anywhere] * (len(moves) + 3),
        out_specs=[anywhere] * len(moves) + [inside] * 2,
        out_shape=move_outs(moves, values) + [jax.ShapeDtypeStruct((block, slim), F32), jax.ShapeDtypeStruct((block, broad), F32)],
        scratch_shapes=[space(many, slim), space(many, slim), space(many - 1, slim), space(many, broad), space(many, broad), space(many - 1, broad)]
        + [sems((3,)), sems((2, 2, many))]
        + move_scratch(moves, values),
        compiler_params=pltpu.CompilerParams(collective_id=number, has_side_effects=True, vmem_limit_bytes=LIMIT),
        name="last_exchange",
    )(*values, thin, wide, half)


def row_forward(size, quarter, own_ref, full_ref, sems):
    me, own = lax.axis_index("dp"), lax.axis_index("head")
    columns = lambda head: pl.ds(pl.multiple_of(head * quarter, 128), quarter)

    def copy(src, dst, stage, k, head):
        return pltpu.make_async_remote_copy(
            src_ref=src, dst_ref=dst, send_sem=sems.at[0, stage, k], recv_sem=sems.at[1, stage, k], device_id=(me, head), device_id_type=MESH
        )

    def source(k):
        return full_ref.at[me ^ k, :, columns(own)] if own_ref is None else own_ref.at[me ^ k]

    def far(k):
        return copy(source(k), full_ref.at[me ^ k, :, columns(own)], 0, k, own ^ 2)

    def near(k):
        return copy(source(k), full_ref.at[me ^ k, :, columns(own)], 1, k, own ^ 1)

    def back(k):
        block = full_ref.at[me ^ k, :, columns(own ^ 2)]
        return copy(block, block, 2, k, own ^ 1)

    return far, near, back


def shard_spread(src, dst, across_sems, side_sems):
    me, own = lax.axis_index("dp"), lax.axis_index("head")

    def copy(a, b, sems, part, j, peer):
        return pltpu.make_async_remote_copy(
            src_ref=a, dst_ref=b, send_sem=sems.at[0, part, j], recv_sem=sems.at[1, part, j], device_id=(peer, own), device_id_type=MESH
        )

    def across(part, j):
        return copy(src.at[part], dst.at[me, part], across_sems, part, j, me ^ (2 * j))

    def side(part, j):
        here = dst.at[me ^ (2 * j), part]
        return copy(src.at[part] if j == 0 else here, here, side_sems, part, j, me ^ 1)

    return across, side


def entry_kernel(parts, order_ref, x_ref, g_ref, zx_ref, rest_ref, fx_ref, fg_ref, fw_ref, row_sems, x_sems, g_sems, line_sems, side_sems, local_sems, land, ready, picks, w_held):
    size, block, quarter = x_ref.shape
    line = size // 2
    me, own = lax.axis_index("dp"), lax.axis_index("head")
    spot = me >> 1
    mine = pl.ds(pl.multiple_of(own * quarter, 128), quarter)
    sources, fulls = (x_ref, g_ref), (fx_ref, fg_ref)
    forwards = [row_forward(size, quarter, ready.at[i], fulls[i], sems) for i, sems in enumerate((x_sems, g_sems))]

    def remote(src, dst, sems, slot, peer):
        return pltpu.make_async_remote_copy(
            src_ref=src, dst_ref=dst, send_sem=sems.at[(0,) + slot], recv_sem=sems.at[(1,) + slot], device_id=(peer, own), device_id_type=MESH
        )

    def rows(which, k):
        return remote(sources[which].at[me ^ k], land.at[which, me], row_sems, (which, k), me ^ k)

    def along(way, part, j):
        sign = 1 - 2 * way
        origin = jnp.clip(me - sign * 2 * (j - 1), 0, size - 1)
        peer = jnp.clip(me + sign * 2, 0, size - 1)
        here = fw_ref.at[origin, part]
        return remote(w_held.at[part] if j == 1 else here, here, line_sems, (way, part, j - 1), peer)

    def came(way, part, j):
        sign = 1 - 2 * way
        here = fw_ref.at[jnp.clip(me - sign * 2 * j, 0, size - 1), part]
        return remote(here, here, line_sems, (way, part, j - 1), me)

    def side(way, part, j):
        sign = 1 - 2 * way
        here = fw_ref.at[jnp.clip(me - sign * 2 * j, 0, size - 1), part]
        return remote(w_held.at[part] if j == 0 else here, here, side_sems, (way, part, j), me ^ 1)

    def goes_on(way):
        return spot < line - 1 if way == 0 else spot > 0

    def arrives(way, j):
        return spot >= j if way == 0 else spot < line - j

    into = [pltpu.make_async_copy(sources[i].at[me], land.at[i, me], local_sems.at[i]) for i in range(2)]
    edge = zx_ref.shape[2]
    into.append(pltpu.make_async_copy(zx_ref, w_held.at[:, :, pl.ds(0, edge)], local_sems.at[2]))
    into.append(pltpu.make_async_copy(rest_ref, w_held.at[:, :, pl.ds(edge, rest_ref.shape[2])], local_sems.at[6]))
    held = [pltpu.make_async_copy(ready.at[i], fulls[i].at[:, :, mine], local_sems.at[3 + i]) for i in range(2)]
    held.append(pltpu.make_async_copy(w_held, fw_ref.at[me], local_sems.at[5]))
    for copy in into:
        copy.start()
    greet([(me ^ k, own) for k in range(1, size)] + [(me, own ^ 1), (me, own ^ 2)])
    order = turn_order(size)
    for k in order:
        rows(0, k).start()
    for copy in into:
        copy.wait()
    for part in range(parts):
        side(0, part, 0).start()
    held[2].start()
    for k in order:
        rows(1, k).start()
    total = size * block
    lane = lax.broadcasted_iota(jnp.int32, (T, T), 1).astype(F32)

    def pick(i, carry):
        wanted = to_col(order_ref[i].astype(F32))
        at = pl.ds(pl.multiple_of(i * T, T), T)
        for j in range(total // T):
            picks[at, j * T : j * T + T] = (wanted == lane + float(T * j)).astype(F32).astype(BF16)
        return carry

    lax.fori_loop(0, total // T, pick, 0)

    def arrange(which):
        step = min(512, total)
        for i in range(total // step):
            value = dot(picks[i * step : (i + 1) * step, :], land[which].reshape(total, quarter)).astype(BF16)
            ready[which, i * step // block : (i + 1) * step // block] = value.reshape(step // block, block, quarter)
        held[which].start()
        far, near, _ = forwards[which]
        for k in range(size):
            far(k).start()
            near(k).start()

    def backs(which, some):
        far, _, back = forwards[which]
        for k in some:
            far(k).wait_recv()
            back(k).start()

    for k in order:
        rows(0, k).wait_recv()
    arrange(0)
    for k in order:
        rows(1, k).wait_recv()
    for way in range(2):

        @pl.when(goes_on(way))
        def _():
            for part in range(parts):
                along(way, part, 1).start()

    arrange(1)
    backs(0, range(size))
    for j in range(1, line):
        for part in range(parts):
            if j == line - 1:
                backs(1, range(part * size // parts, (part + 1) * size // parts))
            for way in range(2):

                @pl.when(arrives(way, j))
                def _():
                    came(way, part, j).wait_recv()
                    side(way, part, j).start()

                if j + 1 < line:

                    @pl.when(arrives(way, j) & goes_on(way))
                    def _():
                        along(way, part, j + 1).start()

    for copy in held:
        copy.wait()
    for which in range(2):
        far, near, back = forwards[which]
        for k in range(size):
            near(k).wait()
            back(k).wait()
            far(k).wait_send()
            if k:
                rows(which, k).wait_send()
    for part in range(parts):
        side(0, part, 0).wait()
        for way in range(2):

            @pl.when(goes_on(way))
            def _():
                along(way, part, 1).wait_send()

            for j in range(1, line):

                @pl.when(arrives(way, j))
                def _():
                    side(way, part, j).wait()

                if j + 1 < line:

                    @pl.when(arrives(way, j) & goes_on(way))
                    def _():
                        along(way, part, j + 1).wait_send()


PARTS = 4


def cut_shard(w):
    return w.reshape(PARTS, w.shape[0] // PARTS, w.shape[1])


def full_shape(size, w):
    return jax.ShapeDtypeStruct((size, PARTS, w.shape[0] // PARTS, w.shape[1]), BF16)


def run_entry(order, tokens, cotangent, w_zx, w_rest, number):
    size = lax.axis_size("dp")
    shard, wide = w_zx.shape[0], w_zx.shape[1] + w_rest.shape[1]
    rows, quarter = tokens.shape
    block = rows // size
    line = size // 2
    anywhere = pl.BlockSpec(memory_space=pl.ANY)
    sems = pltpu.SemaphoreType.DMA
    full = jax.ShapeDtypeStruct((size, block, quarter * 4), BF16)
    came_x, came_g, came_w = pl.pallas_call(
        functools.partial(entry_kernel, PARTS),
        in_specs=[pl.BlockSpec(memory_space=pltpu.VMEM)] + [anywhere] * 4,
        out_specs=[anywhere] * 3,
        out_shape=[full, full, jax.ShapeDtypeStruct((size, PARTS, shard // PARTS, wide), BF16)],
        scratch_shapes=[
            sems((2, 2, size)),
            sems((2, 3, size)),
            sems((2, 3, size)),
            sems((2, 2, PARTS, line)),
            sems((2, 2, PARTS, line)),
            sems((7,)),
            pltpu.VMEM((2, size, block, quarter), BF16),
            pltpu.VMEM((2, size, block, quarter), BF16),
            pltpu.VMEM((rows, rows), BF16),
            pltpu.VMEM((PARTS, shard // PARTS, wide), BF16),
        ],
        compiler_params=pltpu.CompilerParams(collective_id=number, has_side_effects=True, vmem_limit_bytes=LIMIT),
        name="entry",
    )(order, tokens.reshape(size, block, quarter), cotangent.reshape(size, block, quarter), cut_shard(w_zx), cut_shard(w_rest))
    return came_x.reshape(rows, quarter * 4), came_g.reshape(rows, quarter * 4), came_w.reshape(size * shard, wide)


def mm(a, b, contract, kind):
    return lax.dot_general(a, b, (contract, ((), ())), preferred_element_type=F32).astype(kind)


def body(tokens, cotangent, order, lengths, norm_gain, w_zx, w_bc, w_dt, w_out, conv_x, conv_bc, head_params, gate_gain):
    rows, quarter = tokens.shape
    heads = head_params.shape[1]
    width = heads * HEAD
    me = lax.axis_index("head").astype(jnp.int32).reshape(1)
    size = lax.axis_size("dp")
    here = lax.axis_index("dp")
    all_width = width * lax.axis_size("head")
    deep = quarter * lax.axis_size("head")
    own_w = w_zx.shape[0]
    arrange = order.reshape(rows // T, 1, T)

    rest = jnp.concatenate([w_bc, w_dt, norm_gain[:, None], jnp.zeros((own_w, 127 - heads), BF16)], axis=1)
    blocks = lambda value: value.reshape(size, rows // size, quarter)
    full_x, full_g, w_in = run_entry(arrange, tokens, cotangent, w_zx.reshape(own_w, 2 * width), rest, 1)
    normed, inv_one, u_zx, u_bd, gain, w_o = run_project(heads, full_x, w_in, w_out, 2)

    gated = gate_gain
    hp = head_params
    positions = lax.broadcasted_iota(jnp.int32, (lengths.shape[0], LEN), 1)
    mask = (positions < lengths[:, None]).astype(F32).reshape(rows // T, 1, T)

    y, ss, c, cb, st, w_o = run_forward(heads, u_zx, u_bd, conv_x, conv_bc, hp, w_out, w_o, 3)
    w_o = w_o.reshape(deep, width)
    yg, dz, dy, gg, rd_z = run_gate(all_width, full_g, w_o, y, u_zx, gated, mask, ss, 4)

    def total(kept, came, shift):
        own = lax.dynamic_index_in_dim(kept, here >> shift, 0, keepdims=False)
        return own.astype(F32) + jnp.sum(came.astype(F32), axis=0)

    def pairs(grads):
        return grads.reshape(size // 2, 2, own_w, grads.shape[1])

    def fours(grads):
        return grads.reshape(size // 4, 2, -1, own_w, grads.shape[-1])

    scan = functools.partial(run_backward, heads)
    shared = (dy, u_zx, c, cb, u_bd, st, conv_x, conv_bc, hp)
    out_far, out_own = run_pieces([yg], w_o, quarter, "branch_pieces", [], [], 5)
    out_arrived = lax.ppermute(out_far, "head", [(i, i ^ 2) for i in range(lax.axis_size("head"))])
    grad_o, grad_z = run_grads([(full_g, yg), (normed, dz)], "gate_grads", after=[out_far])
    grad_o, grad_z = pairs(grad_o), fours(grad_z)
    def other_half(paired, bit):
        send = lax.dynamic_index_in_dim(paired, 1 - ((here >> bit) & 1), 1, keepdims=False)
        return send, lax.ppermute(send, "dp", [(i, i ^ (1 << bit)) for i in range(size)])

    send_o, came_o = other_half(grad_o, 0)
    send_z, came_z = other_half(grad_z, 1)
    *back0, gx0, gb0, gh0 = scan(0, *shared, (), [], [], 0, [send_o, send_z])
    sent_out = run_home(me, arrange, [out_own, out_arrived], None, deep, "home_out", [back0[0], came_o, came_z])
    got_out = lax.all_to_all(sent_out, "dp", split_axis=0, concat_axis=0, tiled=True)
    *back1, gx1, gb1, gh1 = scan(1, *shared, back0, [], [], 0, [sent_out])
    dux, dbd, rd_x = back1
    grad_x, grad_bd, kept_o, kept_z = run_grads(
        [(normed, dux), (normed, dbd)], "scan_grads", [fours(grad_o), grad_z], [came_o.reshape(came_z.shape), came_z], 8
    )
    grad_x, grad_bd = pairs(grad_x), pairs(grad_bd)
    gb = gb0 + gb1
    d_far, d_own, line_o, line_z, came_x2, got_rows, got_gb = run_pieces(
        [dz, dux, dbd],
        w_in,
        quarter,
        "input_pieces",
        [("direct", "dp", 2), ("direct", "dp", 2), ("half", "dp", 0), ("spread", "head"), ("spread", "head")],
        [kept_o, kept_z, grad_x, rd_z + rd_x, gb],
        9,
        [got_out],
    )
    gb = gb[:5] + jnp.sum(got_gb, axis=0)[:5]
    gh = gh0 + gh1
    ends = jnp.concatenate([gb[3], gb[4]] + [gh[i, :32] for i in range(3)] + [jnp.zeros((width - 4 * N - 96,), F32)])
    small = jnp.concatenate([(gx0 + gx1)[:5], gg[:1], jnp.concatenate([gb[0], gb[1], gb[2]])[None], ends[None]], axis=0)
    d_arrived, got_small, grad_bd, grad_x = run_last([("whole", "head", 2), ("spread", "dp")], [d_far, small], grad_bd, grad_x, came_x2, 10)

    sent_back = run_home(me, arrange, [d_own, d_arrived], [normed, inv_one, gain, rd_z, rd_x, got_rows], deep, "home_back")
    got_back = lax.all_to_all(sent_back, "dp", split_axis=0, concat_axis=0, tiled=True)
    final_out = (tokens.astype(F32) + got_out.astype(F32)).astype(BF16)
    final_back = (cotangent.astype(F32) + got_back.astype(F32)).astype(BF16)

    grad_out, grad_z = total(kept_o, line_o, 2), total(kept_z, line_z, 2)
    small = small + jnp.sum(got_small, axis=0)
    grad_zx = jnp.stack([grad_z, grad_x], axis=1)
    of_gain = jnp.sum(grad_z * w_zx[:, 0].astype(F32), axis=1) + jnp.sum(grad_x * w_zx[:, 1].astype(F32), axis=1)
    of_gain = of_gain + jnp.sum(grad_bd[:, : 2 * N] * w_bc.astype(F32), axis=1)
    of_gain = of_gain + jnp.sum(grad_bd[:, 2 * N : 2 * N + heads] * w_dt.astype(F32), axis=1)
    last = jnp.concatenate([grad_bd[:, : 2 * N], jnp.broadcast_to(of_gain[:, None], (own_w, 128))], axis=1)
    others, = run_exchange([("spread", "head")], [last], 11)
    last = last + jnp.sum(others, axis=0)
    grad_gain = last[:, 2 * N] / norm_gain.astype(F32)
    gx, gg = small[0:5], small[5]
    gb = jnp.concatenate([small[6].reshape(3, 2 * N), small[7, : 4 * N].reshape(2, 2 * N)], axis=0)
    gh = small[7, 4 * N : 4 * N + 96].reshape(3, 32)[:, :heads]
    return (final_out, final_back, grad_gain, grad_zx, last[:, : 2 * N], grad_bd[:, 2 * N : 2 * N + heads], grad_out, gx, gb, gh, gg)


def solution(mesh):
    return jax.shard_map(
        body,
        mesh=mesh,
        in_specs=(
            P("dp", "head"),
            P("dp", "head"),
            P("dp", None),
            P("dp"),
            P("dp"),
            P("dp", None, "head"),
            P("dp", None),
            P("dp", "head"),
            P("dp", "head"),
            P(None, "head"),
            P(),
            P(None, "head"),
            P("head"),
        ),
        out_specs=(
            P("dp", "head"),
            P("dp", "head"),
            P("dp"),
            P("dp", None, "head"),
            P("dp", None),
            P("dp", "head"),
            P("dp", "head"),
            P(None, "head"),
            P(),
            P(None, "head"),
            P("head"),
        ),
        check_vma=False,
    )
```
